32 devices in a mesh: section: 2 (over core), head: 4 (over z), wide: 4 (over y, x).
Axes of the slice: x: 2, y: 2, z: 4, core: 2. Of those that a mesh axis runs over, the one named last changes fastest.
Arguments:
- inputs: bfloat16 [4, 1024, 1536], P(None, ('head', 'wide')), may hold values from -6 to 6
- cotangent: bfloat16 [4, 1024, 1536], P(None, ('head', 'wide')), may hold values from -6 to 6
- norm_gains: float32 [2, 2, 1536], P('section'), may hold values from 0.5 to 1.5
- qkv_weight: bfloat16 [2, 1536, 2048], P('section', ('head', 'wide')), may hold values from -0.15625 to 0.15625
- qkv_bias: float32 [2, 2048], P('section'), may hold values from -3 to 3
- out_weight: bfloat16 [2, 1536, 1536], P('section', ('head', 'wide')), may hold values from -0.625 to 0.625
- gate_weight: bfloat16 [2, 1536, 8960], P('section', ('head', 'wide')), may hold values from -0.15625 to 0.15625
- up_weight: bfloat16 [2, 1536, 8960], P('section', ('head', 'wide')), may hold values from -0.15625 to 0.15625
- down_weight: bfloat16 [2, 1536, 8960], P('section', ('head', 'wide')), may hold values from -0.0625 to 0.0625
Outputs:
- section_outputs: bfloat16 [2, 4, 1024, 1536], P('section', None, ('head', 'wide'))
- input_grads: bfloat16 [2, 4, 1024, 1536], P('section', None, ('head', 'wide'))
- norm_gains_grad: float32 [2, 2, 1536], P('section')
- qkv_weight_grad: float32 [2, 1536, 2048], P('section', ('head', 'wide'))
- qkv_bias_grad: float32 [2, 2048], P('section')
- out_weight_grad: float32 [2, 1536, 1536], P('section', ('head', 'wide'))
- gate_weight_grad: float32 [2, 1536, 8960], P('section', ('head', 'wide'))
- up_weight_grad: float32 [2, 1536, 8960], P('section', ('head', 'wide'))
- down_weight_grad: float32 [2, 1536, 8960], P('section', ('head', 'wide'))
The draws below stay inside these ranges and needn't reach their ends.
All inputs are finite; a program needn't handle non-finite values.
Results may differ from the reference program's by a relative error of at most 0.02.
Values may be sent and summed in bfloat16 or wider, within the bound.
A program may use at most 1.125 GiB of HBM per device.

```python
import jax
import jax.numpy as jnp
from jax import lax

D = 1536
FF = 8960
HEADS = 12
KV = 2
HDIM = 128
MICRO = 4
SECTIONS = 2
QF = 1536
QKVF = 2048
SEQ = 1024
N_HEAD = 4


def raised(entries, own_key, source, target, parts, factor):
    owner, partner = [(jnp.arange(entries.shape[axis_at]) // (entries.shape[axis_at] // parts)).reshape([-1 if axis == axis_at else 1 for axis in range(entries.ndim)]) for axis_at in (source, target)]
    chosen = jax.random.permutation(own_key, parts)[partner]
    strong = (owner == chosen) | (owner == (partner + parts // 2) % parts)
    return jnp.where(strong, factor * entries, entries)


def levels(key, shape, cuts, smallest, high):
    factor_of = 1.0
    for dim, parts in cuts:
        draws = jax.random.uniform(jax.random.fold_in(jax.random.fold_in(key, 6), dim), (parts,), jnp.float32, smallest / len(cuts), high / len(cuts))
        factor_of = factor_of * jnp.repeat(jnp.exp(draws), shape[dim] // parts).reshape((-1,) + (1,) * (len(shape) - 1 - dim))
    return factor_of


def gaussian(stream_key, extent, scale, reach, cuts=(), held_as=jnp.bfloat16):
    gain = levels(stream_key, extent, cuts, -0.22, 0.18) if cuts else 1.0
    drawn = jax.random.normal(stream_key, extent, jnp.float32) * scale * gain
    return jnp.minimum(jnp.maximum(drawn, -reach), reach).astype(held_as)


def heavy_noise(rng, extent, width, limit, split, heavy, kind=jnp.bfloat16):
    array = width * jax.random.normal(rng, extent, jnp.float32)
    if split:
        array = array * levels(rng, extent, split, -0.22, 0.18)
    return jnp.clip(raised(array, jax.random.fold_in(rng, 3), *heavy), -limit, limit).astype(kind)


def setup_inputs(seed: int = 0) -> dict:
    keys = jax.random.split(jax.random.key(seed), 10)
    return {
        "inputs": heavy_noise(keys[0], (MICRO, SEQ, D), 1.0, 6.0, ((1, 16),), (1, 2, 16, 2.0)),
        "cotangent": heavy_noise(keys[1], (MICRO, SEQ, D), 1.0, 6.0, ((1, 16),), (1, 2, 16, 2.0)),
        "norm_gains": jnp.clip(1.0 + 0.1 * jax.random.normal(keys[2], (SECTIONS, 2, D), jnp.float32), 0.5, 1.5),
        "qkv_weight": gaussian(keys[3], (SECTIONS, D, QKVF), D ** -0.5, 0.15625, ((0, 2), (1, 16))),
        "qkv_bias": gaussian(keys[4], (SECTIONS, QKVF), 0.5, 3.0, ((0, 2),), jnp.float32),
        "out_weight": gaussian(keys[5], (SECTIONS, QF, D), (QF // 16) ** -0.5, 0.625, ((0, 2), (1, 16))),
        "gate_weight": gaussian(keys[6], (SECTIONS, D, FF), D ** -0.5, 0.15625, ((0, 2), (1, 16))),
        "up_weight": gaussian(keys[7], (SECTIONS, D, FF), D ** -0.5, 0.15625, ((0, 2), (1, 16))),
        "down_weight": gaussian(keys[8], (SECTIONS, D, FF), FF ** -0.5, 0.0625, ((0, 2), (1, 16))),
    }


EPSILON = 1e-06
ROPE_BASE = 1000000.0
HIGHEST = lax.Precision.HIGHEST

@jax.custom_vjp
def low(v):
    return lax.optimization_barrier(v.astype(jnp.bfloat16)).astype(jnp.float32)

@jax.custom_vjp
def low_back(v):
    return v

def low_keep(v):
    return (low(v), None)

def low_pass(kept, grad):
    return (grad,)

def back_keep(v):
    return (v, None)

def back_low(kept, grad):
    return (low(grad),)
low.defvjp(low_keep, low_pass)
low_back.defvjp(back_keep, back_low)

def product(left, right):
    return jnp.dot(left, right, precision=HIGHEST, preferred_element_type=jnp.float32)

def rotary_tables(positions, head_dim):
    half_dim = head_dim // 2
    frequency = ROPE_BASE ** (-jnp.arange(half_dim, dtype=jnp.float32) / half_dim)
    angles = positions[:, None] * frequency[None, :]
    return (jnp.cos(angles)[:, None, :], jnp.sin(angles)[:, None, :])

def rotate_pairs(tensor, cosine, sine_table):
    half_dim = tensor.shape[-1] // 2
    first_half = tensor[..., :half_dim]
    second_half = tensor[..., half_dim:]
    return jnp.concatenate([first_half * cosine - second_half * sine_table, second_half * cosine + first_half * sine_table], -1)

def decoder_layer(layer_in, gain_first, w_qkv, bias_row, w_out, gain_second, w_gate, w_up, w_down):
    length = layer_in.shape[0]
    query_width = HEADS * HDIM
    kv_width = KV * HDIM
    normed = low(layer_in * lax.rsqrt(lax.optimization_barrier(jnp.mean(layer_in * layer_in, -1, keepdims=True)) + EPSILON) * gain_first)
    qkv = low_back(product(normed, w_qkv) + bias_row)
    cosine, sine_table = rotary_tables(jnp.arange(length).astype(jnp.float32), HDIM)
    queries = low_back(low(rotate_pairs(qkv[:, :query_width].reshape(length, HEADS, HDIM), cosine, sine_table)))
    key_heads = low(rotate_pairs(qkv[:, query_width:query_width + kv_width].reshape(length, KV, HDIM), cosine, sine_table))
    value_heads = low(qkv[:, query_width + kv_width:].reshape(length, KV, HDIM))
    slot_rep = N_HEAD // KV
    key_heads = low_back(jnp.repeat(key_heads, slot_rep, axis=1))
    value_heads = low_back(jnp.repeat(value_heads, slot_rep, axis=1))
    group_size = HEADS // N_HEAD
    key_heads = jnp.repeat(key_heads, group_size, axis=1)
    value_heads = jnp.repeat(value_heads, group_size, axis=1)
    positions = jnp.arange(length)
    allowed = positions[:, None] >= positions[None, :]

    def one_head(items):
        query_one, key_one, value_one = items
        scores = low_back(product(query_one, key_one.T) * HDIM ** (-0.5))
        scores = jnp.where(allowed, scores, -1e+30)
        highest = lax.optimization_barrier(jnp.max(scores, -1, keepdims=True))
        weights_exp = jnp.exp(scores - highest)
        probs = low(weights_exp / lax.optimization_barrier(jnp.sum(weights_exp, -1, keepdims=True)))
        return product(probs, value_one)
    head_out = lax.map(jax.checkpoint(one_head), (queries.transpose(1, 0, 2), key_heads.transpose(1, 0, 2), value_heads.transpose(1, 0, 2)))
    attended = low_back(low(head_out.transpose(1, 0, 2).reshape(length, query_width)))
    midway = layer_in + low_back(product(attended, w_out))
    normed2 = low(midway * lax.rsqrt(lax.optimization_barrier(jnp.mean(midway * midway, -1, keepdims=True)) + EPSILON) * gain_second)
    gate_out = low_back(product(normed2, w_gate))
    up_out = low_back(product(normed2, w_up))
    hidden = low(jax.nn.silu(gate_out) * up_out)
    return midway + low_back(product(hidden, w_down.T))

def section_layer(layer_in, params, which):
    gains, w_qkv, biases, w_out, w_gate, w_up, w_down = params
    return decoder_layer(layer_in, gains[which, 0], w_qkv[which], biases[which], w_out[which], gains[which, 1], w_gate[which], w_up[which], w_down[which])

def forward(layer_in, shift_zero, params):
    carried = low_back(low(section_layer(layer_in, params, 0)) + shift_zero)
    return (carried, section_layer(carried, params, 1))

def reference(inputs, cotangent, norm_gains, qkv_weight, qkv_bias, out_weight, gate_weight, up_weight, down_weight):
    params = (norm_gains.astype(jnp.float32), qkv_weight.astype(jnp.float32), qkv_bias.astype(jnp.float32), out_weight.astype(jnp.float32), gate_weight.astype(jnp.float32), up_weight.astype(jnp.float32), down_weight.astype(jnp.float32))

    def one_batch(totals, items):
        layer_in = items[0].astype(jnp.float32)
        out_grad = items[1].astype(jnp.float32)
        outputs, pull = jax.vjp(forward, layer_in, jnp.zeros_like(layer_in), params)
        d_input, d_shift, d_params = pull((jnp.zeros_like(outputs[0]), out_grad))
        totals = jax.tree.map(jnp.add, totals, d_params)
        return (totals, (outputs[0].astype(jnp.bfloat16), outputs[1].astype(jnp.bfloat16), d_input.astype(jnp.bfloat16), d_shift.astype(jnp.bfloat16)))
    zeros = jax.tree.map(jnp.zeros_like, params)
    totals, stacked = lax.scan(one_batch, zeros, (inputs, cotangent))
    section_outputs = jnp.stack([stacked[0], stacked[1]])
    input_grads = jnp.stack([stacked[2], stacked[3]])
    return (section_outputs, input_grads, totals[0], totals[1], totals[2], totals[3], totals[4], totals[5], totals[6])
```

```python
import jax
import jax.numpy as jnp
from jax import lax
from jax.sharding import PartitionSpec as P

HEADS = 12
KV = 2
HDIM = 128


EPSILON = 1e-06
ROPE_BASE = 1000000.0


def passed_along(block, axis, distance):
    devices = range(lax.axis_size(axis))
    route = [(i - distance, i) for i in devices if i - distance in devices]
    return lax.ppermute(block, axis, route)


def rotary_tables(positions, head_dim):
    half_dim = head_dim // 2
    frequency = ROPE_BASE ** (-jnp.arange(half_dim, dtype=jnp.float32) / half_dim)
    angles = positions[:, None] * frequency[None, :]
    return (jnp.cos(angles)[:, None, :], jnp.sin(angles)[:, None, :])


def rotate_pairs(tensor, cosine, sine_table):
    half_dim = tensor.shape[-1] // 2
    first_half = tensor[..., :half_dim]
    second_half = tensor[..., half_dim:]
    return jnp.concatenate(
        [
            first_half * cosine - second_half * sine_table,
            second_half * cosine + first_half * sine_table,
        ],
        -1,
    )


def rotate_back(tensor, cosine, sine_table):
    half_dim = tensor.shape[-1] // 2
    first_half = tensor[..., :half_dim]
    second_half = tensor[..., half_dim:]
    return jnp.concatenate(
        [
            first_half * cosine + second_half * sine_table,
            second_half * cosine - first_half * sine_table,
        ],
        -1,
    )


def contract_last(left, right):
    return lax.dot_general(
        left, right, (((1,), (1,)), ((), ())), preferred_element_type=jnp.float32
    )


def contract_first(left, right):
    return lax.dot_general(
        left, right, (((0,), (0,)), ((), ())), preferred_element_type=jnp.float32
    )


def attention_scores(query_rows, key_value, query_pos, key_pos):
    head_dim = query_rows.shape[1]
    scores = contract_last(query_rows, key_value[:, :head_dim]) * head_dim ** (-0.5)
    return jnp.where(query_pos[:, None] >= key_pos[None, :], scores, -1e30)


def attend_forward(query_rows, key_value, query_pos, key_pos):
    head_dim = query_rows.shape[1]
    scores = attention_scores(query_rows, key_value, query_pos, key_pos)
    highest = jnp.max(scores, -1, keepdims=True)
    weights_exp = jnp.exp(scores - highest)
    partition = jnp.sum(weights_exp, -1, keepdims=True)
    probs_low = (weights_exp / partition).astype(jnp.bfloat16)
    attended = jnp.dot(probs_low, key_value[:, head_dim:], preferred_element_type=jnp.float32)
    return (attended.astype(jnp.bfloat16), highest + jnp.log(partition))


def attend_backward(query_rows, key_value, query_pos, key_pos, log_total, grad_rows):
    head_dim = query_rows.shape[1]
    scaling = head_dim ** (-0.5)
    scores = attention_scores(query_rows, key_value, query_pos, key_pos)
    probs_full = jnp.exp(scores - log_total)
    grad_probs = contract_last(grad_rows, key_value[:, head_dim:])
    row_dot = jnp.sum(probs_full * grad_probs, -1, keepdims=True)
    grad_scores = (probs_full * (grad_probs - row_dot)).astype(jnp.bfloat16)
    grad_query = (
        jnp.dot(grad_scores, key_value[:, :head_dim], preferred_element_type=jnp.float32) * scaling
    )
    grad_key = contract_first(grad_scores, query_rows) * scaling
    grad_value = contract_first(probs_full.astype(jnp.bfloat16), grad_rows)
    return (grad_query, jnp.concatenate([grad_key, grad_value], 1))


def make_terms(operands, factor):
    (
        normed_all,
        dqkv_all,
        attended_all,
        gattn_all,
        normed2_all,
        dgate_all,
        dup_all,
        gmlp_all,
        hidden_all,
    ) = operands
    pairs = [
        (normed_all, dqkv_all),
        (attended_all, gattn_all),
        (normed2_all, dgate_all),
        (normed2_all, dup_all),
        (gmlp_all, hidden_all),
    ]
    scaled_pairs = [
        (left, (right.astype(jnp.float32) * factor).astype(jnp.bfloat16)) for left, right in pairs
    ]

    def weight_terms(start, count):
        pieces = [contract_first(left, right) for left, right in scaled_pairs]
        return jnp.concatenate(pieces, 1)

    return weight_terms


def local_streamed(
    inputs,
    cotangent,
    norm_gains,
    qkv_weight,
    qkv_bias,
    out_weight,
    gate_weight,
    up_weight,
    down_weight,
):
    head_count = lax.axis_size("head")
    wide_count = lax.axis_size("wide")
    section_pos = lax.axis_index("section")
    head_pos = lax.axis_index("head")
    wide_pos = lax.axis_index("wide")
    micro_count, short_len, width = inputs.shape
    group_size = HEADS // head_count
    slot_rep = head_count // KV
    query_width = HEADS * HDIM
    kv_width = KV * HDIM
    local_rows = head_count * short_len
    seq_len = local_rows * wide_count
    gain_first = norm_gains[0, 0]
    gain_second = norm_gains[0, 1]
    bias_row = qkv_bias[0]
    seq_pos = (
        (head_pos * wide_count + wide_pos) * short_len + jnp.arange(short_len, dtype=jnp.int32)
    ).astype(jnp.float32)
    cosine, sine_table = rotary_tables(seq_pos, HDIM)
    local_index = jnp.arange(local_rows, dtype=jnp.int32)
    query_pos = jnp.tile(
        (local_index // short_len * wide_count + wide_pos) * short_len + local_index % short_len,
        group_size,
    )
    key_index = jnp.arange(seq_len, dtype=jnp.int32)
    key_pos = (
        key_index % local_rows // short_len * wide_count + key_index // local_rows
    ) * short_len + key_index % short_len

    def to_rows(packed):
        return (
            packed.reshape(local_rows, group_size, HDIM)
            .transpose(1, 0, 2)
            .reshape(group_size * local_rows, HDIM)
        )

    def from_rows(rows_in):
        return (
            rows_in.reshape(group_size, local_rows, HDIM)
            .transpose(1, 0, 2)
            .reshape(local_rows, 1, group_size * HDIM)
        )

    weights_fwd = (
        lax.all_gather(qkv_weight[0], ("head", "wide"), axis=0, tiled=True),
        lax.all_gather(out_weight[0], ("head", "wide"), axis=0, tiled=True),
        lax.all_gather(gate_weight[0], ("head", "wide"), axis=0, tiled=True),
        lax.all_gather(up_weight[0], ("head", "wide"), axis=0, tiled=True),
        lax.all_gather(down_weight[0], ("head", "wide"), axis=0, tiled=True),
    )
    incoming = jnp.zeros((short_len, width), jnp.bfloat16)
    records = []
    outputs_list = []
    for step_index in range(micro_count + 1):
        own_input = inputs[min(step_index, micro_count - 1)]
        layer_in = jnp.where(section_pos == 0, own_input, incoming).astype(jnp.float32)
        layer_w_qkv, layer_w_out, layer_w_gate, layer_w_up, layer_w_down = weights_fwd
        scale_first = lax.rsqrt(jnp.mean(layer_in * layer_in, -1, keepdims=True) + EPSILON)
        normed = (layer_in * scale_first * gain_first).astype(jnp.bfloat16)
        qkv = jnp.dot(normed, layer_w_qkv, preferred_element_type=jnp.float32) + bias_row
        queries = rotate_pairs(
            qkv[:, :query_width].reshape(short_len, HEADS, HDIM), cosine, sine_table
        ).astype(jnp.bfloat16)
        key_heads = rotate_pairs(
            qkv[:, query_width : query_width + kv_width].reshape(short_len, KV, HDIM),
            cosine,
            sine_table,
        ).astype(jnp.bfloat16)
        value_heads = (
            qkv[:, query_width + kv_width :].reshape(short_len, KV, HDIM).astype(jnp.bfloat16)
        )
        kv_pack = jnp.repeat(jnp.stack([key_heads, value_heads], 2), slot_rep, axis=1).reshape(
            short_len, head_count, 2 * HDIM
        )
        q_pack = queries.reshape(short_len, head_count, group_size * HDIM)
        q_heads = lax.all_to_all(q_pack, "head", split_axis=1, concat_axis=0, tiled=True)
        kv_heads = lax.all_to_all(kv_pack, "head", split_axis=1, concat_axis=0, tiled=True)
        query_rows = to_rows(q_heads)
        kv_local = kv_heads.reshape(local_rows, 2 * HDIM)
        layer_kv_all = lax.all_gather(kv_local, "wide", axis=0, tiled=True)
        out_rows, log_total = attend_forward(query_rows, layer_kv_all, query_pos, key_pos)
        out_seq = lax.all_to_all(
            from_rows(out_rows), "head", split_axis=0, concat_axis=1, tiled=True
        ).reshape(short_len, query_width)
        midway = layer_in + jnp.dot(out_seq, layer_w_out, preferred_element_type=jnp.float32)
        scale_second = lax.rsqrt(jnp.mean(midway * midway, -1, keepdims=True) + EPSILON)
        normed2 = (midway * scale_second * gain_second).astype(jnp.bfloat16)
        layer_gate_out = jnp.dot(normed2, layer_w_gate, preferred_element_type=jnp.float32)
        up_out = jnp.dot(normed2, layer_w_up, preferred_element_type=jnp.float32)
        hidden = (jax.nn.silu(layer_gate_out) * up_out).astype(jnp.bfloat16)
        result = midway + contract_last(hidden, layer_w_down)
        record = {
            "layer_in": layer_in,
            "scale_first": scale_first,
            "normed": normed,
            "query_rows": query_rows,
            "kv_local": kv_local,
            "log_total": log_total,
            "out_seq": out_seq,
            "midway": midway,
            "scale_second": scale_second,
            "normed2": normed2,
            "gate_out": layer_gate_out,
            "up_out": up_out,
            "hidden": hidden,
        }
        result, record = (result, record)
        sent_value = result.astype(jnp.bfloat16)
        records.append(record)
        outputs_list.append(sent_value)
        if step_index < micro_count:
            incoming = passed_along(sent_value, "section", 1)
    stacked_records = jax.tree.map(lambda *arrays: jnp.stack(arrays), *records)
    section_outputs = lax.dynamic_slice_in_dim(
        jnp.stack(outputs_list), section_pos, micro_count, 0
    )[None]
    weights_back = (
        lax.all_gather(qkv_weight[0], ("head", "wide"), axis=0, tiled=True),
        lax.all_gather(out_weight[0], ("head", "wide"), axis=0, tiled=True),
        lax.all_gather(gate_weight[0], ("head", "wide"), axis=0, tiled=True),
        lax.all_gather(up_weight[0], ("head", "wide"), axis=0, tiled=True),
        lax.all_gather(down_weight[0], ("head", "wide"), axis=0, tiled=True),
    )
    owned_rows = qkv_weight.shape[1]
    qkv_cols = qkv_weight.shape[2]
    ff_cols = gate_weight.shape[2]
    incoming_grad = jnp.zeros((short_len, width), jnp.bfloat16)
    small_totals = (
        jnp.zeros((width,), jnp.float32),
        jnp.zeros((width,), jnp.float32),
        jnp.zeros((bias_row.shape[0],), jnp.float32),
    )
    grads_list = []
    kept_list = []
    for step_index in range(micro_count + 1):
        pick = jnp.clip(step_index - 1 + 2 * section_pos, 0, micro_count)
        record = jax.tree.map(
            lambda array: lax.dynamic_index_in_dim(array, pick, 0, keepdims=False), stacked_records
        )
        own_grad = cotangent[min(step_index, micro_count - 1)]
        out_grad = jnp.where(section_pos == 1, own_grad, incoming_grad).astype(jnp.float32)
        w_qkv, w_out, w_gate, w_up, w_down = weights_back
        g_mlp = out_grad.astype(jnp.bfloat16)
        d_hidden = jnp.dot(g_mlp, w_down, preferred_element_type=jnp.float32)
        gate_out = record["gate_out"]
        sigmoid_gate = jax.nn.sigmoid(gate_out)
        d_gate = (
            d_hidden * record["up_out"] * sigmoid_gate * (1.0 + gate_out * (1.0 - sigmoid_gate))
        ).astype(jnp.bfloat16)
        d_up = (d_hidden * gate_out * sigmoid_gate).astype(jnp.bfloat16)
        d_normed2 = contract_last(d_gate, w_gate) + contract_last(d_up, w_up)
        unit_second = record["midway"] * record["scale_second"]
        gain2_grad = jnp.sum(d_normed2 * unit_second, 0)
        dn_second = d_normed2 * gain_second
        d_midway = (
            record["scale_second"]
            * (dn_second - unit_second * jnp.mean(dn_second * unit_second, -1, keepdims=True))
            + out_grad
        )
        g_attn = d_midway.astype(jnp.bfloat16)
        d_out_seq = contract_last(g_attn, w_out).astype(jnp.bfloat16)
        d_out_heads = lax.all_to_all(
            d_out_seq.reshape(short_len, head_count, group_size * HDIM),
            "head",
            split_axis=1,
            concat_axis=0,
            tiled=True,
        )
        kv_all = lax.all_gather(record["kv_local"], "wide", axis=0, tiled=True)
        grad_query, grad_keyval = attend_backward(
            record["query_rows"],
            kv_all,
            query_pos,
            key_pos,
            record["log_total"],
            to_rows(d_out_heads),
        )
        keyval_local = lax.psum_scatter(
            grad_keyval.astype(jnp.bfloat16), "wide", scatter_dimension=0, tiled=True
        )
        q_back = lax.all_to_all(
            from_rows(grad_query.astype(jnp.bfloat16)),
            "head",
            split_axis=0,
            concat_axis=1,
            tiled=True,
        )
        kv_back = lax.all_to_all(
            keyval_local.reshape(local_rows, 1, 2 * HDIM),
            "head",
            split_axis=0,
            concat_axis=1,
            tiled=True,
        )
        d_queries = rotate_back(
            q_back.astype(jnp.float32).reshape(short_len, HEADS, HDIM), cosine, sine_table
        )
        d_kv = jnp.sum(kv_back.astype(jnp.float32).reshape(short_len, KV, slot_rep, 2, HDIM), 2)
        d_keys = rotate_back(d_kv[:, :, 0], cosine, sine_table)
        d_qkv = jnp.concatenate(
            [
                d_queries.reshape(short_len, query_width),
                d_keys.reshape(short_len, kv_width),
                d_kv[:, :, 1].reshape(short_len, kv_width),
            ],
            1,
        ).astype(jnp.bfloat16)
        bias_grad = jnp.sum(d_qkv.astype(jnp.float32), 0)
        d_normed = contract_last(d_qkv, w_qkv)
        unit_first = record["layer_in"] * record["scale_first"]
        gain1_grad = jnp.sum(d_normed * unit_first, 0)
        dn_first = d_normed * gain_first
        d_layer_in = (
            record["scale_first"]
            * (dn_first - unit_first * jnp.mean(dn_first * unit_first, -1, keepdims=True))
            + d_midway
        )
        kept_grads = (
            record["normed"],
            d_qkv,
            record["out_seq"],
            g_attn,
            record["normed2"],
            d_gate,
            d_up,
            g_mlp,
            record["hidden"],
        )
        d_layer_in, kept_grads, small_parts = (
            d_layer_in,
            kept_grads,
            (gain1_grad, gain2_grad, bias_grad),
        )
        is_valid = jnp.where(
            (step_index - 1 + section_pos >= 0) & (step_index - 1 + section_pos < micro_count),
            1.0,
            0.0,
        )
        small_totals = jax.tree.map(
            lambda total_part, new_part: total_part + is_valid * new_part, small_totals, small_parts
        )
        sent_grad = d_layer_in.astype(jnp.bfloat16)
        grads_list.append(sent_grad)
        kept_list.append(kept_grads)
        if step_index < micro_count:
            incoming_grad = passed_along(sent_grad, "section", -1)
    input_grads = lax.dynamic_slice_in_dim(jnp.stack(grads_list), 1 - section_pos, micro_count, 0)[
        None
    ]
    operands = jax.tree.map(
        lambda *arrays: lax.dynamic_slice_in_dim(
            jnp.stack(arrays), 1 - section_pos, micro_count, 0
        ).reshape(micro_count * short_len, arrays[0].shape[1]),
        *kept_list
    )
    terms = lax.psum_scatter(
        make_terms(operands, 1.0)(jnp.int32(0), owned_rows * lax.axis_size(("head", "wide"))),
        ("head", "wide"),
        scatter_dimension=0,
        tiled=True,
    )
    qkv_grad = terms[:, :qkv_cols]
    out_grad_rows = terms[:, qkv_cols : qkv_cols + width]
    gate_grad = terms[:, qkv_cols + width : qkv_cols + width + ff_cols]
    up_grad = terms[:, qkv_cols + width + ff_cols : qkv_cols + width + 2 * ff_cols]
    down_grad = terms[:, qkv_cols + width + 2 * ff_cols :]
    gain1_total, gain2_total, bias_total = lax.psum(
        (small_totals[0], small_totals[1], small_totals[2]), ("head", "wide")
    )
    gains_grad = jnp.stack([gain1_total, gain2_total])[None]
    return (
        section_outputs,
        input_grads,
        gains_grad,
        qkv_grad[None],
        bias_total[None],
        out_grad_rows[None],
        gate_grad[None],
        up_grad[None],
        down_grad[None],
    )


def both_sections(own):
    section = lax.axis_index("section")
    other = lax.ppermute(own, "section", [(0, 1), (1, 0)])
    first = jnp.where(section == 0, own, other)
    second = jnp.where(section == 0, other, own)
    return first, second


def swap_halves(first, second):
    section = lax.axis_index("section")
    keep = jnp.where(section == 0, first, second)
    give = jnp.where(section == 0, second, first)
    return keep, lax.ppermute(give, "section", [(0, 1), (1, 0)])


def gather_group(block):
    return lax.all_gather(block, ("section", "head"), axis=0, tiled=True)


def scatter_group(block):
    return lax.psum_scatter(block, ("section", "head"), scatter_dimension=0, tiled=True)


def head_rows(tensor):
    tokens = tensor.shape[0]
    repeat = HEADS // KV
    return (
        tensor.reshape(tokens, KV, repeat, HDIM)
        .transpose(1, 2, 0, 3)
        .reshape(KV, repeat * tokens, HDIM)
    )


def token_rows(tensor):
    repeat = HEADS // KV
    tokens = tensor.shape[1] // repeat
    return (
        tensor.reshape(KV, repeat, tokens, HDIM)
        .transpose(2, 0, 1, 3)
        .reshape(tokens, HEADS * HDIM)
    )


def attention_forward(queries, keys, values, allowed):
    scores = (
        jnp.einsum("gqd,kgd->gqk", queries, keys, preferred_element_type=jnp.float32)
        * HDIM**-0.5
    )
    scores = jnp.where(allowed[None], scores, -1e30)
    highest = jnp.max(scores, -1, keepdims=True)
    weights_exp = jnp.exp(scores - highest)
    partition = jnp.sum(weights_exp, -1, keepdims=True)
    probs = (weights_exp / partition).astype(jnp.bfloat16)
    attended = jnp.einsum("gqk,kgd->gqd", probs, values, preferred_element_type=jnp.float32)
    return attended.astype(jnp.bfloat16), highest + jnp.log(partition)


def attention_backward(queries, keys, values, allowed, log_total, grads):
    scaling = HDIM**-0.5
    scores = jnp.einsum("gqd,kgd->gqk", queries, keys, preferred_element_type=jnp.float32)
    scores = jnp.where(allowed[None], scores * scaling, -1e30)
    probs = jnp.exp(scores - log_total)
    d_probs = jnp.einsum("gqd,kgd->gqk", grads, values, preferred_element_type=jnp.float32)
    row_dot = jnp.sum(probs * d_probs, -1, keepdims=True)
    d_scores = (probs * (d_probs - row_dot)).astype(jnp.bfloat16)
    d_queries = (
        jnp.einsum("gqk,kgd->gqd", d_scores, keys, preferred_element_type=jnp.float32) * scaling
    )
    d_keys = (
        jnp.einsum("gqk,gqd->kgd", d_scores, queries, preferred_element_type=jnp.float32) * scaling
    )
    d_values = jnp.einsum(
        "gqk,gqd->kgd", probs.astype(jnp.bfloat16), grads, preferred_element_type=jnp.float32
    )
    return d_queries, d_keys, d_values


def local_grouped(
    inputs,
    cotangent,
    norm_gains,
    qkv_weight,
    qkv_bias,
    out_weight,
    gate_weight,
    up_weight,
    down_weight,
):
    head_count = lax.axis_size("head")
    wide_count = lax.axis_size("wide")
    section_count = lax.axis_size("section")
    section = lax.axis_index("section")
    head = lax.axis_index("head")
    micro_count, short_len, width = inputs.shape
    half_len = short_len // section_count
    tokens = wide_count * half_len
    rows = qkv_weight.shape[1]
    query_width = HEADS * HDIM
    kv_width = KV * HDIM
    qkv_cols = qkv_weight.shape[2]
    ff_cols = gate_weight.shape[2]
    parts = section_count * head_count
    part_cols = -(-ff_cols // (parts * 128)) * 128
    padding = parts * part_cols - ff_cols

    attention_own = lax.all_gather(
        jnp.concatenate([qkv_weight[0], out_weight[0]], 1), ("head", "wide"), axis=0, tiled=True
    )
    attention_weights = both_sections(attention_own)

    def column_parts(weight):
        padded = jnp.pad(weight[0], ((0, 0), (0, padding)))
        return padded.reshape(rows, section_count, head_count, part_cols)

    mlp_parts = jnp.concatenate(
        [column_parts(gate_weight), column_parts(up_weight), column_parts(down_weight)], 3
    ).transpose(1, 2, 0, 3)
    kept = jnp.where(section == 0, mlp_parts[0], mlp_parts[1])
    given = jnp.where(section == 0, mlp_parts[1], mlp_parts[0])
    received = lax.ppermute(given, "section", [(0, 1), (1, 0)])
    mlp_weights = []
    for layer in range(section_count):
        shard = jnp.where(section == layer, kept, received)
        shard = lax.all_to_all(shard, "head", split_axis=0, concat_axis=0, tiled=True)
        whole = lax.all_gather(shard, "wide", axis=0)
        mlp_weights.append(whole.transpose(1, 0, 2, 3).reshape(width, 3 * part_cols))

    small = jnp.concatenate([norm_gains[0, 0], norm_gains[0, 1], qkv_bias[0]])
    small = both_sections(small)

    sides = jnp.concatenate(
        [
            lax.dynamic_slice_in_dim(inputs, section * half_len, half_len, 1),
            lax.dynamic_slice_in_dim(cotangent, section * half_len, half_len, 1),
        ],
        1,
    )
    sides = lax.all_to_all(sides, "wide", split_axis=0, concat_axis=0, tiled=True)
    layer_in = sides[:, :half_len].reshape(tokens, width).astype(jnp.float32)
    last_grad = sides[:, half_len:].reshape(tokens, width)

    def positions_of(section_at, head_at):
        block = (head_at * wide_count + jnp.arange(wide_count, dtype=jnp.int32)) * short_len
        inside = section_at * half_len + jnp.arange(half_len, dtype=jnp.int32)
        return (block[:, None] + inside[None, :]).reshape(-1)

    own_pos = positions_of(section, head)
    key_pos = jnp.concatenate(
        [positions_of(at // head_count, at % head_count) for at in range(parts)]
    )
    allowed = jnp.tile(own_pos, HEADS // KV)[:, None] >= key_pos[None, :]
    cosine, sine_table = rotary_tables(own_pos.astype(jnp.float32), HDIM)

    records = []
    outputs_list = []
    for layer in range(section_count):
        gain_first = small[layer][:width]
        gain_second = small[layer][width : 2 * width]
        bias_row = small[layer][2 * width :]
        w_attention = attention_weights[layer]
        w_mlp = mlp_weights[layer]
        scale_first = lax.rsqrt(jnp.mean(layer_in * layer_in, -1, keepdims=True) + EPSILON)
        normed = (layer_in * scale_first * gain_first).astype(jnp.bfloat16)
        qkv = (
            jnp.dot(normed, w_attention[:, :qkv_cols], preferred_element_type=jnp.float32)
            + bias_row
        )
        queries = rotate_pairs(
            qkv[:, :query_width].reshape(tokens, HEADS, HDIM), cosine, sine_table
        ).astype(jnp.bfloat16)
        key_heads = rotate_pairs(
            qkv[:, query_width : query_width + kv_width].reshape(tokens, KV, HDIM),
            cosine,
            sine_table,
        ).astype(jnp.bfloat16)
        keyval = jnp.concatenate(
            [
                key_heads.reshape(tokens, kv_width),
                qkv[:, query_width + kv_width :].astype(jnp.bfloat16),
            ],
            1,
        )
        keyval = gather_group(keyval)
        keys = keyval[:, :kv_width].reshape(-1, KV, HDIM)
        values = keyval[:, kv_width:].reshape(-1, KV, HDIM)
        queries = head_rows(queries)
        attended, log_total = attention_forward(queries, keys, values, allowed)
        attended = token_rows(attended)
        midway = layer_in + jnp.dot(
            attended, w_attention[:, qkv_cols:], preferred_element_type=jnp.float32
        )
        scale_second = lax.rsqrt(jnp.mean(midway * midway, -1, keepdims=True) + EPSILON)
        normed2 = gather_group((midway * scale_second * gain_second).astype(jnp.bfloat16))
        gate_up = jnp.dot(
            normed2, w_mlp[:, : 2 * part_cols], preferred_element_type=jnp.float32
        )
        hidden = (jax.nn.silu(gate_up[:, :part_cols]) * gate_up[:, part_cols:]).astype(
            jnp.bfloat16
        )
        partial = contract_last(hidden, w_mlp[:, 2 * part_cols :]).astype(jnp.bfloat16)
        result = midway + scatter_group(partial).astype(jnp.float32)
        records.append(
            (
                layer_in,
                scale_first,
                normed,
                queries,
                keys,
                values,
                log_total,
                attended,
                midway,
                scale_second,
                normed2,
                gate_up,
                hidden,
            )
        )
        carried = result.astype(jnp.bfloat16)
        outputs_list.append(carried)
        layer_in = carried.astype(jnp.float32)

    out_grad = last_grad
    grads_list = [None] * section_count
    attention_terms = [None] * section_count
    mlp_terms = [None] * section_count
    small_terms = [None] * section_count
    for layer in reversed(range(section_count)):
        gain_first = small[layer][:width]
        gain_second = small[layer][width : 2 * width]
        w_attention = attention_weights[layer]
        w_mlp = mlp_weights[layer]
        (
            layer_in,
            scale_first,
            normed,
            queries,
            keys,
            values,
            log_total,
            attended,
            midway,
            scale_second,
            normed2,
            gate_up,
            hidden,
        ) = records[layer]
        g_mlp = gather_group(out_grad)
        d_hidden = jnp.dot(g_mlp, w_mlp[:, 2 * part_cols :], preferred_element_type=jnp.float32)
        gate_out = gate_up[:, :part_cols]
        up_out = gate_up[:, part_cols:]
        sigmoid_gate = jax.nn.sigmoid(gate_out)
        d_gate = (
            d_hidden * up_out * sigmoid_gate * (1.0 + gate_out * (1.0 - sigmoid_gate))
        ).astype(jnp.bfloat16)
        d_up = (d_hidden * gate_out * sigmoid_gate).astype(jnp.bfloat16)
        d_gate_up = jnp.concatenate([d_gate, d_up], 1)
        d_normed2 = scatter_group(
            contract_last(d_gate_up, w_mlp[:, : 2 * part_cols]).astype(jnp.bfloat16)
        ).astype(jnp.float32)
        mlp_term = jnp.concatenate(
            [
                contract_first(normed2, d_gate_up).astype(jnp.bfloat16),
                contract_first(g_mlp, hidden).astype(jnp.bfloat16),
            ],
            1,
        )
        mlp_terms[layer] = mlp_term
        out_grad = out_grad.astype(jnp.float32)
        unit_second = midway * scale_second
        gain2_grad = jnp.sum(d_normed2 * unit_second, 0)
        dn_second = d_normed2 * gain_second
        d_midway = (
            scale_second
            * (dn_second - unit_second * jnp.mean(dn_second * unit_second, -1, keepdims=True))
            + out_grad
        )
        g_attn = d_midway.astype(jnp.bfloat16)
        d_attended = contract_last(g_attn, w_attention[:, qkv_cols:]).astype(jnp.bfloat16)
        d_queries, d_keys, d_values = attention_backward(
            queries, keys, values, allowed, log_total, head_rows(d_attended)
        )
        d_keyval = scatter_group(
            jnp.concatenate(
                [d_keys.reshape(-1, kv_width), d_values.reshape(-1, kv_width)], 1
            ).astype(jnp.bfloat16)
        ).astype(jnp.float32)
        d_queries = token_rows(d_queries.astype(jnp.bfloat16)).astype(jnp.float32)
        d_queries = rotate_back(d_queries.reshape(tokens, HEADS, HDIM), cosine, sine_table)
        d_keys = rotate_back(d_keyval[:, :kv_width].reshape(tokens, KV, HDIM), cosine, sine_table)
        d_qkv = jnp.concatenate(
            [
                d_queries.reshape(tokens, query_width),
                d_keys.reshape(tokens, kv_width),
                d_keyval[:, kv_width:],
            ],
            1,
        ).astype(jnp.bfloat16)
        bias_grad = jnp.sum(d_qkv.astype(jnp.float32), 0)
        d_normed = contract_last(d_qkv, w_attention[:, :qkv_cols])
        unit_first = layer_in * scale_first
        gain1_grad = jnp.sum(d_normed * unit_first, 0)
        dn_first = d_normed * gain_first
        d_layer_in = (
            scale_first
            * (dn_first - unit_first * jnp.mean(dn_first * unit_first, -1, keepdims=True))
            + d_midway
        )
        attention_terms[layer] = jnp.concatenate([normed, d_qkv, attended, g_attn], 1)
        small_terms[layer] = jnp.concatenate([gain1_grad, gain2_grad, bias_grad])
        out_grad = d_layer_in.astype(jnp.bfloat16)
        grads_list[layer] = out_grad

    attention_pairs = jnp.concatenate(swap_halves(*attention_terms), 0)
    cuts = [width, width + qkv_cols, width + qkv_cols + query_width]
    pair_normed = attention_pairs[:, : cuts[0]]
    pair_dqkv = attention_pairs[:, cuts[0] : cuts[1]]
    pair_attended = attention_pairs[:, cuts[1] : cuts[2]]
    pair_gattn = attention_pairs[:, cuts[2] :]
    attention_grad = jnp.concatenate(
        [
            contract_first(pair_normed, pair_dqkv).astype(jnp.bfloat16),
            contract_first(pair_attended, pair_gattn).astype(jnp.bfloat16),
        ],
        1,
    )
    attention_grad = attention_grad.reshape(head_count, wide_count, rows, -1).transpose(
        1, 0, 2, 3
    )
    attention_grad = lax.psum_scatter(attention_grad, "wide", scatter_dimension=0)
    attention_grad = lax.psum_scatter(attention_grad, "head", scatter_dimension=0)
    attention_grad = attention_grad.astype(jnp.float32)

    mlp_sums = []
    for layer in range(section_count):
        term = mlp_terms[layer].reshape(head_count, wide_count, rows, -1).transpose(1, 0, 2, 3)
        term = lax.psum_scatter(term, "wide", scatter_dimension=0)
        mlp_sums.append(
            lax.all_to_all(term, "head", split_axis=0, concat_axis=0, tiled=True)
        )
    kept, received = swap_halves(*mlp_sums)
    low_part = jnp.where(section == 0, kept, received)
    high_part = jnp.where(section == 0, received, kept)
    mlp_grad = jnp.stack([low_part, high_part]).transpose(2, 0, 1, 3)

    def whole_columns(index):
        piece = mlp_grad[..., index * part_cols : (index + 1) * part_cols]
        return piece.reshape(rows, parts * part_cols)[:, :ff_cols].astype(jnp.float32)

    small_total = lax.psum(jnp.stack(small_terms), ("section", "head", "wide"))
    small_own = lax.dynamic_index_in_dim(small_total, section, 0, keepdims=False)
    gains_grad = small_own[: 2 * width].reshape(1, 2, width)
    bias_grad = small_own[2 * width :][None]

    def back_to_owners(first, second):
        both = jnp.stack([first, second], 1).reshape(wide_count, half_len, 2, width)
        both = lax.all_to_all(both, "wide", split_axis=0, concat_axis=0, tiled=True)
        kept, received = swap_halves(both[:, :, 0], both[:, :, 1])
        low = jnp.where(section == 0, kept, received)
        high = jnp.where(section == 0, received, kept)
        return jnp.concatenate([low, high], 1)[None]

    return (
        back_to_owners(*outputs_list),
        back_to_owners(*grads_list),
        gains_grad,
        attention_grad[None, :, :qkv_cols],
        bias_grad,
        attention_grad[None, :, qkv_cols:],
        whole_columns(0)[None],
        whole_columns(1)[None],
        whole_columns(2)[None],
    )


def local(inputs, *rest):
    if lax.axis_size("wide") == inputs.shape[0] and lax.axis_size("section") == 2:
        return local_grouped(inputs, *rest)
    return local_streamed(inputs, *rest)


def solution(mesh):
    return jax.shard_map(
        local,
        mesh=mesh,
        in_specs=(
            P(None, ("head", "wide"), None),
            P(None, ("head", "wide"), None),
            P("section", None, None),
            P("section", ("head", "wide"), None),
            P("section", None),
            P("section", ("head", "wide"), None),
            P("section", ("head", "wide"), None),
            P("section", ("head", "wide"), None),
            P("section", ("head", "wide"), None),
        ),
        out_specs=(
            P("section", None, ("head", "wide"), None),
            P("section", None, ("head", "wide"), None),
            P("section", None, None),
            P("section", ("head", "wide"), None),
            P("section", None),
            P("section", ("head", "wide"), None),
            P("section", ("head", "wide"), None),
            P("section", ("head", "wide"), None),
            P("section", ("head", "wide"), None),
        ),
        check_vma=False,
    )
```

```python
from typing import NamedTuple

import jax
import jax.numpy as jnp
from jax import lax
from jax.experimental import pallas as pl
from jax.experimental.pallas import tpu as pltpu
from jax.sharding import PartitionSpec as P

HEADS = 12
KV = 2
HDIM = 128


EPSILON = 1e-06
MESH = pl.DeviceIdType.MESH
SECTION = "section"
HEAD = "head"
WIDE = "wide"
ROPE_BASE = 1000000.0


class Record(NamedTuple):
    layer_in: jax.Array
    scale_first: jax.Array
    normed: jax.Array
    query_rows: jax.Array
    kv_local: jax.Array
    log_total: jax.Array
    out_seq: jax.Array
    midway: jax.Array
    scale_second: jax.Array
    normed2: jax.Array
    gate_out: jax.Array
    up_out: jax.Array
    hidden: jax.Array


def passed_along(block, axis, distance):
    devices = range(lax.axis_size(axis))
    route = [(i - distance, i) for i in devices if i - distance in devices]
    return lax.ppermute(block, axis, route)


def rotary_tables(positions, head_dim):
    half_dim = head_dim // 2
    frequency = ROPE_BASE ** (-jnp.arange(half_dim, dtype=jnp.float32) / half_dim)
    angles = positions[:, None] * frequency[None, :]
    return (jnp.cos(angles)[:, None, :], jnp.sin(angles)[:, None, :])


def rotate_pairs(tensor, cosine, sine_table):
    half_dim = tensor.shape[-1] // 2
    first_half = tensor[..., :half_dim]
    second_half = tensor[..., half_dim:]
    return jnp.concatenate(
        [
            first_half * cosine - second_half * sine_table,
            second_half * cosine + first_half * sine_table,
        ],
        -1,
    )


def rotate_back(tensor, cosine, sine_table):
    half_dim = tensor.shape[-1] // 2
    first_half = tensor[..., :half_dim]
    second_half = tensor[..., half_dim:]
    return jnp.concatenate(
        [
            first_half * cosine + second_half * sine_table,
            second_half * cosine - first_half * sine_table,
        ],
        -1,
    )


def contract_last(left, right):
    return lax.dot_general(
        left, right, (((1,), (1,)), ((), ())), preferred_element_type=jnp.float32
    )


def contract_first(left, right):
    return lax.dot_general(
        left, right, (((0,), (0,)), ((), ())), preferred_element_type=jnp.float32
    )


def attention_scores(query_rows, key_value, query_pos, key_pos):
    head_dim = query_rows.shape[1]
    scores = contract_last(query_rows, key_value[:, :head_dim]) * head_dim ** (-0.5)
    return jnp.where(query_pos[:, None] >= key_pos[None, :], scores, -1e30)


def attend_forward(query_rows, key_value, query_pos, key_pos):
    head_dim = query_rows.shape[1]
    scores = attention_scores(query_rows, key_value, query_pos, key_pos)
    highest = jnp.max(scores, -1, keepdims=True)
    weights_exp = jnp.exp(scores - highest)
    partition = jnp.sum(weights_exp, -1, keepdims=True)
    probs_low = (weights_exp / partition).astype(jnp.bfloat16)
    attended = jnp.dot(probs_low, key_value[:, head_dim:], preferred_element_type=jnp.float32)
    return (attended.astype(jnp.bfloat16), highest + jnp.log(partition))


def attend_backward(query_rows, key_value, query_pos, key_pos, log_total, grad_rows):
    head_dim = query_rows.shape[1]
    scaling = head_dim ** (-0.5)
    scores = attention_scores(query_rows, key_value, query_pos, key_pos)
    probs_full = jnp.exp(scores - log_total)
    grad_probs = contract_last(grad_rows, key_value[:, head_dim:])
    row_dot = jnp.sum(probs_full * grad_probs, -1, keepdims=True)
    grad_scores = (probs_full * (grad_probs - row_dot)).astype(jnp.bfloat16)
    grad_query = (
        jnp.dot(grad_scores, key_value[:, :head_dim], preferred_element_type=jnp.float32) * scaling
    )
    grad_key = contract_first(grad_scores, query_rows) * scaling
    grad_value = contract_first(probs_full.astype(jnp.bfloat16), grad_rows)
    return (grad_query, jnp.concatenate([grad_key, grad_value], 1))


def make_terms(operands, factor):
    (
        normed_all,
        dqkv_all,
        attended_all,
        gattn_all,
        normed2_all,
        dgate_all,
        dup_all,
        gmlp_all,
        hidden_all,
    ) = operands
    pairs = [
        (normed_all, dqkv_all),
        (attended_all, gattn_all),
        (normed2_all, dgate_all),
        (normed2_all, dup_all),
        (gmlp_all, hidden_all),
    ]
    scaled_pairs = [
        (left, (right.astype(jnp.float32) * factor).astype(jnp.bfloat16)) for left, right in pairs
    ]

    def weight_terms(start, count):
        pieces = [contract_first(left, right) for left, right in scaled_pairs]
        return jnp.concatenate(pieces, 1)

    return weight_terms


def local_streamed(
    inputs,
    cotangent,
    norm_gains,
    qkv_weight,
    qkv_bias,
    out_weight,
    gate_weight,
    up_weight,
    down_weight,
):
    head_count = lax.axis_size(HEAD)
    wide_count = lax.axis_size(WIDE)
    section_pos = lax.axis_index(SECTION)
    head_pos = lax.axis_index(HEAD)
    wide_pos = lax.axis_index(WIDE)
    micro_count, short_len, width = inputs.shape
    group_size = HEADS // head_count
    slot_rep = head_count // KV
    query_width = HEADS * HDIM
    kv_width = KV * HDIM
    local_rows = head_count * short_len
    seq_len = local_rows * wide_count
    gain_first = norm_gains[0, 0]
    gain_second = norm_gains[0, 1]
    bias_row = qkv_bias[0]
    seq_pos = (
        (head_pos * wide_count + wide_pos) * short_len + jnp.arange(short_len, dtype=jnp.int32)
    ).astype(jnp.float32)
    cosine, sine_table = rotary_tables(seq_pos, HDIM)
    local_index = jnp.arange(local_rows, dtype=jnp.int32)
    query_pos = jnp.tile(
        (local_index // short_len * wide_count + wide_pos) * short_len + local_index % short_len,
        group_size,
    )
    key_index = jnp.arange(seq_len, dtype=jnp.int32)
    key_pos = (
        key_index % local_rows // short_len * wide_count + key_index // local_rows
    ) * short_len + key_index % short_len

    def to_rows(packed):
        return (
            packed.reshape(local_rows, group_size, HDIM)
            .transpose(1, 0, 2)
            .reshape(group_size * local_rows, HDIM)
        )

    def from_rows(rows_in):
        return (
            rows_in.reshape(group_size, local_rows, HDIM)
            .transpose(1, 0, 2)
            .reshape(local_rows, 1, group_size * HDIM)
        )

    weights_fwd = (
        lax.all_gather(qkv_weight[0], (HEAD, WIDE), axis=0, tiled=True),
        lax.all_gather(out_weight[0], (HEAD, WIDE), axis=0, tiled=True),
        lax.all_gather(gate_weight[0], (HEAD, WIDE), axis=0, tiled=True),
        lax.all_gather(up_weight[0], (HEAD, WIDE), axis=0, tiled=True),
        lax.all_gather(down_weight[0], (HEAD, WIDE), axis=0, tiled=True),
    )
    incoming = jnp.zeros((short_len, width), jnp.bfloat16)
    records = []
    outputs_list = []
    for step_index in range(micro_count + 1):
        own_input = inputs[min(step_index, micro_count - 1)]
        layer_in = jnp.where(section_pos == 0, own_input, incoming).astype(jnp.float32)
        layer_w_qkv, layer_w_out, layer_w_gate, layer_w_up, layer_w_down = weights_fwd
        scale_first = lax.rsqrt(jnp.mean(layer_in * layer_in, -1, keepdims=True) + EPSILON)
        normed = (layer_in * scale_first * gain_first).astype(jnp.bfloat16)
        qkv = jnp.dot(normed, layer_w_qkv, preferred_element_type=jnp.float32) + bias_row
        queries = rotate_pairs(
            qkv[:, :query_width].reshape(short_len, HEADS, HDIM), cosine, sine_table
        ).astype(jnp.bfloat16)
        key_heads = rotate_pairs(
            qkv[:, query_width : query_width + kv_width].reshape(short_len, KV, HDIM),
            cosine,
            sine_table,
        ).astype(jnp.bfloat16)
        value_heads = (
            qkv[:, query_width + kv_width :].reshape(short_len, KV, HDIM).astype(jnp.bfloat16)
        )
        kv_pack = jnp.repeat(jnp.stack([key_heads, value_heads], 2), slot_rep, axis=1).reshape(
            short_len, head_count, 2 * HDIM
        )
        q_pack = queries.reshape(short_len, head_count, group_size * HDIM)
        q_heads = lax.all_to_all(q_pack, HEAD, split_axis=1, concat_axis=0, tiled=True)
        kv_heads = lax.all_to_all(kv_pack, HEAD, split_axis=1, concat_axis=0, tiled=True)
        query_rows = to_rows(q_heads)
        kv_local = kv_heads.reshape(local_rows, 2 * HDIM)
        layer_kv_all = lax.all_gather(kv_local, WIDE, axis=0, tiled=True)
        out_rows, log_total = attend_forward(query_rows, layer_kv_all, query_pos, key_pos)
        out_seq = lax.all_to_all(
            from_rows(out_rows), HEAD, split_axis=0, concat_axis=1, tiled=True
        ).reshape(short_len, query_width)
        midway = layer_in + jnp.dot(out_seq, layer_w_out, preferred_element_type=jnp.float32)
        scale_second = lax.rsqrt(jnp.mean(midway * midway, -1, keepdims=True) + EPSILON)
        normed2 = (midway * scale_second * gain_second).astype(jnp.bfloat16)
        layer_gate_out = jnp.dot(normed2, layer_w_gate, preferred_element_type=jnp.float32)
        up_out = jnp.dot(normed2, layer_w_up, preferred_element_type=jnp.float32)
        hidden = (jax.nn.silu(layer_gate_out) * up_out).astype(jnp.bfloat16)
        result = midway + contract_last(hidden, layer_w_down)
        record = Record(
            layer_in=layer_in,
            scale_first=scale_first,
            normed=normed,
            query_rows=query_rows,
            kv_local=kv_local,
            log_total=log_total,
            out_seq=out_seq,
            midway=midway,
            scale_second=scale_second,
            normed2=normed2,
            gate_out=layer_gate_out,
            up_out=up_out,
            hidden=hidden,
        )
        result, record = (result, record)
        sent_value = result.astype(jnp.bfloat16)
        records.append(record)
        outputs_list.append(sent_value)
        if step_index < micro_count:
            incoming = passed_along(sent_value, SECTION, 1)
    stacked_records = jax.tree.map(lambda *arrays: jnp.stack(arrays), *records)
    section_outputs = lax.dynamic_slice_in_dim(
        jnp.stack(outputs_list), section_pos, micro_count, 0
    )[None]
    weights_back = (
        lax.all_gather(qkv_weight[0], (HEAD, WIDE), axis=0, tiled=True),
        lax.all_gather(out_weight[0], (HEAD, WIDE), axis=0, tiled=True),
        lax.all_gather(gate_weight[0], (HEAD, WIDE), axis=0, tiled=True),
        lax.all_gather(up_weight[0], (HEAD, WIDE), axis=0, tiled=True),
        lax.all_gather(down_weight[0], (HEAD, WIDE), axis=0, tiled=True),
    )
    owned_rows = qkv_weight.shape[1]
    qkv_cols = qkv_weight.shape[2]
    ff_cols = gate_weight.shape[2]
    incoming_grad = jnp.zeros((short_len, width), jnp.bfloat16)
    small_totals = (
        jnp.zeros((width,), jnp.float32),
        jnp.zeros((width,), jnp.float32),
        jnp.zeros((bias_row.shape[0],), jnp.float32),
    )
    grads_list = []
    kept_list = []
    for step_index in range(micro_count + 1):
        pick = jnp.clip(step_index - 1 + 2 * section_pos, 0, micro_count)
        record = jax.tree.map(
            lambda array: lax.dynamic_index_in_dim(array, pick, 0, keepdims=False), stacked_records
        )
        own_grad = cotangent[min(step_index, micro_count - 1)]
        out_grad = jnp.where(section_pos == 1, own_grad, incoming_grad).astype(jnp.float32)
        w_qkv, w_out, w_gate, w_up, w_down = weights_back
        g_mlp = out_grad.astype(jnp.bfloat16)
        d_hidden = jnp.dot(g_mlp, w_down, preferred_element_type=jnp.float32)
        gate_out = record.gate_out
        sigmoid_gate = jax.nn.sigmoid(gate_out)
        d_gate = (
            d_hidden * record.up_out * sigmoid_gate * (1.0 + gate_out * (1.0 - sigmoid_gate))
        ).astype(jnp.bfloat16)
        d_up = (d_hidden * gate_out * sigmoid_gate).astype(jnp.bfloat16)
        d_normed2 = contract_last(d_gate, w_gate) + contract_last(d_up, w_up)
        unit_second = record.midway * record.scale_second
        gain2_grad = jnp.sum(d_normed2 * unit_second, 0)
        dn_second = d_normed2 * gain_second
        d_midway = (
            record.scale_second
            * (dn_second - unit_second * jnp.mean(dn_second * unit_second, -1, keepdims=True))
            + out_grad
        )
        g_attn = d_midway.astype(jnp.bfloat16)
        d_out_seq = contract_last(g_attn, w_out).astype(jnp.bfloat16)
        d_out_heads = lax.all_to_all(
            d_out_seq.reshape(short_len, head_count, group_size * HDIM),
            HEAD,
            split_axis=1,
            concat_axis=0,
            tiled=True,
        )
        kv_all = lax.all_gather(record.kv_local, WIDE, axis=0, tiled=True)
        grad_query, grad_keyval = attend_backward(
            record.query_rows,
            kv_all,
            query_pos,
            key_pos,
            record.log_total,
            to_rows(d_out_heads),
        )
        keyval_local = lax.psum_scatter(
            grad_keyval.astype(jnp.bfloat16), WIDE, scatter_dimension=0, tiled=True
        )
        q_back = lax.all_to_all(
            from_rows(grad_query.astype(jnp.bfloat16)),
            HEAD,
            split_axis=0,
            concat_axis=1,
            tiled=True,
        )
        kv_back = lax.all_to_all(
            keyval_local.reshape(local_rows, 1, 2 * HDIM),
            HEAD,
            split_axis=0,
            concat_axis=1,
            tiled=True,
        )
        d_queries = rotate_back(
            q_back.astype(jnp.float32).reshape(short_len, HEADS, HDIM), cosine, sine_table
        )
        d_kv = jnp.sum(kv_back.astype(jnp.float32).reshape(short_len, KV, slot_rep, 2, HDIM), 2)
        d_keys = rotate_back(d_kv[:, :, 0], cosine, sine_table)
        d_qkv = jnp.concatenate(
            [
                d_queries.reshape(short_len, query_width),
                d_keys.reshape(short_len, kv_width),
                d_kv[:, :, 1].reshape(short_len, kv_width),
            ],
            1,
        ).astype(jnp.bfloat16)
        bias_grad = jnp.sum(d_qkv.astype(jnp.float32), 0)
        d_normed = contract_last(d_qkv, w_qkv)
        unit_first = record.layer_in * record.scale_first
        gain1_grad = jnp.sum(d_normed * unit_first, 0)
        dn_first = d_normed * gain_first
        d_layer_in = (
            record.scale_first
            * (dn_first - unit_first * jnp.mean(dn_first * unit_first, -1, keepdims=True))
            + d_midway
        )
        kept_grads = (
            record.normed,
            d_qkv,
            record.out_seq,
            g_attn,
            record.normed2,
            d_gate,
            d_up,
            g_mlp,
            record.hidden,
        )
        d_layer_in, kept_grads, small_parts = (
            d_layer_in,
            kept_grads,
            (gain1_grad, gain2_grad, bias_grad),
        )
        is_valid = jnp.where(
            (step_index - 1 + section_pos >= 0) & (step_index - 1 + section_pos < micro_count),
            1.0,
            0.0,
        )
        small_totals = jax.tree.map(
            lambda total_part, new_part: total_part + is_valid * new_part, small_totals, small_parts
        )
        sent_grad = d_layer_in.astype(jnp.bfloat16)
        grads_list.append(sent_grad)
        kept_list.append(kept_grads)
        if step_index < micro_count:
            incoming_grad = passed_along(sent_grad, SECTION, -1)
    input_grads = lax.dynamic_slice_in_dim(jnp.stack(grads_list), 1 - section_pos, micro_count, 0)[
        None
    ]
    operands = jax.tree.map(
        lambda *arrays: lax.dynamic_slice_in_dim(
            jnp.stack(arrays), 1 - section_pos, micro_count, 0
        ).reshape(micro_count * short_len, arrays[0].shape[1]),
        *kept_list
    )
    terms = lax.psum_scatter(
        make_terms(operands, 1.0)(jnp.int32(0), owned_rows * lax.axis_size((HEAD, WIDE))),
        (HEAD, WIDE),
        scatter_dimension=0,
        tiled=True,
    )
    qkv_grad = terms[:, :qkv_cols]
    out_grad_rows = terms[:, qkv_cols : qkv_cols + width]
    gate_grad = terms[:, qkv_cols + width : qkv_cols + width + ff_cols]
    up_grad = terms[:, qkv_cols + width + ff_cols : qkv_cols + width + 2 * ff_cols]
    down_grad = terms[:, qkv_cols + width + 2 * ff_cols :]
    gain1_total, gain2_total, bias_total = lax.psum(
        (small_totals[0], small_totals[1], small_totals[2]), (HEAD, WIDE)
    )
    gains_grad = jnp.stack([gain1_total, gain2_total])[None]
    return (
        section_outputs,
        input_grads,
        gains_grad,
        qkv_grad[None],
        bias_total[None],
        out_grad_rows[None],
        gate_grad[None],
        up_grad[None],
        down_grad[None],
    )


def both_sections(own):
    section = lax.axis_index(SECTION)
    other = lax.ppermute(own, SECTION, [(0, 1), (1, 0)])
    first = jnp.where(section == 0, own, other)
    second = jnp.where(section == 0, other, own)
    return first, second


def greet_line():
    section, head = lax.axis_index(SECTION), lax.axis_index(HEAD)
    last = lax.axis_size(HEAD) - 1
    barrier = pltpu.get_barrier_semaphore()
    pl.semaphore_signal(barrier, 1, device_id={SECTION: 1 - section}, device_id_type=MESH)

    @pl.when(head > 0)
    def _():
        pl.semaphore_signal(barrier, 1, device_id={HEAD: head - 1}, device_id_type=MESH)

    @pl.when(head < last)
    def _():
        pl.semaphore_signal(barrier, 1, device_id={HEAD: head + 1}, device_id_type=MESH)

    pl.semaphore_wait(barrier, 1 + jnp.minimum(head, 1) + jnp.minimum(last - head, 1))


def gather_kernel(block, out, local_sem, pair_send, pair_recv, line_send, line_recv):
    section, head = lax.axis_index(SECTION), lax.axis_index(HEAD)
    heads = lax.axis_size(HEAD)
    tokens = block.shape[0]

    def place(section_at, head_at):
        start = (section_at * heads + head_at) * tokens
        return out.at[pl.ds(pl.multiple_of(start, tokens), tokens)]

    def pair(number, head_at, source):
        return pltpu.make_async_remote_copy(
            source,
            place(section, head_at),
            pair_send.at[number],
            pair_recv.at[number],
            device_id={SECTION: 1 - section},
            device_id_type=MESH,
        )

    def line(way, hop, source):
        step = 1 if way == 0 else -1
        return pltpu.make_async_remote_copy(
            source,
            place(section, head - step * hop),
            line_send.at[way, hop],
            line_recv.at[way, hop],
            device_id={HEAD: head + step},
            device_id_type=MESH,
        )

    greet_line()
    ways = ((0, head < heads - 1), (1, head > 0))
    for way, go in ways:

        @pl.when(go)
        def _(way=way):
            line(way, 0, block).start()

    pair(0, head, block).start()
    own = pltpu.make_async_copy(block, place(section, head), local_sem)
    own.start()

    def arrivals(hop):
        yield 0, head - hop, head >= hop, head < heads - 1
        yield 1, head + hop, head + hop < heads, head > 0

    for hop in range(1, heads):
        for way, origin, comes, goes in arrivals(hop):

            @pl.when(comes)
            def _(way=way, origin=origin, goes=goes, hop=hop):
                here = place(section, origin)
                line(way, hop - 1, here).wait_recv()

                @pl.when(goes)
                def _():
                    line(way, hop, here).start()

                pair(2 * hop - 1 + way, origin, here).start()

    own.wait()
    pair(0, head, block).wait_send()
    pltpu.make_async_copy(place(1 - section, head), place(1 - section, head), pair_recv.at[0]).wait()
    for way, go in ways:

        @pl.when(go)
        def _(way=way):
            line(way, 0, block).wait_send()

    for hop in range(1, heads):
        for way, origin, comes, goes in arrivals(hop):

            @pl.when(comes)
            def _(way=way, origin=origin, goes=goes, hop=hop):
                here = place(section, origin)
                there = place(1 - section, origin)
                number = 2 * hop - 1 + way

                @pl.when(goes)
                def _():
                    line(way, hop, here).wait_send()

                pair(number, origin, here).wait_send()
                pltpu.make_async_copy(there, there, pair_recv.at[number]).wait()


def gather_group(block, number):
    heads = lax.axis_size(HEAD)
    tokens, columns = block.shape
    return pl.pallas_call(
        gather_kernel,
        out_shape=jax.ShapeDtypeStruct((2 * heads * tokens, columns), block.dtype),
        in_specs=[pl.BlockSpec(memory_space=pltpu.VMEM)],
        out_specs=pl.BlockSpec(memory_space=pltpu.VMEM),
        scratch_shapes=[
            pltpu.SemaphoreType.DMA,
            pltpu.SemaphoreType.DMA((2 * heads - 1,)),
            pltpu.SemaphoreType.DMA((2 * heads - 1,)),
            pltpu.SemaphoreType.DMA((2, heads)),
            pltpu.SemaphoreType.DMA((2, heads)),
        ],
        compiler_params=pltpu.CompilerParams(
            collective_id=number, has_side_effects=True, vmem_limit_bytes=32 * 2**20
        ),
    )(block)


def scatter_kernel(
    partial, out, sums, pair_buf, line_buf, pair_send, pair_recv, line_send, line_recv
):
    section, head = lax.axis_index(SECTION), lax.axis_index(HEAD)
    heads = lax.axis_size(HEAD)
    tokens = out.shape[0]

    def rows(section_at, head_at):
        start = (section_at * heads + head_at) * tokens
        return pl.ds(pl.multiple_of(start, tokens), tokens)

    def pair(target):
        return pltpu.make_async_remote_copy(
            partial.at[rows(1 - section, target)],
            pair_buf.at[target],
            pair_send.at[target],
            pair_recv.at[target],
            device_id={SECTION: 1 - section},
            device_id_type=MESH,
        )

    def line(way, target):
        step = 1 if way == 0 else -1
        return pltpu.make_async_remote_copy(
            sums.at[target],
            line_buf.at[way, target],
            line_send.at[way, target],
            line_recv.at[way, target],
            device_id={HEAD: head + step},
            device_id_type=MESH,
        )

    greet_line()
    order = []
    for at in range(heads // 2):
        order += [heads - 1 - at, at]
    for target in order:
        pair(target).start()
    for target in order:
        pair(target).wait_recv()
        sums[target] = (
            partial[rows(section, target)].astype(jnp.float32)
            + pair_buf[target].astype(jnp.float32)
        ).astype(sums.dtype)
        if target > 0:

            @pl.when(head == 0)
            def _(target=target):
                line(0, target).start()

        if target < heads - 1:

            @pl.when(head == heads - 1)
            def _(target=target):
                line(1, target).start()

    def pass_on(way, target):
        line(way, target).wait_recv()
        sums[target] = (
            sums[target].astype(jnp.float32) + line_buf[way, target].astype(jnp.float32)
        ).astype(sums.dtype)
        line(way, target).start()

    for at in range(heads - 1):
        right, left = heads - 1 - at, at

        @pl.when((head > 0) & (head < right))
        def _(right=right):
            pass_on(0, right)

        @pl.when((head < heads - 1) & (head > left))
        def _(left=left):
            pass_on(1, left)

    for target in range(heads):

        @pl.when(head == target)
        def _(target=target):
            total = sums[target].astype(jnp.float32)
            if target > 0:
                line(0, target).wait_recv()
                total = total + line_buf[0, target].astype(jnp.float32)
            if target < heads - 1:
                line(1, target).wait_recv()
                total = total + line_buf[1, target].astype(jnp.float32)
            out[...] = total

        pair(target).wait_send()

        @pl.when(head < target)
        def _(target=target):
            line(0, target).wait_send()

        @pl.when(head > target)
        def _(target=target):
            line(1, target).wait_send()


def scatter_group(partial, number):
    heads = lax.axis_size(HEAD)
    tokens = partial.shape[0] // (2 * heads)
    columns = partial.shape[1]
    return pl.pallas_call(
        scatter_kernel,
        out_shape=jax.ShapeDtypeStruct((tokens, columns), jnp.float32),
        in_specs=[pl.BlockSpec(memory_space=pltpu.VMEM)],
        out_specs=pl.BlockSpec(memory_space=pltpu.VMEM),
        scratch_shapes=[
            pltpu.VMEM((heads, tokens, columns), partial.dtype),
            pltpu.VMEM((heads, tokens, columns), partial.dtype),
            pltpu.VMEM((2, heads, tokens, columns), partial.dtype),
            pltpu.SemaphoreType.DMA((heads,)),
            pltpu.SemaphoreType.DMA((heads,)),
            pltpu.SemaphoreType.DMA((2, heads)),
            pltpu.SemaphoreType.DMA((2, heads)),
        ],
        compiler_params=pltpu.CompilerParams(
            collective_id=number, has_side_effects=True, vmem_limit_bytes=48 * 2**20
        ),
    )(partial)


def greet_all(heads):
    section, head, wide = (lax.axis_index(axis) for axis in (SECTION, HEAD, WIDE))
    barrier = pltpu.get_barrier_semaphore()
    partners = [{SECTION: 1 - section}, {WIDE: beside(wide, 0)}, {WIDE: beside(wide, 1)}]
    partners += [{HEAD: lax.rem(head + shift, heads)} for shift in range(1, heads)]
    for partner in partners:
        pl.semaphore_signal(barrier, 1, device_id=partner, device_id_type=MESH)
    pl.semaphore_wait(barrier, len(partners))


def beside(wide, axis):
    low, high = lax.rem(wide, 2), lax.div(wide, 2)
    if axis == 0:
        return high * 2 + (1 - low)
    if axis == 1:
        return (1 - high) * 2 + low
    return (1 - high) * 2 + (1 - low)


def start_kernel(
    qkv_own,
    out_own,
    parts,
    qkv_all,
    out_all,
    first_all,
    second_parts,
    given_first,
    given_second,
    local_sem,
    swap_sem,
    shift_sem,
    line_sem,
    wide_sem,
    half_sem,
    pair_sem,
):
    section, head, wide = (lax.axis_index(axis) for axis in (SECTION, HEAD, WIDE))
    heads, wides = lax.axis_size(HEAD), lax.axis_size(WIDE)
    rows = qkv_own.shape[0]
    half = rows // 2
    owns = (qkv_own, out_own)
    here = [beside(wide, 0), beside(wide, 1), beside(wide, 2)]

    def place(which, layer, head_at, wide_at, start=0, count=None):
        block = head_at * wides + wide_at if which == 1 else wide_at * heads + head_at
        first = pl.multiple_of(block * rows + start, 16)
        span = pl.ds(first, rows if count is None else count)
        return first_all.at[span] if which == 2 else (qkv_all, out_all)[which].at[layer, span]

    def remote(source, target, sems, at, partner):
        return pltpu.make_async_remote_copy(
            source,
            target,
            sems.at[(0,) + at],
            sems.at[(1,) + at],
            device_id=partner,
            device_id_type=MESH,
        )

    other = {SECTION: 1 - section}

    def line(which, way, hop):
        step = 1 if way == 0 else -1
        target = place(which, section, head - step * hop, wide)
        source = owns[which] if hop == 0 else target
        return remote(source, target, line_sem, (which, way, hop), {HEAD: head + step})

    def across(which, axis, number, origin):
        target = place(which, section, origin, wide)
        source = owns[which] if number == 0 and which < 2 else target
        return remote(source, target, wide_sem, (which, axis, number), {WIDE: here[axis]})

    def across_in(which, axis, number, origin):
        target = place(which, section, origin, here[axis])
        return remote(target, target, wide_sem, (which, axis, number), {WIDE: here[axis]})

    def diagonal(which, axis, number, origin):
        target = place(which, section, origin, here[1 - axis], (1 - axis) * half, half)
        return remote(target, target, half_sem, (which, axis, number), {WIDE: here[axis]})

    def diagonal_in(which, axis, number, origin):
        target = place(which, section, origin, here[2], (1 - axis) * half, half)
        return remote(target, target, half_sem, (which, axis, number), {WIDE: here[axis]})

    def pair(which, kind, number, origin, layer):
        if kind == 0:
            target = place(which, layer, origin, wide)
        elif kind in (1, 2):
            target = place(which, layer, origin, here[kind - 1])
        else:
            target = place(which, layer, origin, here[2], (4 - kind) * half, half)
        return remote(target, target, pair_sem, (which, kind, number), other)

    def pair_own(which):
        target = place(which, section, head, wide)
        return remote(owns[which], target, pair_sem, (which, 0, 0), other)

    def swap(target):
        return remote(parts.at[1 - section], target, swap_sem, (), other)

    def shift(layer, source, distance):
        target_head = lax.rem(head + distance, heads)
        target = place(2, 0, head, wide) if layer == 0 else second_parts.at[head]
        return remote(
            source.at[target_head], target, shift_sem, (layer, distance), {HEAD: target_head}
        )

    def shift_in(layer, distance):
        origin = lax.rem(head + heads - distance, heads)
        target = place(2, 0, origin, wide) if layer == 0 else second_parts.at[origin]
        return remote(target, target, shift_sem, (layer, distance), {HEAD: head})

    def shift_all(layer, source):
        for distance in range(1, heads):
            shift(layer, source, distance).start()
        target = place(2, 0, head, wide) if layer == 0 else second_parts.at[head]
        pltpu.make_async_copy(source.at[head], target, local_sem.at[2 + layer]).start()

    def shift_own(layer):
        target = place(2, 0, head, wide) if layer == 0 else second_parts.at[head]
        return pltpu.make_async_copy(target, target, local_sem.at[2 + layer])

    greet_all(heads)
    first = section == 0
    second = section == 1

    for which in (0, 1):
        for way, go in ((0, head < heads - 1), (1, head > 0)):

            @pl.when(go)
            def _(which=which, way=way):
                line(which, way, 0).start()

    @pl.when(first)
    def _():
        swap(given_first).start()

    @pl.when(second)
    def _():
        swap(given_second).start()

    locals_ = [
        pltpu.make_async_copy(owns[which], place(which, section, head, wide), local_sem.at[which])
        for which in (0, 1)
    ]
    for which in (0, 1):
        locals_[which].start()
        for axis in (0, 1):
            across(which, axis, 0, head).start()
        pair_own(which).start()

    def each(hop):
        yield 2 * hop - 1, 0, head - hop, head >= hop, head < heads - 1
        yield 2 * hop, 1, head + hop, head + hop < heads, head > 0

    def forward_halves(number, origin):
        for which in (0, 1):
            for axis in (0, 1):
                across_in(which, axis, number, origin).wait_recv()
                diagonal(which, 1 - axis, number, origin).start()
                pair(which, 1 + axis, number, origin, section).start()

    def finish_halves(number, origin):
        for which in (0, 1):
            for axis in (0, 1):
                diagonal_in(which, axis, number, origin).wait_recv()
                pair(which, 3 + axis, number, origin, section).start()

    for hop in range(1, heads):
        for number, way, origin, comes, goes in each(hop):

            @pl.when(comes)
            def _(number=number, way=way, origin=origin, goes=goes, hop=hop):
                for which in (0, 1):
                    arrived = place(which, section, origin, wide)
                    remote(
                        arrived, arrived, line_sem, (which, way, hop - 1), {HEAD: head}
                    ).wait_recv()

                    @pl.when(goes)
                    def _(which=which):
                        line(which, way, hop).start()

                    for axis in (0, 1):
                        across(which, axis, number, origin).start()
                    pair(which, 0, number, origin, section).start()

        if hop == 1:
            forward_halves(0, head)
        else:
            for number, way, origin, comes, goes in each(hop - 1):

                @pl.when(comes)
                def _(number=number, origin=origin):
                    forward_halves(number, origin)

    @pl.when(first)
    def _():
        swap(given_second).wait_recv()
        shift_all(0, parts.at[0])

    @pl.when(second)
    def _():
        swap(given_first).wait_recv()
        shift_all(0, given_first)

    for number, way, origin, comes, goes in each(heads - 1):

        @pl.when(comes)
        def _(number=number, origin=origin):
            forward_halves(number, origin)

    def spread(number):
        for axis in (0, 1):
            across(2, axis, number, lax.rem(head + heads - number, heads)).start()

    shift_own(0).wait()
    spread(0)
    finish_halves(0, head)
    for hop in range(1, heads):
        for number, way, origin, comes, goes in each(hop):

            @pl.when(comes)
            def _(number=number, origin=origin):
                finish_halves(number, origin)

    for distance in range(1, heads):
        shift_in(0, distance).wait_recv()
        spread(distance)

    @pl.when(first)
    def _():
        shift_all(1, given_second)

    @pl.when(second)
    def _():
        shift_all(1, parts.at[1])

    for number in range(heads):
        origin = lax.rem(head + heads - number, heads)
        for axis in (0, 1):
            across_in(2, axis, number, origin).wait_recv()
            diagonal(2, 1 - axis, number, origin).start()

    for number in range(heads):
        origin = lax.rem(head + heads - number, heads)
        for axis in (0, 1):
            diagonal_in(2, axis, number, origin).wait_recv()
            diagonal(2, axis, number, origin).wait_send()
            across(2, axis, number, origin).wait_send()

    def settle(number, origin):
        for which in (0, 1):
            for axis in (0, 1):
                across(which, axis, number, origin).wait_send()
                diagonal(which, axis, number, origin).wait_send()
            for kind in range(5):
                if kind == 0 and number == 0:
                    pair_own(which).wait_send()
                else:
                    pair(which, kind, number, origin, section).wait_send()
                pair(which, kind, number, origin, 1 - section).wait_recv()

    for which in (0, 1):
        locals_[which].wait()
        for way, go in ((0, head < heads - 1), (1, head > 0)):

            @pl.when(go)
            def _(which=which, way=way):
                line(which, way, 0).wait_send()

    settle(0, head)
    for hop in range(1, heads):
        for number, way, origin, comes, goes in each(hop):

            @pl.when(comes)
            def _(number=number, way=way, origin=origin, goes=goes, hop=hop):
                settle(number, origin)

                @pl.when(goes)
                def _():
                    for which in (0, 1):
                        line(which, way, hop).wait_send()

    swap(given_first).wait_send()
    shift_own(1).wait()
    for distance in range(1, heads):
        for layer in (0, 1):
            shift(layer, given_first, distance).wait_send()
        shift_in(1, distance).wait_recv()


def start_weights(qkv_own, out_own, parts, number):
    heads, wides = lax.axis_size(HEAD), lax.axis_size(WIDE)
    rows, qkv_cols = qkv_own.shape
    out_cols = out_own.shape[1]
    numbers = 2 * heads - 1
    whole = heads * wides * rows
    dtype = parts.dtype
    dma = pltpu.SemaphoreType.DMA
    anywhere = pl.BlockSpec(memory_space=pl.ANY)
    return pl.pallas_call(
        start_kernel,
        out_shape=(
            jax.ShapeDtypeStruct((2, whole, qkv_cols), dtype),
            jax.ShapeDtypeStruct((2, whole, out_cols), dtype),
            jax.ShapeDtypeStruct((whole, parts.shape[3]), dtype),
            jax.ShapeDtypeStruct(parts.shape[1:], dtype),
        ),
        in_specs=[anywhere] * 3,
        out_specs=(anywhere,) * 4,
        scratch_shapes=[
            pltpu.VMEM(parts.shape[1:], dtype),
            pltpu.VMEM(parts.shape[1:], dtype),
            dma((4,)),
            dma((2,)),
            dma((2, 2, heads)),
            dma((2, 2, 2, heads)),
            dma((2, 3, 2, numbers)),
            dma((2, 3, 2, numbers)),
            dma((2, 2, 5, numbers)),
        ],
        compiler_params=pltpu.CompilerParams(
            collective_id=number, has_side_effects=True, vmem_limit_bytes=16 * 2**20
        ),
    )(qkv_own, out_own, parts)


def finish_kernel(
    terms,
    small,
    first_parts,
    second_parts,
    second_total,
    tokens_in,
    totals,
    small_total,
    low_parts,
    high_parts,
    tokens_out,
    near_buf,
    middle,
    far_buf,
    sums,
    line_buf,
    small_sum,
    small_buf,
    shifted,
    give,
    local_sem,
    shift_sem,
    swap_sem,
    near_sem,
    far_sem,
    line_sem,
    small_sem,
    give_sem,
    token_sem,
):
    section, head, wide = (lax.axis_index(axis) for axis in (SECTION, HEAD, WIDE))
    heads, wides = lax.axis_size(HEAD), lax.axis_size(WIDE)
    here = [beside(wide, 0), beside(wide, 1), beside(wide, 2)]
    columns = terms.shape[2] // 2
    spans = [pl.ds(0, columns), pl.ds(columns, columns)]
    other = {SECTION: 1 - section}
    first, second = section == 0, section == 1
    sender_rows = tokens_in.shape[2]

    def remote(source, target, sems, at, partner):
        return pltpu.make_async_remote_copy(
            source,
            target,
            sems.at[(0,) + at],
            sems.at[(1,) + at],
            device_id=partner,
            device_id_type=MESH,
        )

    def shift(distance, target):
        target_head = lax.rem(head + distance, heads)
        return remote(
            first_parts.at[target_head],
            target.at[head],
            shift_sem,
            (distance,),
            {HEAD: target_head},
        )

    def shift_in(distance, target):
        arrived = target.at[lax.rem(head + heads - distance, heads)]
        return remote(arrived, arrived, shift_sem, (distance,), {HEAD: head})

    def near(side, turn, target):
        wide_at = here[side] if turn == 0 else here[2]
        return remote(
            terms.at[wide_at * heads + target, :, spans[side]],
            near_buf.at[side, turn, target],
            near_sem,
            (side, turn, target),
            {WIDE: here[side]},
        )

    def far(side, target):
        return remote(
            middle.at[side, target],
            far_buf.at[side, target],
            far_sem,
            (side, target),
            {WIDE: here[1 - side]},
        )

    def line(way, target):
        step = 1 if way == 0 else -1
        return remote(
            sums.at[target],
            line_buf.at[way, target],
            line_sem,
            (way, target),
            {HEAD: head + step},
        )

    def token_target(layer, which, sender_wide, sender_section):
        first_row = pl.multiple_of(sender_section * sender_rows, 16)
        return tokens_out.at[which, sender_wide, pl.ds(first_row, sender_rows)]

    def token(layer, which, turn):
        wide_at = wide if turn == 3 else here[turn]
        sems = (token_sem.at[0, layer, which, turn], token_sem.at[1, section, which, turn])
        return pltpu.make_async_remote_copy(
            tokens_in.at[which * 2 + layer, wide_at],
            token_target(layer, which, wide, section),
            *sems,
            device_id={SECTION: layer, WIDE: wide_at},
            device_id_type=MESH,
        )

    def token_in(from_section, which, turn):
        wide_at = wide if turn == 3 else here[turn]
        target = token_target(section, which, wide_at, from_section)
        sems = (token_sem.at[0, section, which, turn], token_sem.at[1, from_section, which, turn])
        return pltpu.make_async_remote_copy(
            target, target, *sems, device_id={HEAD: head}, device_id_type=MESH
        )

    barrier = pltpu.get_barrier_semaphore()
    partners = [other] + [{WIDE: wide_at} for wide_at in here]
    partners += [{SECTION: 1 - section, WIDE: wide_at} for wide_at in here]
    partners += [{HEAD: lax.rem(head + distance, heads)} for distance in range(1, heads)]
    for partner in partners:
        pl.semaphore_signal(barrier, 1, device_id=partner, device_id_type=MESH)
    pl.semaphore_wait(barrier, len(partners))

    order = []
    for at in range(heads // 2):
        order += [heads - 1 - at, at]

    def start_near(target):
        for turn in (1, 0):
            for side in (0, 1):
                near(side, turn, target).start()

    start_near(order[0])
    start_near(order[1])

    @pl.when(first)
    def _():
        for distance in range(1, heads):
            shift(distance, low_parts).start()
        remote(second_parts, low_parts, swap_sem, (0,), other).start()
        pltpu.make_async_copy(first_parts.at[head], low_parts.at[head], local_sem.at[0]).start()

    @pl.when(second)
    def _():
        for distance in range(1, heads):
            shift(distance, shifted).start()
        pltpu.make_async_copy(second_parts, high_parts, local_sem.at[1]).start()
        remote(
            first_parts.at[head], high_parts.at[head], swap_sem, (1,), other
        ).start()

    for which in (0, 1):
        for turn in range(4):
            for layer in (0, 1):

                @pl.when((turn < 3) | (section != layer))
                def _(layer=layer, which=which, turn=turn):
                    token(layer, which, turn).start()

        pltpu.make_async_copy(
            tokens_in.at[which * 2 + section, wide],
            token_target(section, which, wide, section),
            local_sem.at[2 + which],
        ).start()

    steps = [other, {WIDE: here[0]}, {WIDE: here[1]}]
    steps += [{HEAD: lax.rem(head + distance, heads)} for distance in range(1, heads)]

    def small_copy(at):
        source = small.at[1 - section] if at == 0 else small_sum.at[min(at, 3)]
        return remote(source, small_buf.at[at], small_sem, (at,), steps[at])

    for at in range(3):
        small_copy(at).start()
        small_copy(at).wait()
        small_sum[at + 1] = (small[section] if at == 0 else small_sum[at]) + small_buf[at]
    for at in range(3, len(steps)):
        small_copy(at).start()

    def across(target):
        for side in (0, 1):
            near(side, 1, target).wait_recv()
            middle[side, target] = (
                terms[here[1 - side] * heads + target, :, spans[side]].astype(jnp.float32)
                + near_buf[side, 1, target].astype(jnp.float32)
            ).astype(middle.dtype)
            far(side, target).start()

    def collect(target):
        for side in (0, 1):
            near(side, 0, target).wait_recv()
            far(side, target).wait_recv()
            sums[target, :, spans[side]] = (
                terms[wide * heads + target, :, spans[side]].astype(jnp.float32)
                + near_buf[side, 0, target].astype(jnp.float32)
                + far_buf[side, target].astype(jnp.float32)
            ).astype(sums.dtype)
        if target > 0:

            @pl.when(head == 0)
            def _():
                line(0, target).start()

        if target < heads - 1:

            @pl.when(head == heads - 1)
            def _():
                line(1, target).start()

    across(order[0])
    for number in range(heads):
        if number + 2 < heads:
            start_near(order[number + 2])
        if number + 1 < heads:
            across(order[number + 1])
        collect(order[number])

    def pass_on(way, target):
        line(way, target).wait_recv()
        sums[target] = (
            sums[target].astype(jnp.float32) + line_buf[way, target].astype(jnp.float32)
        ).astype(sums.dtype)
        line(way, target).start()

    for at in range(heads - 1):
        right, left = heads - 1 - at, at

        @pl.when((head > 0) & (head < right))
        def _(right=right):
            pass_on(0, right)

        @pl.when((head < heads - 1) & (head > left))
        def _(left=left):
            pass_on(1, left)

    @pl.when(second)
    def _():
        for distance in range(1, heads):
            shift_in(distance, shifted).wait_recv()
            origin = lax.rem(head + heads - distance, heads)
            remote(
                shifted.at[origin], high_parts.at[origin], swap_sem, (1 + distance,), other
            ).start()

    whole = small_sum[3]
    for at in range(3, len(steps)):
        small_copy(at).wait()
        whole = whole + small_buf[at]
    small_total[...] = whole

    for target in range(heads):

        @pl.when(head == target)
        def _(target=target):
            value = sums[target].astype(jnp.float32)
            if target > 0:
                line(0, target).wait_recv()
                value = value + line_buf[0, target].astype(jnp.float32)
            if target < heads - 1:
                line(1, target).wait_recv()
                value = value + line_buf[1, target].astype(jnp.float32)
            give[0] = value

        for side in (0, 1):
            for turn in (0, 1):
                near(side, turn, target).wait_send()
            far(side, target).wait_send()

        @pl.when(head < target)
        def _(target=target):
            line(0, target).wait_send()

        @pl.when(head > target)
        def _(target=target):
            line(1, target).wait_send()

    give[1] = second_total[...].astype(jnp.float32)
    handed = remote(give.at[1 - section], totals.at[section], give_sem, (), other)
    handed.start()
    totals[section] = give[section]

    for which in (0, 1):
        pltpu.make_async_copy(
            tokens_in.at[which * 2 + section, wide],
            token_target(section, which, wide, section),
            local_sem.at[2 + which],
        ).wait()
        for turn in range(4):
            for layer in (0, 1):

                @pl.when((turn < 3) | (section != layer))
                def _(layer=layer, which=which, turn=turn):
                    token(layer, which, turn).wait_send()
                    token_in(layer, which, turn).wait_recv()

    @pl.when(first)
    def _():
        for distance in range(1, heads):
            shift(distance, low_parts).wait_send()
            shift_in(distance, low_parts).wait_recv()
        remote(second_parts, low_parts, swap_sem, (0,), other).wait_send()
        pltpu.make_async_copy(first_parts.at[head], low_parts.at[head], local_sem.at[0]).wait()
        for distance in range(heads):
            arrived = high_parts.at[lax.rem(head + heads - distance, heads)]
            remote(arrived, arrived, swap_sem, (1 + distance,), other).wait_recv()

    @pl.when(second)
    def _():
        for distance in range(1, heads):
            shift(distance, shifted).wait_send()
        pltpu.make_async_copy(second_parts, high_parts, local_sem.at[1]).wait()
        for distance in range(heads):
            sent = high_parts.at[lax.rem(head + heads - distance, heads)]
            remote(sent, sent, swap_sem, (1 + distance,), other).wait_send()
        remote(second_parts, low_parts, swap_sem, (0,), other).wait_recv()

    handed.wait_send()
    remote(totals.at[1 - section], totals.at[1 - section], give_sem, (), other).wait_recv()


def finish_weights(terms, small, first_parts, second_parts, second_total, tokens_in, number):
    heads = lax.axis_size(HEAD)
    blocks, rows, columns = terms.shape
    half = columns // 2
    dtype = terms.dtype
    dma = pltpu.SemaphoreType.DMA
    vmem = pl.BlockSpec(memory_space=pltpu.VMEM)
    anywhere = pl.BlockSpec(memory_space=pl.ANY)
    smalls = 2 + heads
    layers, wides, sender_rows, width = tokens_in.shape
    return pl.pallas_call(
        finish_kernel,
        out_shape=(
            jax.ShapeDtypeStruct((2, rows, columns), jnp.float32),
            jax.ShapeDtypeStruct(small.shape[1:], jnp.float32),
            jax.ShapeDtypeStruct(first_parts.shape, dtype),
            jax.ShapeDtypeStruct(first_parts.shape, dtype),
            jax.ShapeDtypeStruct((2, wides, 2 * sender_rows, width), dtype),
        ),
        in_specs=[vmem, vmem, anywhere, anywhere, vmem, anywhere],
        out_specs=(vmem, vmem, anywhere, anywhere, anywhere),
        scratch_shapes=[
            pltpu.VMEM((2, 2, heads, rows, half), dtype),
            pltpu.VMEM((2, heads, rows, half), dtype),
            pltpu.VMEM((2, heads, rows, half), dtype),
            pltpu.VMEM((heads, rows, columns), dtype),
            pltpu.VMEM((2, heads, rows, columns), dtype),
            pltpu.VMEM((4,) + small.shape[1:], jnp.float32),
            pltpu.VMEM((smalls,) + small.shape[1:], jnp.float32),
            pltpu.VMEM(first_parts.shape, dtype),
            pltpu.VMEM((2, rows, columns), jnp.float32),
            dma((4,)),
            dma((2, heads)),
            dma((2, 1 + heads)),
            dma((2, 2, 2, heads)),
            dma((2, 2, heads)),
            dma((2, 2, heads)),
            dma((2, smalls)),
            dma((2,)),
            dma((2, 2, 2, 4)),
        ],
        compiler_params=pltpu.CompilerParams(
            collective_id=number, has_side_effects=True, vmem_limit_bytes=40 * 2**20
        ),
    )(terms, small, first_parts, second_parts, second_total, tokens_in)


def cut_kernel(gate, up, down, parts):
    count, part = parts.shape[0], parts.shape[2] // 3
    for at in range(count):
        size = min(part, gate.shape[1] - at * part)
        for which, weight in enumerate((gate, up, down)):
            start = which * part
            parts[at, :, pl.ds(start, size)] = weight[:, pl.ds(at * part, size)]
            if size < part:
                rest = part - size
                parts[at, :, pl.ds(start + size, rest)] = jnp.zeros(
                    (parts.shape[1], rest), parts.dtype
                )


def cut_parts(gate, up, down, count, part):
    rows, columns = gate.shape
    step = 16
    weight = pl.BlockSpec((step, columns), lambda at: (at, 0))
    return pl.pallas_call(
        cut_kernel,
        grid=(rows // step,),
        out_shape=jax.ShapeDtypeStruct((count, rows, 3 * part), gate.dtype),
        in_specs=[weight] * 3,
        out_specs=pl.BlockSpec((count, step, 3 * part), lambda at: (0, at, 0)),
        compiler_params=pltpu.CompilerParams(vmem_limit_bytes=24 * 2**20),
    )(gate, up, down)


def join_kernel(low, high, gate, up, down):
    count, part = low.shape[0], low.shape[2] // 3
    for at in range(2 * count):
        size = min(part, gate.shape[2] - at * part)
        source = low if at < count else high
        for which, grad in enumerate((gate, up, down)):
            grad[0, :, pl.ds(at * part, size)] = source[
                at % count, :, pl.ds(which * part, size)
            ].astype(grad.dtype)


def join_parts(low, high, columns):
    count, rows, width = low.shape
    step = 16
    part = pl.BlockSpec((count, step, width), lambda at: (0, at, 0))
    grad = pl.BlockSpec((1, step, columns), lambda at: (0, at, 0))
    return pl.pallas_call(
        join_kernel,
        grid=(rows // step,),
        out_shape=(jax.ShapeDtypeStruct((1, rows, columns), jnp.float32),) * 3,
        in_specs=[part] * 2,
        out_specs=(grad,) * 3,
        compiler_params=pltpu.CompilerParams(vmem_limit_bytes=24 * 2**20),
    )(low, high)


def visit(head, step, heads):
    inner_chip = jnp.minimum(jnp.minimum(head, heads - 1 - head), 1)
    at = step + inner_chip * (1 - lax.div(step, 2)) * (1 - 2 * step)
    return at + lax.div(2 * head, heads) * (heads - 1 - 2 * at)


def group_pipeline(block, everyone, out, scratch, prepare, compute, settle):
    (partial, pair_buf, sums, arrive, own_sem, pair_sem, line_sem, swap_sem, direct_sem) = scratch
    section, head = lax.axis_index(SECTION), lax.axis_index(HEAD)
    heads = lax.axis_size(HEAD)
    tokens = block.shape[0]
    other = {SECTION: 1 - section}

    def place(section_at, origin):
        start = (origin * 2 + section_at) * tokens
        return everyone.at[pl.ds(pl.multiple_of(start, tokens), tokens)]

    def remote(source, target, send, receive, partner):
        return pltpu.make_async_remote_copy(
            source, target, send, receive, device_id=partner, device_id_type=MESH
        )

    def pair(origin, source):
        target = place(section, origin)
        return remote(source, target, pair_sem.at[0, origin], pair_sem.at[1, origin], other)

    def pair_in(origin):
        target = place(1 - section, origin)
        return remote(target, target, pair_sem.at[0, origin], pair_sem.at[1, origin], other)

    def line(way, hop, source):
        step = 1 - 2 * way
        target = place(section, head - step * hop)
        sems = (line_sem.at[0, way, hop], line_sem.at[1, way, hop])
        return remote(source, target, *sems, {HEAD: head + step})

    def inside(place_at):
        return (place_at >= 0) & (place_at < heads)

    def accept(way, hop):
        step = 1 - 2 * way
        here = place(section, head - step * hop)
        line(way, hop - 1, here).wait_recv()

        @pl.when(inside(head + step))
        def _():
            line(way, hop, here).start()

        pair(head - step * hop, here).start()

    def swap(origin):
        return remote(
            partial.at[origin, 1 - section],
            pair_buf.at[origin],
            swap_sem.at[0, origin],
            swap_sem.at[1, origin],
            other,
        )

    def direct(origin):
        return remote(
            sums.at[origin],
            arrive.at[head],
            direct_sem.at[0, origin],
            direct_sem.at[1, head],
            {HEAD: origin},
        )

    def deliver(origin):
        swap(origin).wait_recv()
        sums[origin] = (
            partial[origin, section].astype(jnp.float32) + pair_buf[origin].astype(jnp.float32)
        ).astype(sums.dtype)

        @pl.when(origin != head)
        def _():
            direct(origin).start()

    barrier = pltpu.get_barrier_semaphore()
    partners = [other] + [{HEAD: lax.rem(head + shift, heads)} for shift in range(1, heads)]
    for partner in partners:
        pl.semaphore_signal(barrier, 1, device_id=partner, device_id_type=MESH)
    pl.semaphore_wait(barrier, len(partners))

    for way in (0, 1):

        @pl.when(inside(head + 1 - 2 * way))
        def _(way=way):
            line(way, 0, block).start()

    pair(head, block).start()
    own = pltpu.make_async_copy(block, place(section, head), own_sem)
    own.start()
    prepare()
    own.wait()

    def one(step, carry):
        origin = visit(head, step, heads)

        @pl.when(step >= 1)
        def _():
            deliver(visit(head, step - 1, heads))

        @pl.when(step == 1)
        def _():
            for way in (0, 1):

                @pl.when(inside(head - (1 - 2 * way)))
                def _(way=way):
                    accept(way, 1)

        hop = jnp.maximum(origin - head, head - origin)

        @pl.when((step >= 2) & (hop >= 2))
        def _():
            accept(lax.div(jnp.maximum(origin - head, 0) + heads - 2, heads), hop)

        pair_in(origin).wait_recv()
        compute(origin)
        swap(origin).start()
        return carry

    lax.fori_loop(0, heads, one, 0)
    deliver(visit(head, heads - 1, heads))
    settle()
    out[...] = sums[head].astype(jnp.float32)
    for origin in range(heads):

        @pl.when(origin != head)
        def _(origin=origin):
            arrived = arrive.at[origin]
            sems = (direct_sem.at[0, origin], direct_sem.at[1, origin])
            remote(arrived, arrived, *sems, {HEAD: head}).wait_recv()
            out[...] += arrived[...].astype(jnp.float32)

    for origin in range(heads):
        here = place(section, origin)
        pair(origin, here).wait_send()
        swap(origin).wait_send()

        @pl.when(origin != head)
        def _(origin=origin):
            direct(origin).wait_send()

    for way in (0, 1):
        for hop in range(heads):
            step = 1 - 2 * way

            @pl.when(inside(head + step) & inside(head - step * hop))
            def _(way=way, hop=hop):
                line(way, hop, block).wait_send()


def pipeline_scratch(heads, tokens, columns, dtype):
    dma = pltpu.SemaphoreType.DMA
    return [
        pltpu.VMEM((heads, 2, tokens, columns), dtype),
        pltpu.VMEM((heads, tokens, columns), dtype),
        pltpu.VMEM((heads, tokens, columns), dtype),
        pltpu.VMEM((heads, tokens, columns), dtype),
        dma,
        dma((2, heads)),
        dma((2, 2, heads)),
        dma((2, heads)),
        dma((2, heads)),
    ]


PIPELINE_SCRATCH = 9
STEP_COLUMNS = 384
STEP_WIDTH = 512


def chunks(total, size):
    return [(at, min(size, total - at)) for at in range(0, total, size)]


def write_partial(partial, origin, left, weights, columns):
    tokens = partial.shape[2]
    for start, count in chunks(partial.shape[3], STEP_WIDTH):
        piece = contract_last(left, weights[pl.ds(start, count), pl.ds(*columns)])
        piece = piece.astype(partial.dtype)
        partial[origin, 0, :, pl.ds(start, count)] = piece[:tokens]
        partial[origin, 1, :, pl.ds(start, count)] = piece[tokens:]


def forward_kernel(block, weights_hbm, out, everyone, gate_up_hbm, hidden_hbm, *scratch):
    shared, rest = scratch[:PIPELINE_SCRATCH], scratch[PIPELINE_SCRATCH:]
    weights, gate_up, hidden, load_sem, store_sem = rest
    partial = shared[0]
    heads = lax.axis_size(HEAD)
    rows = 2 * block.shape[0]
    part = hidden.shape[1]
    load = pltpu.make_async_copy(weights_hbm, weights, load_sem)

    def stores(origin):
        span = pl.ds(pl.multiple_of(origin * rows, rows), rows)
        return [
            pltpu.make_async_copy(gate_up.at[span], gate_up_hbm.at[span], store_sem.at[0, origin]),
            pltpu.make_async_copy(hidden.at[span], hidden_hbm.at[span], store_sem.at[1, origin]),
        ]

    def prepare():
        load.start()
        load.wait()

    def compute(origin):
        span = pl.ds(pl.multiple_of(origin * rows, rows), rows)
        left = everyone[span, :]
        for start, count in chunks(part, STEP_COLUMNS):
            gate = jnp.dot(
                left, weights[:, pl.ds(start, count)], preferred_element_type=jnp.float32
            )
            up = jnp.dot(
                left, weights[:, pl.ds(part + start, count)], preferred_element_type=jnp.float32
            )
            gate_up[span, pl.ds(start, count)] = gate.astype(gate_up.dtype)
            gate_up[span, pl.ds(part + start, count)] = up.astype(gate_up.dtype)
            hidden[span, pl.ds(start, count)] = (gate / (1.0 + jnp.exp(-gate)) * up).astype(
                hidden.dtype
            )
        write_partial(partial, origin, hidden[span, :], weights, (2 * part, part))
        for store in stores(origin):
            store.start()

    def settle():
        for origin in range(heads):
            for store in stores(origin):
                store.wait()

    group_pipeline(block, everyone, out, shared, prepare, compute, settle)


def backward_kernel(block, weights_hbm, gate_up_hbm, out, everyone, d_gate_up_hbm, *scratch):
    shared, rest = scratch[:PIPELINE_SCRATCH], scratch[PIPELINE_SCRATCH:]
    weights, gate_up, d_gate_up, load_sem, store_sem = rest
    partial = shared[0]
    heads = lax.axis_size(HEAD)
    rows = 2 * block.shape[0]
    part = gate_up.shape[1] // 2
    loads = [
        pltpu.make_async_copy(weights_hbm, weights, load_sem.at[0]),
        pltpu.make_async_copy(gate_up_hbm, gate_up, load_sem.at[1]),
    ]

    def store(origin):
        span = pl.ds(pl.multiple_of(origin * rows, rows), rows)
        return pltpu.make_async_copy(
            d_gate_up.at[span], d_gate_up_hbm.at[span], store_sem.at[origin]
        )

    def prepare():
        for load in loads:
            load.start()
        for load in loads:
            load.wait()

    def compute(origin):
        span = pl.ds(pl.multiple_of(origin * rows, rows), rows)
        left = everyone[span, :]
        for start, count in chunks(part, STEP_COLUMNS):
            d_hidden = jnp.dot(
                left, weights[:, pl.ds(2 * part + start, count)], preferred_element_type=jnp.float32
            )
            gate = gate_up[span, pl.ds(start, count)].astype(jnp.float32)
            up = gate_up[span, pl.ds(part + start, count)].astype(jnp.float32)
            sigmoid = 1.0 / (1.0 + jnp.exp(-gate))
            d_gate = d_hidden * up * sigmoid * (1.0 + gate * (1.0 - sigmoid))
            d_gate_up[span, pl.ds(start, count)] = d_gate.astype(d_gate_up.dtype)
            d_up = d_hidden * gate * sigmoid
            d_gate_up[span, pl.ds(part + start, count)] = d_up.astype(d_gate_up.dtype)
        write_partial(partial, origin, d_gate_up[span, :], weights, (0, 2 * part))
        store(origin).start()

    def settle():
        for origin in range(heads):
            store(origin).wait()

    group_pipeline(block, everyone, out, shared, prepare, compute, settle)


def feed_forward(block, weights, number):
    heads = lax.axis_size(HEAD)
    tokens, width = block.shape
    part = weights.shape[1] // 3
    count = 2 * heads * tokens
    dtype = block.dtype
    vmem = pl.BlockSpec(memory_space=pltpu.VMEM)
    anywhere = pl.BlockSpec(memory_space=pl.ANY)
    return pl.pallas_call(
        forward_kernel,
        out_shape=(
            jax.ShapeDtypeStruct((tokens, width), jnp.float32),
            jax.ShapeDtypeStruct((count, width), dtype),
            jax.ShapeDtypeStruct((count, 2 * part), dtype),
            jax.ShapeDtypeStruct((count, part), dtype),
        ),
        in_specs=[vmem, anywhere],
        out_specs=(vmem, vmem, anywhere, anywhere),
        scratch_shapes=pipeline_scratch(heads, tokens, width, dtype)
        + [
            pltpu.VMEM(weights.shape, dtype),
            pltpu.VMEM((count, 2 * part), dtype),
            pltpu.VMEM((count, part), dtype),
            pltpu.SemaphoreType.DMA,
            pltpu.SemaphoreType.DMA((2, heads)),
        ],
        compiler_params=pltpu.CompilerParams(
            collective_id=number, has_side_effects=True, vmem_limit_bytes=54 * 2**20
        ),
        cost_estimate=pl.CostEstimate(
            flops=6 * count * width * part, bytes_accessed=2 * weights.size, transcendentals=0
        ),
    )(block, weights)


def feed_backward(block, weights, gate_up, number):
    heads = lax.axis_size(HEAD)
    tokens, width = block.shape
    part = weights.shape[1] // 3
    count = 2 * heads * tokens
    dtype = block.dtype
    vmem = pl.BlockSpec(memory_space=pltpu.VMEM)
    anywhere = pl.BlockSpec(memory_space=pl.ANY)
    return pl.pallas_call(
        backward_kernel,
        out_shape=(
            jax.ShapeDtypeStruct((tokens, width), jnp.float32),
            jax.ShapeDtypeStruct((count, width), dtype),
            jax.ShapeDtypeStruct((count, 2 * part), dtype),
        ),
        in_specs=[vmem, anywhere, anywhere],
        out_specs=(vmem, vmem, anywhere),
        scratch_shapes=pipeline_scratch(heads, tokens, width, dtype)
        + [
            pltpu.VMEM(weights.shape, dtype),
            pltpu.VMEM((count, 2 * part), dtype),
            pltpu.VMEM((count, 2 * part), dtype),
            pltpu.SemaphoreType.DMA((2,)),
            pltpu.SemaphoreType.DMA((heads,)),
        ],
        compiler_params=pltpu.CompilerParams(
            collective_id=number, has_side_effects=True, vmem_limit_bytes=54 * 2**20
        ),
        cost_estimate=pl.CostEstimate(
            flops=6 * count * width * part, bytes_accessed=2 * weights.size, transcendentals=0
        ),
    )(block, weights, gate_up)


def head_rows(tensor):
    tokens = tensor.shape[0]
    repeat = HEADS // KV
    return (
        tensor.reshape(tokens, KV, repeat, HDIM)
        .transpose(1, 2, 0, 3)
        .reshape(KV, repeat * tokens, HDIM)
    )


def token_rows(tensor):
    repeat = HEADS // KV
    tokens = tensor.shape[1] // repeat
    return (
        tensor.reshape(KV, repeat, tokens, HDIM)
        .transpose(2, 0, 1, 3)
        .reshape(tokens, HEADS * HDIM)
    )


def attention_forward(queries, keys, values, allowed):
    scores = (
        jnp.einsum("gqd,kgd->gqk", queries, keys, preferred_element_type=jnp.float32)
        * HDIM**-0.5
    )
    scores = jnp.where(allowed[None], scores, -1e30)
    highest = jnp.max(scores, -1, keepdims=True)
    weights_exp = jnp.exp(scores - highest)
    partition = jnp.sum(weights_exp, -1, keepdims=True)
    probs = (weights_exp / partition).astype(jnp.bfloat16)
    attended = jnp.einsum("gqk,kgd->gqd", probs, values, preferred_element_type=jnp.float32)
    return attended.astype(jnp.bfloat16), highest + jnp.log(partition)


def attention_backward(queries, keys, values, allowed, log_total, grads):
    scaling = HDIM**-0.5
    scores = jnp.einsum("gqd,kgd->gqk", queries, keys, preferred_element_type=jnp.float32)
    scores = jnp.where(allowed[None], scores * scaling, -1e30)
    probs = jnp.exp(scores - log_total)
    d_probs = jnp.einsum("gqd,kgd->gqk", grads, values, preferred_element_type=jnp.float32)
    row_dot = jnp.sum(probs * d_probs, -1, keepdims=True)
    d_scores = (probs * (d_probs - row_dot)).astype(jnp.bfloat16)
    d_queries = (
        jnp.einsum("gqk,kgd->gqd", d_scores, keys, preferred_element_type=jnp.float32) * scaling
    )
    d_keys = (
        jnp.einsum("gqk,gqd->kgd", d_scores, queries, preferred_element_type=jnp.float32) * scaling
    )
    d_values = jnp.einsum(
        "gqk,gqd->kgd", probs.astype(jnp.bfloat16), grads, preferred_element_type=jnp.float32
    )
    return d_queries, d_keys, d_values


def local_grouped(
    inputs,
    cotangent,
    norm_gains,
    qkv_weight,
    qkv_bias,
    out_weight,
    gate_weight,
    up_weight,
    down_weight,
):
    head_count = lax.axis_size(HEAD)
    wide_count = lax.axis_size(WIDE)
    section_count = lax.axis_size(SECTION)
    section = lax.axis_index(SECTION)
    head = lax.axis_index(HEAD)
    micro_count, short_len, width = inputs.shape
    half_len = short_len // section_count
    tokens = wide_count * half_len
    rows = qkv_weight.shape[1]
    query_width = HEADS * HDIM
    kv_width = KV * HDIM
    qkv_cols = qkv_weight.shape[2]
    ff_cols = gate_weight.shape[2]
    parts = section_count * head_count
    part_cols = -(-ff_cols // (parts * 128)) * 128

    def inner(array):
        split = array.shape[:-1] + (head_count, wide_count, rows)
        return jnp.swapaxes(array.reshape(split), -3, -2).reshape(array.shape)

    def outer(array):
        split = array.shape[:-1] + (wide_count, head_count, rows)
        return jnp.swapaxes(array.reshape(split), -3, -2).reshape(array.shape)

    mlp_parts = cut_parts(gate_weight[0], up_weight[0], down_weight[0], parts, part_cols)
    qkv_weights, out_weights, first_mlp, second_parts = start_weights(
        qkv_weight[0],
        inner(out_weight[0]),
        mlp_parts.reshape(section_count, head_count, rows, 3 * part_cols),
        5,
    )

    def shift_parts(parts_in):
        pieces = [lax.dynamic_index_in_dim(parts_in, head, 0, keepdims=False)]
        for distance in range(1, head_count):
            target = lax.rem(head + distance, head_count)
            piece = lax.dynamic_index_in_dim(parts_in, target, 0, keepdims=False)
            route = [(at, (at + distance) % head_count) for at in range(head_count)]
            pieces.append(lax.ppermute(piece, HEAD, route))
        order = lax.rem(head + head_count - jnp.arange(head_count), head_count)
        return jnp.stack(pieces)[order]

    second_mlp = lax.all_gather(second_parts, WIDE, axis=0).reshape(width, 3 * part_cols)
    mlp_weights = [first_mlp, second_mlp]

    small = jnp.concatenate([inner(norm_gains[0, 0]), inner(norm_gains[0, 1]), qkv_bias[0]])
    small = both_sections(small)

    sides = jnp.concatenate(
        [
            lax.dynamic_slice_in_dim(inputs, section * half_len, half_len, 1),
            lax.dynamic_slice_in_dim(cotangent, section * half_len, half_len, 1),
        ],
        1,
    )
    sides = lax.all_to_all(sides, WIDE, split_axis=0, concat_axis=0, tiled=True)
    sides = inner(sides)
    layer_in = sides[:, :half_len].reshape(tokens, width).astype(jnp.float32)
    last_grad = sides[:, half_len:].reshape(tokens, width)

    def positions_of(section_at, head_at):
        block = (head_at * wide_count + jnp.arange(wide_count, dtype=jnp.int32)) * short_len
        inside = section_at * half_len + jnp.arange(half_len, dtype=jnp.int32)
        return (block[:, None] + inside[None, :]).reshape(-1)

    own_pos = positions_of(section, head)
    key_pos = jnp.concatenate(
        [positions_of(at // head_count, at % head_count) for at in range(parts)]
    )
    allowed = jnp.tile(own_pos, HEADS // KV)[:, None] >= key_pos[None, :]
    cosine, sine_table = rotary_tables(own_pos.astype(jnp.float32), HDIM)

    records = []
    outputs_list = []
    for layer in range(section_count):
        gain_first = small[layer][:width]
        gain_second = small[layer][width : 2 * width]
        bias_row = small[layer][2 * width :]
        w_qkv = qkv_weights[layer]
        w_out = out_weights[layer]
        w_mlp = mlp_weights[layer]
        scale_first = lax.rsqrt(jnp.mean(layer_in * layer_in, -1, keepdims=True) + EPSILON)
        normed = (layer_in * scale_first * gain_first).astype(jnp.bfloat16)
        qkv = (
            jnp.dot(normed, w_qkv, preferred_element_type=jnp.float32)
            + bias_row
        )
        queries = rotate_pairs(
            qkv[:, :query_width].reshape(tokens, HEADS, HDIM), cosine, sine_table
        ).astype(jnp.bfloat16)
        key_heads = rotate_pairs(
            qkv[:, query_width : query_width + kv_width].reshape(tokens, KV, HDIM),
            cosine,
            sine_table,
        ).astype(jnp.bfloat16)
        keyval = jnp.concatenate(
            [
                key_heads.reshape(tokens, kv_width),
                qkv[:, query_width + kv_width :].astype(jnp.bfloat16),
            ],
            1,
        )
        keyval = gather_group(keyval, 2)
        keys = keyval[:, :kv_width].reshape(-1, KV, HDIM)
        values = keyval[:, kv_width:].reshape(-1, KV, HDIM)
        queries = head_rows(queries)
        attended, log_total = attention_forward(queries, keys, values, allowed)
        attended = token_rows(attended)
        midway = layer_in + jnp.dot(
            attended, w_out, preferred_element_type=jnp.float32
        )
        scale_second = lax.rsqrt(jnp.mean(midway * midway, -1, keepdims=True) + EPSILON)
        normed2 = (midway * scale_second * gain_second).astype(jnp.bfloat16)
        mlp_out, normed2, gate_up, hidden = feed_forward(normed2, w_mlp, 1)
        result = midway + mlp_out
        records.append(
            (
                layer_in,
                scale_first,
                normed,
                queries,
                keys,
                values,
                log_total,
                attended,
                midway,
                scale_second,
                normed2,
                gate_up,
                hidden,
            )
        )
        carried = result.astype(jnp.bfloat16)
        outputs_list.append(carried)
        layer_in = carried.astype(jnp.float32)

    out_grad = last_grad
    grads_list = [None] * section_count
    attention_terms = [None] * section_count
    mlp_terms = [None] * section_count
    small_terms = [None] * section_count
    for layer in reversed(range(section_count)):
        gain_first = small[layer][:width]
        gain_second = small[layer][width : 2 * width]
        w_qkv = qkv_weights[layer]
        w_out = out_weights[layer]
        w_mlp = mlp_weights[layer]
        (
            layer_in,
            scale_first,
            normed,
            queries,
            keys,
            values,
            log_total,
            attended,
            midway,
            scale_second,
            normed2,
            gate_up,
            hidden,
        ) = records[layer]
        d_normed2, g_mlp, d_gate_up = feed_backward(out_grad, w_mlp, gate_up, 3)
        mlp_term = jnp.concatenate(
            [
                contract_first(normed2, d_gate_up).astype(jnp.bfloat16),
                contract_first(g_mlp, hidden).astype(jnp.bfloat16),
            ],
            1,
        )
        mlp_terms[layer] = mlp_term
        out_grad = out_grad.astype(jnp.float32)
        unit_second = midway * scale_second
        gain2_grad = jnp.sum(d_normed2 * unit_second, 0)
        dn_second = d_normed2 * gain_second
        d_midway = (
            scale_second
            * (dn_second - unit_second * jnp.mean(dn_second * unit_second, -1, keepdims=True))
            + out_grad
        )
        g_attn = d_midway.astype(jnp.bfloat16)
        d_attended = contract_last(g_attn, w_out).astype(jnp.bfloat16)
        d_queries, d_keys, d_values = attention_backward(
            queries, keys, values, allowed, log_total, head_rows(d_attended)
        )
        d_keyval = scatter_group(
            jnp.concatenate(
                [d_keys.reshape(-1, kv_width), d_values.reshape(-1, kv_width)], 1
            ).astype(jnp.bfloat16),
            4,
        )
        d_queries = token_rows(d_queries.astype(jnp.bfloat16)).astype(jnp.float32)
        d_queries = rotate_back(d_queries.reshape(tokens, HEADS, HDIM), cosine, sine_table)
        d_keys = rotate_back(d_keyval[:, :kv_width].reshape(tokens, KV, HDIM), cosine, sine_table)
        d_qkv = jnp.concatenate(
            [
                d_queries.reshape(tokens, query_width),
                d_keys.reshape(tokens, kv_width),
                d_keyval[:, kv_width:],
            ],
            1,
        ).astype(jnp.bfloat16)
        bias_grad = jnp.sum(d_qkv.astype(jnp.float32), 0)
        d_normed = contract_last(d_qkv, w_qkv)
        unit_first = layer_in * scale_first
        gain1_grad = jnp.sum(d_normed * unit_first, 0)
        dn_first = d_normed * gain_first
        d_layer_in = (
            scale_first
            * (dn_first - unit_first * jnp.mean(dn_first * unit_first, -1, keepdims=True))
            + d_midway
        )
        halves = [d_qkv.reshape(tokens, 2, -1), g_attn.reshape(tokens, 2, -1)]
        both = jnp.concatenate([normed, inner(attended)], 1)

        def with_half(at):
            cut = [lax.dynamic_index_in_dim(each, at, 1, keepdims=False) for each in halves]
            return jnp.concatenate([both] + cut, 1)

        theirs = lax.ppermute(with_half(1 - section), SECTION, [(0, 1), (1, 0)])
        pair = jnp.concatenate([with_half(section), theirs], 0)
        cut = 2 * width + qkv_cols // 2
        term = jnp.concatenate(
            [
                contract_first(pair[:, :width], pair[:, 2 * width : cut]).astype(jnp.bfloat16),
                contract_first(pair[:, width : 2 * width], pair[:, cut:]).astype(jnp.bfloat16),
            ],
            1,
        )
        attention_terms[layer] = term.reshape(wide_count, head_count, rows, -1)
        small_terms[layer] = jnp.concatenate([gain1_grad, gain2_grad, bias_grad])
        out_grad = d_layer_in.astype(jnp.bfloat16)
        grads_list[layer] = out_grad

    def over_wide(term):
        term = term.reshape(wide_count, head_count, rows, -1)
        return lax.optimization_barrier(lax.psum_scatter(term, WIDE, scatter_dimension=0))

    second_sum = over_wide(mlp_terms[1])
    second_total = lax.psum_scatter(over_wide(attention_terms[1]), HEAD, scatter_dimension=0)
    first_sum = over_wide(mlp_terms[0])
    sides = jnp.stack([outer(each) for each in outputs_list + grads_list])
    totals, small_total, low_parts, high_parts, owned = finish_weights(
        attention_terms[0].reshape(wide_count * head_count, rows, -1),
        jnp.stack(small_terms).reshape(section_count, -1, 128),
        first_sum,
        shift_parts(second_sum),
        second_total,
        sides.reshape(2 * section_count, wide_count, half_len, width),
        6,
    )
    small_total = small_total.reshape(-1)
    gate_grad, up_grad, down_grad = join_parts(low_parts, high_parts, ff_cols)

    def both_halves(start, count):
        return jnp.concatenate([half[:, start : start + count] for half in totals], 1)[None]

    return (
        owned[:1],
        owned[1:],
        outer(small_total[: 2 * width].reshape(1, 2, width)),
        both_halves(0, qkv_cols // 2),
        small_total[2 * width :][None],
        outer(both_halves(qkv_cols // 2, width // 2)),
        gate_grad,
        up_grad,
        down_grad,
    )


def local(inputs, *rest):
    sizes = [lax.axis_size(axis) for axis in (SECTION, WIDE)]
    if sizes == [2, 4] and inputs.shape[0] == 4:
        return local_grouped(inputs, *rest)
    return local_streamed(inputs, *rest)


def solution(mesh):
    return jax.shard_map(
        local,
        mesh=mesh,
        in_specs=(
            P(None, (HEAD, WIDE), None),
            P(None, (HEAD, WIDE), None),
            P(SECTION, None, None),
            P(SECTION, (HEAD, WIDE), None),
            P(SECTION, None),
            P(SECTION, (HEAD, WIDE), None),
            P(SECTION, (HEAD, WIDE), None),
            P(SECTION, (HEAD, WIDE), None),
            P(SECTION, (HEAD, WIDE), None),
        ),
        out_specs=(
            P(SECTION, None, (HEAD, WIDE), None),
            P(SECTION, None, (HEAD, WIDE), None),
            P(SECTION, None, None),
            P(SECTION, (HEAD, WIDE), None),
            P(SECTION, None),
            P(SECTION, (HEAD, WIDE), None),
            P(SECTION, (HEAD, WIDE), None),
            P(SECTION, (HEAD, WIDE), None),
            P(SECTION, (HEAD, WIDE), None),
        ),
        check_vma=False,
    )
```

```python
import functools
from typing import NamedTuple

import jax
import jax.numpy as jnp
import numpy as np
from jax import lax
from jax.experimental import pallas as pl
from jax.experimental.pallas import tpu as pltpu
from jax.sharding import PartitionSpec as P

HEADS = 12
KV = 2
HDIM = 128


EPSILON = 1e-06
MESH = pl.DeviceIdType.MESH
SECTION = "section"
HEAD = "head"
WIDE = "wide"
ROPE_BASE = 1000000.0


class Record(NamedTuple):
    layer_in: jax.Array
    scale_first: jax.Array
    normed: jax.Array
    query_rows: jax.Array
    kv_local: jax.Array
    log_total: jax.Array
    out_seq: jax.Array
    midway: jax.Array
    scale_second: jax.Array
    normed2: jax.Array
    gate_out: jax.Array
    up_out: jax.Array
    hidden: jax.Array


def passed_along(block, axis, distance):
    devices = range(lax.axis_size(axis))
    route = [(i - distance, i) for i in devices if i - distance in devices]
    return lax.ppermute(block, axis, route)


def rotary_tables(positions, head_dim):
    half_dim = head_dim // 2
    frequency = ROPE_BASE ** (-jnp.arange(half_dim, dtype=jnp.float32) / half_dim)
    angles = positions[:, None] * frequency[None, :]
    return (jnp.cos(angles)[:, None, :], jnp.sin(angles)[:, None, :])


def rotate_pairs(tensor, cosine, sine_table):
    half_dim = tensor.shape[-1] // 2
    first_half = tensor[..., :half_dim]
    second_half = tensor[..., half_dim:]
    return jnp.concatenate(
        [
            first_half * cosine - second_half * sine_table,
            second_half * cosine + first_half * sine_table,
        ],
        -1,
    )


def rotate_back(tensor, cosine, sine_table):
    half_dim = tensor.shape[-1] // 2
    first_half = tensor[..., :half_dim]
    second_half = tensor[..., half_dim:]
    return jnp.concatenate(
        [
            first_half * cosine + second_half * sine_table,
            second_half * cosine - first_half * sine_table,
        ],
        -1,
    )


def contract_last(left, right):
    return lax.dot_general(
        left, right, (((1,), (1,)), ((), ())), preferred_element_type=jnp.float32
    )


def contract_first(left, right):
    return lax.dot_general(
        left, right, (((0,), (0,)), ((), ())), preferred_element_type=jnp.float32
    )


def attention_scores(query_rows, key_value, query_pos, key_pos):
    head_dim = query_rows.shape[1]
    scores = contract_last(query_rows, key_value[:, :head_dim]) * head_dim ** (-0.5)
    return jnp.where(query_pos[:, None] >= key_pos[None, :], scores, -1e30)


def attend_forward(query_rows, key_value, query_pos, key_pos):
    head_dim = query_rows.shape[1]
    scores = attention_scores(query_rows, key_value, query_pos, key_pos)
    highest = jnp.max(scores, -1, keepdims=True)
    weights_exp = jnp.exp(scores - highest)
    partition = jnp.sum(weights_exp, -1, keepdims=True)
    probs_low = (weights_exp / partition).astype(jnp.bfloat16)
    attended = jnp.dot(probs_low, key_value[:, head_dim:], preferred_element_type=jnp.float32)
    return (attended.astype(jnp.bfloat16), highest + jnp.log(partition))


def attend_backward(query_rows, key_value, query_pos, key_pos, log_total, grad_rows):
    head_dim = query_rows.shape[1]
    scaling = head_dim ** (-0.5)
    scores = attention_scores(query_rows, key_value, query_pos, key_pos)
    probs_full = jnp.exp(scores - log_total)
    grad_probs = contract_last(grad_rows, key_value[:, head_dim:])
    row_dot = jnp.sum(probs_full * grad_probs, -1, keepdims=True)
    grad_scores = (probs_full * (grad_probs - row_dot)).astype(jnp.bfloat16)
    grad_query = (
        jnp.dot(grad_scores, key_value[:, :head_dim], preferred_element_type=jnp.float32) * scaling
    )
    grad_key = contract_first(grad_scores, query_rows) * scaling
    grad_value = contract_first(probs_full.astype(jnp.bfloat16), grad_rows)
    return (grad_query, jnp.concatenate([grad_key, grad_value], 1))


def make_terms(operands, factor):
    (
        normed_all,
        dqkv_all,
        attended_all,
        gattn_all,
        normed2_all,
        dgate_all,
        dup_all,
        gmlp_all,
        hidden_all,
    ) = operands
    pairs = [
        (normed_all, dqkv_all),
        (attended_all, gattn_all),
        (normed2_all, dgate_all),
        (normed2_all, dup_all),
        (gmlp_all, hidden_all),
    ]
    scaled_pairs = [
        (left, (right.astype(jnp.float32) * factor).astype(jnp.bfloat16)) for left, right in pairs
    ]

    def weight_terms(start, count):
        pieces = [contract_first(left, right) for left, right in scaled_pairs]
        return jnp.concatenate(pieces, 1)

    return weight_terms


def local_streamed(
    inputs,
    cotangent,
    norm_gains,
    qkv_weight,
    qkv_bias,
    out_weight,
    gate_weight,
    up_weight,
    down_weight,
):
    head_count = lax.axis_size(HEAD)
    wide_count = lax.axis_size(WIDE)
    section_pos = lax.axis_index(SECTION)
    head_pos = lax.axis_index(HEAD)
    wide_pos = lax.axis_index(WIDE)
    micro_count, short_len, width = inputs.shape
    group_size = HEADS // head_count
    slot_rep = head_count // KV
    query_width = HEADS * HDIM
    kv_width = KV * HDIM
    local_rows = head_count * short_len
    seq_len = local_rows * wide_count
    gain_first = norm_gains[0, 0]
    gain_second = norm_gains[0, 1]
    bias_row = qkv_bias[0]
    seq_pos = (
        (head_pos * wide_count + wide_pos) * short_len + jnp.arange(short_len, dtype=jnp.int32)
    ).astype(jnp.float32)
    cosine, sine_table = rotary_tables(seq_pos, HDIM)
    local_index = jnp.arange(local_rows, dtype=jnp.int32)
    query_pos = jnp.tile(
        (local_index // short_len * wide_count + wide_pos) * short_len + local_index % short_len,
        group_size,
    )
    key_index = jnp.arange(seq_len, dtype=jnp.int32)
    key_pos = (
        key_index % local_rows // short_len * wide_count + key_index // local_rows
    ) * short_len + key_index % short_len

    def to_rows(packed):
        return (
            packed.reshape(local_rows, group_size, HDIM)
            .transpose(1, 0, 2)
            .reshape(group_size * local_rows, HDIM)
        )

    def from_rows(rows_in):
        return (
            rows_in.reshape(group_size, local_rows, HDIM)
            .transpose(1, 0, 2)
            .reshape(local_rows, 1, group_size * HDIM)
        )

    weights_fwd = (
        lax.all_gather(qkv_weight[0], (HEAD, WIDE), axis=0, tiled=True),
        lax.all_gather(out_weight[0], (HEAD, WIDE), axis=0, tiled=True),
        lax.all_gather(gate_weight[0], (HEAD, WIDE), axis=0, tiled=True),
        lax.all_gather(up_weight[0], (HEAD, WIDE), axis=0, tiled=True),
        lax.all_gather(down_weight[0], (HEAD, WIDE), axis=0, tiled=True),
    )
    incoming = jnp.zeros((short_len, width), jnp.bfloat16)
    records = []
    outputs_list = []
    for step_index in range(micro_count + 1):
        own_input = inputs[min(step_index, micro_count - 1)]
        layer_in = jnp.where(section_pos == 0, own_input, incoming).astype(jnp.float32)
        layer_w_qkv, layer_w_out, layer_w_gate, layer_w_up, layer_w_down = weights_fwd
        scale_first = lax.rsqrt(jnp.mean(layer_in * layer_in, -1, keepdims=True) + EPSILON)
        normed = (layer_in * scale_first * gain_first).astype(jnp.bfloat16)
        qkv = jnp.dot(normed, layer_w_qkv, preferred_element_type=jnp.float32) + bias_row
        queries = rotate_pairs(
            qkv[:, :query_width].reshape(short_len, HEADS, HDIM), cosine, sine_table
        ).astype(jnp.bfloat16)
        key_heads = rotate_pairs(
            qkv[:, query_width : query_width + kv_width].reshape(short_len, KV, HDIM),
            cosine,
            sine_table,
        ).astype(jnp.bfloat16)
        value_heads = (
            qkv[:, query_width + kv_width :].reshape(short_len, KV, HDIM).astype(jnp.bfloat16)
        )
        kv_pack = jnp.repeat(jnp.stack([key_heads, value_heads], 2), slot_rep, axis=1).reshape(
            short_len, head_count, 2 * HDIM
        )
        q_pack = queries.reshape(short_len, head_count, group_size * HDIM)
        q_heads = lax.all_to_all(q_pack, HEAD, split_axis=1, concat_axis=0, tiled=True)
        kv_heads = lax.all_to_all(kv_pack, HEAD, split_axis=1, concat_axis=0, tiled=True)
        query_rows = to_rows(q_heads)
        kv_local = kv_heads.reshape(local_rows, 2 * HDIM)
        layer_kv_all = lax.all_gather(kv_local, WIDE, axis=0, tiled=True)
        out_rows, log_total = attend_forward(query_rows, layer_kv_all, query_pos, key_pos)
        out_seq = lax.all_to_all(
            from_rows(out_rows), HEAD, split_axis=0, concat_axis=1, tiled=True
        ).reshape(short_len, query_width)
        midway = layer_in + jnp.dot(out_seq, layer_w_out, preferred_element_type=jnp.float32)
        scale_second = lax.rsqrt(jnp.mean(midway * midway, -1, keepdims=True) + EPSILON)
        normed2 = (midway * scale_second * gain_second).astype(jnp.bfloat16)
        layer_gate_out = jnp.dot(normed2, layer_w_gate, preferred_element_type=jnp.float32)
        up_out = jnp.dot(normed2, layer_w_up, preferred_element_type=jnp.float32)
        hidden = (jax.nn.silu(layer_gate_out) * up_out).astype(jnp.bfloat16)
        result = midway + contract_last(hidden, layer_w_down)
        record = Record(
            layer_in=layer_in,
            scale_first=scale_first,
            normed=normed,
            query_rows=query_rows,
            kv_local=kv_local,
            log_total=log_total,
            out_seq=out_seq,
            midway=midway,
            scale_second=scale_second,
            normed2=normed2,
            gate_out=layer_gate_out,
            up_out=up_out,
            hidden=hidden,
        )
        result, record = (result, record)
        sent_value = result.astype(jnp.bfloat16)
        records.append(record)
        outputs_list.append(sent_value)
        if step_index < micro_count:
            incoming = passed_along(sent_value, SECTION, 1)
    stacked_records = jax.tree.map(lambda *arrays: jnp.stack(arrays), *records)
    section_outputs = lax.dynamic_slice_in_dim(
        jnp.stack(outputs_list), section_pos, micro_count, 0
    )[None]
    weights_back = (
        lax.all_gather(qkv_weight[0], (HEAD, WIDE), axis=0, tiled=True),
        lax.all_gather(out_weight[0], (HEAD, WIDE), axis=0, tiled=True),
        lax.all_gather(gate_weight[0], (HEAD, WIDE), axis=0, tiled=True),
        lax.all_gather(up_weight[0], (HEAD, WIDE), axis=0, tiled=True),
        lax.all_gather(down_weight[0], (HEAD, WIDE), axis=0, tiled=True),
    )
    owned_rows = qkv_weight.shape[1]
    qkv_cols = qkv_weight.shape[2]
    ff_cols = gate_weight.shape[2]
    incoming_grad = jnp.zeros((short_len, width), jnp.bfloat16)
    small_totals = (
        jnp.zeros((width,), jnp.float32),
        jnp.zeros((width,), jnp.float32),
        jnp.zeros((bias_row.shape[0],), jnp.float32),
    )
    grads_list = []
    kept_list = []
    for step_index in range(micro_count + 1):
        pick = jnp.clip(step_index - 1 + 2 * section_pos, 0, micro_count)
        record = jax.tree.map(
            lambda array: lax.dynamic_index_in_dim(array, pick, 0, keepdims=False), stacked_records
        )
        own_grad = cotangent[min(step_index, micro_count - 1)]
        out_grad = jnp.where(section_pos == 1, own_grad, incoming_grad).astype(jnp.float32)
        w_qkv, w_out, w_gate, w_up, w_down = weights_back
        g_mlp = out_grad.astype(jnp.bfloat16)
        d_hidden = jnp.dot(g_mlp, w_down, preferred_element_type=jnp.float32)
        gate_out = record.gate_out
        sigmoid_gate = jax.nn.sigmoid(gate_out)
        d_gate = (
            d_hidden * record.up_out * sigmoid_gate * (1.0 + gate_out * (1.0 - sigmoid_gate))
        ).astype(jnp.bfloat16)
        d_up = (d_hidden * gate_out * sigmoid_gate).astype(jnp.bfloat16)
        d_normed2 = contract_last(d_gate, w_gate) + contract_last(d_up, w_up)
        unit_second = record.midway * record.scale_second
        gain2_grad = jnp.sum(d_normed2 * unit_second, 0)
        dn_second = d_normed2 * gain_second
        d_midway = (
            record.scale_second
            * (dn_second - unit_second * jnp.mean(dn_second * unit_second, -1, keepdims=True))
            + out_grad
        )
        g_attn = d_midway.astype(jnp.bfloat16)
        d_out_seq = contract_last(g_attn, w_out).astype(jnp.bfloat16)
        d_out_heads = lax.all_to_all(
            d_out_seq.reshape(short_len, head_count, group_size * HDIM),
            HEAD,
            split_axis=1,
            concat_axis=0,
            tiled=True,
        )
        kv_all = lax.all_gather(record.kv_local, WIDE, axis=0, tiled=True)
        grad_query, grad_keyval = attend_backward(
            record.query_rows,
            kv_all,
            query_pos,
            key_pos,
            record.log_total,
            to_rows(d_out_heads),
        )
        keyval_local = lax.psum_scatter(
            grad_keyval.astype(jnp.bfloat16), WIDE, scatter_dimension=0, tiled=True
        )
        q_back = lax.all_to_all(
            from_rows(grad_query.astype(jnp.bfloat16)),
            HEAD,
            split_axis=0,
            concat_axis=1,
            tiled=True,
        )
        kv_back = lax.all_to_all(
            keyval_local.reshape(local_rows, 1, 2 * HDIM),
            HEAD,
            split_axis=0,
            concat_axis=1,
            tiled=True,
        )
        d_queries = rotate_back(
            q_back.astype(jnp.float32).reshape(short_len, HEADS, HDIM), cosine, sine_table
        )
        d_kv = jnp.sum(kv_back.astype(jnp.float32).reshape(short_len, KV, slot_rep, 2, HDIM), 2)
        d_keys = rotate_back(d_kv[:, :, 0], cosine, sine_table)
        d_qkv = jnp.concatenate(
            [
                d_queries.reshape(short_len, query_width),
                d_keys.reshape(short_len, kv_width),
                d_kv[:, :, 1].reshape(short_len, kv_width),
            ],
            1,
        ).astype(jnp.bfloat16)
        bias_grad = jnp.sum(d_qkv.astype(jnp.float32), 0)
        d_normed = contract_last(d_qkv, w_qkv)
        unit_first = record.layer_in * record.scale_first
        gain1_grad = jnp.sum(d_normed * unit_first, 0)
        dn_first = d_normed * gain_first
        d_layer_in = (
            record.scale_first
            * (dn_first - unit_first * jnp.mean(dn_first * unit_first, -1, keepdims=True))
            + d_midway
        )
        kept_grads = (
            record.normed,
            d_qkv,
            record.out_seq,
            g_attn,
            record.normed2,
            d_gate,
            d_up,
            g_mlp,
            record.hidden,
        )
        d_layer_in, kept_grads, small_parts = (
            d_layer_in,
            kept_grads,
            (gain1_grad, gain2_grad, bias_grad),
        )
        is_valid = jnp.where(
            (step_index - 1 + section_pos >= 0) & (step_index - 1 + section_pos < micro_count),
            1.0,
            0.0,
        )
        small_totals = jax.tree.map(
            lambda total_part, new_part: total_part + is_valid * new_part, small_totals, small_parts
        )
        sent_grad = d_layer_in.astype(jnp.bfloat16)
        grads_list.append(sent_grad)
        kept_list.append(kept_grads)
        if step_index < micro_count:
            incoming_grad = passed_along(sent_grad, SECTION, -1)
    input_grads = lax.dynamic_slice_in_dim(jnp.stack(grads_list), 1 - section_pos, micro_count, 0)[
        None
    ]
    operands = jax.tree.map(
        lambda *arrays: lax.dynamic_slice_in_dim(
            jnp.stack(arrays), 1 - section_pos, micro_count, 0
        ).reshape(micro_count * short_len, arrays[0].shape[1]),
        *kept_list
    )
    terms = lax.psum_scatter(
        make_terms(operands, 1.0)(jnp.int32(0), owned_rows * lax.axis_size((HEAD, WIDE))),
        (HEAD, WIDE),
        scatter_dimension=0,
        tiled=True,
    )
    qkv_grad = terms[:, :qkv_cols]
    out_grad_rows = terms[:, qkv_cols : qkv_cols + width]
    gate_grad = terms[:, qkv_cols + width : qkv_cols + width + ff_cols]
    up_grad = terms[:, qkv_cols + width + ff_cols : qkv_cols + width + 2 * ff_cols]
    down_grad = terms[:, qkv_cols + width + 2 * ff_cols :]
    gain1_total, gain2_total, bias_total = lax.psum(
        (small_totals[0], small_totals[1], small_totals[2]), (HEAD, WIDE)
    )
    gains_grad = jnp.stack([gain1_total, gain2_total])[None]
    return (
        section_outputs,
        input_grads,
        gains_grad,
        qkv_grad[None],
        bias_total[None],
        out_grad_rows[None],
        gate_grad[None],
        up_grad[None],
        down_grad[None],
    )


def both_sections(own):
    section = lax.axis_index(SECTION)
    other = lax.ppermute(own, SECTION, [(0, 1), (1, 0)])
    first = jnp.where(section == 0, own, other)
    second = jnp.where(section == 0, other, own)
    return first, second


def greet_all(heads):
    section, head, wide = (lax.axis_index(axis) for axis in (SECTION, HEAD, WIDE))
    barrier = pltpu.get_barrier_semaphore()
    partners = [{SECTION: 1 - section}, {WIDE: beside(wide, 0)}, {WIDE: beside(wide, 1)}]
    partners += [{HEAD: lax.rem(head + shift, heads)} for shift in range(1, heads)]
    for partner in partners:
        pl.semaphore_signal(barrier, 1, device_id=partner, device_id_type=MESH)
    pl.semaphore_wait(barrier, len(partners))


def beside(wide, axis):
    low, high = lax.rem(wide, 2), lax.div(wide, 2)
    if axis == 0:
        return high * 2 + (1 - low)
    if axis == 1:
        return (1 - high) * 2 + low
    return (1 - high) * 2 + (1 - low)


def start_kernel(
    qkv_own,
    out_own,
    parts,
    qkv_all,
    out_all,
    first_all,
    second_parts,
    given_first,
    given_second,
    local_sem,
    swap_sem,
    shift_sem,
    line_sem,
    wide_sem,
    half_sem,
    pair_sem,
):
    section, head, wide = (lax.axis_index(axis) for axis in (SECTION, HEAD, WIDE))
    heads, wides = lax.axis_size(HEAD), lax.axis_size(WIDE)
    rows = qkv_own.shape[0]
    half = rows // 2
    owns = (qkv_own, out_own)
    here = [beside(wide, 0), beside(wide, 1), beside(wide, 2)]

    def place(which, layer, head_at, wide_at, start=0, count=None):
        block = head_at * wides + wide_at if which == 1 else wide_at * heads + head_at
        first = pl.multiple_of(block * rows + start, 16)
        span = pl.ds(first, rows if count is None else count)
        return first_all.at[span] if which == 2 else (qkv_all, out_all)[which].at[layer, span]

    def remote(source, target, sems, at, partner):
        return pltpu.make_async_remote_copy(
            source,
            target,
            sems.at[(0,) + at],
            sems.at[(1,) + at],
            device_id=partner,
            device_id_type=MESH,
        )

    other = {SECTION: 1 - section}

    def line(which, way, hop):
        step = 1 if way == 0 else -1
        target = place(which, section, head - step * hop, wide)
        source = owns[which] if hop == 0 else target
        return remote(source, target, line_sem, (which, way, hop), {HEAD: head + step})

    def across(which, axis, number, origin):
        target = place(which, section, origin, wide)
        source = owns[which] if number == 0 and which < 2 else target
        return remote(source, target, wide_sem, (which, axis, number), {WIDE: here[axis]})

    def across_in(which, axis, number, origin):
        target = place(which, section, origin, here[axis])
        return remote(target, target, wide_sem, (which, axis, number), {WIDE: here[axis]})

    def diagonal(which, axis, number, origin):
        target = place(which, section, origin, here[1 - axis], (1 - axis) * half, half)
        return remote(target, target, half_sem, (which, axis, number), {WIDE: here[axis]})

    def diagonal_in(which, axis, number, origin):
        target = place(which, section, origin, here[2], (1 - axis) * half, half)
        return remote(target, target, half_sem, (which, axis, number), {WIDE: here[axis]})

    def pair(which, kind, number, origin, layer):
        if kind == 0:
            target = place(which, layer, origin, wide)
        elif kind in (1, 2):
            target = place(which, layer, origin, here[kind - 1])
        else:
            target = place(which, layer, origin, here[2], (4 - kind) * half, half)
        return remote(target, target, pair_sem, (which, kind, number), other)

    def pair_own(which):
        target = place(which, section, head, wide)
        return remote(owns[which], target, pair_sem, (which, 0, 0), other)

    def swap(target):
        return remote(parts.at[1 - section], target, swap_sem, (), other)

    def shift(layer, source, distance):
        target_head = lax.rem(head + distance, heads)
        target = place(2, 0, head, wide) if layer == 0 else second_parts.at[head]
        return remote(
            source.at[target_head], target, shift_sem, (layer, distance), {HEAD: target_head}
        )

    def shift_in(layer, distance):
        origin = lax.rem(head + heads - distance, heads)
        target = place(2, 0, origin, wide) if layer == 0 else second_parts.at[origin]
        return remote(target, target, shift_sem, (layer, distance), {HEAD: head})

    def shift_all(layer, source):
        for here_at in range(heads):

            @pl.when(head == here_at)
            def _(here_at=here_at):
                others = [at for at in range(heads) if at != here_at]
                for at in sorted(others, key=lambda at: abs(at - here_at)):
                    shift(layer, source, (at - here_at) % heads).start()

        target = place(2, 0, head, wide) if layer == 0 else second_parts.at[head]
        pltpu.make_async_copy(source.at[head], target, local_sem.at[2 + layer]).start()

    def shift_own(layer):
        target = place(2, 0, head, wide) if layer == 0 else second_parts.at[head]
        return pltpu.make_async_copy(target, target, local_sem.at[2 + layer])

    greet_all(heads)
    first = section == 0
    second = section == 1

    for which in (0, 1):
        for way, go in ((0, head < heads - 1), (1, head > 0)):

            @pl.when(go)
            def _(which=which, way=way):
                line(which, way, 0).start()

    @pl.when(first)
    def _():
        swap(given_first).start()

    @pl.when(second)
    def _():
        swap(given_second).start()

    locals_ = [
        pltpu.make_async_copy(owns[which], place(which, section, head, wide), local_sem.at[which])
        for which in (0, 1)
    ]
    for which in (0, 1):
        locals_[which].start()
        for axis in (0, 1):
            across(which, axis, 0, head).start()
        pair_own(which).start()

    def each(hop):
        yield 2 * hop - 1, 0, head - hop, head >= hop, head < heads - 1
        yield 2 * hop, 1, head + hop, head + hop < heads, head > 0

    def forward_halves(number, origin):
        for which in (0, 1):
            for axis in (0, 1):
                across_in(which, axis, number, origin).wait_recv()
                diagonal(which, 1 - axis, number, origin).start()
                pair(which, 1 + axis, number, origin, section).start()

    def finish_halves(number, origin):
        for which in (0, 1):
            for axis in (0, 1):
                diagonal_in(which, axis, number, origin).wait_recv()
                pair(which, 3 + axis, number, origin, section).start()

    for hop in range(1, heads):
        for number, way, origin, comes, goes in each(hop):

            @pl.when(comes)
            def _(number=number, way=way, origin=origin, goes=goes, hop=hop):
                for which in (0, 1):
                    arrived = place(which, section, origin, wide)
                    remote(
                        arrived, arrived, line_sem, (which, way, hop - 1), {HEAD: head}
                    ).wait_recv()

                    @pl.when(goes)
                    def _(which=which):
                        line(which, way, hop).start()

                    for axis in (0, 1):
                        across(which, axis, number, origin).start()
                    pair(which, 0, number, origin, section).start()

        if hop == 1:
            forward_halves(0, head)
        else:
            for number, way, origin, comes, goes in each(hop - 1):

                @pl.when(comes)
                def _(number=number, origin=origin):
                    forward_halves(number, origin)

    @pl.when(first)
    def _():
        swap(given_second).wait_recv()
        shift_all(0, parts.at[0])

    @pl.when(second)
    def _():
        swap(given_first).wait_recv()
        shift_all(0, given_first)

    for number, way, origin, comes, goes in each(heads - 1):

        @pl.when(comes)
        def _(number=number, origin=origin):
            forward_halves(number, origin)

    def spread(number):
        for axis in (0, 1):
            across(2, axis, number, lax.rem(head + heads - number, heads)).start()

    shift_own(0).wait()
    spread(0)
    finish_halves(0, head)
    for hop in range(1, heads):
        for number, way, origin, comes, goes in each(hop):

            @pl.when(comes)
            def _(number=number, origin=origin):
                finish_halves(number, origin)

    for distance in range(1, heads):
        shift_in(0, distance).wait_recv()
        spread(distance)

    @pl.when(first)
    def _():
        shift_all(1, given_second)

    @pl.when(second)
    def _():
        shift_all(1, parts.at[1])

    for number in range(heads):
        origin = lax.rem(head + heads - number, heads)
        for axis in (0, 1):
            across_in(2, axis, number, origin).wait_recv()
            diagonal(2, 1 - axis, number, origin).start()

    for number in range(heads):
        origin = lax.rem(head + heads - number, heads)
        for axis in (0, 1):
            diagonal_in(2, axis, number, origin).wait_recv()
            diagonal(2, axis, number, origin).wait_send()
            across(2, axis, number, origin).wait_send()

    def settle(number, origin):
        for which in (0, 1):
            for axis in (0, 1):
                across(which, axis, number, origin).wait_send()
                diagonal(which, axis, number, origin).wait_send()
            for kind in range(5):
                if kind == 0 and number == 0:
                    pair_own(which).wait_send()
                else:
                    pair(which, kind, number, origin, section).wait_send()
                pair(which, kind, number, origin, 1 - section).wait_recv()

    for which in (0, 1):
        locals_[which].wait()
        for way, go in ((0, head < heads - 1), (1, head > 0)):

            @pl.when(go)
            def _(which=which, way=way):
                line(which, way, 0).wait_send()

    settle(0, head)
    for hop in range(1, heads):
        for number, way, origin, comes, goes in each(hop):

            @pl.when(comes)
            def _(number=number, way=way, origin=origin, goes=goes, hop=hop):
                settle(number, origin)

                @pl.when(goes)
                def _():
                    for which in (0, 1):
                        line(which, way, hop).wait_send()

    swap(given_first).wait_send()
    shift_own(1).wait()
    for distance in range(1, heads):
        for layer in (0, 1):
            shift(layer, given_first, distance).wait_send()
        shift_in(1, distance).wait_recv()


def start_weights(qkv_own, out_own, parts, number):
    heads, wides = lax.axis_size(HEAD), lax.axis_size(WIDE)
    rows, qkv_cols = qkv_own.shape
    out_cols = out_own.shape[1]
    numbers = 2 * heads - 1
    whole = heads * wides * rows
    dtype = parts.dtype
    dma = pltpu.SemaphoreType.DMA
    anywhere = pl.BlockSpec(memory_space=pl.ANY)
    return pl.pallas_call(
        start_kernel,
        out_shape=(
            jax.ShapeDtypeStruct((2, whole, qkv_cols), dtype),
            jax.ShapeDtypeStruct((2, whole, out_cols), dtype),
            jax.ShapeDtypeStruct((whole, parts.shape[3]), dtype),
            jax.ShapeDtypeStruct(parts.shape[1:], dtype),
        ),
        in_specs=[anywhere] * 3,
        out_specs=(anywhere,) * 4,
        scratch_shapes=[
            pltpu.VMEM(parts.shape[1:], dtype),
            pltpu.VMEM(parts.shape[1:], dtype),
            dma((4,)),
            dma((2,)),
            dma((2, 2, heads)),
            dma((2, 2, 2, heads)),
            dma((2, 3, 2, numbers)),
            dma((2, 3, 2, numbers)),
            dma((2, 2, 5, numbers)),
        ],
        compiler_params=pltpu.CompilerParams(
            collective_id=number, has_side_effects=True, vmem_limit_bytes=60 * 2**20
        ),
    )(qkv_own, out_own, parts)


def finish_kernel(
    first_terms,
    second_terms,
    small,
    first_parts,
    second_parts,
    tokens_in,
    totals,
    small_total,
    low_parts,
    high_parts,
    tokens_out,
    near_buf,
    middle,
    far_buf,
    sums,
    line_buf,
    small_sum,
    small_buf,
    shifted,
    give,
    local_sem,
    shift_sem,
    swap_sem,
    near_sem,
    far_sem,
    line_sem,
    small_sem,
    give_sem,
    token_sem,
):
    section, head, wide = (lax.axis_index(axis) for axis in (SECTION, HEAD, WIDE))
    heads, wides = lax.axis_size(HEAD), lax.axis_size(WIDE)
    here = [beside(wide, 0), beside(wide, 1), beside(wide, 2)]
    columns = first_terms.shape[2]
    terms = (first_terms, second_terms)
    other = {SECTION: 1 - section}
    first, second = section == 0, section == 1
    sender_rows = tokens_in.shape[2]

    def remote(source, target, sems, at, partner):
        return pltpu.make_async_remote_copy(
            source,
            target,
            sems.at[(0,) + at],
            sems.at[(1,) + at],
            device_id=partner,
            device_id_type=MESH,
        )

    def shift(distance, target):
        target_head = lax.rem(head + distance, heads)
        return remote(
            first_parts.at[target_head],
            target.at[head],
            shift_sem,
            (distance,),
            {HEAD: target_head},
        )

    def shift_in(distance, target):
        arrived = target.at[lax.rem(head + heads - distance, heads)]
        return remote(arrived, arrived, shift_sem, (distance,), {HEAD: head})

    def near(side, turn, target):
        wide_at = here[side] if turn == 0 else here[2]
        return remote(
            terms[side].at[wide_at * heads + target],
            near_buf.at[side, turn, target],
            near_sem,
            (side, turn, target),
            {WIDE: here[side]},
        )

    def far(side, target):
        return remote(
            middle.at[side, target],
            far_buf.at[side, target],
            far_sem,
            (side, target),
            {WIDE: here[1 - side]},
        )

    def line(way, target, side):
        step = 1 if way == 0 else -1
        return remote(
            sums.at[target, side],
            line_buf.at[way, target, side],
            line_sem,
            (way, target, side),
            {HEAD: head + step},
        )

    def token_target(layer, which, sender_wide, sender_section):
        first_row = pl.multiple_of(sender_section * sender_rows, 16)
        return tokens_out.at[which, sender_wide, pl.ds(first_row, sender_rows)]

    def token(layer, which, turn):
        wide_at = wide if turn == 3 else here[turn]
        sems = (token_sem.at[0, layer, which, turn], token_sem.at[1, section, which, turn])
        return pltpu.make_async_remote_copy(
            tokens_in.at[which * 2 + layer, wide_at],
            token_target(layer, which, wide, section),
            *sems,
            device_id={SECTION: layer, WIDE: wide_at},
            device_id_type=MESH,
        )

    def token_in(from_section, which, turn):
        wide_at = wide if turn == 3 else here[turn]
        target = token_target(section, which, wide_at, from_section)
        sems = (token_sem.at[0, section, which, turn], token_sem.at[1, from_section, which, turn])
        return pltpu.make_async_remote_copy(
            target, target, *sems, device_id={HEAD: head}, device_id_type=MESH
        )

    barrier = pltpu.get_barrier_semaphore()
    partners = [other] + [{WIDE: wide_at} for wide_at in here]
    partners += [{SECTION: 1 - section, WIDE: wide_at} for wide_at in here]
    partners += [{HEAD: lax.rem(head + distance, heads)} for distance in range(1, heads)]
    for partner in partners:
        pl.semaphore_signal(barrier, 1, device_id=partner, device_id_type=MESH)
    pl.semaphore_wait(barrier, len(partners))

    order = []
    for at in range(heads // 2):
        order += [heads - 1 - at, at]

    def start_near(turn, target):
        for side in (0, 1):
            near(side, turn, target).start()

    start_near(1, order[0])
    start_near(0, order[0])

    @pl.when(first)
    def _():
        for distance in range(1, heads):
            shift(distance, low_parts).start()
        remote(second_parts, low_parts, swap_sem, (0,), other).start()
        pltpu.make_async_copy(first_parts.at[head], low_parts.at[head], local_sem.at[0]).start()

    @pl.when(second)
    def _():
        for distance in range(1, heads):
            shift(distance, shifted).start()
        pltpu.make_async_copy(second_parts, high_parts, local_sem.at[1]).start()
        remote(
            first_parts.at[head], high_parts.at[head], swap_sem, (1,), other
        ).start()

    for which in (0, 1):
        for turn in range(4):
            for layer in (0, 1):

                @pl.when((turn < 3) | (section != layer))
                def _(layer=layer, which=which, turn=turn):
                    token(layer, which, turn).start()

        pltpu.make_async_copy(
            tokens_in.at[which * 2 + section, wide],
            token_target(section, which, wide, section),
            local_sem.at[2 + which],
        ).start()

    steps = [other, {WIDE: here[0]}, {WIDE: here[1]}]
    steps += [{HEAD: lax.rem(head + distance, heads)} for distance in range(1, heads)]

    def small_copy(at):
        source = small.at[1 - section] if at == 0 else small_sum.at[min(at, 3)]
        return remote(source, small_buf.at[at], small_sem, (at,), steps[at])

    for at in range(3):
        small_copy(at).start()
        small_copy(at).wait()
        small_sum[at + 1] = (small[section] if at == 0 else small_sum[at]) + small_buf[at]
    for at in range(3, len(steps)):
        small_copy(at).start()

    def across(number):
        target = order[number]
        for side in (0, 1):
            near(side, 1, target).wait_recv()
            middle[side, target] = (
                terms[side][here[1 - side] * heads + target].astype(jnp.float32)
                + near_buf[side, 1, target].astype(jnp.float32)
            ).astype(middle.dtype)
            far(side, target).start()
        if number + 1 < heads:
            start_near(1, order[number + 1])
        for side in (0, 1):
            near(side, 0, target).wait_recv()
        if number + 1 < heads:
            start_near(0, order[number + 1])

    def collect(target, last):
        for side in (0, 1):
            far(side, target).wait_recv()
            sums[target, side] = (
                terms[side][wide * heads + target].astype(jnp.float32)
                + near_buf[side, 0, target].astype(jnp.float32)
                + far_buf[side, target].astype(jnp.float32)
            ).astype(sums.dtype)
            if target > 0:

                @pl.when(head == 0)
                def _(side=side):
                    line(0, target, side).start()

            if target < heads - 1:

                @pl.when(head == heads - 1)
                def _(side=side):
                    line(1, target, side).start()
                    if last and side == 0:
                        line(1, target, side).wait_send()

    def pass_on(at_head, way, target):
        @pl.when(head == at_head)
        def _():
            for side in (0, 1):
                line(way, target, side).wait_recv()
                sums[target, side] = (
                    sums[target, side].astype(jnp.float32)
                    + line_buf[way, target, side].astype(jnp.float32)
                ).astype(sums.dtype)
                line(way, target, side).start()

    passes = {
        1: [(1, 0, 3)],
        2: [(2, 0, 3), (2, 1, 0)],
        3: [(1, 1, 0), (1, 0, 2), (2, 1, 1)],
    }
    for number, target in enumerate(order):
        across(number)
        collect(target, number == heads - 1)
        for entry in passes.get(number, ()):
            pass_on(*entry)

    @pl.when(second)
    def _():
        for distance in range(1, heads):
            shift_in(distance, shifted).wait_recv()
            origin = lax.rem(head + heads - distance, heads)
            remote(
                shifted.at[origin], high_parts.at[origin], swap_sem, (1 + distance,), other
            ).start()

    whole = small_sum[3]
    for at in range(3, len(steps)):
        small_copy(at).wait()
        whole = whole + small_buf[at]
    small_total[...] = whole

    for target in range(heads):

        @pl.when(head == target)
        def _(target=target):
            for side in (0, 1):
                value = sums[target, side].astype(jnp.float32)
                for way, comes in ((0, target > 0), (1, target < heads - 1)):
                    if comes:
                        line(way, target, side).wait_recv()
                        value = value + line_buf[way, target, side].astype(jnp.float32)
                give[side] = value

        for side in (0, 1):
            for turn in (0, 1):
                near(side, turn, target).wait_send()
            far(side, target).wait_send()

            @pl.when(head < target)
            def _(target=target, side=side):
                line(0, target, side).wait_send()

            early = target == order[-1] and side == 0

            @pl.when((head > target) & ((head < heads - 1) | (not early)))
            def _(target=target, side=side):
                line(1, target, side).wait_send()

    handed = remote(give.at[1 - section], totals.at[section], give_sem, (), other)
    handed.start()
    totals[section] = give[section]

    for which in (0, 1):
        pltpu.make_async_copy(
            tokens_in.at[which * 2 + section, wide],
            token_target(section, which, wide, section),
            local_sem.at[2 + which],
        ).wait()
        for turn in range(4):
            for layer in (0, 1):

                @pl.when((turn < 3) | (section != layer))
                def _(layer=layer, which=which, turn=turn):
                    token(layer, which, turn).wait_send()
                    token_in(layer, which, turn).wait_recv()

    @pl.when(first)
    def _():
        for distance in range(1, heads):
            shift(distance, low_parts).wait_send()
            shift_in(distance, low_parts).wait_recv()
        remote(second_parts, low_parts, swap_sem, (0,), other).wait_send()
        pltpu.make_async_copy(first_parts.at[head], low_parts.at[head], local_sem.at[0]).wait()
        for distance in range(heads):
            arrived = high_parts.at[lax.rem(head + heads - distance, heads)]
            remote(arrived, arrived, swap_sem, (1 + distance,), other).wait_recv()

    @pl.when(second)
    def _():
        for distance in range(1, heads):
            shift(distance, shifted).wait_send()
        pltpu.make_async_copy(second_parts, high_parts, local_sem.at[1]).wait()
        for distance in range(heads):
            sent = high_parts.at[lax.rem(head + heads - distance, heads)]
            remote(sent, sent, swap_sem, (1 + distance,), other).wait_send()
        remote(second_parts, low_parts, swap_sem, (0,), other).wait_recv()

    handed.wait_send()
    remote(totals.at[1 - section], totals.at[1 - section], give_sem, (), other).wait_recv()


def finish_weights(
    first_terms, second_terms, small, first_parts, second_parts, tokens_in, number
):
    heads = lax.axis_size(HEAD)
    blocks, rows, columns = first_terms.shape
    dtype = first_terms.dtype
    dma = pltpu.SemaphoreType.DMA
    vmem = pl.BlockSpec(memory_space=pltpu.VMEM)
    anywhere = pl.BlockSpec(memory_space=pl.ANY)
    smalls = 2 + heads
    layers, wides, sender_rows, width = tokens_in.shape
    return pl.pallas_call(
        finish_kernel,
        out_shape=(
            jax.ShapeDtypeStruct((2, rows, columns), jnp.float32),
            jax.ShapeDtypeStruct(small.shape[1:], jnp.float32),
            jax.ShapeDtypeStruct(first_parts.shape, dtype),
            jax.ShapeDtypeStruct(first_parts.shape, dtype),
            jax.ShapeDtypeStruct((2, wides, 2 * sender_rows, width), dtype),
        ),
        in_specs=[vmem, vmem, vmem, anywhere, anywhere, anywhere],
        out_specs=(vmem, vmem, anywhere, anywhere, anywhere),
        scratch_shapes=[
            pltpu.VMEM((2, 2, heads, rows, columns), dtype),
            pltpu.VMEM((2, heads, rows, columns), dtype),
            pltpu.VMEM((2, heads, rows, columns), dtype),
            pltpu.VMEM((heads, 2, rows, columns), dtype),
            pltpu.VMEM((2, heads, 2, rows, columns), dtype),
            pltpu.VMEM((4,) + small.shape[1:], jnp.float32),
            pltpu.VMEM((smalls,) + small.shape[1:], jnp.float32),
            pltpu.VMEM(first_parts.shape, dtype),
            pltpu.VMEM((2, rows, columns), jnp.float32),
            dma((4,)),
            dma((2, heads)),
            dma((2, 1 + heads)),
            dma((2, 2, 2, heads)),
            dma((2, 2, heads)),
            dma((2, 2, heads, 2)),
            dma((2, smalls)),
            dma((2,)),
            dma((2, 2, 2, 4)),
        ],
        compiler_params=pltpu.CompilerParams(
            collective_id=number, has_side_effects=True, vmem_limit_bytes=60 * 2**20
        ),
    )(first_terms, second_terms, small, first_parts, second_parts, tokens_in)


def cut_kernel(gate, up, down, out, parts, out_inner):
    count, part = parts.shape[0], parts.shape[2] // 3
    heads, wides = lax.axis_size(HEAD), lax.axis_size(WIDE)
    size = out.shape[1] // (heads * wides)
    places = [(head * wides + wide) * size for wide in range(wides) for head in range(heads)]
    whole = out[...]
    out_inner[...] = jnp.concatenate([whole[:, start : start + size] for start in places], 1)
    for at in range(count):
        size = min(part, gate.shape[1] - at * part)
        for which, weight in enumerate((gate, up, down)):
            start = which * part
            parts[at, :, pl.ds(start, size)] = weight[:, pl.ds(at * part, size)]
            if size < part:
                rest = part - size
                parts[at, :, pl.ds(start + size, rest)] = jnp.zeros(
                    (parts.shape[1], rest), parts.dtype
                )


def cut_parts(gate, up, down, out, count, part):
    rows, columns = gate.shape
    step = 16
    weight = pl.BlockSpec((step, columns), lambda at: (at, 0))
    square = pl.BlockSpec((step, out.shape[1]), lambda at: (at, 0))
    return pl.pallas_call(
        cut_kernel,
        grid=(rows // step,),
        out_shape=(
            jax.ShapeDtypeStruct((count, rows, 3 * part), gate.dtype),
            jax.ShapeDtypeStruct(out.shape, out.dtype),
        ),
        in_specs=[weight] * 3 + [square],
        out_specs=(pl.BlockSpec((count, step, 3 * part), lambda at: (0, at, 0)), square),
        compiler_params=pltpu.CompilerParams(vmem_limit_bytes=24 * 2**20),
    )(gate, up, down, out)


def join_kernel(low, high, totals, gate, up, down, qkv, out):
    count, part = low.shape[0], low.shape[2] // 3
    for at in range(2 * count):
        size = min(part, gate.shape[2] - at * part)
        source = low if at < count else high
        for which, grad in enumerate((gate, up, down)):
            grad[0, :, pl.ds(at * part, size)] = source[
                at % count, :, pl.ds(which * part, size)
            ].astype(grad.dtype)
    cut, width = qkv.shape[2] // 2, out.shape[2]
    for at in (0, 1):
        qkv[0, :, pl.ds(at * cut, cut)] = totals[at, :, pl.ds(0, cut)]
    whole = jnp.concatenate([totals[at, :, pl.ds(cut, width // 2)] for at in (0, 1)], 1)
    heads, wides = lax.axis_size(HEAD), lax.axis_size(WIDE)
    size = width // (heads * wides)
    places = [(wide * heads + head) * size for head in range(heads) for wide in range(wides)]
    out[0] = jnp.concatenate([whole[:, start : start + size] for start in places], 1)


def join_parts(low, high, totals, columns, qkv_cols):
    count, rows, width = low.shape
    out_cols = 2 * totals.shape[2] - qkv_cols
    step = 16
    part = pl.BlockSpec((count, step, width), lambda at: (0, at, 0))
    total = pl.BlockSpec((2, step, totals.shape[2]), lambda at: (0, at, 0))
    sizes = (columns, columns, columns, qkv_cols, out_cols)
    return pl.pallas_call(
        join_kernel,
        grid=(rows // step,),
        out_shape=tuple(jax.ShapeDtypeStruct((1, rows, size), jnp.float32) for size in sizes),
        in_specs=[part, part, total],
        out_specs=tuple(pl.BlockSpec((1, step, size), lambda at: (0, at, 0)) for size in sizes),
        compiler_params=pltpu.CompilerParams(vmem_limit_bytes=24 * 2**20),
    )(low, high, totals)


def visit(head, step, heads):
    inner_chip = jnp.minimum(jnp.minimum(head, heads - 1 - head), 1)
    at = step + inner_chip * (1 - lax.div(step, 2)) * (1 - 2 * step)
    return at + lax.div(2 * head, heads) * (heads - 1 - 2 * at)


def group_pipeline(block, everyone, out, scratch, prepare, compute, settle, extras=()):
    (partial, pair_buf, sums, line_buf, own_sem, pair_sem, line_sem, swap_sem, chain_sem) = scratch
    section, head = lax.axis_index(SECTION), lax.axis_index(HEAD)
    heads = lax.axis_size(HEAD)
    tokens = block.shape[0]
    other = {SECTION: 1 - section}

    def place(section_at, origin):
        start = (origin * 2 + section_at) * tokens
        return everyone.at[pl.ds(pl.multiple_of(start, tokens), tokens)]

    def remote(source, target, send, receive, partner):
        return pltpu.make_async_remote_copy(
            source, target, send, receive, device_id=partner, device_id_type=MESH
        )

    def pair(origin, source):
        target = place(section, origin)
        return remote(source, target, pair_sem.at[0, origin], pair_sem.at[1, origin], other)

    def pair_in(origin):
        target = place(1 - section, origin)
        return remote(target, target, pair_sem.at[0, origin], pair_sem.at[1, origin], other)

    def line(way, hop, source):
        step = 1 - 2 * way
        target = place(section, head - step * hop)
        sems = (line_sem.at[0, way, hop], line_sem.at[1, way, hop])
        return remote(source, target, *sems, {HEAD: head + step})

    def inside(place_at):
        return (place_at >= 0) & (place_at < heads)

    def accept(way, hop):
        step = 1 - 2 * way
        here = place(section, head - step * hop)
        line(way, hop - 1, here).wait_recv()

        @pl.when(inside(head + step))
        def _():
            line(way, hop, here).start()

        pair(head - step * hop, here).start()

    def swap(origin):
        return remote(
            partial.at[origin, 1 - section],
            pair_buf.at[origin],
            swap_sem.at[0, origin],
            swap_sem.at[1, origin],
            other,
        )

    def lot(piece):
        size = tokens // CHAIN_PIECES
        return pl.ds(piece * size, size)

    def chain(way, target, piece):
        return remote(
            sums.at[target, lot(piece)],
            line_buf.at[way, target, lot(piece)],
            chain_sem.at[0, way, target, piece],
            chain_sem.at[1, way, target, piece],
            {HEAD: head + 1 - 2 * way},
        )

    def send_pieces(way, target, last):
        for piece in range(CHAIN_PIECES):
            chain(way, target, piece).start()
            if last and piece < CHAIN_PIECES - 1:
                chain(way, target, piece).wait_send()

    def deliver(origin, last=False):
        swap(origin).wait_recv()
        sums[origin] = (
            partial[origin, section].astype(jnp.float32) + pair_buf[origin].astype(jnp.float32)
        ).astype(sums.dtype)

        @pl.when((head == 0) & (origin > 0))
        def _():
            send_pieces(0, origin, last)

        @pl.when((head == heads - 1) & (origin < heads - 1))
        def _():
            send_pieces(1, origin, last)

    def pass_on(way, target, piece):
        chain(way, target, piece).wait_recv()
        here = lot(piece)
        sums[target, here] = (
            sums[target, here].astype(jnp.float32) + line_buf[way, target, here].astype(jnp.float32)
        ).astype(sums.dtype)
        chain(way, target, piece).start()

    barrier = pltpu.get_barrier_semaphore()
    partners = [other] + [{HEAD: lax.rem(head + shift, heads)} for shift in range(1, heads)]
    for partner in partners:
        pl.semaphore_signal(barrier, 1, device_id=partner, device_id_type=MESH)
    pl.semaphore_wait(barrier, len(partners))

    for way in (0, 1):

        @pl.when(inside(head + 1 - 2 * way))
        def _(way=way):
            line(way, 0, block).start()

    pair(head, block).start()
    own = pltpu.make_async_copy(block, place(section, head), own_sem)
    own.start()
    prepare()
    own.wait()

    def one(step, carry):
        origin = visit(head, step, heads)

        @pl.when(step >= 1)
        def _():
            deliver(visit(head, step - 1, heads))

        @pl.when(step == 1)
        def _():
            for way in (0, 1):

                @pl.when(inside(head - (1 - 2 * way)))
                def _(way=way):
                    accept(way, 1)

        hop = jnp.maximum(origin - head, head - origin)

        @pl.when((step >= 2) & (hop >= 2))
        def _():
            accept(lax.div(jnp.maximum(origin - head, 0) + heads - 2, heads), hop)

        pair_in(origin).wait_recv()
        compute(origin)
        swap(origin).start()
        return carry

    lax.fori_loop(0, heads, one, 0)
    deliver(visit(head, heads - 1, heads), True)

    between = (head > 0) & (head < heads - 1)
    side = lax.div(2 * head, heads)
    ends = ((1 - side) * (heads - 1), side * (heads - 1))
    extras = list(extras)

    def work(count):
        for _ in range(min(count, len(extras))):
            extras.pop(0)()

    work(2)

    @pl.when(between)
    def _():
        for piece in range(CHAIN_PIECES):
            pass_on(side, heads - 1 - head, piece)

    for piece in range(CHAIN_PIECES):

        @pl.when(between)
        def _(piece=piece):
            pass_on(side, ends[0], piece)
            pass_on(1 - side, ends[1], piece)

        work(1)

    work(len(extras))
    settle()
    out[...] = sums[head].astype(jnp.float32)
    for way, comes in ((0, head > 0), (1, head < heads - 1)):

        @pl.when(comes)
        def _(way=way):
            for piece in range(CHAIN_PIECES):
                chain(way, head, piece).wait_recv()
            out[...] += line_buf[way, head].astype(jnp.float32)

    for piece in range(CHAIN_PIECES):
        for target in range(1, heads):

            if target < heads - 1 or piece == CHAIN_PIECES - 1:

                @pl.when(head == 0)
                def _(piece=piece, target=target):
                    chain(0, target, piece).wait_send()

                @pl.when(head == heads - 1)
                def _(piece=piece, target=target):
                    chain(1, heads - 1 - target, piece).wait_send()

        @pl.when(between)
        def _(piece=piece):
            chain(side, heads - 1 - head, piece).wait_send()
            chain(side, ends[0], piece).wait_send()
            chain(1 - side, ends[1], piece).wait_send()

    for origin in range(heads):
        here = place(section, origin)
        pair(origin, here).wait_send()
        swap(origin).wait_send()

    for way in (0, 1):
        for hop in range(heads):
            step = 1 - 2 * way

            @pl.when(inside(head + step) & inside(head - step * hop))
            def _(way=way, hop=hop):
                line(way, hop, block).wait_send()


def pipeline_scratch(heads, tokens, columns, dtype):
    dma = pltpu.SemaphoreType.DMA
    return [
        pltpu.VMEM((heads, 2, tokens, columns), dtype),
        pltpu.VMEM((heads, tokens, columns), dtype),
        pltpu.VMEM((heads, tokens, columns), dtype),
        pltpu.VMEM((2, heads, tokens, columns), dtype),
        dma,
        dma((2, heads)),
        dma((2, 2, heads)),
        dma((2, heads)),
        dma((2, 2, heads, CHAIN_PIECES)),
    ]


PIPELINE_SCRATCH = 9
CHAIN_PIECES = 4
TERM_ROWS = 512
TERM_SLOTS = 3
STEP_COLUMNS = 384
STEP_WIDTH = 512


def chunks(total, size):
    return [(at, min(size, total - at)) for at in range(0, total, size)]


def write_partial(partial, origin, left, weights, columns):
    tokens = partial.shape[2]
    for start, count in chunks(partial.shape[3], STEP_WIDTH):
        piece = contract_last(left, weights[pl.ds(start, count), pl.ds(*columns)])
        piece = piece.astype(partial.dtype)
        partial[origin, 0, :, pl.ds(start, count)] = piece[:tokens]
        partial[origin, 1, :, pl.ds(start, count)] = piece[tokens:]


def forward_kernel(block, weights_hbm, out, everyone, gate_up_hbm, hidden_hbm, *scratch):
    shared, rest = scratch[:PIPELINE_SCRATCH], scratch[PIPELINE_SCRATCH:]
    weights, gate_up, hidden, load_sem, store_sem = rest
    partial = shared[0]
    heads = lax.axis_size(HEAD)
    rows = 2 * block.shape[0]
    part = hidden.shape[1]
    load = pltpu.make_async_copy(weights_hbm, weights, load_sem)

    def stores(origin):
        span = pl.ds(pl.multiple_of(origin * rows, rows), rows)
        return [
            pltpu.make_async_copy(gate_up.at[span], gate_up_hbm.at[span], store_sem.at[0, origin]),
            pltpu.make_async_copy(hidden.at[span], hidden_hbm.at[span], store_sem.at[1, origin]),
        ]

    def prepare():
        load.start()
        load.wait()

    def compute(origin):
        span = pl.ds(pl.multiple_of(origin * rows, rows), rows)
        left = everyone[span, :]
        for start, count in chunks(part, STEP_COLUMNS):
            gate = jnp.dot(
                left, weights[:, pl.ds(start, count)], preferred_element_type=jnp.float32
            )
            up = jnp.dot(
                left, weights[:, pl.ds(part + start, count)], preferred_element_type=jnp.float32
            )
            gate_up[span, pl.ds(start, count)] = gate.astype(gate_up.dtype)
            gate_up[span, pl.ds(part + start, count)] = up.astype(gate_up.dtype)
            hidden[span, pl.ds(start, count)] = (gate / (1.0 + jnp.exp(-gate)) * up).astype(
                hidden.dtype
            )
        write_partial(partial, origin, hidden[span, :], weights, (2 * part, part))
        for store in stores(origin):
            store.start()

    def settle():
        for origin in range(heads):
            for store in stores(origin):
                store.wait()

    group_pipeline(block, everyone, out, shared, prepare, compute, settle)


def backward_kernel(
    block, weights_hbm, gate_up_hbm, normed_hbm, hidden_hbm, out, terms_hbm, *scratch
):
    shared, rest = scratch[:PIPELINE_SCRATCH], scratch[PIPELINE_SCRATCH:]
    everyone, weights, gate_up, normed, hidden, d_gate_up, terms, load_sem, term_sem = rest
    partial = shared[0]
    rows = 2 * block.shape[0]
    part = hidden.shape[1]
    sources = ((weights_hbm, weights), (gate_up_hbm, gate_up))
    sources += ((normed_hbm, normed), (hidden_hbm, hidden))
    loads = [
        pltpu.make_async_copy(source, target, load_sem.at[at])
        for at, (source, target) in enumerate(sources)
    ]

    def prepare():
        for load in loads:
            load.start()
        for load in loads[:2]:
            load.wait()

    def compute(origin):
        span = pl.ds(pl.multiple_of(origin * rows, rows), rows)
        left = everyone[span, :]
        for start, count in chunks(part, STEP_COLUMNS):
            d_hidden = jnp.dot(
                left, weights[:, pl.ds(2 * part + start, count)], preferred_element_type=jnp.float32
            )
            gate = gate_up[span, pl.ds(start, count)].astype(jnp.float32)
            up = gate_up[span, pl.ds(part + start, count)].astype(jnp.float32)
            sigmoid = 1.0 / (1.0 + jnp.exp(-gate))
            d_gate = d_hidden * up * sigmoid * (1.0 + gate * (1.0 - sigmoid))
            d_gate_up[span, pl.ds(start, count)] = d_gate.astype(d_gate_up.dtype)
            d_up = d_hidden * gate * sigmoid
            d_gate_up[span, pl.ds(part + start, count)] = d_up.astype(d_gate_up.dtype)
        write_partial(partial, origin, d_gate_up[span, :], weights, (0, 2 * part))

    tiles = [(which, start) for which in range(3) for start, _ in chunks(block.shape[1], TERM_ROWS)]

    def store(number):
        which, start = tiles[number]
        slot = number % TERM_SLOTS
        target = terms_hbm.at[pl.ds(start, TERM_ROWS), pl.ds(which * part, part)]
        return pltpu.make_async_copy(terms.at[slot], target, term_sem.at[slot])

    def tile(number):
        which, start = tiles[number]
        if number == 0:
            for load in loads[2:]:
                load.wait()
        if number >= TERM_SLOTS:
            store(number - TERM_SLOTS).wait()
        left = (everyone if which == 2 else normed)[:, pl.ds(start, TERM_ROWS)]
        right = hidden[...] if which == 2 else d_gate_up[:, pl.ds(which * part, part)]
        terms[number % TERM_SLOTS] = contract_first(left, right).astype(terms.dtype)
        store(number).start()

    def settle():
        for number in range(len(tiles) - TERM_SLOTS, len(tiles)):
            store(number).wait()

    extras = [functools.partial(tile, number) for number in range(len(tiles))]
    group_pipeline(block, everyone, out, shared, prepare, compute, settle, extras)


def feed_forward(block, weights, number):
    heads = lax.axis_size(HEAD)
    tokens, width = block.shape
    part = weights.shape[1] // 3
    count = 2 * heads * tokens
    dtype = block.dtype
    vmem = pl.BlockSpec(memory_space=pltpu.VMEM)
    anywhere = pl.BlockSpec(memory_space=pl.ANY)
    return pl.pallas_call(
        forward_kernel,
        out_shape=(
            jax.ShapeDtypeStruct((tokens, width), jnp.float32),
            jax.ShapeDtypeStruct((count, width), dtype),
            jax.ShapeDtypeStruct((count, 2 * part), dtype),
            jax.ShapeDtypeStruct((count, part), dtype),
        ),
        in_specs=[vmem, anywhere],
        out_specs=(vmem, vmem, anywhere, anywhere),
        scratch_shapes=pipeline_scratch(heads, tokens, width, dtype)
        + [
            pltpu.VMEM(weights.shape, dtype),
            pltpu.VMEM((count, 2 * part), dtype),
            pltpu.VMEM((count, part), dtype),
            pltpu.SemaphoreType.DMA,
            pltpu.SemaphoreType.DMA((2, heads)),
        ],
        compiler_params=pltpu.CompilerParams(
            collective_id=number, has_side_effects=True, vmem_limit_bytes=60 * 2**20
        ),
        cost_estimate=pl.CostEstimate(
            flops=6 * count * width * part, bytes_accessed=2 * weights.size, transcendentals=0
        ),
    )(block, weights)


def feed_backward(block, weights, gate_up, normed, hidden, number):
    heads = lax.axis_size(HEAD)
    tokens, width = block.shape
    part = hidden.shape[1]
    count = 2 * heads * tokens
    dtype = block.dtype
    vmem = pl.BlockSpec(memory_space=pltpu.VMEM)
    anywhere = pl.BlockSpec(memory_space=pl.ANY)
    return pl.pallas_call(
        backward_kernel,
        out_shape=(
            jax.ShapeDtypeStruct((tokens, width), jnp.float32),
            jax.ShapeDtypeStruct(weights.shape, dtype),
        ),
        in_specs=[vmem] + [anywhere] * 4,
        out_specs=(vmem, anywhere),
        scratch_shapes=pipeline_scratch(heads, tokens, width, dtype)
        + [
            pltpu.VMEM((count, width), dtype),
            pltpu.VMEM(weights.shape, dtype),
            pltpu.VMEM(gate_up.shape, dtype),
            pltpu.VMEM((count, width), dtype),
            pltpu.VMEM((count, part), dtype),
            pltpu.VMEM((count, 2 * part), dtype),
            pltpu.VMEM((TERM_SLOTS, TERM_ROWS, part), dtype),
            pltpu.SemaphoreType.DMA((4,)),
            pltpu.SemaphoreType.DMA((TERM_SLOTS,)),
        ],
        compiler_params=pltpu.CompilerParams(
            collective_id=number, has_side_effects=True, vmem_limit_bytes=58 * 2**20
        ),
        cost_estimate=pl.CostEstimate(
            flops=12 * count * width * part, bytes_accessed=4 * weights.size, transcendentals=0
        ),
    )(block, weights, gate_up, normed, hidden)


GROUP = 3


def turn(tensor, cosine, sine):
    return tensor * cosine + pltpu.roll(tensor, tensor.shape[1] // 2, 1) * sine


def attention_grad_kernel(
    layer,
    moves,
    d_normed2,
    midway,
    scale2,
    out_grad,
    gains,
    queries,
    keyval,
    log_total,
    attended,
    normed,
    layer_in,
    scale1,
    cosine,
    sine,
    own_pos,
    key_pos,
    w_out_hbm,
    w_qkv_hbm,
    parts_in,
    d_in,
    small,
    terms_hbm,
    parts_out,
    w_out,
    w_qkv,
    d_midway,
    g_attn,
    d_attended,
    d_qkv,
    d_normed,
    d_keyval,
    terms,
    their_normed,
    their_attended,
    their_g,
    their_d,
    sums,
    pair_buf,
    line_buf,
    load_sem,
    give_sem,
    pair_sem,
    line_sem,
    shift_sem,
):
    section, head = lax.axis_index(SECTION), lax.axis_index(HEAD)
    heads, wides = lax.axis_size(HEAD), lax.axis_size(WIDE)
    tokens, width = normed.shape
    qkv_cols = d_qkv.shape[1]
    kv_width = KV * HDIM
    rows = width // (heads * wides)
    scaling = HDIM**-0.5
    other = {SECTION: 1 - section}

    def remote(source, target, sems, at, partner):
        return pltpu.make_async_remote_copy(
            source,
            target,
            sems.at[(0,) + at],
            sems.at[(1,) + at],
            device_id=partner,
            device_id_type=MESH,
        )

    def half(array, at):
        count = array.shape[1] // 2
        return array.at[:, pl.ds(pl.multiple_of(at * count, 128), count)]

    gives = [
        remote(normed, their_normed, give_sem, (0,), other),
        remote(attended, their_attended, give_sem, (1,), other),
        remote(half(g_attn, 1 - section), their_g, give_sem, (2,), other),
        remote(half(d_qkv, 1 - section), their_d, give_sem, (3,), other),
    ]
    loads = [
        pltpu.make_async_copy(w_out_hbm.at[layer], w_out, load_sem.at[0]),
        pltpu.make_async_copy(w_qkv_hbm.at[layer], w_qkv, load_sem.at[1]),
    ]
    for load in loads:
        load.start()

    def shift(distance):
        target = lax.rem(head + distance, heads)
        return remote(
            parts_in.at[target], parts_out.at[head], shift_sem, (distance,), {HEAD: target}
        )

    def shift_in(distance):
        arrived = parts_out.at[lax.rem(head + heads - distance, heads)]
        return remote(arrived, arrived, shift_sem, (distance,), {HEAD: head})

    def shift_own():
        return pltpu.make_async_copy(parts_in.at[head], parts_out.at[head], load_sem.at[4])

    barrier = pltpu.get_barrier_semaphore()
    partners = [other] + [{HEAD: lax.rem(head + distance, heads)} for distance in range(1, heads)]
    for partner in partners:
        pl.semaphore_signal(barrier, 1, device_id=partner, device_id_type=MESH)
    pl.semaphore_wait(barrier, len(partners))
    for give in gives[:2]:
        give.start()
    if moves:
        shift_own().start()
        for distance in range(1, heads):
            shift(distance).start()

    grad = out_grad[...].astype(jnp.float32)
    unit = midway[...] * scale2[...]
    gain2_grad = jnp.sum(d_normed2[...] * unit, 0, keepdims=True)
    scaled = d_normed2[...] * gains[1:2]
    d_midway[...] = (
        scale2[...] * (scaled - unit * jnp.mean(scaled * unit, -1, keepdims=True)) + grad
    )
    g_attn[...] = d_midway[...].astype(g_attn.dtype)
    gives[2].start()
    small[:, pl.ds(width, width)] = gain2_grad
    loads[0].wait()
    for start, count in chunks(width, STEP_WIDTH):
        d_attended[:, pl.ds(start, count)] = contract_last(
            g_attn[...], w_out[pl.ds(start, count), :]
        ).astype(d_attended.dtype)

    allowed = own_pos[...] >= key_pos[...]
    allowed = jnp.concatenate([allowed.astype(jnp.int32)] * GROUP, 0) > 0
    groups = HEADS // GROUP
    for group in range(groups):
        kv = group * KV // groups
        spans = [pl.ds((group * GROUP + at) * HDIM, HDIM) for at in range(GROUP)]
        query = jnp.concatenate([queries[group * GROUP + at] for at in range(GROUP)], 0)
        total = jnp.concatenate([log_total[group * GROUP + at] for at in range(GROUP)], 0)
        key = keyval[:, pl.ds(kv * HDIM, HDIM)]
        value = keyval[:, pl.ds(kv_width + kv * HDIM, HDIM)]
        d_out = jnp.concatenate([d_attended[:, span] for span in spans], 0)
        scores = jnp.where(allowed, contract_last(query, key) * scaling, -1e30)
        probs = jnp.exp(scores - total)
        d_probs = contract_last(d_out, value)
        row_dot = jnp.sum(probs * d_probs, -1, keepdims=True)
        d_scores = (probs * (d_probs - row_dot)).astype(jnp.bfloat16)
        d_query = jnp.dot(d_scores, key, preferred_element_type=jnp.float32) * scaling
        d_query = d_query.astype(jnp.bfloat16).astype(jnp.float32)
        for at, span in enumerate(spans):
            d_qkv[:, span] = turn(
                d_query[at * tokens : (at + 1) * tokens], cosine[...], sine[...]
            ).astype(d_qkv.dtype)
        d_key = contract_first(d_scores, query) * scaling
        d_value = contract_first(probs.astype(jnp.bfloat16), d_out)
        first = group % (groups // KV) == 0
        for column, part in ((kv * HDIM, d_key), (kv_width + kv * HDIM, d_value)):
            part = part if first else part + d_keyval[:, pl.ds(column, HDIM)]
            d_keyval[:, pl.ds(column, HDIM)] = part

    def place(section_at, head_at):
        return pl.ds(pl.multiple_of((section_at * heads + head_at) * tokens, tokens), tokens)

    sent = terms.at[pl.ds(0, 2 * heads * tokens), pl.ds(0, d_keyval.shape[1])]
    sent[...] = d_keyval[...].astype(sent.dtype)

    def pair(target):
        source = sent.at[place(1 - section, target)]
        return remote(source, pair_buf.at[target], pair_sem, (target,), other)

    def line(way, target):
        partner = {HEAD: head + 1 - 2 * way}
        return remote(sums.at[target], line_buf.at[way, target], line_sem, (way, target), partner)

    order = []
    for at in range(heads // 2):
        order += [heads - 1 - at, at]
    for target in order:
        pair(target).start()
    for target in order:
        pair(target).wait_recv()
        sums[target] = (
            sent[place(section, target), :].astype(jnp.float32)
            + pair_buf[target].astype(jnp.float32)
        ).astype(sums.dtype)
        if target > 0:

            @pl.when(head == 0)
            def _(target=target):
                line(0, target).start()

        if target < heads - 1:

            @pl.when(head == heads - 1)
            def _(target=target):
                line(1, target).start()

    for target in order:
        pair(target).wait_send()

    def pass_on(way, target):
        line(way, target).wait_recv()
        sums[target] = (
            sums[target].astype(jnp.float32) + line_buf[way, target].astype(jnp.float32)
        ).astype(sums.dtype)
        line(way, target).start()

    loads[1].wait()
    for start, count in chunks(width, STEP_WIDTH):
        d_normed[:, pl.ds(start, count)] = contract_last(
            d_qkv[:, pl.ds(0, width)], w_qkv[pl.ds(start, count), pl.ds(0, width)]
        )
    gives[1].wait_recv()
    gives[2].wait_recv()
    pair_g = jnp.concatenate([half(g_attn, section)[...], their_g[...]], 0)

    def out_terms(head_at):
        span = pl.ds(head_at * wides * rows, wides * rows)
        left = jnp.concatenate([attended[:, span], their_attended[:, span]], 0)
        piece = contract_first(left, pair_g).astype(terms.dtype)
        for wide_at in range(wides):
            target = pl.ds((wide_at * heads + head_at) * rows, rows)
            terms[target, pl.ds(qkv_cols // 2, width // 2)] = piece[
                wide_at * rows : (wide_at + 1) * rows
            ]

    for at in range(heads - 1):
        right, left = heads - 1 - at, at

        @pl.when((head > 0) & (head < right))
        def _(right=right):
            pass_on(0, right)

        @pl.when((head < heads - 1) & (head > left))
        def _(left=left):
            pass_on(1, left)

        out_terms(at)

    out_terms(heads - 1)

    def store(at):
        start, count = ((0, qkv_cols // 2), (qkv_cols // 2, width // 2))[at]
        span = pl.ds(start, count)
        return pltpu.make_async_copy(terms.at[:, span], terms_hbm.at[:, span], load_sem.at[2 + at])

    store(1).start()
    d_keyval[pl.ds(0, tokens), :] = sums[head].astype(jnp.float32)
    for way, comes in ((0, head > 0), (1, head < heads - 1)):

        @pl.when(comes)
        def _(way=way):
            line(way, head).wait_recv()
            d_keyval[pl.ds(0, tokens), :] += line_buf[way, head].astype(jnp.float32)

    for kv in range(KV):
        span = pl.ds(kv * HDIM, HDIM)
        d_qkv[:, pl.ds(width + kv * HDIM, HDIM)] = turn(
            d_keyval[pl.ds(0, tokens), span], cosine[...], sine[...]
        ).astype(d_qkv.dtype)
    d_qkv[:, pl.ds(width + kv_width, kv_width)] = d_keyval[
        pl.ds(0, tokens), pl.ds(kv_width, kv_width)
    ].astype(d_qkv.dtype)
    gives[3].start()
    small[:, pl.ds(2 * width, qkv_cols)] = jnp.sum(
        d_qkv[...].astype(jnp.float32), 0, keepdims=True
    )
    rest = pl.ds(width, qkv_cols - width)
    for start, count in chunks(width, STEP_WIDTH):
        d_normed[:, pl.ds(start, count)] += contract_last(
            d_qkv[:, rest], w_qkv[pl.ds(start, count), rest]
        )

    unit = layer_in[...] * scale1[...]
    small[:, pl.ds(0, width)] = jnp.sum(d_normed[...] * unit, 0, keepdims=True)
    scaled = d_normed[...] * gains[0:1]
    d_in[...] = (
        scale1[...] * (scaled - unit * jnp.mean(scaled * unit, -1, keepdims=True)) + d_midway[...]
    ).astype(d_in.dtype)

    gives[0].wait_recv()
    gives[3].wait_recv()
    pair_d = jnp.concatenate([half(d_qkv, section)[...], their_d[...]], 0)
    for start, count in chunks(width, STEP_WIDTH):
        span = pl.ds(start, count)
        left = jnp.concatenate([normed[:, span], their_normed[:, span]], 0)
        terms[span, pl.ds(0, qkv_cols // 2)] = contract_first(left, pair_d).astype(terms.dtype)
    store(0).start()
    for give in gives:
        give.wait_send()
    for target in range(heads):

        @pl.when(head < target)
        def _(target=target):
            line(0, target).wait_send()

        @pl.when(head > target)
        def _(target=target):
            line(1, target).wait_send()

    for at in (0, 1):
        store(at).wait()
    if moves:
        shift_own().wait()
        for distance in range(1, heads):
            shift(distance).wait_send()
            shift_in(distance).wait_recv()


def attention_grad(layer, number, w_out, w_qkv, parts_in, *operands):
    heads = lax.axis_size(HEAD)
    normed = operands[9]
    tokens, width = normed.shape
    qkv_cols = w_qkv.shape[2]
    kv_cols = qkv_cols - width
    dtype = normed.dtype
    float32 = jnp.float32
    dma = pltpu.SemaphoreType.DMA
    vmem = pl.BlockSpec(memory_space=pltpu.VMEM)
    anywhere = pl.BlockSpec(memory_space=pl.ANY)
    columns = qkv_cols // 2 + width // 2
    moves = parts_in is not None
    parts_in = parts_in if moves else jnp.zeros((heads, 16, 128), dtype)
    return pl.pallas_call(
        functools.partial(attention_grad_kernel, layer, moves),
        out_shape=(
            jax.ShapeDtypeStruct((tokens, width), dtype),
            jax.ShapeDtypeStruct((1, 2 * width + qkv_cols), float32),
            jax.ShapeDtypeStruct((width, columns), dtype),
            jax.ShapeDtypeStruct(parts_in.shape, dtype),
        ),
        in_specs=[vmem] * len(operands) + [anywhere] * 3,
        out_specs=(vmem, vmem, anywhere, anywhere),
        scratch_shapes=[
            pltpu.VMEM(w_out.shape[1:], dtype),
            pltpu.VMEM(w_qkv.shape[1:], dtype),
            pltpu.VMEM((tokens, width), float32),
            pltpu.VMEM((tokens, width), dtype),
            pltpu.VMEM((tokens, width), dtype),
            pltpu.VMEM((tokens, qkv_cols), dtype),
            pltpu.VMEM((tokens, width), float32),
            pltpu.VMEM((2 * heads * tokens, kv_cols), float32),
            pltpu.VMEM((width, columns), dtype),
            pltpu.VMEM((tokens, width), dtype),
            pltpu.VMEM((tokens, width), dtype),
            pltpu.VMEM((tokens, width // 2), dtype),
            pltpu.VMEM((tokens, qkv_cols // 2), dtype),
            pltpu.VMEM((heads, tokens, kv_cols), dtype),
            pltpu.VMEM((heads, tokens, kv_cols), dtype),
            pltpu.VMEM((2, heads, tokens, kv_cols), dtype),
            dma((5,)),
            dma((2, 4)),
            dma((2, heads)),
            dma((2, 2, heads)),
            dma((2, heads)),
        ],
        compiler_params=pltpu.CompilerParams(
            collective_id=number, has_side_effects=True, vmem_limit_bytes=60 * 2**20
        ),
        cost_estimate=pl.CostEstimate(
            flops=40 * tokens * width * qkv_cols,
            bytes_accessed=2 * w_out.size + 2 * w_qkv.size,
            transcendentals=0,
        ),
    )(*operands, w_out, w_qkv, parts_in)


def attention_kernel(
    layer,
    moves,
    layer_in,
    gains,
    bias,
    cosine,
    sine,
    own_pos,
    key_pos,
    w_qkv_hbm,
    w_out_hbm,
    parts_in,
    normed,
    queries,
    keyval,
    log_total,
    attended,
    midway,
    normed2,
    scale1,
    scale2,
    parts_out,
    w_qkv,
    w_out,
    mine,
    load_sem,
    pair_sem,
    line_sem,
    shift_sem,
):
    section, head = lax.axis_index(SECTION), lax.axis_index(HEAD)
    heads = lax.axis_size(HEAD)
    tokens, width = normed.shape
    kv_width = KV * HDIM
    other = {SECTION: 1 - section}

    def remote(source, target, sems, at, partner):
        return pltpu.make_async_remote_copy(
            source,
            target,
            sems.at[(0,) + at],
            sems.at[(1,) + at],
            device_id=partner,
            device_id_type=MESH,
        )

    def place(section_at, head_at):
        start = (section_at * heads + head_at) * tokens
        return keyval.at[pl.ds(pl.multiple_of(start, tokens), tokens)]

    def pair(number, head_at, source):
        return remote(source, place(section, head_at), pair_sem, (number,), other)

    def pair_in(number, head_at):
        target = place(1 - section, head_at)
        return remote(target, target, pair_sem, (number,), other)

    def line(way, hop, source):
        step = 1 - 2 * way
        target = place(section, head - step * hop)
        return remote(source, target, line_sem, (way, hop), {HEAD: head + step})

    def shift(distance):
        target = lax.rem(head + distance, heads)
        return remote(
            parts_in.at[target], parts_out.at[head], shift_sem, (distance,), {HEAD: target}
        )

    def shift_in(distance):
        arrived = parts_out.at[lax.rem(head + heads - distance, heads)]
        return remote(arrived, arrived, shift_sem, (distance,), {HEAD: head})

    def shift_own():
        return pltpu.make_async_copy(parts_in.at[head], parts_out.at[head], load_sem.at[3])

    loads = [
        pltpu.make_async_copy(w_qkv_hbm.at[layer], w_qkv, load_sem.at[0]),
        pltpu.make_async_copy(w_out_hbm.at[layer], w_out, load_sem.at[1]),
    ]
    for load in loads:
        load.start()

    scale = lax.rsqrt(
        jnp.mean(layer_in[...] * layer_in[...], -1, keepdims=True) + EPSILON
    )
    scale1[...] = scale
    normed[...] = (layer_in[...] * scale * gains[0:1]).astype(normed.dtype)
    barrier = pltpu.get_barrier_semaphore()
    partners = [other] + [{HEAD: lax.rem(head + distance, heads)} for distance in range(1, heads)]
    for partner in partners:
        pl.semaphore_signal(barrier, 1, device_id=partner, device_id_type=MESH)
    pl.semaphore_wait(barrier, len(partners))

    def project(start, count):
        span = pl.ds(start, count)
        return (
            jnp.dot(normed[...], w_qkv[:, span], preferred_element_type=jnp.float32)
            + bias[:, span]
        )

    loads[0].wait()
    for kv in range(KV):
        key = project(width + kv * HDIM, HDIM)
        mine[:, pl.ds(kv * HDIM, HDIM)] = turn(key, cosine[...], sine[...]).astype(mine.dtype)
    mine[:, pl.ds(kv_width, kv_width)] = project(width + kv_width, kv_width).astype(mine.dtype)
    ways = ((0, head < heads - 1), (1, head > 0))
    for way, go in ways:

        @pl.when(go)
        def _(way=way):
            line(way, 0, mine).start()

    pair(0, head, mine).start()
    own = pltpu.make_async_copy(mine, place(section, head), load_sem.at[2])
    own.start()
    if moves:
        shift_own().start()
        for here_at in range(heads):

            @pl.when(head == here_at)
            def _(here_at=here_at):
                others = [at for at in range(heads) if at != here_at]
                for at in sorted(others, key=lambda at: abs(at - here_at)):
                    shift((at - here_at) % heads).start()

    def arrivals(hop):
        yield 0, head - hop, head >= hop, head < heads - 1
        yield 1, head + hop, head + hop < heads, head > 0

    per_hop = HEADS // (heads - 1)
    for hop in range(1, heads):
        start = (hop - 1) * per_hop * HDIM
        block = project(start, per_hop * HDIM)
        for at in range(per_hop):
            query = block[:, at * HDIM : (at + 1) * HDIM]
            queries[(hop - 1) * per_hop + at] = turn(query, cosine[...], sine[...]).astype(
                queries.dtype
            )
        for way, origin, comes, goes in arrivals(hop):

            @pl.when(comes)
            def _(way=way, origin=origin, goes=goes, hop=hop):
                here = place(section, origin)
                line(way, hop - 1, here).wait_recv()

                @pl.when(goes)
                def _():
                    line(way, hop, here).start()

                pair(2 * hop - 1 + way, origin, here).start()

    own.wait()
    pair_in(0, head).wait_recv()
    for hop in range(1, heads):
        for way, origin, comes, goes in arrivals(hop):

            @pl.when(comes)
            def _(way=way, origin=origin, hop=hop):
                pair_in(2 * hop - 1 + way, origin).wait_recv()

    allowed = own_pos[...] >= key_pos[...]
    allowed = jnp.concatenate([allowed.astype(jnp.int32)] * GROUP, 0) > 0
    groups = HEADS // GROUP
    for group in range(groups):
        kv = group * KV // groups
        query = jnp.concatenate([queries[group * GROUP + at] for at in range(GROUP)], 0)
        key = keyval[:, pl.ds(kv * HDIM, HDIM)]
        value = keyval[:, pl.ds(kv_width + kv * HDIM, HDIM)]
        scores = jnp.where(allowed, contract_last(query, key) * HDIM**-0.5, -1e30)
        highest = jnp.max(scores, -1, keepdims=True)
        weights_exp = jnp.exp(scores - highest)
        partition = jnp.sum(weights_exp, -1, keepdims=True)
        probs = (weights_exp / partition).astype(jnp.bfloat16)
        result = jnp.dot(probs, value, preferred_element_type=jnp.float32)
        total = highest + jnp.log(partition)
        for at in range(GROUP):
            span = slice(at * tokens, (at + 1) * tokens)
            attended[:, pl.ds((group * GROUP + at) * HDIM, HDIM)] = result[span].astype(
                attended.dtype
            )
            log_total[group * GROUP + at] = total[span]

    loads[1].wait()
    for start, count in chunks(width, STEP_WIDTH):
        span = pl.ds(start, count)
        midway[:, span] = layer_in[:, span] + jnp.dot(
            attended[...], w_out[:, span], preferred_element_type=jnp.float32
        )
    scale = lax.rsqrt(jnp.mean(midway[...] * midway[...], -1, keepdims=True) + EPSILON)
    scale2[...] = scale
    normed2[...] = (midway[...] * scale * gains[1:2]).astype(normed2.dtype)

    pair(0, head, mine).wait_send()
    for way, go in ways:

        @pl.when(go)
        def _(way=way):
            line(way, 0, mine).wait_send()

    for hop in range(1, heads):
        for way, origin, comes, goes in arrivals(hop):

            @pl.when(comes)
            def _(way=way, origin=origin, goes=goes, hop=hop):
                here = place(section, origin)

                @pl.when(goes)
                def _():
                    line(way, hop, here).wait_send()

                pair(2 * hop - 1 + way, origin, here).wait_send()

    if moves:
        shift_own().wait()
        for distance in range(1, heads):
            shift(distance).wait_send()
            shift_in(distance).wait_recv()


def attention_forward(layer, number, w_qkv, w_out, parts_in, *operands):
    heads = lax.axis_size(HEAD)
    tokens, width = operands[0].shape
    kv_cols = w_qkv.shape[2] - width
    dtype = w_qkv.dtype
    float32 = jnp.float32
    dma = pltpu.SemaphoreType.DMA
    vmem = pl.BlockSpec(memory_space=pltpu.VMEM)
    anywhere = pl.BlockSpec(memory_space=pl.ANY)
    moves = parts_in is not None
    parts_in = parts_in if moves else jnp.zeros((heads, 16, 128), dtype)
    return pl.pallas_call(
        functools.partial(attention_kernel, layer, moves),
        out_shape=(
            jax.ShapeDtypeStruct((tokens, width), dtype),
            jax.ShapeDtypeStruct((HEADS, tokens, HDIM), dtype),
            jax.ShapeDtypeStruct((2 * heads * tokens, kv_cols), dtype),
            jax.ShapeDtypeStruct((HEADS, tokens, 1), float32),
            jax.ShapeDtypeStruct((tokens, width), dtype),
            jax.ShapeDtypeStruct((tokens, width), float32),
            jax.ShapeDtypeStruct((tokens, width), dtype),
            jax.ShapeDtypeStruct((tokens, 1), float32),
            jax.ShapeDtypeStruct((tokens, 1), float32),
            jax.ShapeDtypeStruct(parts_in.shape, dtype),
        ),
        in_specs=[vmem] * len(operands) + [anywhere] * 3,
        out_specs=(vmem,) * 9 + (anywhere,),
        scratch_shapes=[
            pltpu.VMEM(w_qkv.shape[1:], dtype),
            pltpu.VMEM(w_out.shape[1:], dtype),
            pltpu.VMEM((tokens, kv_cols), dtype),
            dma((4,)),
            dma((2, 2 * heads - 1)),
            dma((2, 2, heads)),
            dma((2, heads)),
        ],
        compiler_params=pltpu.CompilerParams(
            collective_id=number, has_side_effects=True, vmem_limit_bytes=60 * 2**20
        ),
        cost_estimate=pl.CostEstimate(
            flops=20 * tokens * width * w_qkv.shape[2],
            bytes_accessed=2 * w_out.size + 2 * w_qkv.size,
            transcendentals=0,
        ),
    )(*operands, w_qkv, w_out, parts_in)


def local_grouped(
    inputs,
    cotangent,
    norm_gains,
    qkv_weight,
    qkv_bias,
    out_weight,
    gate_weight,
    up_weight,
    down_weight,
):
    head_count = lax.axis_size(HEAD)
    wide_count = lax.axis_size(WIDE)
    section_count = lax.axis_size(SECTION)
    section = lax.axis_index(SECTION)
    head = lax.axis_index(HEAD)
    micro_count, short_len, width = inputs.shape
    half_len = short_len // section_count
    tokens = wide_count * half_len
    rows = qkv_weight.shape[1]
    query_width = HEADS * HDIM
    kv_width = KV * HDIM
    qkv_cols = qkv_weight.shape[2]
    ff_cols = gate_weight.shape[2]
    parts = section_count * head_count
    part_cols = -(-ff_cols // (parts * 128)) * 128

    def inner(array):
        split = array.shape[:-1] + (head_count, wide_count, rows)
        return jnp.swapaxes(array.reshape(split), -3, -2).reshape(array.shape)

    def outer(array):
        split = array.shape[:-1] + (wide_count, head_count, rows)
        return jnp.swapaxes(array.reshape(split), -3, -2).reshape(array.shape)

    mlp_parts, out_own = cut_parts(
        gate_weight[0], up_weight[0], down_weight[0], out_weight[0], parts, part_cols
    )
    qkv_weights, out_weights, first_mlp, second_parts = start_weights(
        qkv_weight[0],
        out_own,
        mlp_parts.reshape(section_count, head_count, rows, 3 * part_cols),
        5,
    )


    second_mlp = lax.all_gather(second_parts, WIDE, axis=0).reshape(width, 3 * part_cols)
    mlp_weights = [first_mlp, second_mlp]

    small = jnp.concatenate([inner(norm_gains[0, 0]), inner(norm_gains[0, 1]), qkv_bias[0]])
    small = both_sections(small)

    sides = jnp.concatenate(
        [
            lax.dynamic_slice_in_dim(inputs, section * half_len, half_len, 1),
            lax.dynamic_slice_in_dim(cotangent, section * half_len, half_len, 1),
        ],
        1,
    )
    sides = lax.all_to_all(sides, WIDE, split_axis=0, concat_axis=0, tiled=True)
    sides = inner(sides)
    layer_in = sides[:, :half_len].reshape(tokens, width).astype(jnp.float32)
    last_grad = sides[:, half_len:].reshape(tokens, width)

    order = np.indices((section_count, head_count, wide_count, half_len)).reshape(4, -1)
    key_pos = (order[1] * wide_count + order[2]) * short_len + order[0] * half_len + order[3]
    half_dim = HDIM // 2
    angles = key_pos[:, None] * ROPE_BASE ** (-np.arange(half_dim) / half_dim)
    tables = np.concatenate([np.cos(angles)] * 2 + [np.sin(angles), -np.sin(angles)], 1)
    first_row = (section * head_count + head) * tokens
    own_table = lax.dynamic_slice_in_dim(jnp.asarray(tables, jnp.float32), first_row, tokens, 0)
    head_cosine, head_sine = own_table[:, :HDIM], own_table[:, HDIM:]
    key_pos = jnp.asarray(key_pos, jnp.int32)
    own_pos = lax.dynamic_slice_in_dim(key_pos, first_row, tokens, 0)

    records = []
    outputs_list = []
    for layer in range(section_count):
        (
            normed,
            queries,
            keyval,
            log_total,
            attended,
            midway,
            normed2,
            scale_first,
            scale_second,
            _,
        ) = attention_forward(
            layer,
            (2, 8)[layer],
            qkv_weights,
            out_weights,
            None,
            layer_in,
            small[layer][: 2 * width].reshape(2, width),
            small[layer][2 * width :][None],
            head_cosine,
            -head_sine,
            own_pos[:, None],
            key_pos[None, :],
        )
        w_mlp = mlp_weights[layer]
        mlp_out, normed2, gate_up, hidden = feed_forward(normed2, w_mlp, 1)
        result = midway + mlp_out
        records.append(
            (
                layer_in,
                scale_first,
                normed,
                queries,
                keyval,
                log_total,
                attended,
                midway,
                scale_second,
                normed2,
                gate_up,
                hidden,
            )
        )
        carried = result.astype(jnp.bfloat16)
        outputs_list.append(carried)
        layer_in = carried.astype(jnp.float32)

    out_grad = last_grad
    grads_list = [None] * section_count
    attention_terms = [None] * section_count
    small_terms = [None] * section_count
    for layer in reversed(range(section_count)):
        w_mlp = mlp_weights[layer]
        (
            layer_in,
            scale_first,
            normed,
            queries,
            keyval,
            log_total,
            attended,
            midway,
            scale_second,
            normed2,
            gate_up,
            hidden,
        ) = records[layer]
        d_normed2, mlp_term = feed_backward(out_grad, w_mlp, gate_up, normed2, hidden, 3)
        mlp_term = mlp_term.reshape(wide_count, head_count, rows, -1)
        mlp_sum = lax.psum_scatter(mlp_term, WIDE, scatter_dimension=0)
        if layer == 1:
            second_sum = lax.optimization_barrier(mlp_sum)
        out_grad, small_terms[layer], attention_terms[layer], second_parts = attention_grad(
            layer,
            (4, 7)[layer],
            out_weights,
            qkv_weights,
            second_sum if layer == 0 else None,
            d_normed2,
            midway,
            scale_second,
            out_grad,
            small[layer][: 2 * width].reshape(2, width),
            queries,
            keyval,
            log_total,
            attended,
            normed,
            layer_in,
            scale_first,
            head_cosine,
            head_sine,
            own_pos[:, None],
            key_pos[None, :],
        )
        grads_list[layer] = out_grad

    sides = jnp.stack([outer(each) for each in outputs_list + grads_list])
    totals, small_total, low_parts, high_parts, owned = finish_weights(
        *[term.reshape(wide_count * head_count, rows, -1) for term in attention_terms],
        jnp.stack(small_terms).reshape(section_count, -1, 128),
        mlp_sum,
        second_parts,
        sides.reshape(2 * section_count, wide_count, half_len, width),
        6,
    )
    small_total = small_total.reshape(-1)
    gate_grad, up_grad, down_grad, qkv_grad, out_weight_grad = join_parts(
        low_parts, high_parts, totals, ff_cols, qkv_cols
    )
    return (
        owned[:1],
        owned[1:],
        outer(small_total[: 2 * width].reshape(1, 2, width)),
        qkv_grad,
        small_total[2 * width :][None],
        out_weight_grad,
        gate_grad,
        up_grad,
        down_grad,
    )


def local(inputs, *rest):
    sizes = [lax.axis_size(axis) for axis in (SECTION, HEAD, WIDE)]
    if sizes == [2, 4, 4] and inputs.shape[0] == 4:
        return local_grouped(inputs, *rest)
    return local_streamed(inputs, *rest)


def solution(mesh):
    return jax.shard_map(
        local,
        mesh=mesh,
        in_specs=(
            P(None, (HEAD, WIDE), None),
            P(None, (HEAD, WIDE), None),
            P(SECTION, None, None),
            P(SECTION, (HEAD, WIDE), None),
            P(SECTION, None),
            P(SECTION, (HEAD, WIDE), None),
            P(SECTION, (HEAD, WIDE), None),
            P(SECTION, (HEAD, WIDE), None),
            P(SECTION, (HEAD, WIDE), None),
        ),
        out_specs=(
            P(SECTION, None, (HEAD, WIDE), None),
            P(SECTION, None, (HEAD, WIDE), None),
            P(SECTION, None, None),
            P(SECTION, (HEAD, WIDE), None),
            P(SECTION, None),
            P(SECTION, (HEAD, WIDE), None),
            P(SECTION, (HEAD, WIDE), None),
            P(SECTION, (HEAD, WIDE), None),
            P(SECTION, (HEAD, WIDE), None),
        ),
        check_vma=False,
    )
```

```python
import functools
from typing import NamedTuple

import jax
import jax.numpy as jnp
import numpy as np
from jax import lax
from jax.experimental import pallas as pl
from jax.experimental.pallas import tpu as pltpu
from jax.sharding import PartitionSpec as P

HEADS = 12
KV = 2
HDIM = 128


EPSILON = 1e-06
MESH = pl.DeviceIdType.MESH
SECTION = "section"
HEAD = "head"
WIDE = "wide"
ROPE_BASE = 1000000.0


class Record(NamedTuple):
    layer_in: jax.Array
    scale_first: jax.Array
    normed: jax.Array
    query_rows: jax.Array
    kv_local: jax.Array
    log_total: jax.Array
    out_seq: jax.Array
    midway: jax.Array
    scale_second: jax.Array
    normed2: jax.Array
    gate_out: jax.Array
    up_out: jax.Array
    hidden: jax.Array


def passed_along(block, axis, distance):
    devices = range(lax.axis_size(axis))
    route = [(i - distance, i) for i in devices if i - distance in devices]
    return lax.ppermute(block, axis, route)


def rotary_tables(positions, head_dim):
    half_dim = head_dim // 2
    frequency = ROPE_BASE ** (-jnp.arange(half_dim, dtype=jnp.float32) / half_dim)
    angles = positions[:, None] * frequency[None, :]
    return (jnp.cos(angles)[:, None, :], jnp.sin(angles)[:, None, :])


def rotate_pairs(tensor, cosine, sine_table):
    half_dim = tensor.shape[-1] // 2
    first_half = tensor[..., :half_dim]
    second_half = tensor[..., half_dim:]
    return jnp.concatenate(
        [
            first_half * cosine - second_half * sine_table,
            second_half * cosine + first_half * sine_table,
        ],
        -1,
    )


def rotate_back(tensor, cosine, sine_table):
    half_dim = tensor.shape[-1] // 2
    first_half = tensor[..., :half_dim]
    second_half = tensor[..., half_dim:]
    return jnp.concatenate(
        [
            first_half * cosine + second_half * sine_table,
            second_half * cosine - first_half * sine_table,
        ],
        -1,
    )


def contract_last(left, right):
    return lax.dot_general(
        left, right, (((1,), (1,)), ((), ())), preferred_element_type=jnp.float32
    )


def contract_first(left, right):
    return lax.dot_general(
        left, right, (((0,), (0,)), ((), ())), preferred_element_type=jnp.float32
    )


def attention_scores(query_rows, key_value, query_pos, key_pos):
    head_dim = query_rows.shape[1]
    scores = contract_last(query_rows, key_value[:, :head_dim]) * head_dim ** (-0.5)
    return jnp.where(query_pos[:, None] >= key_pos[None, :], scores, -1e30)


def attend_forward(query_rows, key_value, query_pos, key_pos):
    head_dim = query_rows.shape[1]
    scores = attention_scores(query_rows, key_value, query_pos, key_pos)
    highest = jnp.max(scores, -1, keepdims=True)
    weights_exp = jnp.exp(scores - highest)
    partition = jnp.sum(weights_exp, -1, keepdims=True)
    probs_low = (weights_exp / partition).astype(jnp.bfloat16)
    attended = jnp.dot(probs_low, key_value[:, head_dim:], preferred_element_type=jnp.float32)
    return (attended.astype(jnp.bfloat16), highest + jnp.log(partition))


def attend_backward(query_rows, key_value, query_pos, key_pos, log_total, grad_rows):
    head_dim = query_rows.shape[1]
    scaling = head_dim ** (-0.5)
    scores = attention_scores(query_rows, key_value, query_pos, key_pos)
    probs_full = jnp.exp(scores - log_total)
    grad_probs = contract_last(grad_rows, key_value[:, head_dim:])
    row_dot = jnp.sum(probs_full * grad_probs, -1, keepdims=True)
    grad_scores = (probs_full * (grad_probs - row_dot)).astype(jnp.bfloat16)
    grad_query = (
        jnp.dot(grad_scores, key_value[:, :head_dim], preferred_element_type=jnp.float32) * scaling
    )
    grad_key = contract_first(grad_scores, query_rows) * scaling
    grad_value = contract_first(probs_full.astype(jnp.bfloat16), grad_rows)
    return (grad_query, jnp.concatenate([grad_key, grad_value], 1))


def make_terms(operands, factor):
    (
        normed_all,
        dqkv_all,
        attended_all,
        gattn_all,
        normed2_all,
        dgate_all,
        dup_all,
        gmlp_all,
        hidden_all,
    ) = operands
    pairs = [
        (normed_all, dqkv_all),
        (attended_all, gattn_all),
        (normed2_all, dgate_all),
        (normed2_all, dup_all),
        (gmlp_all, hidden_all),
    ]
    scaled_pairs = [
        (left, (right.astype(jnp.float32) * factor).astype(jnp.bfloat16)) for left, right in pairs
    ]

    def weight_terms(start, count):
        pieces = [contract_first(left, right) for left, right in scaled_pairs]
        return jnp.concatenate(pieces, 1)

    return weight_terms


def local_streamed(
    inputs,
    cotangent,
    norm_gains,
    qkv_weight,
    qkv_bias,
    out_weight,
    gate_weight,
    up_weight,
    down_weight,
):
    head_count = lax.axis_size(HEAD)
    wide_count = lax.axis_size(WIDE)
    section_pos = lax.axis_index(SECTION)
    head_pos = lax.axis_index(HEAD)
    wide_pos = lax.axis_index(WIDE)
    micro_count, short_len, width = inputs.shape
    group_size = HEADS // head_count
    slot_rep = head_count // KV
    query_width = HEADS * HDIM
    kv_width = KV * HDIM
    local_rows = head_count * short_len
    seq_len = local_rows * wide_count
    gain_first = norm_gains[0, 0]
    gain_second = norm_gains[0, 1]
    bias_row = qkv_bias[0]
    seq_pos = (
        (head_pos * wide_count + wide_pos) * short_len + jnp.arange(short_len, dtype=jnp.int32)
    ).astype(jnp.float32)
    cosine, sine_table = rotary_tables(seq_pos, HDIM)
    local_index = jnp.arange(local_rows, dtype=jnp.int32)
    query_pos = jnp.tile(
        (local_index // short_len * wide_count + wide_pos) * short_len + local_index % short_len,
        group_size,
    )
    key_index = jnp.arange(seq_len, dtype=jnp.int32)
    key_pos = (
        key_index % local_rows // short_len * wide_count + key_index // local_rows
    ) * short_len + key_index % short_len

    def to_rows(packed):
        return (
            packed.reshape(local_rows, group_size, HDIM)
            .transpose(1, 0, 2)
            .reshape(group_size * local_rows, HDIM)
        )

    def from_rows(rows_in):
        return (
            rows_in.reshape(group_size, local_rows, HDIM)
            .transpose(1, 0, 2)
            .reshape(local_rows, 1, group_size * HDIM)
        )

    weights_fwd = (
        lax.all_gather(qkv_weight[0], (HEAD, WIDE), axis=0, tiled=True),
        lax.all_gather(out_weight[0], (HEAD, WIDE), axis=0, tiled=True),
        lax.all_gather(gate_weight[0], (HEAD, WIDE), axis=0, tiled=True),
        lax.all_gather(up_weight[0], (HEAD, WIDE), axis=0, tiled=True),
        lax.all_gather(down_weight[0], (HEAD, WIDE), axis=0, tiled=True),
    )
    incoming = jnp.zeros((short_len, width), jnp.bfloat16)
    records = []
    outputs_list = []
    for step_index in range(micro_count + 1):
        own_input = inputs[min(step_index, micro_count - 1)]
        layer_in = jnp.where(section_pos == 0, own_input, incoming).astype(jnp.float32)
        layer_w_qkv, layer_w_out, layer_w_gate, layer_w_up, layer_w_down = weights_fwd
        scale_first = lax.rsqrt(jnp.mean(layer_in * layer_in, -1, keepdims=True) + EPSILON)
        normed = (layer_in * scale_first * gain_first).astype(jnp.bfloat16)
        qkv = jnp.dot(normed, layer_w_qkv, preferred_element_type=jnp.float32) + bias_row
        queries = rotate_pairs(
            qkv[:, :query_width].reshape(short_len, HEADS, HDIM), cosine, sine_table
        ).astype(jnp.bfloat16)
        key_heads = rotate_pairs(
            qkv[:, query_width : query_width + kv_width].reshape(short_len, KV, HDIM),
            cosine,
            sine_table,
        ).astype(jnp.bfloat16)
        value_heads = (
            qkv[:, query_width + kv_width :].reshape(short_len, KV, HDIM).astype(jnp.bfloat16)
        )
        kv_pack = jnp.repeat(jnp.stack([key_heads, value_heads], 2), slot_rep, axis=1).reshape(
            short_len, head_count, 2 * HDIM
        )
        q_pack = queries.reshape(short_len, head_count, group_size * HDIM)
        q_heads = lax.all_to_all(q_pack, HEAD, split_axis=1, concat_axis=0, tiled=True)
        kv_heads = lax.all_to_all(kv_pack, HEAD, split_axis=1, concat_axis=0, tiled=True)
        query_rows = to_rows(q_heads)
        kv_local = kv_heads.reshape(local_rows, 2 * HDIM)
        layer_kv_all = lax.all_gather(kv_local, WIDE, axis=0, tiled=True)
        out_rows, log_total = attend_forward(query_rows, layer_kv_all, query_pos, key_pos)
        out_seq = lax.all_to_all(
            from_rows(out_rows), HEAD, split_axis=0, concat_axis=1, tiled=True
        ).reshape(short_len, query_width)
        midway = layer_in + jnp.dot(out_seq, layer_w_out, preferred_element_type=jnp.float32)
        scale_second = lax.rsqrt(jnp.mean(midway * midway, -1, keepdims=True) + EPSILON)
        normed2 = (midway * scale_second * gain_second).astype(jnp.bfloat16)
        layer_gate_out = jnp.dot(normed2, layer_w_gate, preferred_element_type=jnp.float32)
        up_out = jnp.dot(normed2, layer_w_up, preferred_element_type=jnp.float32)
        hidden = (jax.nn.silu(layer_gate_out) * up_out).astype(jnp.bfloat16)
        result = midway + contract_last(hidden, layer_w_down)
        record = Record(
            layer_in=layer_in,
            scale_first=scale_first,
            normed=normed,
            query_rows=query_rows,
            kv_local=kv_local,
            log_total=log_total,
            out_seq=out_seq,
            midway=midway,
            scale_second=scale_second,
            normed2=normed2,
            gate_out=layer_gate_out,
            up_out=up_out,
            hidden=hidden,
        )
        result, record = (result, record)
        sent_value = result.astype(jnp.bfloat16)
        records.append(record)
        outputs_list.append(sent_value)
        if step_index < micro_count:
            incoming = passed_along(sent_value, SECTION, 1)
    stacked_records = jax.tree.map(lambda *arrays: jnp.stack(arrays), *records)
    section_outputs = lax.dynamic_slice_in_dim(
        jnp.stack(outputs_list), section_pos, micro_count, 0
    )[None]
    weights_back = (
        lax.all_gather(qkv_weight[0], (HEAD, WIDE), axis=0, tiled=True),
        lax.all_gather(out_weight[0], (HEAD, WIDE), axis=0, tiled=True),
        lax.all_gather(gate_weight[0], (HEAD, WIDE), axis=0, tiled=True),
        lax.all_gather(up_weight[0], (HEAD, WIDE), axis=0, tiled=True),
        lax.all_gather(down_weight[0], (HEAD, WIDE), axis=0, tiled=True),
    )
    owned_rows = qkv_weight.shape[1]
    qkv_cols = qkv_weight.shape[2]
    ff_cols = gate_weight.shape[2]
    incoming_grad = jnp.zeros((short_len, width), jnp.bfloat16)
    small_totals = (
        jnp.zeros((width,), jnp.float32),
        jnp.zeros((width,), jnp.float32),
        jnp.zeros((bias_row.shape[0],), jnp.float32),
    )
    grads_list = []
    kept_list = []
    for step_index in range(micro_count + 1):
        pick = jnp.clip(step_index - 1 + 2 * section_pos, 0, micro_count)
        record = jax.tree.map(
            lambda array: lax.dynamic_index_in_dim(array, pick, 0, keepdims=False), stacked_records
        )
        own_grad = cotangent[min(step_index, micro_count - 1)]
        out_grad = jnp.where(section_pos == 1, own_grad, incoming_grad).astype(jnp.float32)
        w_qkv, w_out, w_gate, w_up, w_down = weights_back
        g_mlp = out_grad.astype(jnp.bfloat16)
        d_hidden = jnp.dot(g_mlp, w_down, preferred_element_type=jnp.float32)
        gate_out = record.gate_out
        sigmoid_gate = jax.nn.sigmoid(gate_out)
        d_gate = (
            d_hidden * record.up_out * sigmoid_gate * (1.0 + gate_out * (1.0 - sigmoid_gate))
        ).astype(jnp.bfloat16)
        d_up = (d_hidden * gate_out * sigmoid_gate).astype(jnp.bfloat16)
        d_normed2 = contract_last(d_gate, w_gate) + contract_last(d_up, w_up)
        unit_second = record.midway * record.scale_second
        gain2_grad = jnp.sum(d_normed2 * unit_second, 0)
        dn_second = d_normed2 * gain_second
        d_midway = (
            record.scale_second
            * (dn_second - unit_second * jnp.mean(dn_second * unit_second, -1, keepdims=True))
            + out_grad
        )
        g_attn = d_midway.astype(jnp.bfloat16)
        d_out_seq = contract_last(g_attn, w_out).astype(jnp.bfloat16)
        d_out_heads = lax.all_to_all(
            d_out_seq.reshape(short_len, head_count, group_size * HDIM),
            HEAD,
            split_axis=1,
            concat_axis=0,
            tiled=True,
        )
        kv_all = lax.all_gather(record.kv_local, WIDE, axis=0, tiled=True)
        grad_query, grad_keyval = attend_backward(
            record.query_rows,
            kv_all,
            query_pos,
            key_pos,
            record.log_total,
            to_rows(d_out_heads),
        )
        keyval_local = lax.psum_scatter(
            grad_keyval.astype(jnp.bfloat16), WIDE, scatter_dimension=0, tiled=True
        )
        q_back = lax.all_to_all(
            from_rows(grad_query.astype(jnp.bfloat16)),
            HEAD,
            split_axis=0,
            concat_axis=1,
            tiled=True,
        )
        kv_back = lax.all_to_all(
            keyval_local.reshape(local_rows, 1, 2 * HDIM),
            HEAD,
            split_axis=0,
            concat_axis=1,
            tiled=True,
        )
        d_queries = rotate_back(
            q_back.astype(jnp.float32).reshape(short_len, HEADS, HDIM), cosine, sine_table
        )
        d_kv = jnp.sum(kv_back.astype(jnp.float32).reshape(short_len, KV, slot_rep, 2, HDIM), 2)
        d_keys = rotate_back(d_kv[:, :, 0], cosine, sine_table)
        d_qkv = jnp.concatenate(
            [
                d_queries.reshape(short_len, query_width),
                d_keys.reshape(short_len, kv_width),
                d_kv[:, :, 1].reshape(short_len, kv_width),
            ],
            1,
        ).astype(jnp.bfloat16)
        bias_grad = jnp.sum(d_qkv.astype(jnp.float32), 0)
        d_normed = contract_last(d_qkv, w_qkv)
        unit_first = record.layer_in * record.scale_first
        gain1_grad = jnp.sum(d_normed * unit_first, 0)
        dn_first = d_normed * gain_first
        d_layer_in = (
            record.scale_first
            * (dn_first - unit_first * jnp.mean(dn_first * unit_first, -1, keepdims=True))
            + d_midway
        )
        kept_grads = (
            record.normed,
            d_qkv,
            record.out_seq,
            g_attn,
            record.normed2,
            d_gate,
            d_up,
            g_mlp,
            record.hidden,
        )
        d_layer_in, kept_grads, small_parts = (
            d_layer_in,
            kept_grads,
            (gain1_grad, gain2_grad, bias_grad),
        )
        is_valid = jnp.where(
            (step_index - 1 + section_pos >= 0) & (step_index - 1 + section_pos < micro_count),
            1.0,
            0.0,
        )
        small_totals = jax.tree.map(
            lambda total_part, new_part: total_part + is_valid * new_part, small_totals, small_parts
        )
        sent_grad = d_layer_in.astype(jnp.bfloat16)
        grads_list.append(sent_grad)
        kept_list.append(kept_grads)
        if step_index < micro_count:
            incoming_grad = passed_along(sent_grad, SECTION, -1)
    input_grads = lax.dynamic_slice_in_dim(jnp.stack(grads_list), 1 - section_pos, micro_count, 0)[
        None
    ]
    operands = jax.tree.map(
        lambda *arrays: lax.dynamic_slice_in_dim(
            jnp.stack(arrays), 1 - section_pos, micro_count, 0
        ).reshape(micro_count * short_len, arrays[0].shape[1]),
        *kept_list
    )
    terms = lax.psum_scatter(
        make_terms(operands, 1.0)(jnp.int32(0), owned_rows * lax.axis_size((HEAD, WIDE))),
        (HEAD, WIDE),
        scatter_dimension=0,
        tiled=True,
    )
    qkv_grad = terms[:, :qkv_cols]
    out_grad_rows = terms[:, qkv_cols : qkv_cols + width]
    gate_grad = terms[:, qkv_cols + width : qkv_cols + width + ff_cols]
    up_grad = terms[:, qkv_cols + width + ff_cols : qkv_cols + width + 2 * ff_cols]
    down_grad = terms[:, qkv_cols + width + 2 * ff_cols :]
    gain1_total, gain2_total, bias_total = lax.psum(
        (small_totals[0], small_totals[1], small_totals[2]), (HEAD, WIDE)
    )
    gains_grad = jnp.stack([gain1_total, gain2_total])[None]
    return (
        section_outputs,
        input_grads,
        gains_grad,
        qkv_grad[None],
        bias_total[None],
        out_grad_rows[None],
        gate_grad[None],
        up_grad[None],
        down_grad[None],
    )


def greet_all(heads):
    section, head, wide = (lax.axis_index(axis) for axis in (SECTION, HEAD, WIDE))
    barrier = pltpu.get_barrier_semaphore()
    partners = [{SECTION: 1 - section}] + [{WIDE: beside(wide, axis)} for axis in (0, 1, 2)]
    partners += [{HEAD: lax.rem(head + shift, heads)} for shift in range(1, heads)]
    for partner in partners:
        pl.semaphore_signal(barrier, 1, device_id=partner, device_id_type=MESH)
    pl.semaphore_wait(barrier, len(partners))


def beside(wide, axis):
    low, high = lax.rem(wide, 2), lax.div(wide, 2)
    if axis == 0:
        return high * 2 + (1 - low)
    if axis == 1:
        return (1 - high) * 2 + low
    return (1 - high) * 2 + (1 - low)


def start_kernel(
    qkv_own,
    out_own,
    parts,
    sides,
    small_own,
    cosine,
    sine,
    own_pos,
    key_pos,
    qkv_all,
    out_all,
    first_all,
    second_parts,
    tokens_in,
    grad_in,
    grad_near,
    grad_far,
    small_all,
    *refs,
):
    results, refs = refs[:9], refs[9:]
    scratch, refs = refs[:6], refs[6:]
    (
        block,
        layer_in,
        given_first,
        given_second,
        small_sem,
        local_sem,
        swap_sem,
        shift_sem,
        line_sem,
        wide_sem,
        half_sem,
        pair_sem,
        token_sem,
        near_sem,
    ) = refs
    section, head, wide = (lax.axis_index(axis) for axis in (SECTION, HEAD, WIDE))
    heads, wides = lax.axis_size(HEAD), lax.axis_size(WIDE)
    rows = qkv_own.shape[0]
    half = rows // 2
    owns = (qkv_own, out_own)
    here = [beside(wide, 0), beside(wide, 1), beside(wide, 2)]

    def place(which, layer, head_at, wide_at, start=0, count=None):
        block = head_at * wides + wide_at if which == 1 else wide_at * heads + head_at
        first = pl.multiple_of(block * rows + start, 16)
        span = pl.ds(first, rows if count is None else count)
        return first_all.at[span] if which == 2 else (qkv_all, out_all)[which].at[layer, span]

    def remote(source, target, sems, at, partner):
        return pltpu.make_async_remote_copy(
            source,
            target,
            sems.at[(0,) + at],
            sems.at[(1,) + at],
            device_id=partner,
            device_id_type=MESH,
        )

    other = {SECTION: 1 - section}

    def line(which, way, hop):
        step = 1 if way == 0 else -1
        target = place(which, section, head - step * hop, wide)
        source = owns[which] if hop == 0 else target
        return remote(source, target, line_sem, (which, way, hop), {HEAD: head + step})

    def across(which, axis, number, origin):
        target = place(which, section, origin, wide)
        source = owns[which] if number == 0 and which < 2 else target
        return remote(source, target, wide_sem, (which, axis, number), {WIDE: here[axis]})

    def across_in(which, axis, number, origin):
        target = place(which, section, origin, here[axis])
        return remote(target, target, wide_sem, (which, axis, number), {WIDE: here[axis]})

    def diagonal(which, axis, number, origin):
        target = place(which, section, origin, here[1 - axis], (1 - axis) * half, half)
        return remote(target, target, half_sem, (which, axis, number), {WIDE: here[axis]})

    def diagonal_in(which, axis, number, origin):
        target = place(which, section, origin, here[2], (1 - axis) * half, half)
        return remote(target, target, half_sem, (which, axis, number), {WIDE: here[axis]})

    def pair(which, kind, number, origin, layer):
        if kind == 0:
            target = place(which, layer, origin, wide)
        elif kind in (1, 2):
            target = place(which, layer, origin, here[kind - 1])
        else:
            target = place(which, layer, origin, here[2], (4 - kind) * half, half)
        return remote(target, target, pair_sem, (which, kind, number), other)

    def pair_own(which):
        target = place(which, section, head, wide)
        return remote(owns[which], target, pair_sem, (which, 0, 0), other)

    def swap(target):
        return remote(parts.at[1 - section], target, swap_sem, (), other)

    def shift(layer, source, distance):
        target_head = lax.rem(head + distance, heads)
        target = place(2, 0, head, wide) if layer == 0 else second_parts.at[head]
        return remote(
            source.at[target_head], target, shift_sem, (layer, distance), {HEAD: target_head}
        )

    def shift_in(layer, distance):
        origin = lax.rem(head + heads - distance, heads)
        target = place(2, 0, origin, wide) if layer == 0 else second_parts.at[origin]
        return remote(target, target, shift_sem, (layer, distance), {HEAD: head})

    def shift_all(layer, source):
        for here_at in range(heads):

            @pl.when(head == here_at)
            def _(here_at=here_at):
                others = [at for at in range(heads) if at != here_at]
                for at in sorted(others, key=lambda at: abs(at - here_at)):
                    shift(layer, source, (at - here_at) % heads).start()

        target = place(2, 0, head, wide) if layer == 0 else second_parts.at[head]
        pltpu.make_async_copy(source.at[head], target, local_sem.at[2 + layer]).start()

    def shift_own(layer):
        target = place(2, 0, head, wide) if layer == 0 else second_parts.at[head]
        return pltpu.make_async_copy(target, target, local_sem.at[2 + layer])

    shares = (tokens_in, grad_in)
    share_rows = sides.shape[2]
    tokens = grad_in.shape[0]

    def share(which, wide_at):
        return shares[which].at[pl.ds(pl.multiple_of(wide_at * share_rows, 16), share_rows)]

    def token(which, axis):
        source = sides.at[which, here[axis]]
        return remote(source, share(which, wide), token_sem, (which, axis), {WIDE: here[axis]})

    def token_in(which, axis):
        target = share(which, here[axis])
        return remote(target, target, token_sem, (which, axis), {WIDE: here[axis]})

    def token_own(which):
        return pltpu.make_async_copy(
            sides.at[which, wide], share(which, wide), local_sem.at[4 + which]
        )

    def swaps():
        yield block_swap(grad_in, grad_near, near_sem.at[0], head, 1)
        yield block_swap(grad_in, grad_far, near_sem.at[1], head, 3)

    greet_all(heads)
    first = section == 0
    second = section == 1

    for which in (0, 1):
        for way, go in ((0, head < heads - 1), (1, head > 0)):

            @pl.when(go)
            def _(which=which, way=way):
                line(which, way, 0).start()

    for which in (0, 1):
        for axis in (0, 1, 2):
            token(which, axis).start()
        token_own(which).start()

    small_all[section] = small_own[...]
    small_give = remote(small_own, small_all.at[section], small_sem, (), other)
    small_give.start()

    @pl.when(first)
    def _():
        swap(given_first).start()

    @pl.when(second)
    def _():
        swap(given_second).start()

    locals_ = [
        pltpu.make_async_copy(owns[which], place(which, section, head, wide), local_sem.at[which])
        for which in (0, 1)
    ]
    for which in (0, 1):
        locals_[which].start()
        for axis in (0, 1):
            across(which, axis, 0, head).start()
        pair_own(which).start()

    def each(hop):
        yield 2 * hop - 1, 0, head - hop, head >= hop, head < heads - 1
        yield 2 * hop, 1, head + hop, head + hop < heads, head > 0

    def forward_halves(number, origin):
        for which in (0, 1):
            for axis in (0, 1):
                across_in(which, axis, number, origin).wait_recv()
                diagonal(which, 1 - axis, number, origin).start()
                pair(which, 1 + axis, number, origin, section).start()

    def finish_halves(number, origin):
        for which in (0, 1):
            for axis in (0, 1):
                diagonal_in(which, axis, number, origin).wait_recv()
                pair(which, 3 + axis, number, origin, section).start()

    for hop in range(1, heads):
        for number, way, origin, comes, goes in each(hop):

            @pl.when(comes)
            def _(number=number, way=way, origin=origin, goes=goes, hop=hop):
                for which in (0, 1):
                    arrived = place(which, section, origin, wide)
                    remote(
                        arrived, arrived, line_sem, (which, way, hop - 1), {HEAD: head}
                    ).wait_recv()

                    @pl.when(goes)
                    def _(which=which):
                        line(which, way, hop).start()

                    for axis in (0, 1):
                        across(which, axis, number, origin).start()
                    pair(which, 0, number, origin, section).start()

        if hop == 1:
            forward_halves(0, head)
        else:
            for number, way, origin, comes, goes in each(hop - 1):

                @pl.when(comes)
                def _(number=number, origin=origin):
                    forward_halves(number, origin)

    @pl.when(first)
    def _():
        swap(given_second).wait_recv()
        shift_all(0, parts.at[0])

    @pl.when(second)
    def _():
        swap(given_first).wait_recv()
        shift_all(0, given_first)

    for number, way, origin, comes, goes in each(heads - 1):

        @pl.when(comes)
        def _(number=number, origin=origin):
            forward_halves(number, origin)

    def spread(number):
        for axis in (0, 1):
            across(2, axis, number, lax.rem(head + heads - number, heads)).start()

    shift_own(0).wait()
    spread(0)
    finish_halves(0, head)
    for hop in range(1, heads):
        for number, way, origin, comes, goes in each(hop):

            @pl.when(comes)
            def _(number=number, origin=origin):
                finish_halves(number, origin)

    for distance in range(1, heads):
        shift_in(0, distance).wait_recv()
        spread(distance)

    for which in (0, 1):
        token_own(which).wait()
        for axis in (0, 1, 2):
            token_in(which, axis).wait_recv()
            token(which, axis).wait_send()

    def forward_part(number):
        origin = lax.rem(head + heads - number, heads)
        for axis in (0, 1):
            across_in(2, axis, number, origin).wait_recv()
            diagonal(2, 1 - axis, number, origin).start()

    def received(number, origin):
        for which in (0, 1):
            for kind in range(5):
                pair(which, kind, number, origin, 1 - section).wait_recv()

    def all_received():
        received(0, head)
        for hop in range(1, heads):
            for number, way, origin, comes, goes in each(hop):

                @pl.when(comes)
                def _(number=number, origin=origin):
                    received(number, origin)

    pl.when(second)(all_received)
    for which in (0, 1):
        locals_[which].wait()
    loads = [
        pltpu.make_async_copy(qkv_all.at[0], scratch[0], local_sem.at[7]),
        pltpu.make_async_copy(out_all.at[0], scratch[1], local_sem.at[8]),
    ]
    fetch = pltpu.make_async_copy(tokens_in, block, local_sem.at[9])
    for load in loads:
        load.start()
    fetch.start()
    fetch.wait()
    layer_in[...] = block[...].astype(jnp.float32)
    small_give.wait_send()
    small_theirs = small_all.at[1 - section]
    remote(small_theirs, small_theirs, small_sem, (), other).wait_recv()
    operands = (layer_in, small_all, cosine, sine, own_pos, key_pos)

    def met():
        @pl.when(first)
        def _():
            shift_all(1, given_second)

        @pl.when(second)
        def _():
            shift_all(1, parts.at[1])

        for swap_block in swaps():
            swap_block.start()
        forward_part(1)

    attention_body(
        0, operands, results, scratch, loads, lambda: None, lambda: forward_part(0), met
    )
    for number in range(2, heads):
        forward_part(number)

    for number in range(heads):
        origin = lax.rem(head + heads - number, heads)
        for axis in (0, 1):
            diagonal_in(2, axis, number, origin).wait_recv()
            diagonal(2, axis, number, origin).wait_send()
            across(2, axis, number, origin).wait_send()

    def settle(number, origin):
        for which in (0, 1):
            for axis in (0, 1):
                across(which, axis, number, origin).wait_send()
                diagonal(which, axis, number, origin).wait_send()
            for kind in range(5):
                if kind == 0 and number == 0:
                    pair_own(which).wait_send()
                else:
                    pair(which, kind, number, origin, section).wait_send()

    for which in (0, 1):
        for way, go in ((0, head < heads - 1), (1, head > 0)):

            @pl.when(go)
            def _(which=which, way=way):
                line(which, way, 0).wait_send()

    for swap_block in swaps():
        swap_block.wait()
    settle(0, head)
    for hop in range(1, heads):
        for number, way, origin, comes, goes in each(hop):

            @pl.when(comes)
            def _(number=number, way=way, origin=origin, goes=goes, hop=hop):
                settle(number, origin)

                @pl.when(goes)
                def _():
                    for which in (0, 1):
                        line(which, way, hop).wait_send()

    pl.when(first)(all_received)
    swap(given_first).wait_send()
    shift_own(1).wait()
    for distance in range(1, heads):
        for layer in (0, 1):
            shift(layer, given_first, distance).wait_send()
        shift_in(1, distance).wait_recv()


def start_weights(number, qkv_own, out_own, parts, sides, small_own, *tables):
    heads, wides = lax.axis_size(HEAD), lax.axis_size(WIDE)
    rows, qkv_cols = qkv_own.shape
    out_cols = out_own.shape[1]
    numbers = 2 * heads - 1
    tokens = sides.shape[1] * sides.shape[2]
    whole = heads * wides * rows
    dtype = parts.dtype
    dma = pltpu.SemaphoreType.DMA
    anywhere = pl.BlockSpec(memory_space=pl.ANY)
    vmem = pl.BlockSpec(memory_space=pltpu.VMEM)
    return pl.pallas_call(
        start_kernel,
        out_shape=(
            jax.ShapeDtypeStruct((2, whole, qkv_cols), dtype),
            jax.ShapeDtypeStruct((2, whole, out_cols), dtype),
            jax.ShapeDtypeStruct((whole, parts.shape[3]), dtype),
            jax.ShapeDtypeStruct(parts.shape[1:], dtype),
            jax.ShapeDtypeStruct((tokens, out_cols), dtype),
            jax.ShapeDtypeStruct((tokens, out_cols), dtype),
            jax.ShapeDtypeStruct((tokens, out_cols), dtype),
            jax.ShapeDtypeStruct((tokens, out_cols), dtype),
            jax.ShapeDtypeStruct((2,) + small_own.shape, jnp.float32),
        )
        + attention_shapes(tokens, out_cols, qkv_cols - out_cols, heads, dtype),
        in_specs=[anywhere] * 4 + [vmem] * 5,
        out_specs=(anywhere,) * 8 + (vmem,) * 10,
        scratch_shapes=attention_scratch(tokens, out_cols, qkv_cols, heads, dtype)
        + [
            pltpu.VMEM((tokens, out_cols), dtype),
            pltpu.VMEM((tokens, out_cols), jnp.float32),
            pltpu.VMEM(parts.shape[1:], dtype),
            pltpu.VMEM(parts.shape[1:], dtype),
            dma((2,)),
            dma((10,)),
            dma((2,)),
            dma((2, 2, heads)),
            dma((2, 2, 2, heads)),
            dma((2, 3, 2, numbers)),
            dma((2, 3, 2, numbers)),
            dma((2, 2, 5, numbers)),
            dma((2, 2, 3)),
            dma((2, 2)),
        ],
        compiler_params=pltpu.CompilerParams(
            collective_id=number, has_side_effects=True, vmem_limit_bytes=60 * 2**20
        ),
    )(qkv_own, out_own, parts, sides, small_own, *tables)


def finish_kernel(
    first_terms,
    second_terms,
    small,
    first_parts,
    second_parts,
    tokens_in,
    totals,
    small_total,
    low_parts,
    high_parts,
    tokens_out,
    near_buf,
    middle,
    far_buf,
    sums,
    line_buf,
    small_sum,
    small_buf,
    shifted,
    give,
    local_sem,
    shift_sem,
    swap_sem,
    near_sem,
    far_sem,
    line_sem,
    small_sem,
    give_sem,
    token_sem,
):
    section, head, wide = (lax.axis_index(axis) for axis in (SECTION, HEAD, WIDE))
    heads, wides = lax.axis_size(HEAD), lax.axis_size(WIDE)
    here = [beside(wide, 0), beside(wide, 1), beside(wide, 2)]
    columns = first_terms.shape[2]
    terms = (first_terms, second_terms)
    other = {SECTION: 1 - section}
    first, second = section == 0, section == 1
    sender_rows = tokens_in.shape[2]

    def remote(source, target, sems, at, partner):
        return pltpu.make_async_remote_copy(
            source,
            target,
            sems.at[(0,) + at],
            sems.at[(1,) + at],
            device_id=partner,
            device_id_type=MESH,
        )

    def shift(distance, target):
        target_head = lax.rem(head + distance, heads)
        return remote(
            first_parts.at[target_head],
            target.at[head],
            shift_sem,
            (distance,),
            {HEAD: target_head},
        )

    def shift_in(distance, target):
        arrived = target.at[lax.rem(head + heads - distance, heads)]
        return remote(arrived, arrived, shift_sem, (distance,), {HEAD: head})

    def near(side, turn, target):
        wide_at = here[side] if turn == 0 else here[2]
        return remote(
            terms[side].at[wide_at * heads + target],
            near_buf.at[side, turn, target],
            near_sem,
            (side, turn, target),
            {WIDE: here[side]},
        )

    def far(side, target):
        return remote(
            middle.at[side, target],
            far_buf.at[side, target],
            far_sem,
            (side, target),
            {WIDE: here[1 - side]},
        )

    def line(way, target, side):
        step = 1 if way == 0 else -1
        return remote(
            sums.at[target, side],
            line_buf.at[way, target, side],
            line_sem,
            (way, target, side),
            {HEAD: head + step},
        )

    def token_target(layer, which, sender_wide, sender_section):
        first_row = pl.multiple_of(sender_section * sender_rows, 16)
        return tokens_out.at[which, sender_wide, pl.ds(first_row, sender_rows)]

    def token(layer, which, turn):
        wide_at = wide if turn == 3 else here[turn]
        sems = (token_sem.at[0, layer, which, turn], token_sem.at[1, section, which, turn])
        return pltpu.make_async_remote_copy(
            tokens_in.at[which * 2 + layer, wide_at],
            token_target(layer, which, wide, section),
            *sems,
            device_id={SECTION: layer, WIDE: wide_at},
            device_id_type=MESH,
        )

    def token_in(from_section, which, turn):
        wide_at = wide if turn == 3 else here[turn]
        target = token_target(section, which, wide_at, from_section)
        sems = (token_sem.at[0, section, which, turn], token_sem.at[1, from_section, which, turn])
        return pltpu.make_async_remote_copy(
            target, target, *sems, device_id={HEAD: head}, device_id_type=MESH
        )

    barrier = pltpu.get_barrier_semaphore()
    partners = [other] + [{WIDE: wide_at} for wide_at in here]
    partners += [{SECTION: 1 - section, WIDE: wide_at} for wide_at in here]
    partners += [{HEAD: lax.rem(head + distance, heads)} for distance in range(1, heads)]
    for partner in partners:
        pl.semaphore_signal(barrier, 1, device_id=partner, device_id_type=MESH)
    pl.semaphore_wait(barrier, len(partners))

    order = []
    for at in range(heads // 2):
        order += [heads - 1 - at, at]

    def start_near(turn, target):
        for side in (0, 1):
            near(side, turn, target).start()

    start_near(1, order[0])
    start_near(0, order[0])

    @pl.when(first)
    def _():
        for distance in range(1, heads):
            shift(distance, low_parts).start()
        remote(second_parts, low_parts, swap_sem, (0,), other).start()
        pltpu.make_async_copy(first_parts.at[head], low_parts.at[head], local_sem.at[0]).start()

    @pl.when(second)
    def _():
        for distance in range(1, heads):
            shift(distance, shifted).start()
        pltpu.make_async_copy(second_parts, high_parts, local_sem.at[1]).start()
        remote(
            first_parts.at[head], high_parts.at[head], swap_sem, (1,), other
        ).start()

    steps = [other, {WIDE: here[0]}, {WIDE: here[1]}]
    steps += [{HEAD: lax.rem(head + distance, heads)} for distance in range(1, heads)]

    def small_copy(at):
        source = small.at[1 - section] if at == 0 else small_sum.at[min(at, 3)]
        return remote(source, small_buf.at[at], small_sem, (at,), steps[at])

    for at in range(3):
        small_copy(at).start()
        small_copy(at).wait()
        small_sum[at + 1] = (small[section] if at == 0 else small_sum[at]) + small_buf[at]
    for at in range(3, len(steps)):
        small_copy(at).start()

    def across(number):
        target = order[number]
        for side in (0, 1):
            near(side, 1, target).wait_recv()
            middle[side, target] = (
                terms[side][here[1 - side] * heads + target].astype(jnp.float32)
                + near_buf[side, 1, target].astype(jnp.float32)
            ).astype(middle.dtype)
            far(side, target).start()
        if number + 1 < heads:
            start_near(1, order[number + 1])
        for side in (0, 1):
            near(side, 0, target).wait_recv()
        if number + 1 < heads:
            start_near(0, order[number + 1])

    def collect(target, last):
        for side in (0, 1):
            far(side, target).wait_recv()
            sums[target, side] = (
                terms[side][wide * heads + target].astype(jnp.float32)
                + near_buf[side, 0, target].astype(jnp.float32)
                + far_buf[side, target].astype(jnp.float32)
            ).astype(sums.dtype)
            if target > 0:

                @pl.when(head == 0)
                def _(side=side):
                    line(0, target, side).start()

            if target < heads - 1:

                @pl.when(head == heads - 1)
                def _(side=side):
                    line(1, target, side).start()
                    if last and side == 0:
                        line(1, target, side).wait_send()

    def pass_on(at_head, way, target):
        @pl.when(head == at_head)
        def _():
            for side in (0, 1):
                line(way, target, side).wait_recv()
                sums[target, side] = (
                    sums[target, side].astype(jnp.float32)
                    + line_buf[way, target, side].astype(jnp.float32)
                ).astype(sums.dtype)
                line(way, target, side).start()

    def send_tokens():
        for which in (0, 1):
            for turn in range(4):
                for layer in (0, 1):

                    @pl.when((turn < 3) | (section != layer))
                    def _(layer=layer, which=which, turn=turn):
                        token(layer, which, turn).start()

            pltpu.make_async_copy(
                tokens_in.at[which * 2 + section, wide],
                token_target(section, which, wide, section),
                local_sem.at[2 + which],
            ).start()

    passes = {
        1: [(1, 0, 3)],
        2: [(2, 0, 3), (2, 1, 0)],
        3: [(1, 1, 0), (1, 0, 2), (2, 1, 1)],
    }
    for number, target in enumerate(order):
        across(number)
        if number == heads - 1:
            send_tokens()
        collect(target, number == heads - 1)
        for entry in passes.get(number, ()):
            pass_on(*entry)

    @pl.when(second)
    def _():
        for distance in range(1, heads):
            shift_in(distance, shifted).wait_recv()
            origin = lax.rem(head + heads - distance, heads)
            remote(
                shifted.at[origin], high_parts.at[origin], swap_sem, (1 + distance,), other
            ).start()

    whole = small_sum[3]
    for at in range(3, len(steps)):
        small_copy(at).wait()
        whole = whole + small_buf[at]
    small_total[...] = whole

    for target in range(heads):

        @pl.when(head == target)
        def _(target=target):
            for side in (0, 1):
                value = sums[target, side].astype(jnp.float32)
                for way, comes in ((0, target > 0), (1, target < heads - 1)):
                    if comes:
                        line(way, target, side).wait_recv()
                        value = value + line_buf[way, target, side].astype(jnp.float32)
                give[side] = value

        for side in (0, 1):
            for turn in (0, 1):
                near(side, turn, target).wait_send()
            far(side, target).wait_send()

            @pl.when(head < target)
            def _(target=target, side=side):
                line(0, target, side).wait_send()

            early = target == order[-1] and side == 0

            @pl.when((head > target) & ((head < heads - 1) | (not early)))
            def _(target=target, side=side):
                line(1, target, side).wait_send()

    handed = remote(give.at[1 - section], totals.at[section], give_sem, (), other)
    handed.start()
    totals[section] = give[section]

    for which in (0, 1):
        pltpu.make_async_copy(
            tokens_in.at[which * 2 + section, wide],
            token_target(section, which, wide, section),
            local_sem.at[2 + which],
        ).wait()
        for turn in range(4):
            for layer in (0, 1):

                @pl.when((turn < 3) | (section != layer))
                def _(layer=layer, which=which, turn=turn):
                    token(layer, which, turn).wait_send()
                    token_in(layer, which, turn).wait_recv()

    @pl.when(first)
    def _():
        for distance in range(1, heads):
            shift(distance, low_parts).wait_send()
            shift_in(distance, low_parts).wait_recv()
        remote(second_parts, low_parts, swap_sem, (0,), other).wait_send()
        pltpu.make_async_copy(first_parts.at[head], low_parts.at[head], local_sem.at[0]).wait()
        for distance in range(heads):
            arrived = high_parts.at[lax.rem(head + heads - distance, heads)]
            remote(arrived, arrived, swap_sem, (1 + distance,), other).wait_recv()

    @pl.when(second)
    def _():
        for distance in range(1, heads):
            shift(distance, shifted).wait_send()
        pltpu.make_async_copy(second_parts, high_parts, local_sem.at[1]).wait()
        for distance in range(heads):
            sent = high_parts.at[lax.rem(head + heads - distance, heads)]
            remote(sent, sent, swap_sem, (1 + distance,), other).wait_send()
        remote(second_parts, low_parts, swap_sem, (0,), other).wait_recv()

    handed.wait_send()
    remote(totals.at[1 - section], totals.at[1 - section], give_sem, (), other).wait_recv()


def finish_weights(
    first_terms, second_terms, small, first_parts, second_parts, tokens_in, number
):
    heads = lax.axis_size(HEAD)
    blocks, rows, columns = first_terms.shape
    dtype = first_terms.dtype
    dma = pltpu.SemaphoreType.DMA
    vmem = pl.BlockSpec(memory_space=pltpu.VMEM)
    anywhere = pl.BlockSpec(memory_space=pl.ANY)
    smalls = 2 + heads
    layers, wides, sender_rows, width = tokens_in.shape
    return pl.pallas_call(
        finish_kernel,
        out_shape=(
            jax.ShapeDtypeStruct((2, rows, columns), jnp.float32),
            jax.ShapeDtypeStruct(small.shape[1:], jnp.float32),
            jax.ShapeDtypeStruct(first_parts.shape, dtype),
            jax.ShapeDtypeStruct(first_parts.shape, dtype),
            jax.ShapeDtypeStruct((2, wides, 2 * sender_rows, width), dtype),
        ),
        in_specs=[vmem, vmem, vmem, anywhere, anywhere, anywhere],
        out_specs=(vmem, vmem, anywhere, anywhere, anywhere),
        scratch_shapes=[
            pltpu.VMEM((2, 2, heads, rows, columns), dtype),
            pltpu.VMEM((2, heads, rows, columns), dtype),
            pltpu.VMEM((2, heads, rows, columns), dtype),
            pltpu.VMEM((heads, 2, rows, columns), dtype),
            pltpu.VMEM((2, heads, 2, rows, columns), dtype),
            pltpu.VMEM((4,) + small.shape[1:], jnp.float32),
            pltpu.VMEM((smalls,) + small.shape[1:], jnp.float32),
            pltpu.VMEM(first_parts.shape, dtype),
            pltpu.VMEM((2, rows, columns), jnp.float32),
            dma((4,)),
            dma((2, heads)),
            dma((2, 1 + heads)),
            dma((2, 2, 2, heads)),
            dma((2, 2, heads)),
            dma((2, 2, heads, 2)),
            dma((2, smalls)),
            dma((2,)),
            dma((2, 2, 2, 4)),
        ],
        compiler_params=pltpu.CompilerParams(
            collective_id=number, has_side_effects=True, vmem_limit_bytes=60 * 2**20
        ),
    )(first_terms, second_terms, small, first_parts, second_parts, tokens_in)


def cut_kernel(
    gate, up, down, out, sides, gains, bias, parts, out_inner, sides_inner, small
):
    count, part = parts.shape[0], parts.shape[2] // 3
    heads, wides = lax.axis_size(HEAD), lax.axis_size(WIDE)
    size = out.shape[1] // (heads * wides)
    places = [(head * wides + wide) * size for wide in range(wides) for head in range(heads)]

    def inner(whole):
        return jnp.concatenate([whole[:, start : start + size] for start in places], 1)

    out_inner[...] = inner(out[...])

    @pl.when(pl.program_id(0) == 0)
    def _():
        sides_inner[...] = inner(sides[...])
        scales = inner(gains[...])
        width = gains.shape[1]
        for at in (0, 1):
            small[:, pl.ds(at * width, width)] = scales[at : at + 1]
        small[:, pl.ds(2 * width, bias.shape[1])] = bias[...]

    for at in range(count):
        size = min(part, gate.shape[1] - at * part)
        for which, weight in enumerate((gate, up, down)):
            start = which * part
            parts[at, :, pl.ds(start, size)] = weight[:, pl.ds(at * part, size)]
            if size < part:
                rest = part - size
                parts[at, :, pl.ds(start + size, rest)] = jnp.zeros(
                    (parts.shape[1], rest), parts.dtype
                )


def cut_parts(gate, up, down, out, sides, gains, bias, count, part):
    rows, columns = gate.shape
    step = 16
    weight = pl.BlockSpec((step, columns), lambda at: (at, 0))
    square = pl.BlockSpec((step, out.shape[1]), lambda at: (at, 0))
    wholes = [
        pl.BlockSpec(shape, lambda at: (0, 0))
        for shape in (sides.shape, gains.shape, bias.shape, (1, gains.size + bias.size))
    ]
    return pl.pallas_call(
        cut_kernel,
        grid=(rows // step,),
        out_shape=(
            jax.ShapeDtypeStruct((count, rows, 3 * part), gate.dtype),
            jax.ShapeDtypeStruct(out.shape, out.dtype),
            jax.ShapeDtypeStruct(sides.shape, sides.dtype),
            jax.ShapeDtypeStruct((1, gains.size + bias.size), jnp.float32),
        ),
        in_specs=[weight] * 3 + [square] + wholes[:3],
        out_specs=(
            pl.BlockSpec((count, step, 3 * part), lambda at: (0, at, 0)),
            square,
            wholes[0],
            wholes[3],
        ),
        compiler_params=pltpu.CompilerParams(vmem_limit_bytes=24 * 2**20),
    )(gate, up, down, out, sides, gains, bias)


def join_kernel(low, high, totals, gate, up, down, qkv, out):
    count, part = low.shape[0], low.shape[2] // 3
    for at in range(2 * count):
        size = min(part, gate.shape[2] - at * part)
        source = low if at < count else high
        for which, grad in enumerate((gate, up, down)):
            grad[0, :, pl.ds(at * part, size)] = source[
                at % count, :, pl.ds(which * part, size)
            ].astype(grad.dtype)
    cut, width = qkv.shape[2] // 2, out.shape[2]
    for at in (0, 1):
        qkv[0, :, pl.ds(at * cut, cut)] = totals[at, :, pl.ds(0, cut)]
    whole = jnp.concatenate([totals[at, :, pl.ds(cut, width // 2)] for at in (0, 1)], 1)
    heads, wides = lax.axis_size(HEAD), lax.axis_size(WIDE)
    size = width // (heads * wides)
    places = [(wide * heads + head) * size for head in range(heads) for wide in range(wides)]
    out[0] = jnp.concatenate([whole[:, start : start + size] for start in places], 1)


def join_parts(low, high, totals, columns, qkv_cols):
    count, rows, width = low.shape
    out_cols = 2 * totals.shape[2] - qkv_cols
    step = 16
    part = pl.BlockSpec((count, step, width), lambda at: (0, at, 0))
    total = pl.BlockSpec((2, step, totals.shape[2]), lambda at: (0, at, 0))
    sizes = (columns, columns, columns, qkv_cols, out_cols)
    return pl.pallas_call(
        join_kernel,
        grid=(rows // step,),
        out_shape=tuple(jax.ShapeDtypeStruct((1, rows, size), jnp.float32) for size in sizes),
        in_specs=[part, part, total],
        out_specs=tuple(pl.BlockSpec((1, step, size), lambda at: (0, at, 0)) for size in sizes),
        compiler_params=pltpu.CompilerParams(vmem_limit_bytes=24 * 2**20),
    )(low, high, totals)


def partner_of(head, turn):
    if turn == 1:
        return head + 1 - 2 * lax.rem(head, 2)
    return lax.rem(head + 2, 4) if turn == 2 else 3 - head


def block_swap(source, target, sems, head, turn):
    return pltpu.make_async_remote_copy(
        source,
        target,
        sems.at[0],
        sems.at[1],
        device_id={HEAD: partner_of(head, turn)},
        device_id_type=MESH,
    )


def visit(head, step, heads):
    inner_chip = jnp.minimum(jnp.minimum(head, heads - 1 - head), 1)
    at = step + inner_chip * (1 - lax.div(step, 2)) * (1 - 2 * step)
    return at + lax.div(2 * head, heads) * (heads - 1 - 2 * at)


def group_pipeline(block, everyone, outs, scratch, prepare, compute, settle, extras=()):
    (partial, pair_buf, sums, line_buf, own_sem, pair_sem, line_sem, swap_sem, chain_sem) = scratch
    section, head = lax.axis_index(SECTION), lax.axis_index(HEAD)
    heads = lax.axis_size(HEAD)
    tokens = block.shape[0]
    other = {SECTION: 1 - section}

    def place(section_at, origin):
        start = (origin * 2 + section_at) * tokens
        return everyone.at[pl.ds(pl.multiple_of(start, tokens), tokens)]

    def remote(source, target, send, receive, partner):
        return pltpu.make_async_remote_copy(
            source, target, send, receive, device_id=partner, device_id_type=MESH
        )

    def pair(origin, source):
        target = place(section, origin)
        return remote(source, target, pair_sem.at[0, origin], pair_sem.at[1, origin], other)

    def pair_in(origin):
        target = place(1 - section, origin)
        return remote(target, target, pair_sem.at[0, origin], pair_sem.at[1, origin], other)

    def line(way, hop, source):
        step = 1 - 2 * way
        target = place(section, head - step * hop)
        sems = (line_sem.at[0, way, hop], line_sem.at[1, way, hop])
        return remote(source, target, *sems, {HEAD: head + step})

    def inside(place_at):
        return (place_at >= 0) & (place_at < heads)

    def accept(way, hop):
        step = 1 - 2 * way
        here = place(section, head - step * hop)
        line(way, hop - 1, here).wait_recv()

        @pl.when(inside(head + step))
        def _():
            line(way, hop, here).start()

        pair(head - step * hop, here).start()

    def swap(origin):
        return remote(
            partial.at[origin, 1 - section],
            pair_buf.at[origin],
            swap_sem.at[0, origin],
            swap_sem.at[1, origin],
            other,
        )

    def lot(piece):
        size = tokens // CHAIN_PIECES
        return pl.ds(piece * size, size)

    def chain(way, target, piece):
        return remote(
            sums.at[target, lot(piece)],
            line_buf.at[way, target, lot(piece)],
            chain_sem.at[0, way, target, piece],
            chain_sem.at[1, way, target, piece],
            {HEAD: head + 1 - 2 * way},
        )

    def send_pieces(way, target, last):
        for piece in range(CHAIN_PIECES):
            chain(way, target, piece).start()
            if last and piece < CHAIN_PIECES - 1:
                chain(way, target, piece).wait_send()

    def deliver(origin, last=False):
        swap(origin).wait_recv()
        sums[origin] = (
            partial[origin, section].astype(jnp.float32) + pair_buf[origin].astype(jnp.float32)
        ).astype(sums.dtype)

        @pl.when((head == 0) & (origin > 0))
        def _():
            send_pieces(0, origin, last)

        @pl.when((head == heads - 1) & (origin < heads - 1))
        def _():
            send_pieces(1, origin, last)

    def pass_on(way, target, piece):
        chain(way, target, piece).wait_recv()
        here = lot(piece)
        sums[target, here] = (
            sums[target, here].astype(jnp.float32) + line_buf[way, target, here].astype(jnp.float32)
        ).astype(sums.dtype)
        chain(way, target, piece).start()

    barrier = pltpu.get_barrier_semaphore()
    partners = [other] + [{HEAD: lax.rem(head + shift, heads)} for shift in range(1, heads)]
    for partner in partners:
        pl.semaphore_signal(barrier, 1, device_id=partner, device_id_type=MESH)
    pl.semaphore_wait(barrier, len(partners))

    for way in (0, 1):

        @pl.when(inside(head + 1 - 2 * way))
        def _(way=way):
            line(way, 0, block).start()

    pair(head, block).start()
    own = pltpu.make_async_copy(block, place(section, head), own_sem)
    own.start()
    prepare()
    own.wait()

    def one(step, carry):
        origin = visit(head, step, heads)

        @pl.when(step >= 1)
        def _():
            deliver(visit(head, step - 1, heads))

        @pl.when(step == 1)
        def _():
            for way in (0, 1):

                @pl.when(inside(head - (1 - 2 * way)))
                def _(way=way):
                    accept(way, 1)

        hop = jnp.maximum(origin - head, head - origin)

        @pl.when((step >= 2) & (hop >= 2))
        def _():
            accept(lax.div(jnp.maximum(origin - head, 0) + heads - 2, heads), hop)

        pair_in(origin).wait_recv()
        compute(origin)
        swap(origin).start()
        return carry

    lax.fori_loop(0, heads, one, 0)
    deliver(visit(head, heads - 1, heads), True)

    between = (head > 0) & (head < heads - 1)
    side = lax.div(2 * head, heads)
    ends = ((1 - side) * (heads - 1), side * (heads - 1))
    extras = list(extras)

    def work(count):
        for _ in range(min(count, len(extras))):
            extras.pop(0)()

    work(2)

    @pl.when(between)
    def _():
        for piece in range(CHAIN_PIECES):
            pass_on(side, heads - 1 - head, piece)

    for piece in range(CHAIN_PIECES):

        @pl.when(between)
        def _(piece=piece):
            pass_on(side, ends[0], piece)
            pass_on(1 - side, ends[1], piece)

        work(1)

    work(len(extras))
    settle()
    spans = [pl.ds(at * block.shape[1], block.shape[1]) for at in range(len(outs))]
    for out, span in zip(outs, spans):
        out[...] = sums[head, :, span].astype(jnp.float32)
    for way, comes in ((0, head > 0), (1, head < heads - 1)):

        @pl.when(comes)
        def _(way=way):
            for piece in range(CHAIN_PIECES):
                chain(way, head, piece).wait_recv()
            for out, span in zip(outs, spans):
                out[...] += line_buf[way, head, :, span].astype(jnp.float32)

    for piece in range(CHAIN_PIECES):
        for target in range(1, heads):

            if target < heads - 1 or piece == CHAIN_PIECES - 1:

                @pl.when(head == 0)
                def _(piece=piece, target=target):
                    chain(0, target, piece).wait_send()

                @pl.when(head == heads - 1)
                def _(piece=piece, target=target):
                    chain(1, heads - 1 - target, piece).wait_send()

        @pl.when(between)
        def _(piece=piece):
            chain(side, heads - 1 - head, piece).wait_send()
            chain(side, ends[0], piece).wait_send()
            chain(1 - side, ends[1], piece).wait_send()

    for origin in range(heads):
        here = place(section, origin)
        pair(origin, here).wait_send()
        swap(origin).wait_send()

    for way in (0, 1):
        for hop in range(heads):
            step = 1 - 2 * way

            @pl.when(inside(head + step) & inside(head - step * hop))
            def _(way=way, hop=hop):
                line(way, hop, block).wait_send()


def pipeline_scratch(heads, tokens, columns, dtype):
    dma = pltpu.SemaphoreType.DMA
    return [
        pltpu.VMEM((heads, 2, tokens, columns), dtype),
        pltpu.VMEM((heads, tokens, columns), dtype),
        pltpu.VMEM((heads, tokens, columns), dtype),
        pltpu.VMEM((2, heads, tokens, columns), dtype),
        dma,
        dma((2, heads)),
        dma((2, 2, heads)),
        dma((2, heads)),
        dma((2, 2, heads, CHAIN_PIECES)),
    ]


PIPELINE_SCRATCH = 9
CHAIN_PIECES = 4
TERM_ROWS = 512
TERM_SLOTS = 3
STEP_COLUMNS = 384
STEP_WIDTH = 512


def chunks(total, size):
    return [(at, min(size, total - at)) for at in range(0, total, size)]


def write_partial(partial, origin, left, weights, columns, offset=0):
    tokens = partial.shape[2]
    for start, count in chunks(weights.shape[0], STEP_WIDTH):
        piece = contract_last(left, weights[pl.ds(start, count), pl.ds(*columns)])
        piece = piece.astype(partial.dtype)
        partial[origin, 0, :, pl.ds(offset + start, count)] = piece[:tokens]
        partial[origin, 1, :, pl.ds(offset + start, count)] = piece[tokens:]


def forward_kernel(block, weights_hbm, out, everyone, gate_up_hbm, hidden_hbm, *scratch):
    shared, rest = scratch[:PIPELINE_SCRATCH], scratch[PIPELINE_SCRATCH:]
    weights, gate_up, hidden, load_sem, store_sem = rest
    partial = shared[0]
    heads = lax.axis_size(HEAD)
    rows = 2 * block.shape[0]
    part = hidden.shape[1]
    load = pltpu.make_async_copy(weights_hbm, weights, load_sem)

    def stores(origin):
        span = pl.ds(pl.multiple_of(origin * rows, rows), rows)
        return [
            pltpu.make_async_copy(gate_up.at[span], gate_up_hbm.at[span], store_sem.at[0, origin]),
            pltpu.make_async_copy(hidden.at[span], hidden_hbm.at[span], store_sem.at[1, origin]),
        ]

    def prepare():
        load.start()
        load.wait()

    def compute(origin):
        span = pl.ds(pl.multiple_of(origin * rows, rows), rows)
        left = everyone[span, :]
        for start, count in chunks(part, STEP_COLUMNS):
            gate = jnp.dot(
                left, weights[:, pl.ds(start, count)], preferred_element_type=jnp.float32
            )
            up = jnp.dot(
                left, weights[:, pl.ds(part + start, count)], preferred_element_type=jnp.float32
            )
            gate_up[span, pl.ds(start, count)] = gate.astype(gate_up.dtype)
            gate_up[span, pl.ds(part + start, count)] = up.astype(gate_up.dtype)
            hidden[span, pl.ds(start, count)] = (gate / (1.0 + jnp.exp(-gate)) * up).astype(
                hidden.dtype
            )
        write_partial(partial, origin, hidden[span, :], weights, (2 * part, part))
        for store in stores(origin):
            store.start()

    def settle():
        for origin in range(heads):
            for store in stores(origin):
                store.wait()

    group_pipeline(block, everyone, (out,), shared, prepare, compute, settle)


def term_tiles(operands, part, terms, terms_hbm, term_sem, loads=()):
    lefts, rights = operands
    width = terms_hbm.shape[0]
    tiles = [(which, start) for which in range(3) for start, _ in chunks(width, TERM_ROWS)]

    def store(number):
        which, start = tiles[number]
        slot = number % TERM_SLOTS
        target = terms_hbm.at[pl.ds(start, TERM_ROWS), pl.ds(which * part, part)]
        return pltpu.make_async_copy(terms.at[slot], target, term_sem.at[slot])

    def tile(number):
        which, start = tiles[number]
        if number == 0:
            for load in loads:
                load.wait()
        if number >= TERM_SLOTS:
            store(number - TERM_SLOTS).wait()
        left = lefts[which][:, pl.ds(start, TERM_ROWS)]
        right = rights[which][:, pl.ds(which % 2 * part if which < 2 else 0, part)]
        terms[number % TERM_SLOTS] = contract_first(left, right).astype(terms.dtype)
        store(number).start()

    def settle():
        for number in range(len(tiles) - TERM_SLOTS, len(tiles)):
            store(number).wait()

    return [functools.partial(tile, number) for number in range(len(tiles))], settle


def backward_kernel(
    block, weights_hbm, gate_up_hbm, normed_hbm, hidden_hbm, out, terms_hbm, *scratch
):
    shared, rest = scratch[:PIPELINE_SCRATCH], scratch[PIPELINE_SCRATCH:]
    everyone, weights, gate_up, normed, hidden, d_gate_up, terms, load_sem, term_sem = rest
    partial = shared[0]
    rows = 2 * block.shape[0]
    part = hidden.shape[1]
    sources = ((weights_hbm, weights), (gate_up_hbm, gate_up))
    sources += ((normed_hbm, normed), (hidden_hbm, hidden))
    loads = [
        pltpu.make_async_copy(source, target, load_sem.at[at])
        for at, (source, target) in enumerate(sources)
    ]

    def prepare():
        for load in loads:
            load.start()
        for load in loads[:2]:
            load.wait()

    def compute(origin):
        span = pl.ds(pl.multiple_of(origin * rows, rows), rows)
        left = everyone[span, :]
        for start, count in chunks(part, STEP_COLUMNS):
            d_hidden = jnp.dot(
                left, weights[:, pl.ds(2 * part + start, count)], preferred_element_type=jnp.float32
            )
            gate = gate_up[span, pl.ds(start, count)].astype(jnp.float32)
            up = gate_up[span, pl.ds(part + start, count)].astype(jnp.float32)
            sigmoid = 1.0 / (1.0 + jnp.exp(-gate))
            d_gate = d_hidden * up * sigmoid * (1.0 + gate * (1.0 - sigmoid))
            d_gate_up[span, pl.ds(start, count)] = d_gate.astype(d_gate_up.dtype)
            d_up = d_hidden * gate * sigmoid
            d_gate_up[span, pl.ds(part + start, count)] = d_up.astype(d_gate_up.dtype)
        write_partial(partial, origin, d_gate_up[span, :], weights, (0, 2 * part))

    operands = (normed, normed, everyone), (d_gate_up, d_gate_up, hidden)
    extras, settle = term_tiles(operands, part, terms, terms_hbm, term_sem, loads[2:])
    group_pipeline(block, everyone, (out,), shared, prepare, compute, settle, extras)


def turning_kernel(block, weights_hbm, *refs):
    blocks, (out, d_out, terms_hbm), scratch = refs[:4], refs[4:7], refs[7:]
    shared, rest = scratch[:PIPELINE_SCRATCH], scratch[PIPELINE_SCRATCH:]
    everyone, weights, grads, hidden, d_gate_up, terms, load_sem, give_sem, term_sem = rest
    partial = shared[0]
    rows, width = 2 * block.shape[0], block.shape[1]
    part = hidden.shape[1]
    section, head = lax.axis_index(SECTION), lax.axis_index(HEAD)
    tokens = block.shape[0]
    load = pltpu.make_async_copy(weights_hbm, weights, load_sem.at[4])

    def place(section_at, turn):
        origin = head if turn == 0 else partner_of(head, turn)
        first_row = pl.multiple_of((origin * 2 + section_at) * tokens, tokens)
        return grads.at[pl.ds(first_row, tokens)]

    def own(turn):
        return pltpu.make_async_copy(blocks[turn], place(section, turn), load_sem.at[turn])

    def give(turn, section_at):
        return pltpu.make_async_remote_copy(
            blocks[turn],
            place(section_at, turn),
            give_sem.at[0, turn],
            give_sem.at[1, turn],
            device_id={SECTION: 1 - section},
            device_id_type=MESH,
        )

    def prepare():
        load.start()
        for turn in range(4):
            own(turn).start()
            give(turn, section).start()
        for turn in range(4):
            own(turn).wait()
            give(turn, section).wait_send()
            give(turn, 1 - section).wait_recv()
        load.wait()

    def compute(origin):
        span = pl.ds(pl.multiple_of(origin * rows, rows), rows)
        left, grad = everyone[span, :], grads[span, :]
        for start, count in chunks(part, STEP_COLUMNS):
            gate, up, d_hidden = [
                jnp.dot(
                    source,
                    weights[:, pl.ds(which * part + start, count)],
                    preferred_element_type=jnp.float32,
                )
                for which, source in enumerate((left, left, grad))
            ]
            sigmoid = 1.0 / (1.0 + jnp.exp(-gate))
            hidden[span, pl.ds(start, count)] = (gate * sigmoid * up).astype(hidden.dtype)
            d_gate = d_hidden * up * sigmoid * (1.0 + gate * (1.0 - sigmoid))
            d_gate_up[span, pl.ds(start, count)] = d_gate.astype(d_gate_up.dtype)
            d_up = d_hidden * gate * sigmoid
            d_gate_up[span, pl.ds(part + start, count)] = d_up.astype(d_gate_up.dtype)
        write_partial(partial, origin, hidden[span, :], weights, (2 * part, part))
        write_partial(partial, origin, d_gate_up[span, :], weights, (0, 2 * part), width)

    operands = (everyone, everyone, grads), (d_gate_up, d_gate_up, hidden)
    extras, settle = term_tiles(operands, part, terms, terms_hbm, term_sem)
    group_pipeline(block, everyone, (out, d_out), shared, prepare, compute, settle, extras)


def turning_point(block, weights, grads, number):
    heads = lax.axis_size(HEAD)
    tokens, width = block.shape
    part = weights.shape[1] // 3
    count = 2 * heads * tokens
    dtype = block.dtype
    vmem = pl.BlockSpec(memory_space=pltpu.VMEM)
    anywhere = pl.BlockSpec(memory_space=pl.ANY)
    return pl.pallas_call(
        turning_kernel,
        out_shape=(
            jax.ShapeDtypeStruct((tokens, width), jnp.float32),
            jax.ShapeDtypeStruct((tokens, width), jnp.float32),
            jax.ShapeDtypeStruct(weights.shape, dtype),
        ),
        in_specs=[vmem] + [anywhere] * 5,
        out_specs=(vmem, vmem, anywhere),
        scratch_shapes=pipeline_scratch(heads, tokens, 2 * width, dtype)
        + [
            pltpu.VMEM((count, width), dtype),
            pltpu.VMEM(weights.shape, dtype),
            pltpu.VMEM((count, width), dtype),
            pltpu.VMEM((count, part), dtype),
            pltpu.VMEM((count, 2 * part), dtype),
            pltpu.VMEM((TERM_SLOTS, TERM_ROWS, part), dtype),
            pltpu.SemaphoreType.DMA((5,)),
            pltpu.SemaphoreType.DMA((2, 4)),
            pltpu.SemaphoreType.DMA((TERM_SLOTS,)),
        ],
        compiler_params=pltpu.CompilerParams(
            collective_id=number, has_side_effects=True, vmem_limit_bytes=60 * 2**20
        ),
        cost_estimate=pl.CostEstimate(
            flops=18 * count * width * part, bytes_accessed=4 * weights.size, transcendentals=0
        ),
    )(block, weights, *grads)


def feed_forward(block, weights, number):
    heads = lax.axis_size(HEAD)
    tokens, width = block.shape
    part = weights.shape[1] // 3
    count = 2 * heads * tokens
    dtype = block.dtype
    vmem = pl.BlockSpec(memory_space=pltpu.VMEM)
    anywhere = pl.BlockSpec(memory_space=pl.ANY)
    return pl.pallas_call(
        forward_kernel,
        out_shape=(
            jax.ShapeDtypeStruct((tokens, width), jnp.float32),
            jax.ShapeDtypeStruct((count, width), dtype),
            jax.ShapeDtypeStruct((count, 2 * part), dtype),
            jax.ShapeDtypeStruct((count, part), dtype),
        ),
        in_specs=[vmem, anywhere],
        out_specs=(vmem, vmem, anywhere, anywhere),
        scratch_shapes=pipeline_scratch(heads, tokens, width, dtype)
        + [
            pltpu.VMEM(weights.shape, dtype),
            pltpu.VMEM((count, 2 * part), dtype),
            pltpu.VMEM((count, part), dtype),
            pltpu.SemaphoreType.DMA,
            pltpu.SemaphoreType.DMA((2, heads)),
        ],
        compiler_params=pltpu.CompilerParams(
            collective_id=number, has_side_effects=True, vmem_limit_bytes=60 * 2**20
        ),
        cost_estimate=pl.CostEstimate(
            flops=6 * count * width * part, bytes_accessed=2 * weights.size, transcendentals=0
        ),
    )(block, weights)


def feed_backward(block, weights, gate_up, normed, hidden, number):
    heads = lax.axis_size(HEAD)
    tokens, width = block.shape
    part = hidden.shape[1]
    count = 2 * heads * tokens
    dtype = block.dtype
    vmem = pl.BlockSpec(memory_space=pltpu.VMEM)
    anywhere = pl.BlockSpec(memory_space=pl.ANY)
    return pl.pallas_call(
        backward_kernel,
        out_shape=(
            jax.ShapeDtypeStruct((tokens, width), jnp.float32),
            jax.ShapeDtypeStruct(weights.shape, dtype),
        ),
        in_specs=[vmem] + [anywhere] * 4,
        out_specs=(vmem, anywhere),
        scratch_shapes=pipeline_scratch(heads, tokens, width, dtype)
        + [
            pltpu.VMEM((count, width), dtype),
            pltpu.VMEM(weights.shape, dtype),
            pltpu.VMEM(gate_up.shape, dtype),
            pltpu.VMEM((count, width), dtype),
            pltpu.VMEM((count, part), dtype),
            pltpu.VMEM((count, 2 * part), dtype),
            pltpu.VMEM((TERM_SLOTS, TERM_ROWS, part), dtype),
            pltpu.SemaphoreType.DMA((4,)),
            pltpu.SemaphoreType.DMA((TERM_SLOTS,)),
        ],
        compiler_params=pltpu.CompilerParams(
            collective_id=number, has_side_effects=True, vmem_limit_bytes=58 * 2**20
        ),
        cost_estimate=pl.CostEstimate(
            flops=12 * count * width * part, bytes_accessed=4 * weights.size, transcendentals=0
        ),
    )(block, weights, gate_up, normed, hidden)


GROUP = 3


def turn(tensor, cosine, sine):
    return tensor * cosine + pltpu.roll(tensor, tensor.shape[1] // 2, 1) * sine


def attention_grad_kernel(
    layer,
    moves,
    d_normed2,
    midway,
    scale2,
    out_grad,
    small_rows,
    queries,
    keyval,
    log_total,
    attended,
    normed,
    layer_in,
    scale1,
    cosine,
    sine,
    own_pos,
    key_pos,
    w_out_hbm,
    w_qkv_hbm,
    parts_in,
    d_in,
    small,
    terms_hbm,
    parts_out,
    w_out,
    w_qkv,
    d_midway,
    g_attn,
    d_attended,
    d_qkv,
    d_normed,
    d_keyval,
    terms,
    their_normed,
    their_attended,
    their_g,
    their_d,
    sums,
    pair_buf,
    line_buf,
    load_sem,
    give_sem,
    pair_sem,
    line_sem,
    shift_sem,
):
    section, head = lax.axis_index(SECTION), lax.axis_index(HEAD)
    heads, wides = lax.axis_size(HEAD), lax.axis_size(WIDE)
    tokens, width = normed.shape
    qkv_cols = d_qkv.shape[1]
    kv_width = KV * HDIM
    rows = width // (heads * wides)
    scaling = HDIM**-0.5
    other = {SECTION: 1 - section}

    def remote(source, target, sems, at, partner):
        return pltpu.make_async_remote_copy(
            source,
            target,
            sems.at[(0,) + at],
            sems.at[(1,) + at],
            device_id=partner,
            device_id_type=MESH,
        )

    def half(array, at):
        count = array.shape[1] // 2
        return array.at[:, pl.ds(pl.multiple_of(at * count, 128), count)]

    gives = [
        remote(normed, their_normed, give_sem, (0,), other),
        remote(attended, their_attended, give_sem, (1,), other),
        remote(half(g_attn, 1 - section), their_g, give_sem, (2,), other),
        remote(half(d_qkv, 1 - section), their_d, give_sem, (3,), other),
    ]
    loads = [
        pltpu.make_async_copy(w_out_hbm.at[layer], w_out, load_sem.at[0]),
        pltpu.make_async_copy(w_qkv_hbm.at[layer], w_qkv, load_sem.at[1]),
    ]
    for load in loads:
        load.start()

    def shift(distance):
        target = lax.rem(head + distance, heads)
        return remote(
            parts_in.at[target], parts_out.at[head], shift_sem, (distance,), {HEAD: target}
        )

    def shift_in(distance):
        arrived = parts_out.at[lax.rem(head + heads - distance, heads)]
        return remote(arrived, arrived, shift_sem, (distance,), {HEAD: head})

    def shift_own():
        return pltpu.make_async_copy(parts_in.at[head], parts_out.at[head], load_sem.at[4])

    barrier = pltpu.get_barrier_semaphore()
    partners = [other] + [{HEAD: lax.rem(head + distance, heads)} for distance in range(1, heads)]
    for partner in partners:
        pl.semaphore_signal(barrier, 1, device_id=partner, device_id_type=MESH)
    pl.semaphore_wait(barrier, len(partners))
    for give in gives[:2]:
        give.start()
    if moves:
        shift_own().start()
        for distance in range(1, heads):
            shift(distance).start()

    grad = out_grad[...].astype(jnp.float32)
    unit = midway[...] * scale2[...]
    gain2_grad = jnp.sum(d_normed2[...] * unit, 0, keepdims=True)
    scaled = d_normed2[...] * small_rows[layer, :, pl.ds(width, width)]
    d_midway[...] = (
        scale2[...] * (scaled - unit * jnp.mean(scaled * unit, -1, keepdims=True)) + grad
    )
    g_attn[...] = d_midway[...].astype(g_attn.dtype)
    gives[2].start()
    small[:, pl.ds(width, width)] = gain2_grad
    loads[0].wait()
    for start, count in chunks(width, STEP_WIDTH):
        d_attended[:, pl.ds(start, count)] = contract_last(
            g_attn[...], w_out[pl.ds(start, count), :]
        ).astype(d_attended.dtype)

    allowed = own_pos[...] >= key_pos[...]
    allowed = jnp.concatenate([allowed.astype(jnp.int32)] * GROUP, 0) > 0
    groups = HEADS // GROUP
    for group in range(groups):
        kv = group * KV // groups
        spans = [pl.ds((group * GROUP + at) * HDIM, HDIM) for at in range(GROUP)]
        query = jnp.concatenate([queries[group * GROUP + at] for at in range(GROUP)], 0)
        total = jnp.concatenate([log_total[group * GROUP + at] for at in range(GROUP)], 0)
        key = keyval[:, pl.ds(kv * HDIM, HDIM)]
        value = keyval[:, pl.ds(kv_width + kv * HDIM, HDIM)]
        d_out = jnp.concatenate([d_attended[:, span] for span in spans], 0)
        scores = jnp.where(allowed, contract_last(query, key) * scaling, -1e30)
        probs = jnp.exp(scores - total)
        d_probs = contract_last(d_out, value)
        row_dot = jnp.sum(probs * d_probs, -1, keepdims=True)
        d_scores = (probs * (d_probs - row_dot)).astype(jnp.bfloat16)
        d_query = jnp.dot(d_scores, key, preferred_element_type=jnp.float32) * scaling
        d_query = d_query.astype(jnp.bfloat16).astype(jnp.float32)
        for at, span in enumerate(spans):
            d_qkv[:, span] = turn(
                d_query[at * tokens : (at + 1) * tokens], cosine[...], sine[...]
            ).astype(d_qkv.dtype)
        d_key = contract_first(d_scores, query) * scaling
        d_value = contract_first(probs.astype(jnp.bfloat16), d_out)
        first = group % (groups // KV) == 0
        for column, part in ((kv * HDIM, d_key), (kv_width + kv * HDIM, d_value)):
            part = part if first else part + d_keyval[:, pl.ds(column, HDIM)]
            d_keyval[:, pl.ds(column, HDIM)] = part

    def place(section_at, head_at):
        return pl.ds(pl.multiple_of((section_at * heads + head_at) * tokens, tokens), tokens)

    sent = terms.at[pl.ds(0, 2 * heads * tokens), pl.ds(0, d_keyval.shape[1])]
    sent[...] = d_keyval[...].astype(sent.dtype)

    def pair(target):
        source = sent.at[place(1 - section, target)]
        return remote(source, pair_buf.at[target], pair_sem, (target,), other)

    def line(way, target):
        partner = {HEAD: head + 1 - 2 * way}
        return remote(sums.at[target], line_buf.at[way, target], line_sem, (way, target), partner)

    order = []
    for at in range(heads // 2):
        order += [heads - 1 - at, at]
    for target in order:
        pair(target).start()
    for target in order:
        pair(target).wait_recv()
        sums[target] = (
            sent[place(section, target), :].astype(jnp.float32)
            + pair_buf[target].astype(jnp.float32)
        ).astype(sums.dtype)
        if target > 0:

            @pl.when(head == 0)
            def _(target=target):
                line(0, target).start()

        if target < heads - 1:

            @pl.when(head == heads - 1)
            def _(target=target):
                line(1, target).start()

    for target in order:
        pair(target).wait_send()

    def pass_on(way, target):
        line(way, target).wait_recv()
        sums[target] = (
            sums[target].astype(jnp.float32) + line_buf[way, target].astype(jnp.float32)
        ).astype(sums.dtype)
        line(way, target).start()

    loads[1].wait()
    for start, count in chunks(width, STEP_WIDTH):
        d_normed[:, pl.ds(start, count)] = contract_last(
            d_qkv[:, pl.ds(0, width)], w_qkv[pl.ds(start, count), pl.ds(0, width)]
        )
    gives[1].wait_recv()
    gives[2].wait_recv()
    pair_g = jnp.concatenate([half(g_attn, section)[...], their_g[...]], 0)

    def out_terms(head_at):
        span = pl.ds(head_at * wides * rows, wides * rows)
        left = jnp.concatenate([attended[:, span], their_attended[:, span]], 0)
        piece = contract_first(left, pair_g).astype(terms.dtype)
        for wide_at in range(wides):
            target = pl.ds((wide_at * heads + head_at) * rows, rows)
            terms[target, pl.ds(qkv_cols // 2, width // 2)] = piece[
                wide_at * rows : (wide_at + 1) * rows
            ]

    for at in range(heads - 1):
        right, left = heads - 1 - at, at

        @pl.when((head > 0) & (head < right))
        def _(right=right):
            pass_on(0, right)

        @pl.when((head < heads - 1) & (head > left))
        def _(left=left):
            pass_on(1, left)

        out_terms(at)

    out_terms(heads - 1)

    def store(at):
        start, count = ((0, qkv_cols // 2), (qkv_cols // 2, width // 2))[at]
        span = pl.ds(start, count)
        return pltpu.make_async_copy(terms.at[:, span], terms_hbm.at[:, span], load_sem.at[2 + at])

    store(1).start()
    d_keyval[pl.ds(0, tokens), :] = sums[head].astype(jnp.float32)
    for way, comes in ((0, head > 0), (1, head < heads - 1)):

        @pl.when(comes)
        def _(way=way):
            line(way, head).wait_recv()
            d_keyval[pl.ds(0, tokens), :] += line_buf[way, head].astype(jnp.float32)

    for kv in range(KV):
        span = pl.ds(kv * HDIM, HDIM)
        d_qkv[:, pl.ds(width + kv * HDIM, HDIM)] = turn(
            d_keyval[pl.ds(0, tokens), span], cosine[...], sine[...]
        ).astype(d_qkv.dtype)
    d_qkv[:, pl.ds(width + kv_width, kv_width)] = d_keyval[
        pl.ds(0, tokens), pl.ds(kv_width, kv_width)
    ].astype(d_qkv.dtype)
    gives[3].start()
    small[:, pl.ds(2 * width, qkv_cols)] = jnp.sum(
        d_qkv[...].astype(jnp.float32), 0, keepdims=True
    )
    rest = pl.ds(width, qkv_cols - width)
    for start, count in chunks(width, STEP_WIDTH):
        d_normed[:, pl.ds(start, count)] += contract_last(
            d_qkv[:, rest], w_qkv[pl.ds(start, count), rest]
        )

    unit = layer_in[...] * scale1[...]
    small[:, pl.ds(0, width)] = jnp.sum(d_normed[...] * unit, 0, keepdims=True)
    scaled = d_normed[...] * small_rows[layer, :, pl.ds(0, width)]
    d_in[...] = (
        scale1[...] * (scaled - unit * jnp.mean(scaled * unit, -1, keepdims=True)) + d_midway[...]
    ).astype(d_in.dtype)

    gives[0].wait_recv()
    gives[3].wait_recv()
    pair_d = jnp.concatenate([half(d_qkv, section)[...], their_d[...]], 0)
    for start, count in chunks(width, STEP_WIDTH):
        span = pl.ds(start, count)
        left = jnp.concatenate([normed[:, span], their_normed[:, span]], 0)
        terms[span, pl.ds(0, qkv_cols // 2)] = contract_first(left, pair_d).astype(terms.dtype)
    store(0).start()
    for give in gives:
        give.wait_send()
    for target in range(heads):

        @pl.when(head < target)
        def _(target=target):
            line(0, target).wait_send()

        @pl.when(head > target)
        def _(target=target):
            line(1, target).wait_send()

    for at in (0, 1):
        store(at).wait()
    if moves:
        shift_own().wait()
        for distance in range(1, heads):
            shift(distance).wait_send()
            shift_in(distance).wait_recv()


def attention_grad(layer, number, w_out, w_qkv, parts_in, *operands):
    heads = lax.axis_size(HEAD)
    normed = operands[9]
    tokens, width = normed.shape
    qkv_cols = w_qkv.shape[2]
    kv_cols = qkv_cols - width
    dtype = normed.dtype
    float32 = jnp.float32
    dma = pltpu.SemaphoreType.DMA
    vmem = pl.BlockSpec(memory_space=pltpu.VMEM)
    anywhere = pl.BlockSpec(memory_space=pl.ANY)
    columns = qkv_cols // 2 + width // 2
    moves = parts_in is not None
    parts_in = parts_in if moves else jnp.zeros((heads, 16, 128), dtype)
    return pl.pallas_call(
        functools.partial(attention_grad_kernel, layer, moves),
        out_shape=(
            jax.ShapeDtypeStruct((tokens, width), dtype),
            jax.ShapeDtypeStruct((1, 2 * width + qkv_cols), float32),
            jax.ShapeDtypeStruct((width, columns), dtype),
            jax.ShapeDtypeStruct(parts_in.shape, dtype),
        ),
        in_specs=[vmem] * len(operands) + [anywhere] * 3,
        out_specs=(vmem, vmem, anywhere, anywhere),
        scratch_shapes=[
            pltpu.VMEM(w_out.shape[1:], dtype),
            pltpu.VMEM(w_qkv.shape[1:], dtype),
            pltpu.VMEM((tokens, width), float32),
            pltpu.VMEM((tokens, width), dtype),
            pltpu.VMEM((tokens, width), dtype),
            pltpu.VMEM((tokens, qkv_cols), dtype),
            pltpu.VMEM((tokens, width), float32),
            pltpu.VMEM((2 * heads * tokens, kv_cols), float32),
            pltpu.VMEM((width, columns), dtype),
            pltpu.VMEM((tokens, width), dtype),
            pltpu.VMEM((tokens, width), dtype),
            pltpu.VMEM((tokens, width // 2), dtype),
            pltpu.VMEM((tokens, qkv_cols // 2), dtype),
            pltpu.VMEM((heads, tokens, kv_cols), dtype),
            pltpu.VMEM((heads, tokens, kv_cols), dtype),
            pltpu.VMEM((2, heads, tokens, kv_cols), dtype),
            dma((5,)),
            dma((2, 4)),
            dma((2, heads)),
            dma((2, 2, heads)),
            dma((2, heads)),
        ],
        compiler_params=pltpu.CompilerParams(
            collective_id=number, has_side_effects=True, vmem_limit_bytes=60 * 2**20
        ),
        cost_estimate=pl.CostEstimate(
            flops=40 * tokens * width * qkv_cols,
            bytes_accessed=2 * w_out.size + 2 * w_qkv.size,
            transcendentals=0,
        ),
    )(*operands, w_out, w_qkv, parts_in)


def attention_body(
    layer, operands, results, scratch, loads, ready, breath=lambda: None, met=lambda: None
):
    layer_in, small, cosine, sine, own_pos, key_pos = operands
    normed, queries, keyval, log_total, attended, midway, normed2, scale1, scale2 = results
    w_qkv, w_out, mine, own_sem, pair_sem, line_sem = scratch
    section, head = lax.axis_index(SECTION), lax.axis_index(HEAD)
    heads = lax.axis_size(HEAD)
    tokens, width = normed.shape
    kv_width = KV * HDIM
    other = {SECTION: 1 - section}

    def gain(at):
        return small[layer, :, pl.ds(at * width, width)]

    def remote(source, target, sems, at, partner):
        return pltpu.make_async_remote_copy(
            source,
            target,
            sems.at[(0,) + at],
            sems.at[(1,) + at],
            device_id=partner,
            device_id_type=MESH,
        )

    def place(section_at, head_at):
        start = (section_at * heads + head_at) * tokens
        return keyval.at[pl.ds(pl.multiple_of(start, tokens), tokens)]

    def pair(number, head_at, source):
        return remote(source, place(section, head_at), pair_sem, (number,), other)

    def pair_in(number, head_at):
        target = place(1 - section, head_at)
        return remote(target, target, pair_sem, (number,), other)

    def line(way, hop, source):
        step = 1 - 2 * way
        target = place(section, head - step * hop)
        return remote(source, target, line_sem, (way, hop), {HEAD: head + step})

    scale = lax.rsqrt(
        jnp.mean(layer_in[...] * layer_in[...], -1, keepdims=True) + EPSILON
    )
    scale1[...] = scale
    normed[...] = (layer_in[...] * scale * gain(0)).astype(normed.dtype)
    ready()

    def project(start, count):
        span = pl.ds(start, count)
        return (
            jnp.dot(normed[...], w_qkv[:, span], preferred_element_type=jnp.float32)
            + small[layer, :, pl.ds(2 * width + start, count)]
        )

    loads[0].wait()
    for kv in range(KV):
        key = project(width + kv * HDIM, HDIM)
        mine[:, pl.ds(kv * HDIM, HDIM)] = turn(key, cosine[...], sine[...]).astype(mine.dtype)
    mine[:, pl.ds(kv_width, kv_width)] = project(width + kv_width, kv_width).astype(mine.dtype)
    ways = ((0, head < heads - 1), (1, head > 0))
    for way, go in ways:

        @pl.when(go)
        def _(way=way):
            line(way, 0, mine).start()

    pair(0, head, mine).start()
    own = pltpu.make_async_copy(mine, place(section, head), own_sem)
    own.start()
    breath()

    def arrivals(hop):
        yield 0, head - hop, head >= hop, head < heads - 1
        yield 1, head + hop, head + hop < heads, head > 0

    per_hop = HEADS // (heads - 1)
    for hop in range(1, heads):
        start = (hop - 1) * per_hop * HDIM
        block = project(start, per_hop * HDIM)
        for at in range(per_hop):
            query = block[:, at * HDIM : (at + 1) * HDIM]
            queries[(hop - 1) * per_hop + at] = turn(query, cosine[...], sine[...]).astype(
                queries.dtype
            )
        for way, origin, comes, goes in arrivals(hop):

            @pl.when(comes)
            def _(way=way, origin=origin, goes=goes, hop=hop):
                here = place(section, origin)
                line(way, hop - 1, here).wait_recv()

                @pl.when(goes)
                def _():
                    line(way, hop, here).start()

                pair(2 * hop - 1 + way, origin, here).start()

    own.wait()
    pair_in(0, head).wait_recv()
    for hop in range(1, heads):
        for way, origin, comes, goes in arrivals(hop):

            @pl.when(comes)
            def _(way=way, origin=origin, hop=hop):
                pair_in(2 * hop - 1 + way, origin).wait_recv()

    met()
    allowed = own_pos[...] >= key_pos[...]
    allowed = jnp.concatenate([allowed.astype(jnp.int32)] * GROUP, 0) > 0
    groups = HEADS // GROUP
    for group in range(groups):
        kv = group * KV // groups
        query = jnp.concatenate([queries[group * GROUP + at] for at in range(GROUP)], 0)
        key = keyval[:, pl.ds(kv * HDIM, HDIM)]
        value = keyval[:, pl.ds(kv_width + kv * HDIM, HDIM)]
        scores = jnp.where(allowed, contract_last(query, key) * HDIM**-0.5, -1e30)
        highest = jnp.max(scores, -1, keepdims=True)
        weights_exp = jnp.exp(scores - highest)
        partition = jnp.sum(weights_exp, -1, keepdims=True)
        probs = (weights_exp / partition).astype(jnp.bfloat16)
        result = jnp.dot(probs, value, preferred_element_type=jnp.float32)
        total = highest + jnp.log(partition)
        for at in range(GROUP):
            span = slice(at * tokens, (at + 1) * tokens)
            attended[:, pl.ds((group * GROUP + at) * HDIM, HDIM)] = result[span].astype(
                attended.dtype
            )
            log_total[group * GROUP + at] = total[span]

    loads[1].wait()
    for start, count in chunks(width, STEP_WIDTH):
        span = pl.ds(start, count)
        midway[:, span] = layer_in[:, span] + jnp.dot(
            attended[...], w_out[:, span], preferred_element_type=jnp.float32
        )
    scale = lax.rsqrt(jnp.mean(midway[...] * midway[...], -1, keepdims=True) + EPSILON)
    scale2[...] = scale
    normed2[...] = (midway[...] * scale * gain(1)).astype(normed2.dtype)

    pair(0, head, mine).wait_send()
    for way, go in ways:

        @pl.when(go)
        def _(way=way):
            line(way, 0, mine).wait_send()

    for hop in range(1, heads):
        for way, origin, comes, goes in arrivals(hop):

            @pl.when(comes)
            def _(way=way, origin=origin, goes=goes, hop=hop):
                here = place(section, origin)

                @pl.when(goes)
                def _():
                    line(way, hop, here).wait_send()

                pair(2 * hop - 1 + way, origin, here).wait_send()


def attention_kernel(layer, *refs):
    operands, (w_qkv_hbm, w_out_hbm, swap_in), refs = refs[:6], refs[6:9], refs[9:]
    results, swap_out, scratch, (load_sem, swap_sem) = refs[:9], refs[9], refs[10:16], refs[16:]
    section, head = lax.axis_index(SECTION), lax.axis_index(HEAD)
    heads = lax.axis_size(HEAD)
    loads = [
        pltpu.make_async_copy(w_qkv_hbm.at[layer], scratch[0], load_sem.at[0]),
        pltpu.make_async_copy(w_out_hbm.at[layer], scratch[1], load_sem.at[1]),
    ]
    for load in loads:
        load.start()

    def ready():
        barrier = pltpu.get_barrier_semaphore()
        partners = [{SECTION: 1 - section}]
        partners += [{HEAD: lax.rem(head + distance, heads)} for distance in range(1, heads)]
        for partner in partners:
            pl.semaphore_signal(barrier, 1, device_id=partner, device_id_type=MESH)
        pl.semaphore_wait(barrier, len(partners))

    swap = block_swap(swap_in, swap_out, swap_sem, head, 2)
    attention_body(layer, operands, results, scratch, loads, ready, met=swap.start)
    swap.wait()


def attention_shapes(tokens, width, kv_cols, heads, dtype):
    float32 = jnp.float32
    return (
        jax.ShapeDtypeStruct((tokens, width), dtype),
        jax.ShapeDtypeStruct((HEADS, tokens, HDIM), dtype),
        jax.ShapeDtypeStruct((2 * heads * tokens, kv_cols), dtype),
        jax.ShapeDtypeStruct((HEADS, tokens, 1), float32),
        jax.ShapeDtypeStruct((tokens, width), dtype),
        jax.ShapeDtypeStruct((tokens, width), float32),
        jax.ShapeDtypeStruct((tokens, width), dtype),
        jax.ShapeDtypeStruct((tokens, 1), float32),
        jax.ShapeDtypeStruct((tokens, 1), float32),
    )


def attention_scratch(tokens, width, qkv_cols, heads, dtype):
    dma = pltpu.SemaphoreType.DMA
    return [
        pltpu.VMEM((width, qkv_cols), dtype),
        pltpu.VMEM((width, width), dtype),
        pltpu.VMEM((tokens, qkv_cols - width), dtype),
        dma,
        dma((2, 2 * heads - 1)),
        dma((2, 2, heads)),
    ]


def attention_forward(layer, number, w_qkv, w_out, swap_in, *operands):
    heads = lax.axis_size(HEAD)
    tokens, width = operands[0].shape
    qkv_cols = w_qkv.shape[2]
    dtype = w_qkv.dtype
    vmem = pl.BlockSpec(memory_space=pltpu.VMEM)
    anywhere = pl.BlockSpec(memory_space=pl.ANY)
    return pl.pallas_call(
        functools.partial(attention_kernel, layer),
        out_shape=attention_shapes(tokens, width, qkv_cols - width, heads, dtype)
        + (jax.ShapeDtypeStruct(swap_in.shape, dtype),),
        in_specs=[vmem] * len(operands) + [anywhere] * 3,
        out_specs=(vmem,) * 9 + (anywhere,),
        scratch_shapes=attention_scratch(tokens, width, qkv_cols, heads, dtype)
        + [pltpu.SemaphoreType.DMA((2,)), pltpu.SemaphoreType.DMA((2,))],
        compiler_params=pltpu.CompilerParams(
            collective_id=number, has_side_effects=True, vmem_limit_bytes=60 * 2**20
        ),
        cost_estimate=pl.CostEstimate(
            flops=20 * tokens * width * qkv_cols,
            bytes_accessed=2 * w_out.size + 2 * w_qkv.size,
            transcendentals=0,
        ),
    )(*operands, w_qkv, w_out, swap_in)


def local_grouped(
    inputs,
    cotangent,
    norm_gains,
    qkv_weight,
    qkv_bias,
    out_weight,
    gate_weight,
    up_weight,
    down_weight,
):
    head_count = lax.axis_size(HEAD)
    wide_count = lax.axis_size(WIDE)
    section_count = lax.axis_size(SECTION)
    section = lax.axis_index(SECTION)
    head = lax.axis_index(HEAD)
    micro_count, short_len, width = inputs.shape
    half_len = short_len // section_count
    tokens = wide_count * half_len
    rows = qkv_weight.shape[1]
    query_width = HEADS * HDIM
    kv_width = KV * HDIM
    qkv_cols = qkv_weight.shape[2]
    ff_cols = gate_weight.shape[2]
    parts = section_count * head_count
    part_cols = -(-ff_cols // (parts * 128)) * 128

    def inner(array):
        split = array.shape[:-1] + (head_count, wide_count, rows)
        return jnp.swapaxes(array.reshape(split), -3, -2).reshape(array.shape)

    def outer(array):
        split = array.shape[:-1] + (wide_count, head_count, rows)
        return jnp.swapaxes(array.reshape(split), -3, -2).reshape(array.shape)

    sides = jnp.stack(
        [
            lax.dynamic_slice_in_dim(each, section * half_len, half_len, 1)
            for each in (inputs, cotangent)
        ]
    )
    mlp_parts, out_own, sides, small_own = cut_parts(
        gate_weight[0],
        up_weight[0],
        down_weight[0],
        out_weight[0],
        sides.reshape(-1, width),
        norm_gains[0],
        qkv_bias,
        parts,
        part_cols,
    )
    order = np.indices((section_count, head_count, wide_count, half_len)).reshape(4, -1)
    key_pos = (order[1] * wide_count + order[2]) * short_len + order[0] * half_len + order[3]
    half_dim = HDIM // 2
    angles = key_pos[:, None] * ROPE_BASE ** (-np.arange(half_dim) / half_dim)
    tables = np.concatenate([np.cos(angles)] * 2 + [np.sin(angles), -np.sin(angles)], 1)
    first_row = (section * head_count + head) * tokens
    own_table = lax.dynamic_slice_in_dim(jnp.asarray(tables, jnp.float32), first_row, tokens, 0)
    head_cosine, head_sine = own_table[:, :HDIM], own_table[:, HDIM:]
    key_pos = jnp.asarray(key_pos, jnp.int32)
    own_pos = lax.dynamic_slice_in_dim(key_pos, first_row, tokens, 0)
    tables = (head_cosine, -head_sine, own_pos[:, None], key_pos[None, :])

    (
        qkv_weights,
        out_weights,
        first_mlp,
        second_parts,
        tokens_in,
        last_grad,
        grad_near,
        grad_far,
        small,
        *first_attention,
    ) = start_weights(
        5,
        qkv_weight[0],
        out_own,
        mlp_parts.reshape(section_count, head_count, rows, 3 * part_cols),
        sides.reshape(2, micro_count, half_len, width),
        small_own,
        *tables,
    )
    second_mlp = lax.all_gather(second_parts, WIDE, axis=0).reshape(width, 3 * part_cols)
    mlp_weights = [first_mlp, second_mlp]

    layer_in = tokens_in.astype(jnp.float32)

    records = []
    outputs_list = []
    for layer in range(section_count):
        attention = first_attention
        if layer > 0:
            *attention, grad_mid = attention_forward(
                layer, 8, qkv_weights, out_weights, last_grad, layer_in, small, *tables
            )
        (
            normed,
            queries,
            keyval,
            log_total,
            attended,
            midway,
            normed2,
            scale_first,
            scale_second,
        ) = attention
        w_mlp = mlp_weights[layer]
        if layer == section_count - 1:
            grads = (last_grad, grad_near, grad_mid, grad_far)
            mlp_out, d_normed2, mlp_term = turning_point(normed2, w_mlp, grads, 1)
            gate_up = hidden = None
        else:
            mlp_out, normed2, gate_up, hidden = feed_forward(normed2, w_mlp, 9)
        result = midway + mlp_out
        records.append(
            (
                layer_in,
                scale_first,
                normed,
                queries,
                keyval,
                log_total,
                attended,
                midway,
                scale_second,
                normed2,
                gate_up,
                hidden,
            )
        )
        carried = result.astype(jnp.bfloat16)
        outputs_list.append(carried)
        layer_in = carried.astype(jnp.float32)

    out_grad = last_grad
    grads_list = [None] * section_count
    attention_terms = [None] * section_count
    small_terms = [None] * section_count
    for layer in reversed(range(section_count)):
        w_mlp = mlp_weights[layer]
        (
            layer_in,
            scale_first,
            normed,
            queries,
            keyval,
            log_total,
            attended,
            midway,
            scale_second,
            normed2,
            gate_up,
            hidden,
        ) = records[layer]
        if layer < section_count - 1:
            d_normed2, mlp_term = feed_backward(out_grad, w_mlp, gate_up, normed2, hidden, 3)
        mlp_term = mlp_term.reshape(wide_count, head_count, rows, -1)
        mlp_sum = lax.psum_scatter(mlp_term, WIDE, scatter_dimension=0)
        if layer == 1:
            second_sum = lax.optimization_barrier(mlp_sum)
        out_grad, small_terms[layer], attention_terms[layer], second_parts = attention_grad(
            layer,
            (4, 7)[layer],
            out_weights,
            qkv_weights,
            second_sum if layer == 0 else None,
            d_normed2,
            midway,
            scale_second,
            out_grad,
            small,
            queries,
            keyval,
            log_total,
            attended,
            normed,
            layer_in,
            scale_first,
            head_cosine,
            head_sine,
            *tables[2:],
        )
        grads_list[layer] = out_grad

    sides = jnp.stack([outer(each) for each in outputs_list + grads_list])
    totals, small_total, low_parts, high_parts, owned = finish_weights(
        *[term.reshape(wide_count * head_count, rows, -1) for term in attention_terms],
        jnp.stack(small_terms).reshape(section_count, -1, 128),
        mlp_sum,
        second_parts,
        sides.reshape(2 * section_count, wide_count, half_len, width),
        6,
    )
    small_total = small_total.reshape(-1)
    gate_grad, up_grad, down_grad, qkv_grad, out_weight_grad = join_parts(
        low_parts, high_parts, totals, ff_cols, qkv_cols
    )
    return (
        owned[:1],
        owned[1:],
        outer(small_total[: 2 * width].reshape(1, 2, width)),
        qkv_grad,
        small_total[2 * width :][None],
        out_weight_grad,
        gate_grad,
        up_grad,
        down_grad,
    )


def local(inputs, *rest):
    sizes = [lax.axis_size(axis) for axis in (SECTION, HEAD, WIDE)]
    if sizes == [2, 4, 4] and inputs.shape[0] == 4:
        return local_grouped(inputs, *rest)
    return local_streamed(inputs, *rest)


def solution(mesh):
    return jax.shard_map(
        local,
        mesh=mesh,
        in_specs=(
            P(None, (HEAD, WIDE), None),
            P(None, (HEAD, WIDE), None),
            P(SECTION, None, None),
            P(SECTION, (HEAD, WIDE), None),
            P(SECTION, None),
            P(SECTION, (HEAD, WIDE), None),
            P(SECTION, (HEAD, WIDE), None),
            P(SECTION, (HEAD, WIDE), None),
            P(SECTION, (HEAD, WIDE), None),
        ),
        out_specs=(
            P(SECTION, None, (HEAD, WIDE), None),
            P(SECTION, None, (HEAD, WIDE), None),
            P(SECTION, None, None),
            P(SECTION, (HEAD, WIDE), None),
            P(SECTION, None),
            P(SECTION, (HEAD, WIDE), None),
            P(SECTION, (HEAD, WIDE), None),
            P(SECTION, (HEAD, WIDE), None),
            P(SECTION, (HEAD, WIDE), None),
        ),
        check_vma=False,
    )
```

```python
import functools
from typing import NamedTuple

import jax
import jax.numpy as jnp
import numpy as np
from jax import lax
from jax.experimental import pallas as pl
from jax.experimental.pallas import tpu as pltpu
from jax.sharding import PartitionSpec as P

HEADS = 12
KV = 2
HDIM = 128


EPSILON = 1e-06
MESH = pl.DeviceIdType.MESH
CUTS = 2
SECTION = "section"
HEAD = "head"
WIDE = "wide"
ROPE_BASE = 1000000.0


class Record(NamedTuple):
    layer_in: jax.Array
    scale_first: jax.Array
    normed: jax.Array
    query_rows: jax.Array
    kv_local: jax.Array
    log_total: jax.Array
    out_seq: jax.Array
    midway: jax.Array
    scale_second: jax.Array
    normed2: jax.Array
    gate_out: jax.Array
    up_out: jax.Array
    hidden: jax.Array


def passed_along(block, axis, distance):
    devices = range(lax.axis_size(axis))
    route = [(i - distance, i) for i in devices if i - distance in devices]
    return lax.ppermute(block, axis, route)


def rotary_tables(positions, head_dim):
    half_dim = head_dim // 2
    frequency = ROPE_BASE ** (-jnp.arange(half_dim, dtype=jnp.float32) / half_dim)
    angles = positions[:, None] * frequency[None, :]
    return (jnp.cos(angles)[:, None, :], jnp.sin(angles)[:, None, :])


def rotate_pairs(tensor, cosine, sine_table):
    half_dim = tensor.shape[-1] // 2
    first_half = tensor[..., :half_dim]
    second_half = tensor[..., half_dim:]
    return jnp.concatenate(
        [
            first_half * cosine - second_half * sine_table,
            second_half * cosine + first_half * sine_table,
        ],
        -1,
    )


def rotate_back(tensor, cosine, sine_table):
    half_dim = tensor.shape[-1] // 2
    first_half = tensor[..., :half_dim]
    second_half = tensor[..., half_dim:]
    return jnp.concatenate(
        [
            first_half * cosine + second_half * sine_table,
            second_half * cosine - first_half * sine_table,
        ],
        -1,
    )


def contract_last(left, right):
    return lax.dot_general(
        left, right, (((1,), (1,)), ((), ())), preferred_element_type=jnp.float32
    )


def contract_first(left, right):
    return lax.dot_general(
        left, right, (((0,), (0,)), ((), ())), preferred_element_type=jnp.float32
    )


def attention_scores(query_rows, key_value, query_pos, key_pos):
    head_dim = query_rows.shape[1]
    scores = contract_last(query_rows, key_value[:, :head_dim]) * head_dim ** (-0.5)
    return jnp.where(query_pos[:, None] >= key_pos[None, :], scores, -1e30)


def attend_forward(query_rows, key_value, query_pos, key_pos):
    head_dim = query_rows.shape[1]
    scores = attention_scores(query_rows, key_value, query_pos, key_pos)
    highest = jnp.max(scores, -1, keepdims=True)
    weights_exp = jnp.exp(scores - highest)
    partition = jnp.sum(weights_exp, -1, keepdims=True)
    probs_low = (weights_exp / partition).astype(jnp.bfloat16)
    attended = jnp.dot(probs_low, key_value[:, head_dim:], preferred_element_type=jnp.float32)
    return (attended.astype(jnp.bfloat16), highest + jnp.log(partition))


def attend_backward(query_rows, key_value, query_pos, key_pos, log_total, grad_rows):
    head_dim = query_rows.shape[1]
    scaling = head_dim ** (-0.5)
    scores = attention_scores(query_rows, key_value, query_pos, key_pos)
    probs_full = jnp.exp(scores - log_total)
    grad_probs = contract_last(grad_rows, key_value[:, head_dim:])
    row_dot = jnp.sum(probs_full * grad_probs, -1, keepdims=True)
    grad_scores = (probs_full * (grad_probs - row_dot)).astype(jnp.bfloat16)
    grad_query = (
        jnp.dot(grad_scores, key_value[:, :head_dim], preferred_element_type=jnp.float32) * scaling
    )
    grad_key = contract_first(grad_scores, query_rows) * scaling
    grad_value = contract_first(probs_full.astype(jnp.bfloat16), grad_rows)
    return (grad_query, jnp.concatenate([grad_key, grad_value], 1))


def make_terms(operands, factor):
    (
        normed_all,
        dqkv_all,
        attended_all,
        gattn_all,
        normed2_all,
        dgate_all,
        dup_all,
        gmlp_all,
        hidden_all,
    ) = operands
    pairs = [
        (normed_all, dqkv_all),
        (attended_all, gattn_all),
        (normed2_all, dgate_all),
        (normed2_all, dup_all),
        (gmlp_all, hidden_all),
    ]
    scaled_pairs = [
        (left, (right.astype(jnp.float32) * factor).astype(jnp.bfloat16)) for left, right in pairs
    ]

    def weight_terms(start, count):
        pieces = [contract_first(left, right) for left, right in scaled_pairs]
        return jnp.concatenate(pieces, 1)

    return weight_terms


def local_streamed(
    inputs,
    cotangent,
    norm_gains,
    qkv_weight,
    qkv_bias,
    out_weight,
    gate_weight,
    up_weight,
    down_weight,
):
    head_count = lax.axis_size(HEAD)
    wide_count = lax.axis_size(WIDE)
    section_pos = lax.axis_index(SECTION)
    head_pos = lax.axis_index(HEAD)
    wide_pos = lax.axis_index(WIDE)
    micro_count, short_len, width = inputs.shape
    group_size = HEADS // head_count
    slot_rep = head_count // KV
    query_width = HEADS * HDIM
    kv_width = KV * HDIM
    local_rows = head_count * short_len
    seq_len = local_rows * wide_count
    gain_first = norm_gains[0, 0]
    gain_second = norm_gains[0, 1]
    bias_row = qkv_bias[0]
    seq_pos = (
        (head_pos * wide_count + wide_pos) * short_len + jnp.arange(short_len, dtype=jnp.int32)
    ).astype(jnp.float32)
    cosine, sine_table = rotary_tables(seq_pos, HDIM)
    local_index = jnp.arange(local_rows, dtype=jnp.int32)
    query_pos = jnp.tile(
        (local_index // short_len * wide_count + wide_pos) * short_len + local_index % short_len,
        group_size,
    )
    key_index = jnp.arange(seq_len, dtype=jnp.int32)
    key_pos = (
        key_index % local_rows // short_len * wide_count + key_index // local_rows
    ) * short_len + key_index % short_len

    def to_rows(packed):
        return (
            packed.reshape(local_rows, group_size, HDIM)
            .transpose(1, 0, 2)
            .reshape(group_size * local_rows, HDIM)
        )

    def from_rows(rows_in):
        return (
            rows_in.reshape(group_size, local_rows, HDIM)
            .transpose(1, 0, 2)
            .reshape(local_rows, 1, group_size * HDIM)
        )

    weights_fwd = (
        lax.all_gather(qkv_weight[0], (HEAD, WIDE), axis=0, tiled=True),
        lax.all_gather(out_weight[0], (HEAD, WIDE), axis=0, tiled=True),
        lax.all_gather(gate_weight[0], (HEAD, WIDE), axis=0, tiled=True),
        lax.all_gather(up_weight[0], (HEAD, WIDE), axis=0, tiled=True),
        lax.all_gather(down_weight[0], (HEAD, WIDE), axis=0, tiled=True),
    )
    incoming = jnp.zeros((short_len, width), jnp.bfloat16)
    records = []
    outputs_list = []
    for step_index in range(micro_count + 1):
        own_input = inputs[min(step_index, micro_count - 1)]
        layer_in = jnp.where(section_pos == 0, own_input, incoming).astype(jnp.float32)
        layer_w_qkv, layer_w_out, layer_w_gate, layer_w_up, layer_w_down = weights_fwd
        scale_first = lax.rsqrt(jnp.mean(layer_in * layer_in, -1, keepdims=True) + EPSILON)
        normed = (layer_in * scale_first * gain_first).astype(jnp.bfloat16)
        qkv = jnp.dot(normed, layer_w_qkv, preferred_element_type=jnp.float32) + bias_row
        queries = rotate_pairs(
            qkv[:, :query_width].reshape(short_len, HEADS, HDIM), cosine, sine_table
        ).astype(jnp.bfloat16)
        key_heads = rotate_pairs(
            qkv[:, query_width : query_width + kv_width].reshape(short_len, KV, HDIM),
            cosine,
            sine_table,
        ).astype(jnp.bfloat16)
        value_heads = (
            qkv[:, query_width + kv_width :].reshape(short_len, KV, HDIM).astype(jnp.bfloat16)
        )
        kv_pack = jnp.repeat(jnp.stack([key_heads, value_heads], 2), slot_rep, axis=1).reshape(
            short_len, head_count, 2 * HDIM
        )
        q_pack = queries.reshape(short_len, head_count, group_size * HDIM)
        q_heads = lax.all_to_all(q_pack, HEAD, split_axis=1, concat_axis=0, tiled=True)
        kv_heads = lax.all_to_all(kv_pack, HEAD, split_axis=1, concat_axis=0, tiled=True)
        query_rows = to_rows(q_heads)
        kv_local = kv_heads.reshape(local_rows, 2 * HDIM)
        layer_kv_all = lax.all_gather(kv_local, WIDE, axis=0, tiled=True)
        out_rows, log_total = attend_forward(query_rows, layer_kv_all, query_pos, key_pos)
        out_seq = lax.all_to_all(
            from_rows(out_rows), HEAD, split_axis=0, concat_axis=1, tiled=True
        ).reshape(short_len, query_width)
        midway = layer_in + jnp.dot(out_seq, layer_w_out, preferred_element_type=jnp.float32)
        scale_second = lax.rsqrt(jnp.mean(midway * midway, -1, keepdims=True) + EPSILON)
        normed2 = (midway * scale_second * gain_second).astype(jnp.bfloat16)
        layer_gate_out = jnp.dot(normed2, layer_w_gate, preferred_element_type=jnp.float32)
        up_out = jnp.dot(normed2, layer_w_up, preferred_element_type=jnp.float32)
        hidden = (jax.nn.silu(layer_gate_out) * up_out).astype(jnp.bfloat16)
        result = midway + contract_last(hidden, layer_w_down)
        record = Record(
            layer_in=layer_in,
            scale_first=scale_first,
            normed=normed,
            query_rows=query_rows,
            kv_local=kv_local,
            log_total=log_total,
            out_seq=out_seq,
            midway=midway,
            scale_second=scale_second,
            normed2=normed2,
            gate_out=layer_gate_out,
            up_out=up_out,
            hidden=hidden,
        )
        result, record = (result, record)
        sent_value = result.astype(jnp.bfloat16)
        records.append(record)
        outputs_list.append(sent_value)
        if step_index < micro_count:
            incoming = passed_along(sent_value, SECTION, 1)
    stacked_records = jax.tree.map(lambda *arrays: jnp.stack(arrays), *records)
    section_outputs = lax.dynamic_slice_in_dim(
        jnp.stack(outputs_list), section_pos, micro_count, 0
    )[None]
    weights_back = (
        lax.all_gather(qkv_weight[0], (HEAD, WIDE), axis=0, tiled=True),
        lax.all_gather(out_weight[0], (HEAD, WIDE), axis=0, tiled=True),
        lax.all_gather(gate_weight[0], (HEAD, WIDE), axis=0, tiled=True),
        lax.all_gather(up_weight[0], (HEAD, WIDE), axis=0, tiled=True),
        lax.all_gather(down_weight[0], (HEAD, WIDE), axis=0, tiled=True),
    )
    owned_rows = qkv_weight.shape[1]
    qkv_cols = qkv_weight.shape[2]
    ff_cols = gate_weight.shape[2]
    incoming_grad = jnp.zeros((short_len, width), jnp.bfloat16)
    small_totals = (
        jnp.zeros((width,), jnp.float32),
        jnp.zeros((width,), jnp.float32),
        jnp.zeros((bias_row.shape[0],), jnp.float32),
    )
    grads_list = []
    kept_list = []
    for step_index in range(micro_count + 1):
        pick = jnp.clip(step_index - 1 + 2 * section_pos, 0, micro_count)
        record = jax.tree.map(
            lambda array: lax.dynamic_index_in_dim(array, pick, 0, keepdims=False), stacked_records
        )
        own_grad = cotangent[min(step_index, micro_count - 1)]
        out_grad = jnp.where(section_pos == 1, own_grad, incoming_grad).astype(jnp.float32)
        w_qkv, w_out, w_gate, w_up, w_down = weights_back
        g_mlp = out_grad.astype(jnp.bfloat16)
        d_hidden = jnp.dot(g_mlp, w_down, preferred_element_type=jnp.float32)
        gate_out = record.gate_out
        sigmoid_gate = jax.nn.sigmoid(gate_out)
        d_gate = (
            d_hidden * record.up_out * sigmoid_gate * (1.0 + gate_out * (1.0 - sigmoid_gate))
        ).astype(jnp.bfloat16)
        d_up = (d_hidden * gate_out * sigmoid_gate).astype(jnp.bfloat16)
        d_normed2 = contract_last(d_gate, w_gate) + contract_last(d_up, w_up)
        unit_second = record.midway * record.scale_second
        gain2_grad = jnp.sum(d_normed2 * unit_second, 0)
        dn_second = d_normed2 * gain_second
        d_midway = (
            record.scale_second
            * (dn_second - unit_second * jnp.mean(dn_second * unit_second, -1, keepdims=True))
            + out_grad
        )
        g_attn = d_midway.astype(jnp.bfloat16)
        d_out_seq = contract_last(g_attn, w_out).astype(jnp.bfloat16)
        d_out_heads = lax.all_to_all(
            d_out_seq.reshape(short_len, head_count, group_size * HDIM),
            HEAD,
            split_axis=1,
            concat_axis=0,
            tiled=True,
        )
        kv_all = lax.all_gather(record.kv_local, WIDE, axis=0, tiled=True)
        grad_query, grad_keyval = attend_backward(
            record.query_rows,
            kv_all,
            query_pos,
            key_pos,
            record.log_total,
            to_rows(d_out_heads),
        )
        keyval_local = lax.psum_scatter(
            grad_keyval.astype(jnp.bfloat16), WIDE, scatter_dimension=0, tiled=True
        )
        q_back = lax.all_to_all(
            from_rows(grad_query.astype(jnp.bfloat16)),
            HEAD,
            split_axis=0,
            concat_axis=1,
            tiled=True,
        )
        kv_back = lax.all_to_all(
            keyval_local.reshape(local_rows, 1, 2 * HDIM),
            HEAD,
            split_axis=0,
            concat_axis=1,
            tiled=True,
        )
        d_queries = rotate_back(
            q_back.astype(jnp.float32).reshape(short_len, HEADS, HDIM), cosine, sine_table
        )
        d_kv = jnp.sum(kv_back.astype(jnp.float32).reshape(short_len, KV, slot_rep, 2, HDIM), 2)
        d_keys = rotate_back(d_kv[:, :, 0], cosine, sine_table)
        d_qkv = jnp.concatenate(
            [
                d_queries.reshape(short_len, query_width),
                d_keys.reshape(short_len, kv_width),
                d_kv[:, :, 1].reshape(short_len, kv_width),
            ],
            1,
        ).astype(jnp.bfloat16)
        bias_grad = jnp.sum(d_qkv.astype(jnp.float32), 0)
        d_normed = contract_last(d_qkv, w_qkv)
        unit_first = record.layer_in * record.scale_first
        gain1_grad = jnp.sum(d_normed * unit_first, 0)
        dn_first = d_normed * gain_first
        d_layer_in = (
            record.scale_first
            * (dn_first - unit_first * jnp.mean(dn_first * unit_first, -1, keepdims=True))
            + d_midway
        )
        kept_grads = (
            record.normed,
            d_qkv,
            record.out_seq,
            g_attn,
            record.normed2,
            d_gate,
            d_up,
            g_mlp,
            record.hidden,
        )
        d_layer_in, kept_grads, small_parts = (
            d_layer_in,
            kept_grads,
            (gain1_grad, gain2_grad, bias_grad),
        )
        is_valid = jnp.where(
            (step_index - 1 + section_pos >= 0) & (step_index - 1 + section_pos < micro_count),
            1.0,
            0.0,
        )
        small_totals = jax.tree.map(
            lambda total_part, new_part: total_part + is_valid * new_part, small_totals, small_parts
        )
        sent_grad = d_layer_in.astype(jnp.bfloat16)
        grads_list.append(sent_grad)
        kept_list.append(kept_grads)
        if step_index < micro_count:
            incoming_grad = passed_along(sent_grad, SECTION, -1)
    input_grads = lax.dynamic_slice_in_dim(jnp.stack(grads_list), 1 - section_pos, micro_count, 0)[
        None
    ]
    operands = jax.tree.map(
        lambda *arrays: lax.dynamic_slice_in_dim(
            jnp.stack(arrays), 1 - section_pos, micro_count, 0
        ).reshape(micro_count * short_len, arrays[0].shape[1]),
        *kept_list
    )
    terms = lax.psum_scatter(
        make_terms(operands, 1.0)(jnp.int32(0), owned_rows * lax.axis_size((HEAD, WIDE))),
        (HEAD, WIDE),
        scatter_dimension=0,
        tiled=True,
    )
    qkv_grad = terms[:, :qkv_cols]
    out_grad_rows = terms[:, qkv_cols : qkv_cols + width]
    gate_grad = terms[:, qkv_cols + width : qkv_cols + width + ff_cols]
    up_grad = terms[:, qkv_cols + width + ff_cols : qkv_cols + width + 2 * ff_cols]
    down_grad = terms[:, qkv_cols + width + 2 * ff_cols :]
    gain1_total, gain2_total, bias_total = lax.psum(
        (small_totals[0], small_totals[1], small_totals[2]), (HEAD, WIDE)
    )
    gains_grad = jnp.stack([gain1_total, gain2_total])[None]
    return (
        section_outputs,
        input_grads,
        gains_grad,
        qkv_grad[None],
        bias_total[None],
        out_grad_rows[None],
        gate_grad[None],
        up_grad[None],
        down_grad[None],
    )


def greet_all(heads):
    section, head, wide = (lax.axis_index(axis) for axis in (SECTION, HEAD, WIDE))
    barrier = pltpu.get_barrier_semaphore()
    partners = [{SECTION: 1 - section}] + [{WIDE: beside(wide, axis)} for axis in (0, 1, 2)]
    partners += [{HEAD: lax.rem(head + shift, heads)} for shift in range(1, heads)]
    for partner in partners:
        pl.semaphore_signal(barrier, 1, device_id=partner, device_id_type=MESH)
    pl.semaphore_wait(barrier, len(partners))


def beside(wide, axis):
    low, high = lax.rem(wide, 2), lax.div(wide, 2)
    if axis == 0:
        return high * 2 + (1 - low)
    if axis == 1:
        return (1 - high) * 2 + low
    return (1 - high) * 2 + (1 - low)


def start_kernel(
    qkv_own,
    out_own,
    parts,
    sides,
    small_own,
    cosine,
    sine,
    own_pos,
    key_pos,
    qkv_all,
    out_all,
    first_all,
    second_parts,
    tokens_in,
    grad_in,
    grad_near,
    grad_far,
    small_all,
    *refs,
):
    results, refs = refs[:9], refs[9:]
    scratch, refs = refs[:6], refs[6:]
    (
        block,
        layer_in,
        given_first,
        given_second,
        small_sem,
        local_sem,
        swap_sem,
        shift_sem,
        line_sem,
        wide_sem,
        half_sem,
        pair_sem,
        token_sem,
        near_sem,
    ) = refs
    section, head, wide = (lax.axis_index(axis) for axis in (SECTION, HEAD, WIDE))
    heads, wides = lax.axis_size(HEAD), lax.axis_size(WIDE)
    rows = qkv_own.shape[0]
    half = rows // 2
    owns = (qkv_own, out_own)
    here = [beside(wide, 0), beside(wide, 1), beside(wide, 2)]

    def place(which, layer, head_at, wide_at, start=0, count=None):
        block = head_at * wides + wide_at if which == 1 else wide_at * heads + head_at
        first = pl.multiple_of(block * rows + start, 16)
        span = pl.ds(first, rows if count is None else count)
        return first_all.at[span] if which == 2 else (qkv_all, out_all)[which].at[layer, span]

    def remote(source, target, sems, at, partner):
        return pltpu.make_async_remote_copy(
            source,
            target,
            sems.at[(0,) + at],
            sems.at[(1,) + at],
            device_id=partner,
            device_id_type=MESH,
        )

    other = {SECTION: 1 - section}

    def line(which, way, hop):
        step = 1 if way == 0 else -1
        target = place(which, section, head - step * hop, wide)
        source = owns[which] if hop == 0 else target
        return remote(source, target, line_sem, (which, way, hop), {HEAD: head + step})

    def across(which, axis, number, origin):
        target = place(which, section, origin, wide)
        source = owns[which] if number == 0 and which < 2 else target
        return remote(source, target, wide_sem, (which, axis, number), {WIDE: here[axis]})

    def across_in(which, axis, number, origin):
        target = place(which, section, origin, here[axis])
        return remote(target, target, wide_sem, (which, axis, number), {WIDE: here[axis]})

    def diagonal(which, axis, number, origin):
        target = place(which, section, origin, here[1 - axis], (1 - axis) * half, half)
        return remote(target, target, half_sem, (which, axis, number), {WIDE: here[axis]})

    def diagonal_in(which, axis, number, origin):
        target = place(which, section, origin, here[2], (1 - axis) * half, half)
        return remote(target, target, half_sem, (which, axis, number), {WIDE: here[axis]})

    def pair(which, kind, number, origin, layer):
        if kind == 0:
            target = place(which, layer, origin, wide)
        elif kind in (1, 2):
            target = place(which, layer, origin, here[kind - 1])
        else:
            target = place(which, layer, origin, here[2], (4 - kind) * half, half)
        return remote(target, target, pair_sem, (which, kind, number), other)

    def pair_own(which):
        target = place(which, section, head, wide)
        return remote(owns[which], target, pair_sem, (which, 0, 0), other)

    def swap(target):
        return remote(parts.at[1 - section], target, swap_sem, (), other)

    def shift(layer, source, distance):
        target_head = lax.rem(head + distance, heads)
        target = place(2, 0, head, wide) if layer == 0 else second_parts.at[head]
        return remote(
            source.at[target_head], target, shift_sem, (layer, distance), {HEAD: target_head}
        )

    def shift_in(layer, distance):
        origin = lax.rem(head + heads - distance, heads)
        target = place(2, 0, origin, wide) if layer == 0 else second_parts.at[origin]
        return remote(target, target, shift_sem, (layer, distance), {HEAD: head})

    def shift_all(layer, source):
        for here_at in range(heads):

            @pl.when(head == here_at)
            def _(here_at=here_at):
                others = [at for at in range(heads) if at != here_at]
                for at in sorted(others, key=lambda at: abs(at - here_at)):
                    shift(layer, source, (at - here_at) % heads).start()

        target = place(2, 0, head, wide) if layer == 0 else second_parts.at[head]
        pltpu.make_async_copy(source.at[head], target, local_sem.at[2 + layer]).start()

    def shift_own(layer):
        target = place(2, 0, head, wide) if layer == 0 else second_parts.at[head]
        return pltpu.make_async_copy(target, target, local_sem.at[2 + layer])

    shares = (tokens_in, grad_in)
    share_rows = sides.shape[2]
    tokens = grad_in.shape[0]

    def share(which, wide_at):
        return shares[which].at[pl.ds(pl.multiple_of(wide_at * share_rows, 16), share_rows)]

    def token(which, axis):
        source = sides.at[which, here[axis]]
        return remote(source, share(which, wide), token_sem, (which, axis), {WIDE: here[axis]})

    def token_in(which, axis):
        target = share(which, here[axis])
        return remote(target, target, token_sem, (which, axis), {WIDE: here[axis]})

    def token_own(which):
        return pltpu.make_async_copy(
            sides.at[which, wide], share(which, wide), local_sem.at[4 + which]
        )

    def swaps():
        yield block_swap(grad_in, grad_near, near_sem.at[0], head, 1)
        yield block_swap(grad_in, grad_far, near_sem.at[1], head, 3)

    greet_all(heads)
    first = section == 0
    second = section == 1

    for which in (0, 1):
        for way, go in ((0, head < heads - 1), (1, head > 0)):

            @pl.when(go)
            def _(which=which, way=way):
                line(which, way, 0).start()

    for which in (0, 1):
        for axis in (0, 1, 2):
            token(which, axis).start()
        token_own(which).start()

    small_all[section] = small_own[...]
    small_give = remote(small_own, small_all.at[section], small_sem, (), other)
    small_give.start()

    @pl.when(first)
    def _():
        swap(given_first).start()

    @pl.when(second)
    def _():
        swap(given_second).start()

    locals_ = [
        pltpu.make_async_copy(owns[which], place(which, section, head, wide), local_sem.at[which])
        for which in (0, 1)
    ]
    for which in (0, 1):
        locals_[which].start()
        for axis in (0, 1):
            across(which, axis, 0, head).start()
        pair_own(which).start()

    def each(hop):
        yield 2 * hop - 1, 0, head - hop, head >= hop, head < heads - 1
        yield 2 * hop, 1, head + hop, head + hop < heads, head > 0

    def forward_halves(number, origin):
        for which in (0, 1):
            for axis in (0, 1):
                across_in(which, axis, number, origin).wait_recv()
                diagonal(which, 1 - axis, number, origin).start()
                pair(which, 1 + axis, number, origin, section).start()

    def finish_halves(number, origin):
        for which in (0, 1):
            for axis in (0, 1):
                diagonal_in(which, axis, number, origin).wait_recv()
                pair(which, 3 + axis, number, origin, section).start()

    for hop in range(1, heads):
        for number, way, origin, comes, goes in each(hop):

            @pl.when(comes)
            def _(number=number, way=way, origin=origin, goes=goes, hop=hop):
                for which in (0, 1):
                    arrived = place(which, section, origin, wide)
                    remote(
                        arrived, arrived, line_sem, (which, way, hop - 1), {HEAD: head}
                    ).wait_recv()

                    @pl.when(goes)
                    def _(which=which):
                        line(which, way, hop).start()

                    for axis in (0, 1):
                        across(which, axis, number, origin).start()
                    pair(which, 0, number, origin, section).start()

        if hop == 1:
            forward_halves(0, head)
        else:
            for number, way, origin, comes, goes in each(hop - 1):

                @pl.when(comes)
                def _(number=number, origin=origin):
                    forward_halves(number, origin)

    @pl.when(first)
    def _():
        swap(given_second).wait_recv()
        shift_all(0, parts.at[0])

    @pl.when(second)
    def _():
        swap(given_first).wait_recv()
        shift_all(0, given_first)

    for number, way, origin, comes, goes in each(heads - 1):

        @pl.when(comes)
        def _(number=number, origin=origin):
            forward_halves(number, origin)

    def spread(number):
        for axis in (0, 1):
            across(2, axis, number, lax.rem(head + heads - number, heads)).start()

    shift_own(0).wait()
    spread(0)
    finish_halves(0, head)
    for hop in range(1, heads):
        for number, way, origin, comes, goes in each(hop):

            @pl.when(comes)
            def _(number=number, origin=origin):
                finish_halves(number, origin)

    for distance in range(1, heads):
        shift_in(0, distance).wait_recv()
        spread(distance)

    for which in (0, 1):
        token_own(which).wait()
        for axis in (0, 1, 2):
            token_in(which, axis).wait_recv()
            token(which, axis).wait_send()

    def forward_part(number):
        origin = lax.rem(head + heads - number, heads)
        for axis in (0, 1):
            across_in(2, axis, number, origin).wait_recv()
            diagonal(2, 1 - axis, number, origin).start()

    def received(number, origin):
        for which in (0, 1):
            for kind in range(5):
                pair(which, kind, number, origin, 1 - section).wait_recv()

    def all_received():
        received(0, head)
        for hop in range(1, heads):
            for number, way, origin, comes, goes in each(hop):

                @pl.when(comes)
                def _(number=number, origin=origin):
                    received(number, origin)

    pl.when(second)(all_received)
    for which in (0, 1):
        locals_[which].wait()
    loads = [
        pltpu.make_async_copy(qkv_all.at[0], scratch[0], local_sem.at[7]),
        pltpu.make_async_copy(out_all.at[0], scratch[1], local_sem.at[8]),
    ]
    fetch = pltpu.make_async_copy(tokens_in, block, local_sem.at[9])
    for load in loads:
        load.start()
    fetch.start()
    fetch.wait()
    layer_in[...] = block[...].astype(jnp.float32)
    small_give.wait_send()
    small_theirs = small_all.at[1 - section]
    remote(small_theirs, small_theirs, small_sem, (), other).wait_recv()
    operands = (layer_in, small_all, cosine, sine, own_pos, key_pos)

    def met():
        @pl.when(first)
        def _():
            shift_all(1, given_second)

        @pl.when(second)
        def _():
            shift_all(1, parts.at[1])

        for swap_block in swaps():
            swap_block.start()
        forward_part(1)

    attention_body(
        0, operands, results, scratch, loads, lambda: None, lambda: forward_part(0), met
    )
    for number in range(2, heads):
        forward_part(number)

    for number in range(heads):
        origin = lax.rem(head + heads - number, heads)
        for axis in (0, 1):
            diagonal_in(2, axis, number, origin).wait_recv()
            diagonal(2, axis, number, origin).wait_send()
            across(2, axis, number, origin).wait_send()

    def settle(number, origin):
        for which in (0, 1):
            for axis in (0, 1):
                across(which, axis, number, origin).wait_send()
                diagonal(which, axis, number, origin).wait_send()
            for kind in range(5):
                if kind == 0 and number == 0:
                    pair_own(which).wait_send()
                else:
                    pair(which, kind, number, origin, section).wait_send()

    for which in (0, 1):
        for way, go in ((0, head < heads - 1), (1, head > 0)):

            @pl.when(go)
            def _(which=which, way=way):
                line(which, way, 0).wait_send()

    for swap_block in swaps():
        swap_block.wait()
    settle(0, head)
    for hop in range(1, heads):
        for number, way, origin, comes, goes in each(hop):

            @pl.when(comes)
            def _(number=number, way=way, origin=origin, goes=goes, hop=hop):
                settle(number, origin)

                @pl.when(goes)
                def _():
                    for which in (0, 1):
                        line(which, way, hop).wait_send()

    pl.when(first)(all_received)
    swap(given_first).wait_send()
    shift_own(1).wait()
    for distance in range(1, heads):
        for layer in (0, 1):
            shift(layer, given_first, distance).wait_send()
        shift_in(1, distance).wait_recv()


def start_weights(number, qkv_own, out_own, parts, sides, small_own, *tables):
    heads, wides = lax.axis_size(HEAD), lax.axis_size(WIDE)
    rows, qkv_cols = qkv_own.shape
    out_cols = out_own.shape[1]
    numbers = 2 * heads - 1
    tokens = sides.shape[1] * sides.shape[2]
    whole = heads * wides * rows
    dtype = parts.dtype
    dma = pltpu.SemaphoreType.DMA
    anywhere = pl.BlockSpec(memory_space=pl.ANY)
    vmem = pl.BlockSpec(memory_space=pltpu.VMEM)
    return pl.pallas_call(
        start_kernel,
        out_shape=(
            jax.ShapeDtypeStruct((2, whole, qkv_cols), dtype),
            jax.ShapeDtypeStruct((2, whole, out_cols), dtype),
            jax.ShapeDtypeStruct((whole, parts.shape[3]), dtype),
            jax.ShapeDtypeStruct(parts.shape[1:], dtype),
            jax.ShapeDtypeStruct((tokens, out_cols), dtype),
            jax.ShapeDtypeStruct((tokens, out_cols), dtype),
            jax.ShapeDtypeStruct((tokens, out_cols), dtype),
            jax.ShapeDtypeStruct((tokens, out_cols), dtype),
            jax.ShapeDtypeStruct((2,) + small_own.shape, jnp.float32),
        )
        + attention_shapes(tokens, out_cols, qkv_cols - out_cols, heads, dtype),
        in_specs=[anywhere] * 4 + [vmem] * 5,
        out_specs=(anywhere,) * 8 + (vmem,) * 10,
        scratch_shapes=attention_scratch(tokens, out_cols, qkv_cols, heads, dtype)
        + [
            pltpu.VMEM((tokens, out_cols), dtype),
            pltpu.VMEM((tokens, out_cols), jnp.float32),
            pltpu.VMEM(parts.shape[1:], dtype),
            pltpu.VMEM(parts.shape[1:], dtype),
            dma((2,)),
            dma((10,)),
            dma((2,)),
            dma((2, 2, heads)),
            dma((2, 2, 2, heads)),
            dma((2, 3, 2, numbers)),
            dma((2, 3, 2, numbers)),
            dma((2, 2, 5, numbers)),
            dma((2, 2, 3)),
            dma((2, 2)),
        ],
        compiler_params=pltpu.CompilerParams(
            collective_id=number, has_side_effects=True, vmem_limit_bytes=60 * 2**20
        ),
    )(qkv_own, out_own, parts, sides, small_own, *tables)


def finish_kernel(
    first_terms,
    second_terms,
    small,
    first_parts,
    second_parts,
    tokens_in,
    totals,
    small_total,
    low_parts,
    high_parts,
    tokens_out,
    near_buf,
    middle,
    far_buf,
    sums,
    line_buf,
    small_sum,
    small_buf,
    shifted,
    give,
    local_sem,
    shift_sem,
    swap_sem,
    near_sem,
    far_sem,
    line_sem,
    small_sem,
    give_sem,
    token_sem,
):
    section, head, wide = (lax.axis_index(axis) for axis in (SECTION, HEAD, WIDE))
    heads, wides = lax.axis_size(HEAD), lax.axis_size(WIDE)
    here = [beside(wide, 0), beside(wide, 1), beside(wide, 2)]
    rows, columns = first_terms.shape[1:]
    lots = heads * CUTS
    terms = (first_terms, second_terms)
    other = {SECTION: 1 - section}
    first, second = section == 0, section == 1
    sender_rows = tokens_in.shape[2]

    def remote(source, target, sems, at, partner):
        return pltpu.make_async_remote_copy(
            source,
            target,
            sems.at[(0,) + at],
            sems.at[(1,) + at],
            device_id=partner,
            device_id_type=MESH,
        )

    def shift(distance, target):
        target_head = lax.rem(head + distance, heads)
        return remote(
            first_parts.at[target_head],
            target.at[head],
            shift_sem,
            (distance,),
            {HEAD: target_head},
        )

    def shift_in(distance, target):
        arrived = target.at[lax.rem(head + heads - distance, heads)]
        return remote(arrived, arrived, shift_sem, (distance,), {HEAD: head})

    def near(side, turn, target):
        wide_at = here[side] if turn == 0 else here[2]
        return remote(
            terms[side].at[wide_at * lots + target],
            near_buf.at[side, turn, target],
            near_sem,
            (side, turn, target),
            {WIDE: here[side]},
        )

    def far(side, target):
        return remote(
            middle.at[side, target],
            far_buf.at[side, target],
            far_sem,
            (side, target),
            {WIDE: here[1 - side]},
        )

    def line(way, target, side):
        step = 1 if way == 0 else -1
        return remote(
            sums.at[target, side],
            line_buf.at[way, target, side],
            line_sem,
            (way, target, side),
            {HEAD: head + step},
        )

    def token_target(layer, which, sender_wide, sender_section):
        first_row = pl.multiple_of(sender_section * sender_rows, 16)
        return tokens_out.at[which, sender_wide, pl.ds(first_row, sender_rows)]

    def token(layer, which, turn):
        wide_at = wide if turn == 3 else here[turn]
        sems = (token_sem.at[0, layer, which, turn], token_sem.at[1, section, which, turn])
        return pltpu.make_async_remote_copy(
            tokens_in.at[which * 2 + layer, wide_at],
            token_target(layer, which, wide, section),
            *sems,
            device_id={SECTION: layer, WIDE: wide_at},
            device_id_type=MESH,
        )

    def token_in(from_section, which, turn):
        wide_at = wide if turn == 3 else here[turn]
        target = token_target(section, which, wide_at, from_section)
        sems = (token_sem.at[0, section, which, turn], token_sem.at[1, from_section, which, turn])
        return pltpu.make_async_remote_copy(
            target, target, *sems, device_id={HEAD: head}, device_id_type=MESH
        )

    barrier = pltpu.get_barrier_semaphore()
    partners = [other] + [{WIDE: wide_at} for wide_at in here]
    partners += [{SECTION: 1 - section, WIDE: wide_at} for wide_at in here]
    partners += [{HEAD: lax.rem(head + distance, heads)} for distance in range(1, heads)]
    for partner in partners:
        pl.semaphore_signal(barrier, 1, device_id=partner, device_id_type=MESH)
    pl.semaphore_wait(barrier, len(partners))

    order = []
    for at in range(heads // 2):
        for chip in (heads - 1 - at, at):
            order += [chip * CUTS + cut for cut in range(CUTS)]

    def start_near(turn, target):
        for side in (0, 1):
            near(side, turn, target).start()

    start_near(1, order[0])
    start_near(0, order[0])

    @pl.when(first)
    def _():
        for distance in range(1, heads):
            shift(distance, low_parts).start()
        remote(second_parts, low_parts, swap_sem, (0,), other).start()
        pltpu.make_async_copy(first_parts.at[head], low_parts.at[head], local_sem.at[0]).start()

    @pl.when(second)
    def _():
        for distance in range(1, heads):
            shift(distance, shifted).start()
        pltpu.make_async_copy(second_parts, high_parts, local_sem.at[1]).start()
        remote(
            first_parts.at[head], high_parts.at[head], swap_sem, (1,), other
        ).start()

    steps = [other, {WIDE: here[0]}, {WIDE: here[1]}]
    steps += [{HEAD: lax.rem(head + distance, heads)} for distance in range(1, heads)]

    def small_copy(at):
        source = small.at[1 - section] if at == 0 else small_sum.at[min(at, 3)]
        return remote(source, small_buf.at[at], small_sem, (at,), steps[at])

    for at in range(3):
        small_copy(at).start()
        small_copy(at).wait()
        small_sum[at + 1] = (small[section] if at == 0 else small_sum[at]) + small_buf[at]
    for at in range(3, len(steps)):
        small_copy(at).start()

    def across(number):
        target = order[number]
        for side in (0, 1):
            near(side, 1, target).wait_recv()
            middle[side, target] = (
                terms[side][here[1 - side] * lots + target].astype(jnp.float32)
                + near_buf[side, 1, target].astype(jnp.float32)
            ).astype(middle.dtype)
            far(side, target).start()
        if number + 1 < lots:
            start_near(1, order[number + 1])
        for side in (0, 1):
            near(side, 0, target).wait_recv()
        if number + 1 < lots:
            start_near(0, order[number + 1])

    def collect(target, last):
        for side in (0, 1):
            far(side, target).wait_recv()
            sums[target, side] = (
                terms[side][wide * lots + target].astype(jnp.float32)
                + near_buf[side, 0, target].astype(jnp.float32)
                + far_buf[side, target].astype(jnp.float32)
            ).astype(sums.dtype)
            if target >= CUTS:

                @pl.when(head == 0)
                def _(side=side):
                    line(0, target, side).start()

            if target < lots - CUTS:

                @pl.when(head == heads - 1)
                def _(side=side):
                    line(1, target, side).start()

    def pass_on(at_head, way, target):
        @pl.when(head == at_head)
        def _():
            for side in (0, 1):
                line(way, target, side).wait_recv()
                sums[target, side] = (
                    sums[target, side].astype(jnp.float32)
                    + line_buf[way, target, side].astype(jnp.float32)
                ).astype(sums.dtype)
                line(way, target, side).start()

    def send_tokens():
        for which in (0, 1):
            for turn in range(4):
                for layer in (0, 1):

                    @pl.when((turn < 3) | (section != layer))
                    def _(layer=layer, which=which, turn=turn):
                        token(layer, which, turn).start()

            pltpu.make_async_copy(
                tokens_in.at[which * 2 + section, wide],
                token_target(section, which, wide, section),
                local_sem.at[2 + which],
            ).start()

    passes = {
        1: [(1, 0, 3)],
        2: [(2, 0, 3), (2, 1, 0)],
        3: [(1, 1, 0), (1, 0, 2), (2, 1, 1)],
    }
    for number, target in enumerate(order):
        across(number)
        if number == lots - 1:
            send_tokens()
        collect(target, number == lots - 1)
        for at_head, way, chip in passes.get(number // CUTS, ()):
            pass_on(at_head, way, chip * CUTS + number % CUTS)

    @pl.when(second)
    def _():
        for distance in range(1, heads):
            shift_in(distance, shifted).wait_recv()
            origin = lax.rem(head + heads - distance, heads)
            remote(
                shifted.at[origin], high_parts.at[origin], swap_sem, (1 + distance,), other
            ).start()

    whole = small_sum[3]
    for at in range(3, len(steps)):
        small_copy(at).wait()
        whole = whole + small_buf[at]
    small_total[...] = whole

    for target in range(lots):
        chip = target // CUTS

        @pl.when(head == chip)
        def _(target=target, chip=chip):
            for side in (0, 1):
                value = sums[target, side].astype(jnp.float32)
                for way, comes in ((0, chip > 0), (1, chip < heads - 1)):
                    if comes:
                        line(way, target, side).wait_recv()
                        value = value + line_buf[way, target, side].astype(jnp.float32)
                give[side, pl.ds(target % CUTS * rows, rows)] = value

        for side in (0, 1):
            for turn in (0, 1):
                near(side, turn, target).wait_send()
            far(side, target).wait_send()

            @pl.when(head < chip)
            def _(target=target, side=side):
                line(0, target, side).wait_send()

            @pl.when(head > chip)
            def _(target=target, side=side):
                line(1, target, side).wait_send()

    handed = remote(give.at[1 - section], totals.at[section], give_sem, (), other)
    handed.start()
    totals[section] = give[section]

    for which in (0, 1):
        pltpu.make_async_copy(
            tokens_in.at[which * 2 + section, wide],
            token_target(section, which, wide, section),
            local_sem.at[2 + which],
        ).wait()
        for turn in range(4):
            for layer in (0, 1):

                @pl.when((turn < 3) | (section != layer))
                def _(layer=layer, which=which, turn=turn):
                    token(layer, which, turn).wait_send()
                    token_in(layer, which, turn).wait_recv()

    @pl.when(first)
    def _():
        for distance in range(1, heads):
            shift(distance, low_parts).wait_send()
            shift_in(distance, low_parts).wait_recv()
        remote(second_parts, low_parts, swap_sem, (0,), other).wait_send()
        pltpu.make_async_copy(first_parts.at[head], low_parts.at[head], local_sem.at[0]).wait()
        for distance in range(heads):
            arrived = high_parts.at[lax.rem(head + heads - distance, heads)]
            remote(arrived, arrived, swap_sem, (1 + distance,), other).wait_recv()

    @pl.when(second)
    def _():
        for distance in range(1, heads):
            shift(distance, shifted).wait_send()
        pltpu.make_async_copy(second_parts, high_parts, local_sem.at[1]).wait()
        for distance in range(heads):
            sent = high_parts.at[lax.rem(head + heads - distance, heads)]
            remote(sent, sent, swap_sem, (1 + distance,), other).wait_send()
        remote(second_parts, low_parts, swap_sem, (0,), other).wait_recv()

    handed.wait_send()
    remote(totals.at[1 - section], totals.at[1 - section], give_sem, (), other).wait_recv()


def finish_weights(
    first_terms, second_terms, small, first_parts, second_parts, tokens_in, number
):
    heads = lax.axis_size(HEAD)
    first_terms, second_terms = [
        terms.reshape(terms.shape[0] * CUTS, -1, terms.shape[2])
        for terms in (first_terms, second_terms)
    ]
    blocks, rows, columns = first_terms.shape
    lots = heads * CUTS
    dtype = first_terms.dtype
    dma = pltpu.SemaphoreType.DMA
    vmem = pl.BlockSpec(memory_space=pltpu.VMEM)
    anywhere = pl.BlockSpec(memory_space=pl.ANY)
    smalls = 2 + heads
    layers, wides, sender_rows, width = tokens_in.shape
    return pl.pallas_call(
        finish_kernel,
        out_shape=(
            jax.ShapeDtypeStruct((2, rows * CUTS, columns), jnp.float32),
            jax.ShapeDtypeStruct(small.shape[1:], jnp.float32),
            jax.ShapeDtypeStruct(first_parts.shape, dtype),
            jax.ShapeDtypeStruct(first_parts.shape, dtype),
            jax.ShapeDtypeStruct((2, wides, 2 * sender_rows, width), dtype),
        ),
        in_specs=[vmem, vmem, vmem, anywhere, anywhere, anywhere],
        out_specs=(vmem, vmem, anywhere, anywhere, anywhere),
        scratch_shapes=[
            pltpu.VMEM((2, 2, lots, rows, columns), dtype),
            pltpu.VMEM((2, lots, rows, columns), dtype),
            pltpu.VMEM((2, lots, rows, columns), dtype),
            pltpu.VMEM((lots, 2, rows, columns), dtype),
            pltpu.VMEM((2, lots, 2, rows, columns), dtype),
            pltpu.VMEM((4,) + small.shape[1:], jnp.float32),
            pltpu.VMEM((smalls,) + small.shape[1:], jnp.float32),
            pltpu.VMEM(first_parts.shape, dtype),
            pltpu.VMEM((2, rows * CUTS, columns), jnp.float32),
            dma((4,)),
            dma((2, heads)),
            dma((2, 1 + heads)),
            dma((2, 2, 2, lots)),
            dma((2, 2, lots)),
            dma((2, 2, lots, 2)),
            dma((2, smalls)),
            dma((2,)),
            dma((2, 2, 2, 4)),
        ],
        compiler_params=pltpu.CompilerParams(
            collective_id=number, has_side_effects=True, vmem_limit_bytes=60 * 2**20
        ),
    )(first_terms, second_terms, small, first_parts, second_parts, tokens_in)


def cut_kernel(
    gate, up, down, out, sides, gains, bias, parts, out_inner, sides_inner, small
):
    count, part = parts.shape[0], parts.shape[2] // 3
    heads, wides = lax.axis_size(HEAD), lax.axis_size(WIDE)
    size = out.shape[1] // (heads * wides)
    places = [(head * wides + wide) * size for wide in range(wides) for head in range(heads)]

    def inner(whole):
        return jnp.concatenate([whole[:, start : start + size] for start in places], 1)

    out_inner[...] = inner(out[...])

    @pl.when(pl.program_id(0) == 0)
    def _():
        sides_inner[...] = inner(sides[...])
        scales = inner(gains[...])
        width = gains.shape[1]
        for at in (0, 1):
            small[:, pl.ds(at * width, width)] = scales[at : at + 1]
        small[:, pl.ds(2 * width, bias.shape[1])] = bias[...]

    for at in range(count):
        size = min(part, gate.shape[1] - at * part)
        for which, weight in enumerate((gate, up, down)):
            start = which * part
            parts[at, :, pl.ds(start, size)] = weight[:, pl.ds(at * part, size)]
            if size < part:
                rest = part - size
                parts[at, :, pl.ds(start + size, rest)] = jnp.zeros(
                    (parts.shape[1], rest), parts.dtype
                )


def cut_parts(gate, up, down, out, sides, gains, bias, count, part):
    rows, columns = gate.shape
    step = 16
    weight = pl.BlockSpec((step, columns), lambda at: (at, 0))
    square = pl.BlockSpec((step, out.shape[1]), lambda at: (at, 0))
    wholes = [
        pl.BlockSpec(shape, lambda at: (0, 0))
        for shape in (sides.shape, gains.shape, bias.shape, (1, gains.size + bias.size))
    ]
    return pl.pallas_call(
        cut_kernel,
        grid=(rows // step,),
        out_shape=(
            jax.ShapeDtypeStruct((count, rows, 3 * part), gate.dtype),
            jax.ShapeDtypeStruct(out.shape, out.dtype),
            jax.ShapeDtypeStruct(sides.shape, sides.dtype),
            jax.ShapeDtypeStruct((1, gains.size + bias.size), jnp.float32),
        ),
        in_specs=[weight] * 3 + [square] + wholes[:3],
        out_specs=(
            pl.BlockSpec((count, step, 3 * part), lambda at: (0, at, 0)),
            square,
            wholes[0],
            wholes[3],
        ),
        compiler_params=pltpu.CompilerParams(vmem_limit_bytes=24 * 2**20),
    )(gate, up, down, out, sides, gains, bias)


def join_kernel(low, high, totals, small, gate, up, down, qkv, out, gains, bias):
    count, part = low.shape[0], low.shape[2] // 3
    for at in range(2 * count):
        size = min(part, gate.shape[2] - at * part)
        source = low if at < count else high
        for which, grad in enumerate((gate, up, down)):
            grad[0, :, pl.ds(at * part, size)] = source[
                at % count, :, pl.ds(which * part, size)
            ].astype(grad.dtype)
    cut, width = qkv.shape[2] // 2, out.shape[2]
    for at in (0, 1):
        qkv[0, :, pl.ds(at * cut, cut)] = totals[at, :, pl.ds(0, cut)]
    whole = jnp.concatenate([totals[at, :, pl.ds(cut, width // 2)] for at in (0, 1)], 1)
    heads, wides = lax.axis_size(HEAD), lax.axis_size(WIDE)
    size = width // (heads * wides)
    places = [(wide * heads + head) * size for head in range(heads) for wide in range(wides)]

    def outer(array):
        return jnp.concatenate([array[:, start : start + size] for start in places], 1)

    out[0] = outer(whole)

    @pl.when(pl.program_id(0) == 0)
    def _():
        for at in (0, 1):
            gains[0, at : at + 1] = outer(small[:, at * width : (at + 1) * width])
        bias[...] = small[:, pl.ds(2 * width, bias.shape[1])]


def join_parts(low, high, totals, small, columns, qkv_cols):
    count, rows, width = low.shape
    out_cols = 2 * totals.shape[2] - qkv_cols
    step = 16
    part = pl.BlockSpec((count, step, width), lambda at: (0, at, 0))
    total = pl.BlockSpec((2, step, totals.shape[2]), lambda at: (0, at, 0))
    sizes = (columns, columns, columns, qkv_cols, out_cols)
    return pl.pallas_call(
        join_kernel,
        grid=(rows // step,),
        out_shape=tuple(jax.ShapeDtypeStruct((1, rows, size), jnp.float32) for size in sizes)
        + (
            jax.ShapeDtypeStruct((1, 2, out_cols), jnp.float32),
            jax.ShapeDtypeStruct((1, qkv_cols), jnp.float32),
        ),
        in_specs=[part, part, total, pl.BlockSpec(small.shape, lambda at: (0, 0))],
        out_specs=tuple(pl.BlockSpec((1, step, size), lambda at: (0, at, 0)) for size in sizes)
        + (
            pl.BlockSpec((1, 2, out_cols), lambda at: (0, 0, 0)),
            pl.BlockSpec((1, qkv_cols), lambda at: (0, 0)),
        ),
        compiler_params=pltpu.CompilerParams(vmem_limit_bytes=24 * 2**20),
    )(low, high, totals, small)


def partner_of(head, turn):
    if turn == 1:
        return head + 1 - 2 * lax.rem(head, 2)
    return lax.rem(head + 2, 4) if turn == 2 else 3 - head


def block_swap(source, target, sems, head, turn):
    return pltpu.make_async_remote_copy(
        source,
        target,
        sems.at[0],
        sems.at[1],
        device_id={HEAD: partner_of(head, turn)},
        device_id_type=MESH,
    )


def visit(head, step, heads):
    inner_chip = jnp.minimum(jnp.minimum(head, heads - 1 - head), 1)
    at = step + inner_chip * (1 - lax.div(step, 2)) * (1 - 2 * step)
    return at + lax.div(2 * head, heads) * (heads - 1 - 2 * at)


def group_pipeline(block, everyone, outs, scratch, prepare, compute, settle, extras=()):
    (partial, pair_buf, sums, line_buf, own_sem, pair_sem, line_sem, swap_sem, chain_sem) = scratch
    section, head = lax.axis_index(SECTION), lax.axis_index(HEAD)
    heads = lax.axis_size(HEAD)
    tokens = block.shape[0]
    other = {SECTION: 1 - section}

    def place(section_at, origin, piece=None):
        size = tokens if piece is None else tokens // GATHER_PIECES
        start = (origin * 2 + section_at) * tokens + (piece or 0) * size
        return everyone.at[pl.ds(pl.multiple_of(start, size), size)]

    def remote(source, target, send, receive, partner):
        return pltpu.make_async_remote_copy(
            source, target, send, receive, device_id=partner, device_id_type=MESH
        )

    def pair(origin, source):
        target = place(section, origin)
        return remote(source, target, pair_sem.at[0, origin], pair_sem.at[1, origin], other)

    def pair_in(origin):
        target = place(1 - section, origin)
        return remote(target, target, pair_sem.at[0, origin], pair_sem.at[1, origin], other)

    def line(way, hop, piece):
        step = 1 - 2 * way
        size = tokens // GATHER_PIECES
        target = place(section, head - step * hop, piece)
        own = type(hop) is int and hop == 0
        source = block.at[pl.ds(piece * size, size)] if own else target
        sems = (line_sem.at[0, way, hop, piece], line_sem.at[1, way, hop, piece])
        return remote(source, target, *sems, {HEAD: head + step})

    def inside(place_at):
        return (place_at >= 0) & (place_at < heads)

    def accept(way, hop):
        step = 1 - 2 * way
        for piece in range(GATHER_PIECES):
            here = place(section, head - step * hop, piece)
            sems = (line_sem.at[0, way, hop - 1, piece], line_sem.at[1, way, hop - 1, piece])
            remote(here, here, *sems, {HEAD: head}).wait_recv()

            @pl.when(inside(head + step))
            def _(piece=piece):
                line(way, hop, piece).start()

        pair(head - step * hop, place(section, head - step * hop)).start()

    def swap(origin):
        return remote(
            partial.at[origin, 1 - section],
            pair_buf.at[origin],
            swap_sem.at[0, origin],
            swap_sem.at[1, origin],
            other,
        )

    def lot(piece):
        size = tokens // CHAIN_PIECES
        return pl.ds(piece * size, size)

    def chain(way, target, piece):
        return remote(
            sums.at[target, lot(piece)],
            line_buf.at[way, target, lot(piece)],
            chain_sem.at[0, way, target, piece],
            chain_sem.at[1, way, target, piece],
            {HEAD: head + 1 - 2 * way},
        )

    def send_pieces(way, target, last):
        for piece in range(CHAIN_PIECES):
            chain(way, target, piece).start()
            if last and piece < CHAIN_PIECES - 1:
                chain(way, target, piece).wait_send()

    def deliver(origin, last=False):
        swap(origin).wait_recv()
        sums[origin] = (
            partial[origin, section].astype(jnp.float32) + pair_buf[origin].astype(jnp.float32)
        ).astype(sums.dtype)

        @pl.when((head == 0) & (origin > 0))
        def _():
            send_pieces(0, origin, last)

        @pl.when((head == heads - 1) & (origin < heads - 1))
        def _():
            send_pieces(1, origin, last)

    def pass_on(way, target, piece):
        chain(way, target, piece).wait_recv()
        here = lot(piece)
        sums[target, here] = (
            sums[target, here].astype(jnp.float32) + line_buf[way, target, here].astype(jnp.float32)
        ).astype(sums.dtype)
        chain(way, target, piece).start()

    barrier = pltpu.get_barrier_semaphore()
    partners = [other] + [{HEAD: lax.rem(head + shift, heads)} for shift in range(1, heads)]
    for partner in partners:
        pl.semaphore_signal(barrier, 1, device_id=partner, device_id_type=MESH)
    pl.semaphore_wait(barrier, len(partners))

    for way in (0, 1):

        @pl.when(inside(head + 1 - 2 * way))
        def _(way=way):
            for piece in range(GATHER_PIECES):
                line(way, 0, piece).start()

    pair(head, block).start()
    own = pltpu.make_async_copy(block, place(section, head), own_sem)
    own.start()
    prepare()
    own.wait()

    def one(step, carry):
        origin = visit(head, step, heads)

        @pl.when(step >= 1)
        def _():
            deliver(visit(head, step - 1, heads))

        @pl.when(step == 1)
        def _():
            for way in (0, 1):

                @pl.when(inside(head - (1 - 2 * way)))
                def _(way=way):
                    accept(way, 1)

        hop = jnp.maximum(origin - head, head - origin)

        @pl.when((step >= 2) & (hop >= 2))
        def _():
            accept(lax.div(jnp.maximum(origin - head, 0) + heads - 2, heads), hop)

        pair_in(origin).wait_recv()
        compute(origin)
        swap(origin).start()
        return carry

    lax.fori_loop(0, heads, one, 0)
    deliver(visit(head, heads - 1, heads), True)

    between = (head > 0) & (head < heads - 1)
    side = lax.div(2 * head, heads)
    ends = ((1 - side) * (heads - 1), side * (heads - 1))
    extras = list(extras)

    def work(count):
        for _ in range(min(count, len(extras))):
            extras.pop(0)()

    work(2)

    @pl.when(between)
    def _():
        for piece in range(CHAIN_PIECES):
            pass_on(side, heads - 1 - head, piece)

    for piece in range(CHAIN_PIECES):

        @pl.when(between)
        def _(piece=piece):
            pass_on(side, ends[0], piece)
            pass_on(1 - side, ends[1], piece)

        work(1)

    work(len(extras))
    settle()
    spans = [pl.ds(at * block.shape[1], block.shape[1]) for at in range(len(outs))]
    for out, span in zip(outs, spans):
        out[...] = sums[head, :, span].astype(jnp.float32)
    for way, comes in ((0, head > 0), (1, head < heads - 1)):

        @pl.when(comes)
        def _(way=way):
            for piece in range(CHAIN_PIECES):
                chain(way, head, piece).wait_recv()
            for out, span in zip(outs, spans):
                out[...] += line_buf[way, head, :, span].astype(jnp.float32)

    for piece in range(CHAIN_PIECES):
        for target in range(1, heads):

            if target < heads - 1 or piece == CHAIN_PIECES - 1:

                @pl.when(head == 0)
                def _(piece=piece, target=target):
                    chain(0, target, piece).wait_send()

                @pl.when(head == heads - 1)
                def _(piece=piece, target=target):
                    chain(1, heads - 1 - target, piece).wait_send()

        @pl.when(between)
        def _(piece=piece):
            chain(side, heads - 1 - head, piece).wait_send()
            chain(side, ends[0], piece).wait_send()
            chain(1 - side, ends[1], piece).wait_send()

    for origin in range(heads):
        here = place(section, origin)
        pair(origin, here).wait_send()
        swap(origin).wait_send()

    for way in (0, 1):
        for hop in range(heads):
            step = 1 - 2 * way

            @pl.when(inside(head + step) & inside(head - step * hop))
            def _(way=way, hop=hop):
                for piece in range(GATHER_PIECES):
                    line(way, hop, piece).wait_send()


def pipeline_scratch(heads, tokens, columns, dtype):
    dma = pltpu.SemaphoreType.DMA
    return [
        pltpu.VMEM((heads, 2, tokens, columns), dtype),
        pltpu.VMEM((heads, tokens, columns), dtype),
        pltpu.VMEM((heads, tokens, columns), dtype),
        pltpu.VMEM((2, heads, tokens, columns), dtype),
        dma,
        dma((2, heads)),
        dma((2, 2, heads, GATHER_PIECES)),
        dma((2, heads)),
        dma((2, 2, heads, CHAIN_PIECES)),
    ]


PIPELINE_SCRATCH = 9
CHAIN_PIECES = 4
GATHER_PIECES = 2
TERM_ROWS = 512
TERM_SLOTS = 3
STEP_COLUMNS = 384
STEP_WIDTH = 512


def chunks(total, size):
    return [(at, min(size, total - at)) for at in range(0, total, size)]


def write_partial(partial, origin, left, weights, columns, offset=0):
    tokens = partial.shape[2]
    for start, count in chunks(weights.shape[0], STEP_WIDTH):
        piece = contract_last(left, weights[pl.ds(start, count), pl.ds(*columns)])
        piece = piece.astype(partial.dtype)
        partial[origin, 0, :, pl.ds(offset + start, count)] = piece[:tokens]
        partial[origin, 1, :, pl.ds(offset + start, count)] = piece[tokens:]


def forward_kernel(block, weights_hbm, out, everyone, gate_up_hbm, hidden_hbm, *scratch):
    shared, rest = scratch[:PIPELINE_SCRATCH], scratch[PIPELINE_SCRATCH:]
    weights, gate_up, hidden, load_sem, store_sem = rest
    partial = shared[0]
    heads = lax.axis_size(HEAD)
    rows = 2 * block.shape[0]
    part = hidden.shape[1]
    load = pltpu.make_async_copy(weights_hbm, weights, load_sem)

    def stores(origin):
        span = pl.ds(pl.multiple_of(origin * rows, rows), rows)
        return [
            pltpu.make_async_copy(gate_up.at[span], gate_up_hbm.at[span], store_sem.at[0, origin]),
            pltpu.make_async_copy(hidden.at[span], hidden_hbm.at[span], store_sem.at[1, origin]),
        ]

    def prepare():
        load.start()
        load.wait()

    def compute(origin):
        span = pl.ds(pl.multiple_of(origin * rows, rows), rows)
        left = everyone[span, :]
        for start, count in chunks(part, STEP_COLUMNS):
            gate = jnp.dot(
                left, weights[:, pl.ds(start, count)], preferred_element_type=jnp.float32
            )
            up = jnp.dot(
                left, weights[:, pl.ds(part + start, count)], preferred_element_type=jnp.float32
            )
            gate_up[span, pl.ds(start, count)] = gate.astype(gate_up.dtype)
            gate_up[span, pl.ds(part + start, count)] = up.astype(gate_up.dtype)
            hidden[span, pl.ds(start, count)] = (gate / (1.0 + jnp.exp(-gate)) * up).astype(
                hidden.dtype
            )
        write_partial(partial, origin, hidden[span, :], weights, (2 * part, part))
        for store in stores(origin):
            store.start()

    def settle():
        for origin in range(heads):
            for store in stores(origin):
                store.wait()

    group_pipeline(block, everyone, (out,), shared, prepare, compute, settle)


def term_tiles(operands, part, terms, terms_hbm, term_sem, loads=()):
    lefts, rights = operands
    width = terms_hbm.shape[0]
    tiles = [(which, start) for which in range(3) for start, _ in chunks(width, TERM_ROWS)]

    def store(number):
        which, start = tiles[number]
        slot = number % TERM_SLOTS
        target = terms_hbm.at[pl.ds(start, TERM_ROWS), pl.ds(which * part, part)]
        return pltpu.make_async_copy(terms.at[slot], target, term_sem.at[slot])

    def tile(number):
        which, start = tiles[number]
        if number == 0:
            for load in loads:
                load.wait()
        if number >= TERM_SLOTS:
            store(number - TERM_SLOTS).wait()
        left = lefts[which][:, pl.ds(start, TERM_ROWS)]
        right = rights[which][:, pl.ds(which % 2 * part if which < 2 else 0, part)]
        terms[number % TERM_SLOTS] = contract_first(left, right).astype(terms.dtype)
        store(number).start()

    def settle():
        for number in range(len(tiles) - TERM_SLOTS, len(tiles)):
            store(number).wait()

    return [functools.partial(tile, number) for number in range(len(tiles))], settle


def backward_kernel(
    block, weights_hbm, gate_up_hbm, normed_hbm, hidden_hbm, out, terms_hbm, *scratch
):
    shared, rest = scratch[:PIPELINE_SCRATCH], scratch[PIPELINE_SCRATCH:]
    everyone, weights, gate_up, normed, hidden, d_gate_up, terms, load_sem, term_sem = rest
    partial = shared[0]
    rows = 2 * block.shape[0]
    part = hidden.shape[1]
    sources = ((weights_hbm, weights), (gate_up_hbm, gate_up))
    sources += ((normed_hbm, normed), (hidden_hbm, hidden))
    loads = [
        pltpu.make_async_copy(source, target, load_sem.at[at])
        for at, (source, target) in enumerate(sources)
    ]

    def prepare():
        for load in loads:
            load.start()
        for load in loads[:2]:
            load.wait()

    def compute(origin):
        span = pl.ds(pl.multiple_of(origin * rows, rows), rows)
        left = everyone[span, :]
        for start, count in chunks(part, STEP_COLUMNS):
            d_hidden = jnp.dot(
                left, weights[:, pl.ds(2 * part + start, count)], preferred_element_type=jnp.float32
            )
            gate = gate_up[span, pl.ds(start, count)].astype(jnp.float32)
            up = gate_up[span, pl.ds(part + start, count)].astype(jnp.float32)
            sigmoid = 1.0 / (1.0 + jnp.exp(-gate))
            d_gate = d_hidden * up * sigmoid * (1.0 + gate * (1.0 - sigmoid))
            d_gate_up[span, pl.ds(start, count)] = d_gate.astype(d_gate_up.dtype)
            d_up = d_hidden * gate * sigmoid
            d_gate_up[span, pl.ds(part + start, count)] = d_up.astype(d_gate_up.dtype)
        write_partial(partial, origin, d_gate_up[span, :], weights, (0, 2 * part))

    operands = (normed, normed, everyone), (d_gate_up, d_gate_up, hidden)
    extras, settle = term_tiles(operands, part, terms, terms_hbm, term_sem, loads[2:])
    group_pipeline(block, everyone, (out,), shared, prepare, compute, settle, extras)


def turning_kernel(block, weights_hbm, *refs):
    blocks, (out, d_out, terms_hbm), scratch = refs[:4], refs[4:7], refs[7:]
    shared, rest = scratch[:PIPELINE_SCRATCH], scratch[PIPELINE_SCRATCH:]
    everyone, weights, grads, hidden, d_gate_up, terms, load_sem, give_sem, term_sem = rest
    partial = shared[0]
    rows, width = 2 * block.shape[0], block.shape[1]
    part = hidden.shape[1]
    section, head = lax.axis_index(SECTION), lax.axis_index(HEAD)
    tokens = block.shape[0]
    load = pltpu.make_async_copy(weights_hbm, weights, load_sem.at[4])

    def place(section_at, turn):
        origin = head if turn == 0 else partner_of(head, turn)
        first_row = pl.multiple_of((origin * 2 + section_at) * tokens, tokens)
        return grads.at[pl.ds(first_row, tokens)]

    def own(turn):
        return pltpu.make_async_copy(blocks[turn], place(section, turn), load_sem.at[turn])

    def give(turn, section_at):
        return pltpu.make_async_remote_copy(
            blocks[turn],
            place(section_at, turn),
            give_sem.at[0, turn],
            give_sem.at[1, turn],
            device_id={SECTION: 1 - section},
            device_id_type=MESH,
        )

    def prepare():
        load.start()
        for turn in range(4):
            own(turn).start()
            give(turn, section).start()
        for turn in range(4):
            own(turn).wait()
            give(turn, section).wait_send()
            give(turn, 1 - section).wait_recv()
        load.wait()

    def compute(origin):
        span = pl.ds(pl.multiple_of(origin * rows, rows), rows)
        left, grad = everyone[span, :], grads[span, :]
        for start, count in chunks(part, STEP_COLUMNS):
            gate, up, d_hidden = [
                jnp.dot(
                    source,
                    weights[:, pl.ds(which * part + start, count)],
                    preferred_element_type=jnp.float32,
                )
                for which, source in enumerate((left, left, grad))
            ]
            sigmoid = 1.0 / (1.0 + jnp.exp(-gate))
            hidden[span, pl.ds(start, count)] = (gate * sigmoid * up).astype(hidden.dtype)
            d_gate = d_hidden * up * sigmoid * (1.0 + gate * (1.0 - sigmoid))
            d_gate_up[span, pl.ds(start, count)] = d_gate.astype(d_gate_up.dtype)
            d_up = d_hidden * gate * sigmoid
            d_gate_up[span, pl.ds(part + start, count)] = d_up.astype(d_gate_up.dtype)
        write_partial(partial, origin, hidden[span, :], weights, (2 * part, part))
        write_partial(partial, origin, d_gate_up[span, :], weights, (0, 2 * part), width)

    operands = (everyone, everyone, grads), (d_gate_up, d_gate_up, hidden)
    extras, settle = term_tiles(operands, part, terms, terms_hbm, term_sem)
    group_pipeline(block, everyone, (out, d_out), shared, prepare, compute, settle, extras)


def turning_point(block, weights, grads, number):
    heads = lax.axis_size(HEAD)
    tokens, width = block.shape
    part = weights.shape[1] // 3
    count = 2 * heads * tokens
    dtype = block.dtype
    vmem = pl.BlockSpec(memory_space=pltpu.VMEM)
    anywhere = pl.BlockSpec(memory_space=pl.ANY)
    return pl.pallas_call(
        turning_kernel,
        out_shape=(
            jax.ShapeDtypeStruct((tokens, width), jnp.float32),
            jax.ShapeDtypeStruct((tokens, width), jnp.float32),
            jax.ShapeDtypeStruct(weights.shape, dtype),
        ),
        in_specs=[vmem] + [anywhere] * 5,
        out_specs=(vmem, vmem, anywhere),
        scratch_shapes=pipeline_scratch(heads, tokens, 2 * width, dtype)
        + [
            pltpu.VMEM((count, width), dtype),
            pltpu.VMEM(weights.shape, dtype),
            pltpu.VMEM((count, width), dtype),
            pltpu.VMEM((count, part), dtype),
            pltpu.VMEM((count, 2 * part), dtype),
            pltpu.VMEM((TERM_SLOTS, TERM_ROWS, part), dtype),
            pltpu.SemaphoreType.DMA((5,)),
            pltpu.SemaphoreType.DMA((2, 4)),
            pltpu.SemaphoreType.DMA((TERM_SLOTS,)),
        ],
        compiler_params=pltpu.CompilerParams(
            collective_id=number, has_side_effects=True, vmem_limit_bytes=60 * 2**20
        ),
        cost_estimate=pl.CostEstimate(
            flops=18 * count * width * part, bytes_accessed=4 * weights.size, transcendentals=0
        ),
    )(block, weights, *grads)


def feed_forward(block, weights, number):
    heads = lax.axis_size(HEAD)
    tokens, width = block.shape
    part = weights.shape[1] // 3
    count = 2 * heads * tokens
    dtype = block.dtype
    vmem = pl.BlockSpec(memory_space=pltpu.VMEM)
    anywhere = pl.BlockSpec(memory_space=pl.ANY)
    return pl.pallas_call(
        forward_kernel,
        out_shape=(
            jax.ShapeDtypeStruct((tokens, width), jnp.float32),
            jax.ShapeDtypeStruct((count, width), dtype),
            jax.ShapeDtypeStruct((count, 2 * part), dtype),
            jax.ShapeDtypeStruct((count, part), dtype),
        ),
        in_specs=[vmem, anywhere],
        out_specs=(vmem, vmem, anywhere, anywhere),
        scratch_shapes=pipeline_scratch(heads, tokens, width, dtype)
        + [
            pltpu.VMEM(weights.shape, dtype),
            pltpu.VMEM((count, 2 * part), dtype),
            pltpu.VMEM((count, part), dtype),
            pltpu.SemaphoreType.DMA,
            pltpu.SemaphoreType.DMA((2, heads)),
        ],
        compiler_params=pltpu.CompilerParams(
            collective_id=number, has_side_effects=True, vmem_limit_bytes=60 * 2**20
        ),
        cost_estimate=pl.CostEstimate(
            flops=6 * count * width * part, bytes_accessed=2 * weights.size, transcendentals=0
        ),
    )(block, weights)


def feed_backward(block, weights, gate_up, normed, hidden, number):
    heads = lax.axis_size(HEAD)
    tokens, width = block.shape
    part = hidden.shape[1]
    count = 2 * heads * tokens
    dtype = block.dtype
    vmem = pl.BlockSpec(memory_space=pltpu.VMEM)
    anywhere = pl.BlockSpec(memory_space=pl.ANY)
    return pl.pallas_call(
        backward_kernel,
        out_shape=(
            jax.ShapeDtypeStruct((tokens, width), jnp.float32),
            jax.ShapeDtypeStruct(weights.shape, dtype),
        ),
        in_specs=[vmem] + [anywhere] * 4,
        out_specs=(vmem, anywhere),
        scratch_shapes=pipeline_scratch(heads, tokens, width, dtype)
        + [
            pltpu.VMEM((count, width), dtype),
            pltpu.VMEM(weights.shape, dtype),
            pltpu.VMEM(gate_up.shape, dtype),
            pltpu.VMEM((count, width), dtype),
            pltpu.VMEM((count, part), dtype),
            pltpu.VMEM((count, 2 * part), dtype),
            pltpu.VMEM((TERM_SLOTS, TERM_ROWS, part), dtype),
            pltpu.SemaphoreType.DMA((4,)),
            pltpu.SemaphoreType.DMA((TERM_SLOTS,)),
        ],
        compiler_params=pltpu.CompilerParams(
            collective_id=number, has_side_effects=True, vmem_limit_bytes=58 * 2**20
        ),
        cost_estimate=pl.CostEstimate(
            flops=12 * count * width * part, bytes_accessed=4 * weights.size, transcendentals=0
        ),
    )(block, weights, gate_up, normed, hidden)


GROUP = 3


def turn(tensor, cosine, sine):
    return tensor * cosine + pltpu.roll(tensor, tensor.shape[1] // 2, 1) * sine


def attention_grad_kernel(
    layer,
    moves,
    d_normed2,
    midway,
    scale2,
    out_grad,
    small_rows,
    queries,
    keyval,
    log_total,
    attended,
    normed,
    layer_in,
    scale1,
    cosine,
    sine,
    own_pos,
    key_pos,
    w_out_hbm,
    w_qkv_hbm,
    parts_in,
    d_in,
    small,
    terms_hbm,
    parts_out,
    w_out,
    w_qkv,
    d_midway,
    g_attn,
    d_attended,
    d_qkv,
    d_normed,
    d_keyval,
    terms,
    their_normed,
    their_attended,
    their_g,
    their_d,
    sums,
    pair_buf,
    line_buf,
    load_sem,
    give_sem,
    pair_sem,
    line_sem,
    shift_sem,
):
    section, head = lax.axis_index(SECTION), lax.axis_index(HEAD)
    heads, wides = lax.axis_size(HEAD), lax.axis_size(WIDE)
    tokens, width = normed.shape
    qkv_cols = d_qkv.shape[1]
    kv_width = KV * HDIM
    rows = width // (heads * wides)
    scaling = HDIM**-0.5
    other = {SECTION: 1 - section}

    def remote(source, target, sems, at, partner):
        return pltpu.make_async_remote_copy(
            source,
            target,
            sems.at[(0,) + at],
            sems.at[(1,) + at],
            device_id=partner,
            device_id_type=MESH,
        )

    def half(array, at):
        count = array.shape[1] // 2
        return array.at[:, pl.ds(pl.multiple_of(at * count, 128), count)]

    gives = [
        remote(normed, their_normed, give_sem, (0,), other),
        remote(attended, their_attended, give_sem, (1,), other),
        remote(half(g_attn, 1 - section), their_g, give_sem, (2,), other),
        remote(half(d_qkv, 1 - section), their_d, give_sem, (3,), other),
    ]
    loads = [
        pltpu.make_async_copy(w_out_hbm.at[layer], w_out, load_sem.at[0]),
        pltpu.make_async_copy(w_qkv_hbm.at[layer], w_qkv, load_sem.at[1]),
    ]
    for load in loads:
        load.start()

    def shift(distance):
        target = lax.rem(head + distance, heads)
        return remote(
            parts_in.at[target], parts_out.at[head], shift_sem, (distance,), {HEAD: target}
        )

    def shift_in(distance):
        arrived = parts_out.at[lax.rem(head + heads - distance, heads)]
        return remote(arrived, arrived, shift_sem, (distance,), {HEAD: head})

    def shift_own():
        return pltpu.make_async_copy(parts_in.at[head], parts_out.at[head], load_sem.at[4])

    barrier = pltpu.get_barrier_semaphore()
    partners = [other] + [{HEAD: lax.rem(head + distance, heads)} for distance in range(1, heads)]
    for partner in partners:
        pl.semaphore_signal(barrier, 1, device_id=partner, device_id_type=MESH)
    pl.semaphore_wait(barrier, len(partners))
    for give in gives[:2]:
        give.start()
    if moves:
        shift_own().start()
        for distance in range(1, heads):
            shift(distance).start()

    grad = out_grad[...].astype(jnp.float32)
    unit = midway[...] * scale2[...]
    gain2_grad = jnp.sum(d_normed2[...] * unit, 0, keepdims=True)
    scaled = d_normed2[...] * small_rows[layer, :, pl.ds(width, width)]
    d_midway[...] = (
        scale2[...] * (scaled - unit * jnp.mean(scaled * unit, -1, keepdims=True)) + grad
    )
    g_attn[...] = d_midway[...].astype(g_attn.dtype)
    gives[2].start()
    small[:, pl.ds(width, width)] = gain2_grad
    loads[0].wait()
    for start, count in chunks(width, STEP_WIDTH):
        d_attended[:, pl.ds(start, count)] = contract_last(
            g_attn[...], w_out[pl.ds(start, count), :]
        ).astype(d_attended.dtype)

    allowed = own_pos[...] >= key_pos[...]
    allowed = jnp.concatenate([allowed.astype(jnp.int32)] * GROUP, 0) > 0
    groups = HEADS // GROUP
    for group in range(groups):
        kv = group * KV // groups
        spans = [pl.ds((group * GROUP + at) * HDIM, HDIM) for at in range(GROUP)]
        query = jnp.concatenate([queries[group * GROUP + at] for at in range(GROUP)], 0)
        total = jnp.concatenate([log_total[group * GROUP + at] for at in range(GROUP)], 0)
        key = keyval[:, pl.ds(kv * HDIM, HDIM)]
        value = keyval[:, pl.ds(kv_width + kv * HDIM, HDIM)]
        d_out = jnp.concatenate([d_attended[:, span] for span in spans], 0)
        scores = jnp.where(allowed, contract_last(query, key) * scaling, -1e30)
        probs = jnp.exp(scores - total)
        d_probs = contract_last(d_out, value)
        row_dot = jnp.sum(probs * d_probs, -1, keepdims=True)
        d_scores = (probs * (d_probs - row_dot)).astype(jnp.bfloat16)
        d_query = jnp.dot(d_scores, key, preferred_element_type=jnp.float32) * scaling
        d_query = d_query.astype(jnp.bfloat16).astype(jnp.float32)
        for at, span in enumerate(spans):
            d_qkv[:, span] = turn(
                d_query[at * tokens : (at + 1) * tokens], cosine[...], sine[...]
            ).astype(d_qkv.dtype)
        d_key = contract_first(d_scores, query) * scaling
        d_value = contract_first(probs.astype(jnp.bfloat16), d_out)
        first = group % (groups // KV) == 0
        for column, part in ((kv * HDIM, d_key), (kv_width + kv * HDIM, d_value)):
            part = part if first else part + d_keyval[:, pl.ds(column, HDIM)]
            d_keyval[:, pl.ds(column, HDIM)] = part

    def place(section_at, head_at):
        return pl.ds(pl.multiple_of((section_at * heads + head_at) * tokens, tokens), tokens)

    sent = terms.at[pl.ds(0, 2 * heads * tokens), pl.ds(0, d_keyval.shape[1])]
    sent[...] = d_keyval[...].astype(sent.dtype)

    def pair(target):
        source = sent.at[place(1 - section, target)]
        return remote(source, pair_buf.at[target], pair_sem, (target,), other)

    def line(way, target):
        partner = {HEAD: head + 1 - 2 * way}
        return remote(sums.at[target], line_buf.at[way, target], line_sem, (way, target), partner)

    order = []
    for at in range(heads // 2):
        order += [heads - 1 - at, at]
    for target in order:
        pair(target).start()
    for target in order:
        pair(target).wait_recv()
        sums[target] = (
            sent[place(section, target), :].astype(jnp.float32)
            + pair_buf[target].astype(jnp.float32)
        ).astype(sums.dtype)
        if target > 0:

            @pl.when(head == 0)
            def _(target=target):
                line(0, target).start()

        if target < heads - 1:

            @pl.when(head == heads - 1)
            def _(target=target):
                line(1, target).start()

    for target in order:
        pair(target).wait_send()

    def pass_on(way, target):
        line(way, target).wait_recv()
        sums[target] = (
            sums[target].astype(jnp.float32) + line_buf[way, target].astype(jnp.float32)
        ).astype(sums.dtype)
        line(way, target).start()

    loads[1].wait()
    for start, count in chunks(width, STEP_WIDTH):
        d_normed[:, pl.ds(start, count)] = contract_last(
            d_qkv[:, pl.ds(0, width)], w_qkv[pl.ds(start, count), pl.ds(0, width)]
        )
    gives[1].wait_recv()
    gives[2].wait_recv()
    pair_g = jnp.concatenate([half(g_attn, section)[...], their_g[...]], 0)

    def out_terms(head_at):
        span = pl.ds(head_at * wides * rows, wides * rows)
        left = jnp.concatenate([attended[:, span], their_attended[:, span]], 0)
        piece = contract_first(left, pair_g).astype(terms.dtype)
        for wide_at in range(wides):
            target = pl.ds((wide_at * heads + head_at) * rows, rows)
            terms[target, pl.ds(qkv_cols // 2, width // 2)] = piece[
                wide_at * rows : (wide_at + 1) * rows
            ]

    for at in range(heads - 1):
        right, left = heads - 1 - at, at

        @pl.when((head > 0) & (head < right))
        def _(right=right):
            pass_on(0, right)

        @pl.when((head < heads - 1) & (head > left))
        def _(left=left):
            pass_on(1, left)

        out_terms(at)

    out_terms(heads - 1)

    def store(at):
        start, count = ((0, qkv_cols // 2), (qkv_cols // 2, width // 2))[at]
        span = pl.ds(start, count)
        return pltpu.make_async_copy(terms.at[:, span], terms_hbm.at[:, span], load_sem.at[2 + at])

    store(1).start()
    d_keyval[pl.ds(0, tokens), :] = sums[head].astype(jnp.float32)
    for way, comes in ((0, head > 0), (1, head < heads - 1)):

        @pl.when(comes)
        def _(way=way):
            line(way, head).wait_recv()
            d_keyval[pl.ds(0, tokens), :] += line_buf[way, head].astype(jnp.float32)

    for kv in range(KV):
        span = pl.ds(kv * HDIM, HDIM)
        d_qkv[:, pl.ds(width + kv * HDIM, HDIM)] = turn(
            d_keyval[pl.ds(0, tokens), span], cosine[...], sine[...]
        ).astype(d_qkv.dtype)
    d_qkv[:, pl.ds(width + kv_width, kv_width)] = d_keyval[
        pl.ds(0, tokens), pl.ds(kv_width, kv_width)
    ].astype(d_qkv.dtype)
    gives[3].start()
    small[:, pl.ds(2 * width, qkv_cols)] = jnp.sum(
        d_qkv[...].astype(jnp.float32), 0, keepdims=True
    )
    rest = pl.ds(width, qkv_cols - width)
    for start, count in chunks(width, STEP_WIDTH):
        d_normed[:, pl.ds(start, count)] += contract_last(
            d_qkv[:, rest], w_qkv[pl.ds(start, count), rest]
        )

    unit = layer_in[...] * scale1[...]
    small[:, pl.ds(0, width)] = jnp.sum(d_normed[...] * unit, 0, keepdims=True)
    scaled = d_normed[...] * small_rows[layer, :, pl.ds(0, width)]
    d_in[...] = (
        scale1[...] * (scaled - unit * jnp.mean(scaled * unit, -1, keepdims=True)) + d_midway[...]
    ).astype(d_in.dtype)

    gives[0].wait_recv()
    gives[3].wait_recv()
    pair_d = jnp.concatenate([half(d_qkv, section)[...], their_d[...]], 0)
    for start, count in chunks(width, STEP_WIDTH):
        span = pl.ds(start, count)
        left = jnp.concatenate([normed[:, span], their_normed[:, span]], 0)
        terms[span, pl.ds(0, qkv_cols // 2)] = contract_first(left, pair_d).astype(terms.dtype)
    store(0).start()
    for give in gives:
        give.wait_send()
    for target in range(heads):

        @pl.when(head < target)
        def _(target=target):
            line(0, target).wait_send()

        @pl.when(head > target)
        def _(target=target):
            line(1, target).wait_send()

    for at in (0, 1):
        store(at).wait()
    if moves:
        shift_own().wait()
        for distance in range(1, heads):
            shift(distance).wait_send()
            shift_in(distance).wait_recv()


def attention_grad(layer, number, w_out, w_qkv, parts_in, *operands):
    heads = lax.axis_size(HEAD)
    normed = operands[9]
    tokens, width = normed.shape
    qkv_cols = w_qkv.shape[2]
    kv_cols = qkv_cols - width
    dtype = normed.dtype
    float32 = jnp.float32
    dma = pltpu.SemaphoreType.DMA
    vmem = pl.BlockSpec(memory_space=pltpu.VMEM)
    anywhere = pl.BlockSpec(memory_space=pl.ANY)
    columns = qkv_cols // 2 + width // 2
    moves = parts_in is not None
    parts_in = parts_in if moves else jnp.zeros((heads, 16, 128), dtype)
    return pl.pallas_call(
        functools.partial(attention_grad_kernel, layer, moves),
        out_shape=(
            jax.ShapeDtypeStruct((tokens, width), dtype),
            jax.ShapeDtypeStruct((1, 2 * width + qkv_cols), float32),
            jax.ShapeDtypeStruct((width, columns), dtype),
            jax.ShapeDtypeStruct(parts_in.shape, dtype),
        ),
        in_specs=[vmem] * len(operands) + [anywhere] * 3,
        out_specs=(vmem, vmem, anywhere, anywhere),
        scratch_shapes=[
            pltpu.VMEM(w_out.shape[1:], dtype),
            pltpu.VMEM(w_qkv.shape[1:], dtype),
            pltpu.VMEM((tokens, width), float32),
            pltpu.VMEM((tokens, width), dtype),
            pltpu.VMEM((tokens, width), dtype),
            pltpu.VMEM((tokens, qkv_cols), dtype),
            pltpu.VMEM((tokens, width), float32),
            pltpu.VMEM((2 * heads * tokens, kv_cols), float32),
            pltpu.VMEM((width, columns), dtype),
            pltpu.VMEM((tokens, width), dtype),
            pltpu.VMEM((tokens, width), dtype),
            pltpu.VMEM((tokens, width // 2), dtype),
            pltpu.VMEM((tokens, qkv_cols // 2), dtype),
            pltpu.VMEM((heads, tokens, kv_cols), dtype),
            pltpu.VMEM((heads, tokens, kv_cols), dtype),
            pltpu.VMEM((2, heads, tokens, kv_cols), dtype),
            dma((5,)),
            dma((2, 4)),
            dma((2, heads)),
            dma((2, 2, heads)),
            dma((2, heads)),
        ],
        compiler_params=pltpu.CompilerParams(
            collective_id=number, has_side_effects=True, vmem_limit_bytes=60 * 2**20
        ),
        cost_estimate=pl.CostEstimate(
            flops=40 * tokens * width * qkv_cols,
            bytes_accessed=2 * w_out.size + 2 * w_qkv.size,
            transcendentals=0,
        ),
    )(*operands, w_out, w_qkv, parts_in)


def attention_body(
    layer, operands, results, scratch, loads, ready, breath=lambda: None, met=lambda: None
):
    layer_in, small, cosine, sine, own_pos, key_pos = operands
    normed, queries, keyval, log_total, attended, midway, normed2, scale1, scale2 = results
    w_qkv, w_out, mine, own_sem, pair_sem, line_sem = scratch
    section, head = lax.axis_index(SECTION), lax.axis_index(HEAD)
    heads = lax.axis_size(HEAD)
    tokens, width = normed.shape
    kv_width = KV * HDIM
    other = {SECTION: 1 - section}

    def gain(at):
        return small[layer, :, pl.ds(at * width, width)]

    def remote(source, target, sems, at, partner):
        return pltpu.make_async_remote_copy(
            source,
            target,
            sems.at[(0,) + at],
            sems.at[(1,) + at],
            device_id=partner,
            device_id_type=MESH,
        )

    def place(section_at, head_at):
        start = (section_at * heads + head_at) * tokens
        return keyval.at[pl.ds(pl.multiple_of(start, tokens), tokens)]

    def pair(number, head_at, source):
        return remote(source, place(section, head_at), pair_sem, (number,), other)

    def pair_in(number, head_at):
        target = place(1 - section, head_at)
        return remote(target, target, pair_sem, (number,), other)

    def line(way, hop, source):
        step = 1 - 2 * way
        target = place(section, head - step * hop)
        return remote(source, target, line_sem, (way, hop), {HEAD: head + step})

    scale = lax.rsqrt(
        jnp.mean(layer_in[...] * layer_in[...], -1, keepdims=True) + EPSILON
    )
    scale1[...] = scale
    normed[...] = (layer_in[...] * scale * gain(0)).astype(normed.dtype)
    ready()

    def project(start, count):
        span = pl.ds(start, count)
        return (
            jnp.dot(normed[...], w_qkv[:, span], preferred_element_type=jnp.float32)
            + small[layer, :, pl.ds(2 * width + start, count)]
        )

    loads[0].wait()
    for kv in range(KV):
        key = project(width + kv * HDIM, HDIM)
        mine[:, pl.ds(kv * HDIM, HDIM)] = turn(key, cosine[...], sine[...]).astype(mine.dtype)
    mine[:, pl.ds(kv_width, kv_width)] = project(width + kv_width, kv_width).astype(mine.dtype)
    ways = ((0, head < heads - 1), (1, head > 0))
    for way, go in ways:

        @pl.when(go)
        def _(way=way):
            line(way, 0, mine).start()

    pair(0, head, mine).start()
    own = pltpu.make_async_copy(mine, place(section, head), own_sem)
    own.start()
    breath()

    def arrivals(hop):
        yield 0, head - hop, head >= hop, head < heads - 1
        yield 1, head + hop, head + hop < heads, head > 0

    per_hop = HEADS // (heads - 1)
    for hop in range(1, heads):
        start = (hop - 1) * per_hop * HDIM
        block = project(start, per_hop * HDIM)
        for at in range(per_hop):
            query = block[:, at * HDIM : (at + 1) * HDIM]
            queries[(hop - 1) * per_hop + at] = turn(query, cosine[...], sine[...]).astype(
                queries.dtype
            )
        for way, origin, comes, goes in arrivals(hop):

            @pl.when(comes)
            def _(way=way, origin=origin, goes=goes, hop=hop):
                here = place(section, origin)
                line(way, hop - 1, here).wait_recv()

                @pl.when(goes)
                def _():
                    line(way, hop, here).start()

                pair(2 * hop - 1 + way, origin, here).start()

    own.wait()
    pair_in(0, head).wait_recv()
    for hop in range(1, heads):
        for way, origin, comes, goes in arrivals(hop):

            @pl.when(comes)
            def _(way=way, origin=origin, hop=hop):
                pair_in(2 * hop - 1 + way, origin).wait_recv()

    met()
    allowed = own_pos[...] >= key_pos[...]
    allowed = jnp.concatenate([allowed.astype(jnp.int32)] * GROUP, 0) > 0
    groups = HEADS // GROUP
    for group in range(groups):
        kv = group * KV // groups
        query = jnp.concatenate([queries[group * GROUP + at] for at in range(GROUP)], 0)
        key = keyval[:, pl.ds(kv * HDIM, HDIM)]
        value = keyval[:, pl.ds(kv_width + kv * HDIM, HDIM)]
        scores = jnp.where(allowed, contract_last(query, key) * HDIM**-0.5, -1e30)
        highest = jnp.max(scores, -1, keepdims=True)
        weights_exp = jnp.exp(scores - highest)
        partition = jnp.sum(weights_exp, -1, keepdims=True)
        probs = (weights_exp / partition).astype(jnp.bfloat16)
        result = jnp.dot(probs, value, preferred_element_type=jnp.float32)
        total = highest + jnp.log(partition)
        for at in range(GROUP):
            span = slice(at * tokens, (at + 1) * tokens)
            attended[:, pl.ds((group * GROUP + at) * HDIM, HDIM)] = result[span].astype(
                attended.dtype
            )
            log_total[group * GROUP + at] = total[span]

    loads[1].wait()
    for start, count in chunks(width, STEP_WIDTH):
        span = pl.ds(start, count)
        midway[:, span] = layer_in[:, span] + jnp.dot(
            attended[...], w_out[:, span], preferred_element_type=jnp.float32
        )
    scale = lax.rsqrt(jnp.mean(midway[...] * midway[...], -1, keepdims=True) + EPSILON)
    scale2[...] = scale
    normed2[...] = (midway[...] * scale * gain(1)).astype(normed2.dtype)

    pair(0, head, mine).wait_send()
    for way, go in ways:

        @pl.when(go)
        def _(way=way):
            line(way, 0, mine).wait_send()

    for hop in range(1, heads):
        for way, origin, comes, goes in arrivals(hop):

            @pl.when(comes)
            def _(way=way, origin=origin, goes=goes, hop=hop):
                here = place(section, origin)

                @pl.when(goes)
                def _():
                    line(way, hop, here).wait_send()

                pair(2 * hop - 1 + way, origin, here).wait_send()


def attention_kernel(layer, *refs):
    operands, (w_qkv_hbm, w_out_hbm, swap_in), refs = refs[:6], refs[6:9], refs[9:]
    results, swap_out, scratch, (load_sem, swap_sem) = refs[:9], refs[9], refs[10:16], refs[16:]
    section, head = lax.axis_index(SECTION), lax.axis_index(HEAD)
    heads = lax.axis_size(HEAD)
    loads = [
        pltpu.make_async_copy(w_qkv_hbm.at[layer], scratch[0], load_sem.at[0]),
        pltpu.make_async_copy(w_out_hbm.at[layer], scratch[1], load_sem.at[1]),
    ]
    for load in loads:
        load.start()

    def ready():
        barrier = pltpu.get_barrier_semaphore()
        partners = [{SECTION: 1 - section}]
        partners += [{HEAD: lax.rem(head + distance, heads)} for distance in range(1, heads)]
        for partner in partners:
            pl.semaphore_signal(barrier, 1, device_id=partner, device_id_type=MESH)
        pl.semaphore_wait(barrier, len(partners))

    swap = block_swap(swap_in, swap_out, swap_sem, head, 2)
    attention_body(layer, operands, results, scratch, loads, ready, met=swap.start)
    swap.wait()


def attention_shapes(tokens, width, kv_cols, heads, dtype):
    float32 = jnp.float32
    return (
        jax.ShapeDtypeStruct((tokens, width), dtype),
        jax.ShapeDtypeStruct((HEADS, tokens, HDIM), dtype),
        jax.ShapeDtypeStruct((2 * heads * tokens, kv_cols), dtype),
        jax.ShapeDtypeStruct((HEADS, tokens, 1), float32),
        jax.ShapeDtypeStruct((tokens, width), dtype),
        jax.ShapeDtypeStruct((tokens, width), float32),
        jax.ShapeDtypeStruct((tokens, width), dtype),
        jax.ShapeDtypeStruct((tokens, 1), float32),
        jax.ShapeDtypeStruct((tokens, 1), float32),
    )


def attention_scratch(tokens, width, qkv_cols, heads, dtype):
    dma = pltpu.SemaphoreType.DMA
    return [
        pltpu.VMEM((width, qkv_cols), dtype),
        pltpu.VMEM((width, width), dtype),
        pltpu.VMEM((tokens, qkv_cols - width), dtype),
        dma,
        dma((2, 2 * heads - 1)),
        dma((2, 2, heads)),
    ]


def attention_forward(layer, number, w_qkv, w_out, swap_in, *operands):
    heads = lax.axis_size(HEAD)
    tokens, width = operands[0].shape
    qkv_cols = w_qkv.shape[2]
    dtype = w_qkv.dtype
    vmem = pl.BlockSpec(memory_space=pltpu.VMEM)
    anywhere = pl.BlockSpec(memory_space=pl.ANY)
    return pl.pallas_call(
        functools.partial(attention_kernel, layer),
        out_shape=attention_shapes(tokens, width, qkv_cols - width, heads, dtype)
        + (jax.ShapeDtypeStruct(swap_in.shape, dtype),),
        in_specs=[vmem] * len(operands) + [anywhere] * 3,
        out_specs=(vmem,) * 9 + (anywhere,),
        scratch_shapes=attention_scratch(tokens, width, qkv_cols, heads, dtype)
        + [pltpu.SemaphoreType.DMA((2,)), pltpu.SemaphoreType.DMA((2,))],
        compiler_params=pltpu.CompilerParams(
            collective_id=number, has_side_effects=True, vmem_limit_bytes=60 * 2**20
        ),
        cost_estimate=pl.CostEstimate(
            flops=20 * tokens * width * qkv_cols,
            bytes_accessed=2 * w_out.size + 2 * w_qkv.size,
            transcendentals=0,
        ),
    )(*operands, w_qkv, w_out, swap_in)


def local_grouped(
    inputs,
    cotangent,
    norm_gains,
    qkv_weight,
    qkv_bias,
    out_weight,
    gate_weight,
    up_weight,
    down_weight,
):
    head_count = lax.axis_size(HEAD)
    wide_count = lax.axis_size(WIDE)
    section_count = lax.axis_size(SECTION)
    section = lax.axis_index(SECTION)
    head = lax.axis_index(HEAD)
    micro_count, short_len, width = inputs.shape
    half_len = short_len // section_count
    tokens = wide_count * half_len
    rows = qkv_weight.shape[1]
    query_width = HEADS * HDIM
    kv_width = KV * HDIM
    qkv_cols = qkv_weight.shape[2]
    ff_cols = gate_weight.shape[2]
    parts = section_count * head_count
    part_cols = -(-ff_cols // (parts * 128)) * 128

    def inner(array):
        split = array.shape[:-1] + (head_count, wide_count, rows)
        return jnp.swapaxes(array.reshape(split), -3, -2).reshape(array.shape)

    def outer(array):
        split = array.shape[:-1] + (wide_count, head_count, rows)
        return jnp.swapaxes(array.reshape(split), -3, -2).reshape(array.shape)

    sides = jnp.stack(
        [
            lax.dynamic_slice_in_dim(each, section * half_len, half_len, 1)
            for each in (inputs, cotangent)
        ]
    )
    mlp_parts, out_own, sides, small_own = cut_parts(
        gate_weight[0],
        up_weight[0],
        down_weight[0],
        out_weight[0],
        sides.reshape(-1, width),
        norm_gains[0],
        qkv_bias,
        parts,
        part_cols,
    )
    order = np.indices((section_count, head_count, wide_count, half_len)).reshape(4, -1)
    key_pos = (order[1] * wide_count + order[2]) * short_len + order[0] * half_len + order[3]
    half_dim = HDIM // 2
    angles = key_pos[:, None] * ROPE_BASE ** (-np.arange(half_dim) / half_dim)
    tables = np.concatenate([np.cos(angles)] * 2 + [np.sin(angles), -np.sin(angles)], 1)
    first_row = (section * head_count + head) * tokens
    own_table = lax.dynamic_slice_in_dim(jnp.asarray(tables, jnp.float32), first_row, tokens, 0)
    head_cosine, head_sine = own_table[:, :HDIM], own_table[:, HDIM:]
    key_pos = jnp.asarray(key_pos, jnp.int32)
    own_pos = lax.dynamic_slice_in_dim(key_pos, first_row, tokens, 0)
    tables = (head_cosine, -head_sine, own_pos[:, None], key_pos[None, :])

    (
        qkv_weights,
        out_weights,
        first_mlp,
        second_parts,
        tokens_in,
        last_grad,
        grad_near,
        grad_far,
        small,
        *first_attention,
    ) = start_weights(
        5,
        qkv_weight[0],
        out_own,
        mlp_parts.reshape(section_count, head_count, rows, 3 * part_cols),
        sides.reshape(2, micro_count, half_len, width),
        small_own,
        *tables,
    )
    second_mlp = lax.all_gather(second_parts, WIDE, axis=0).reshape(width, 3 * part_cols)
    mlp_weights = [first_mlp, second_mlp]

    layer_in = tokens_in.astype(jnp.float32)

    records = []
    outputs_list = []
    for layer in range(section_count):
        attention = first_attention
        if layer > 0:
            *attention, grad_mid = attention_forward(
                layer, 8, qkv_weights, out_weights, last_grad, layer_in, small, *tables
            )
        (
            normed,
            queries,
            keyval,
            log_total,
            attended,
            midway,
            normed2,
            scale_first,
            scale_second,
        ) = attention
        w_mlp = mlp_weights[layer]
        if layer == section_count - 1:
            grads = (last_grad, grad_near, grad_mid, grad_far)
            mlp_out, d_normed2, mlp_term = turning_point(normed2, w_mlp, grads, 1)
            gate_up = hidden = None
        else:
            mlp_out, normed2, gate_up, hidden = feed_forward(normed2, w_mlp, 9)
        result = midway + mlp_out
        records.append(
            (
                layer_in,
                scale_first,
                normed,
                queries,
                keyval,
                log_total,
                attended,
                midway,
                scale_second,
                normed2,
                gate_up,
                hidden,
            )
        )
        carried = result.astype(jnp.bfloat16)
        outputs_list.append(carried)
        layer_in = carried.astype(jnp.float32)

    out_grad = last_grad
    grads_list = [None] * section_count
    attention_terms = [None] * section_count
    small_terms = [None] * section_count
    for layer in reversed(range(section_count)):
        w_mlp = mlp_weights[layer]
        (
            layer_in,
            scale_first,
            normed,
            queries,
            keyval,
            log_total,
            attended,
            midway,
            scale_second,
            normed2,
            gate_up,
            hidden,
        ) = records[layer]
        if layer < section_count - 1:
            d_normed2, mlp_term = feed_backward(out_grad, w_mlp, gate_up, normed2, hidden, 3)
        mlp_term = mlp_term.reshape(wide_count, head_count, rows, -1)
        mlp_sum = lax.psum_scatter(mlp_term, WIDE, scatter_dimension=0)
        if layer == 1:
            second_sum = lax.optimization_barrier(mlp_sum)
        out_grad, small_terms[layer], attention_terms[layer], second_parts = attention_grad(
            layer,
            (4, 7)[layer],
            out_weights,
            qkv_weights,
            second_sum if layer == 0 else None,
            d_normed2,
            midway,
            scale_second,
            out_grad,
            small,
            queries,
            keyval,
            log_total,
            attended,
            normed,
            layer_in,
            scale_first,
            head_cosine,
            head_sine,
            *tables[2:],
        )
        grads_list[layer] = out_grad

    sides = jnp.stack([outer(each) for each in outputs_list + grads_list])
    totals, small_total, low_parts, high_parts, owned = finish_weights(
        *[term.reshape(wide_count * head_count, rows, -1) for term in attention_terms],
        jnp.stack(small_terms),
        mlp_sum,
        second_parts,
        sides.reshape(2 * section_count, wide_count, half_len, width),
        6,
    )
    gate_grad, up_grad, down_grad, qkv_grad, out_weight_grad, gains_grad, bias_grad = join_parts(
        low_parts, high_parts, totals, small_total, ff_cols, qkv_cols
    )
    return (
        owned[:1],
        owned[1:],
        gains_grad,
        qkv_grad,
        bias_grad,
        out_weight_grad,
        gate_grad,
        up_grad,
        down_grad,
    )


def local(inputs, *rest):
    sizes = [lax.axis_size(axis) for axis in (SECTION, HEAD, WIDE)]
    if sizes == [2, 4, 4] and inputs.shape[0] == 4:
        return local_grouped(inputs, *rest)
    return local_streamed(inputs, *rest)


def solution(mesh):
    return jax.shard_map(
        local,
        mesh=mesh,
        in_specs=(
            P(None, (HEAD, WIDE), None),
            P(None, (HEAD, WIDE), None),
            P(SECTION, None, None),
            P(SECTION, (HEAD, WIDE), None),
            P(SECTION, None),
            P(SECTION, (HEAD, WIDE), None),
            P(SECTION, (HEAD, WIDE), None),
            P(SECTION, (HEAD, WIDE), None),
            P(SECTION, (HEAD, WIDE), None),
        ),
        out_specs=(
            P(SECTION, None, (HEAD, WIDE), None),
            P(SECTION, None, (HEAD, WIDE), None),
            P(SECTION, None, None),
            P(SECTION, (HEAD, WIDE), None),
            P(SECTION, None),
            P(SECTION, (HEAD, WIDE), None),
            P(SECTION, (HEAD, WIDE), None),
            P(SECTION, (HEAD, WIDE), None),
            P(SECTION, (HEAD, WIDE), None),
        ),
        check_vma=False,
    )
```

```python
import functools
from typing import NamedTuple

import jax
import jax.numpy as jnp
import numpy as np
from jax import lax
from jax.experimental import pallas as pl
from jax.experimental.pallas import tpu as pltpu
from jax.sharding import PartitionSpec as P

HEADS = 12
KV = 2
HDIM = 128


EPSILON = 1e-06
MESH = pl.DeviceIdType.MESH
CUTS = 2
SECTION = "section"
HEAD = "head"
WIDE = "wide"
ROPE_BASE = 1000000.0


class Record(NamedTuple):
    layer_in: jax.Array
    scale_first: jax.Array
    normed: jax.Array
    query_rows: jax.Array
    kv_local: jax.Array
    log_total: jax.Array
    out_seq: jax.Array
    midway: jax.Array
    scale_second: jax.Array
    normed2: jax.Array
    gate_out: jax.Array
    up_out: jax.Array
    hidden: jax.Array


def passed_along(block, axis, distance):
    devices = range(lax.axis_size(axis))
    route = [(i - distance, i) for i in devices if i - distance in devices]
    return lax.ppermute(block, axis, route)


def rotary_tables(positions, head_dim):
    half_dim = head_dim // 2
    frequency = ROPE_BASE ** (-jnp.arange(half_dim, dtype=jnp.float32) / half_dim)
    angles = positions[:, None] * frequency[None, :]
    return (jnp.cos(angles)[:, None, :], jnp.sin(angles)[:, None, :])


def rotate_pairs(tensor, cosine, sine_table):
    half_dim = tensor.shape[-1] // 2
    first_half = tensor[..., :half_dim]
    second_half = tensor[..., half_dim:]
    return jnp.concatenate(
        [
            first_half * cosine - second_half * sine_table,
            second_half * cosine + first_half * sine_table,
        ],
        -1,
    )


def rotate_back(tensor, cosine, sine_table):
    half_dim = tensor.shape[-1] // 2
    first_half = tensor[..., :half_dim]
    second_half = tensor[..., half_dim:]
    return jnp.concatenate(
        [
            first_half * cosine + second_half * sine_table,
            second_half * cosine - first_half * sine_table,
        ],
        -1,
    )


def contract_last(left, right):
    return lax.dot_general(
        left, right, (((1,), (1,)), ((), ())), preferred_element_type=jnp.float32
    )


def contract_first(left, right):
    return lax.dot_general(
        left, right, (((0,), (0,)), ((), ())), preferred_element_type=jnp.float32
    )


def attention_scores(query_rows, key_value, query_pos, key_pos):
    head_dim = query_rows.shape[1]
    scores = contract_last(query_rows, key_value[:, :head_dim]) * head_dim ** (-0.5)
    return jnp.where(query_pos[:, None] >= key_pos[None, :], scores, -1e30)


def attend_forward(query_rows, key_value, query_pos, key_pos):
    head_dim = query_rows.shape[1]
    scores = attention_scores(query_rows, key_value, query_pos, key_pos)
    highest = jnp.max(scores, -1, keepdims=True)
    weights_exp = jnp.exp(scores - highest)
    partition = jnp.sum(weights_exp, -1, keepdims=True)
    probs_low = (weights_exp / partition).astype(jnp.bfloat16)
    attended = jnp.dot(probs_low, key_value[:, head_dim:], preferred_element_type=jnp.float32)
    return (attended.astype(jnp.bfloat16), highest + jnp.log(partition))


def attend_backward(query_rows, key_value, query_pos, key_pos, log_total, grad_rows):
    head_dim = query_rows.shape[1]
    scaling = head_dim ** (-0.5)
    scores = attention_scores(query_rows, key_value, query_pos, key_pos)
    probs_full = jnp.exp(scores - log_total)
    grad_probs = contract_last(grad_rows, key_value[:, head_dim:])
    row_dot = jnp.sum(probs_full * grad_probs, -1, keepdims=True)
    grad_scores = (probs_full * (grad_probs - row_dot)).astype(jnp.bfloat16)
    grad_query = (
        jnp.dot(grad_scores, key_value[:, :head_dim], preferred_element_type=jnp.float32) * scaling
    )
    grad_key = contract_first(grad_scores, query_rows) * scaling
    grad_value = contract_first(probs_full.astype(jnp.bfloat16), grad_rows)
    return (grad_query, jnp.concatenate([grad_key, grad_value], 1))


def make_terms(operands, factor):
    (
        normed_all,
        dqkv_all,
        attended_all,
        gattn_all,
        normed2_all,
        dgate_all,
        dup_all,
        gmlp_all,
        hidden_all,
    ) = operands
    pairs = [
        (normed_all, dqkv_all),
        (attended_all, gattn_all),
        (normed2_all, dgate_all),
        (normed2_all, dup_all),
        (gmlp_all, hidden_all),
    ]
    scaled_pairs = [
        (left, (right.astype(jnp.float32) * factor).astype(jnp.bfloat16)) for left, right in pairs
    ]

    def weight_terms(start, count):
        pieces = [contract_first(left, right) for left, right in scaled_pairs]
        return jnp.concatenate(pieces, 1)

    return weight_terms


def local_streamed(
    inputs,
    cotangent,
    norm_gains,
    qkv_weight,
    qkv_bias,
    out_weight,
    gate_weight,
    up_weight,
    down_weight,
):
    head_count = lax.axis_size(HEAD)
    wide_count = lax.axis_size(WIDE)
    section_pos = lax.axis_index(SECTION)
    head_pos = lax.axis_index(HEAD)
    wide_pos = lax.axis_index(WIDE)
    micro_count, short_len, width = inputs.shape
    group_size = HEADS // head_count
    slot_rep = head_count // KV
    query_width = HEADS * HDIM
    kv_width = KV * HDIM
    local_rows = head_count * short_len
    seq_len = local_rows * wide_count
    gain_first = norm_gains[0, 0]
    gain_second = norm_gains[0, 1]
    bias_row = qkv_bias[0]
    seq_pos = (
        (head_pos * wide_count + wide_pos) * short_len + jnp.arange(short_len, dtype=jnp.int32)
    ).astype(jnp.float32)
    cosine, sine_table = rotary_tables(seq_pos, HDIM)
    local_index = jnp.arange(local_rows, dtype=jnp.int32)
    query_pos = jnp.tile(
        (local_index // short_len * wide_count + wide_pos) * short_len + local_index % short_len,
        group_size,
    )
    key_index = jnp.arange(seq_len, dtype=jnp.int32)
    key_pos = (
        key_index % local_rows // short_len * wide_count + key_index // local_rows
    ) * short_len + key_index % short_len

    def to_rows(packed):
        return (
            packed.reshape(local_rows, group_size, HDIM)
            .transpose(1, 0, 2)
            .reshape(group_size * local_rows, HDIM)
        )

    def from_rows(rows_in):
        return (
            rows_in.reshape(group_size, local_rows, HDIM)
            .transpose(1, 0, 2)
            .reshape(local_rows, 1, group_size * HDIM)
        )

    weights_fwd = (
        lax.all_gather(qkv_weight[0], (HEAD, WIDE), axis=0, tiled=True),
        lax.all_gather(out_weight[0], (HEAD, WIDE), axis=0, tiled=True),
        lax.all_gather(gate_weight[0], (HEAD, WIDE), axis=0, tiled=True),
        lax.all_gather(up_weight[0], (HEAD, WIDE), axis=0, tiled=True),
        lax.all_gather(down_weight[0], (HEAD, WIDE), axis=0, tiled=True),
    )
    incoming = jnp.zeros((short_len, width), jnp.bfloat16)
    records = []
    outputs_list = []
    for step_index in range(micro_count + 1):
        own_input = inputs[min(step_index, micro_count - 1)]
        layer_in = jnp.where(section_pos == 0, own_input, incoming).astype(jnp.float32)
        layer_w_qkv, layer_w_out, layer_w_gate, layer_w_up, layer_w_down = weights_fwd
        scale_first = lax.rsqrt(jnp.mean(layer_in * layer_in, -1, keepdims=True) + EPSILON)
        normed = (layer_in * scale_first * gain_first).astype(jnp.bfloat16)
        qkv = jnp.dot(normed, layer_w_qkv, preferred_element_type=jnp.float32) + bias_row
        queries = rotate_pairs(
            qkv[:, :query_width].reshape(short_len, HEADS, HDIM), cosine, sine_table
        ).astype(jnp.bfloat16)
        key_heads = rotate_pairs(
            qkv[:, query_width : query_width + kv_width].reshape(short_len, KV, HDIM),
            cosine,
            sine_table,
        ).astype(jnp.bfloat16)
        value_heads = (
            qkv[:, query_width + kv_width :].reshape(short_len, KV, HDIM).astype(jnp.bfloat16)
        )
        kv_pack = jnp.repeat(jnp.stack([key_heads, value_heads], 2), slot_rep, axis=1).reshape(
            short_len, head_count, 2 * HDIM
        )
        q_pack = queries.reshape(short_len, head_count, group_size * HDIM)
        q_heads = lax.all_to_all(q_pack, HEAD, split_axis=1, concat_axis=0, tiled=True)
        kv_heads = lax.all_to_all(kv_pack, HEAD, split_axis=1, concat_axis=0, tiled=True)
        query_rows = to_rows(q_heads)
        kv_local = kv_heads.reshape(local_rows, 2 * HDIM)
        layer_kv_all = lax.all_gather(kv_local, WIDE, axis=0, tiled=True)
        out_rows, log_total = attend_forward(query_rows, layer_kv_all, query_pos, key_pos)
        out_seq = lax.all_to_all(
            from_rows(out_rows), HEAD, split_axis=0, concat_axis=1, tiled=True
        ).reshape(short_len, query_width)
        midway = layer_in + jnp.dot(out_seq, layer_w_out, preferred_element_type=jnp.float32)
        scale_second = lax.rsqrt(jnp.mean(midway * midway, -1, keepdims=True) + EPSILON)
        normed2 = (midway * scale_second * gain_second).astype(jnp.bfloat16)
        layer_gate_out = jnp.dot(normed2, layer_w_gate, preferred_element_type=jnp.float32)
        up_out = jnp.dot(normed2, layer_w_up, preferred_element_type=jnp.float32)
        hidden = (jax.nn.silu(layer_gate_out) * up_out).astype(jnp.bfloat16)
        result = midway + contract_last(hidden, layer_w_down)
        record = Record(
            layer_in=layer_in,
            scale_first=scale_first,
            normed=normed,
            query_rows=query_rows,
            kv_local=kv_local,
            log_total=log_total,
            out_seq=out_seq,
            midway=midway,
            scale_second=scale_second,
            normed2=normed2,
            gate_out=layer_gate_out,
            up_out=up_out,
            hidden=hidden,
        )
        result, record = (result, record)
        sent_value = result.astype(jnp.bfloat16)
        records.append(record)
        outputs_list.append(sent_value)
        if step_index < micro_count:
            incoming = passed_along(sent_value, SECTION, 1)
    stacked_records = jax.tree.map(lambda *arrays: jnp.stack(arrays), *records)
    section_outputs = lax.dynamic_slice_in_dim(
        jnp.stack(outputs_list), section_pos, micro_count, 0
    )[None]
    weights_back = (
        lax.all_gather(qkv_weight[0], (HEAD, WIDE), axis=0, tiled=True),
        lax.all_gather(out_weight[0], (HEAD, WIDE), axis=0, tiled=True),
        lax.all_gather(gate_weight[0], (HEAD, WIDE), axis=0, tiled=True),
        lax.all_gather(up_weight[0], (HEAD, WIDE), axis=0, tiled=True),
        lax.all_gather(down_weight[0], (HEAD, WIDE), axis=0, tiled=True),
    )
    owned_rows = qkv_weight.shape[1]
    qkv_cols = qkv_weight.shape[2]
    ff_cols = gate_weight.shape[2]
    incoming_grad = jnp.zeros((short_len, width), jnp.bfloat16)
    small_totals = (
        jnp.zeros((width,), jnp.float32),
        jnp.zeros((width,), jnp.float32),
        jnp.zeros((bias_row.shape[0],), jnp.float32),
    )
    grads_list = []
    kept_list = []
    for step_index in range(micro_count + 1):
        pick = jnp.clip(step_index - 1 + 2 * section_pos, 0, micro_count)
        record = jax.tree.map(
            lambda array: lax.dynamic_index_in_dim(array, pick, 0, keepdims=False), stacked_records
        )
        own_grad = cotangent[min(step_index, micro_count - 1)]
        out_grad = jnp.where(section_pos == 1, own_grad, incoming_grad).astype(jnp.float32)
        w_qkv, w_out, w_gate, w_up, w_down = weights_back
        g_mlp = out_grad.astype(jnp.bfloat16)
        d_hidden = jnp.dot(g_mlp, w_down, preferred_element_type=jnp.float32)
        gate_out = record.gate_out
        sigmoid_gate = jax.nn.sigmoid(gate_out)
        d_gate = (
            d_hidden * record.up_out * sigmoid_gate * (1.0 + gate_out * (1.0 - sigmoid_gate))
        ).astype(jnp.bfloat16)
        d_up = (d_hidden * gate_out * sigmoid_gate).astype(jnp.bfloat16)
        d_normed2 = contract_last(d_gate, w_gate) + contract_last(d_up, w_up)
        unit_second = record.midway * record.scale_second
        gain2_grad = jnp.sum(d_normed2 * unit_second, 0)
        dn_second = d_normed2 * gain_second
        d_midway = (
            record.scale_second
            * (dn_second - unit_second * jnp.mean(dn_second * unit_second, -1, keepdims=True))
            + out_grad
        )
        g_attn = d_midway.astype(jnp.bfloat16)
        d_out_seq = contract_last(g_attn, w_out).astype(jnp.bfloat16)
        d_out_heads = lax.all_to_all(
            d_out_seq.reshape(short_len, head_count, group_size * HDIM),
            HEAD,
            split_axis=1,
            concat_axis=0,
            tiled=True,
        )
        kv_all = lax.all_gather(record.kv_local, WIDE, axis=0, tiled=True)
        grad_query, grad_keyval = attend_backward(
            record.query_rows,
            kv_all,
            query_pos,
            key_pos,
            record.log_total,
            to_rows(d_out_heads),
        )
        keyval_local = lax.psum_scatter(
            grad_keyval.astype(jnp.bfloat16), WIDE, scatter_dimension=0, tiled=True
        )
        q_back = lax.all_to_all(
            from_rows(grad_query.astype(jnp.bfloat16)),
            HEAD,
            split_axis=0,
            concat_axis=1,
            tiled=True,
        )
        kv_back = lax.all_to_all(
            keyval_local.reshape(local_rows, 1, 2 * HDIM),
            HEAD,
            split_axis=0,
            concat_axis=1,
            tiled=True,
        )
        d_queries = rotate_back(
            q_back.astype(jnp.float32).reshape(short_len, HEADS, HDIM), cosine, sine_table
        )
        d_kv = jnp.sum(kv_back.astype(jnp.float32).reshape(short_len, KV, slot_rep, 2, HDIM), 2)
        d_keys = rotate_back(d_kv[:, :, 0], cosine, sine_table)
        d_qkv = jnp.concatenate(
            [
                d_queries.reshape(short_len, query_width),
                d_keys.reshape(short_len, kv_width),
                d_kv[:, :, 1].reshape(short_len, kv_width),
            ],
            1,
        ).astype(jnp.bfloat16)
        bias_grad = jnp.sum(d_qkv.astype(jnp.float32), 0)
        d_normed = contract_last(d_qkv, w_qkv)
        unit_first = record.layer_in * record.scale_first
        gain1_grad = jnp.sum(d_normed * unit_first, 0)
        dn_first = d_normed * gain_first
        d_layer_in = (
            record.scale_first
            * (dn_first - unit_first * jnp.mean(dn_first * unit_first, -1, keepdims=True))
            + d_midway
        )
        kept_grads = (
            record.normed,
            d_qkv,
            record.out_seq,
            g_attn,
            record.normed2,
            d_gate,
            d_up,
            g_mlp,
            record.hidden,
        )
        d_layer_in, kept_grads, small_parts = (
            d_layer_in,
            kept_grads,
            (gain1_grad, gain2_grad, bias_grad),
        )
        is_valid = jnp.where(
            (step_index - 1 + section_pos >= 0) & (step_index - 1 + section_pos < micro_count),
            1.0,
            0.0,
        )
        small_totals = jax.tree.map(
            lambda total_part, new_part: total_part + is_valid * new_part, small_totals, small_parts
        )
        sent_grad = d_layer_in.astype(jnp.bfloat16)
        grads_list.append(sent_grad)
        kept_list.append(kept_grads)
        if step_index < micro_count:
            incoming_grad = passed_along(sent_grad, SECTION, -1)
    input_grads = lax.dynamic_slice_in_dim(jnp.stack(grads_list), 1 - section_pos, micro_count, 0)[
        None
    ]
    operands = jax.tree.map(
        lambda *arrays: lax.dynamic_slice_in_dim(
            jnp.stack(arrays), 1 - section_pos, micro_count, 0
        ).reshape(micro_count * short_len, arrays[0].shape[1]),
        *kept_list
    )
    terms = lax.psum_scatter(
        make_terms(operands, 1.0)(jnp.int32(0), owned_rows * lax.axis_size((HEAD, WIDE))),
        (HEAD, WIDE),
        scatter_dimension=0,
        tiled=True,
    )
    qkv_grad = terms[:, :qkv_cols]
    out_grad_rows = terms[:, qkv_cols : qkv_cols + width]
    gate_grad = terms[:, qkv_cols + width : qkv_cols + width + ff_cols]
    up_grad = terms[:, qkv_cols + width + ff_cols : qkv_cols + width + 2 * ff_cols]
    down_grad = terms[:, qkv_cols + width + 2 * ff_cols :]
    gain1_total, gain2_total, bias_total = lax.psum(
        (small_totals[0], small_totals[1], small_totals[2]), (HEAD, WIDE)
    )
    gains_grad = jnp.stack([gain1_total, gain2_total])[None]
    return (
        section_outputs,
        input_grads,
        gains_grad,
        qkv_grad[None],
        bias_total[None],
        out_grad_rows[None],
        gate_grad[None],
        up_grad[None],
        down_grad[None],
    )


def greet_all(heads):
    section, head, wide = (lax.axis_index(axis) for axis in (SECTION, HEAD, WIDE))
    barrier = pltpu.get_barrier_semaphore()
    partners = [{SECTION: 1 - section}] + [{WIDE: beside(wide, axis)} for axis in (0, 1, 2)]
    partners += [{HEAD: lax.rem(head + shift, heads)} for shift in range(1, heads)]
    for partner in partners:
        pl.semaphore_signal(barrier, 1, device_id=partner, device_id_type=MESH)
    pl.semaphore_wait(barrier, len(partners))


def beside(wide, axis):
    low, high = lax.rem(wide, 2), lax.div(wide, 2)
    if axis == 0:
        return high * 2 + (1 - low)
    if axis == 1:
        return (1 - high) * 2 + low
    return (1 - high) * 2 + (1 - low)


def start_kernel(
    qkv_own,
    out_own,
    parts,
    sides,
    small_own,
    cosine,
    sine,
    own_pos,
    key_pos,
    qkv_all,
    out_all,
    first_all,
    second_parts,
    tokens_in,
    grad_in,
    grad_near,
    grad_far,
    small_all,
    *refs,
):
    results, refs = refs[:9], refs[9:]
    scratch, refs = refs[:6], refs[6:]
    (
        block,
        layer_in,
        given_first,
        given_second,
        small_sem,
        local_sem,
        swap_sem,
        shift_sem,
        line_sem,
        wide_sem,
        half_sem,
        pair_sem,
        token_sem,
        near_sem,
    ) = refs
    section, head, wide = (lax.axis_index(axis) for axis in (SECTION, HEAD, WIDE))
    heads, wides = lax.axis_size(HEAD), lax.axis_size(WIDE)
    rows = qkv_own.shape[0]
    half = rows // 2
    owns = (qkv_own, out_own)
    here = [beside(wide, 0), beside(wide, 1), beside(wide, 2)]

    def place(which, layer, head_at, wide_at, start=0, count=None):
        block = head_at * wides + wide_at if which == 1 else wide_at * heads + head_at
        first = pl.multiple_of(block * rows + start, 16)
        span = pl.ds(first, rows if count is None else count)
        return first_all.at[span] if which == 2 else (qkv_all, out_all)[which].at[layer, span]

    def remote(source, target, sems, at, partner):
        return pltpu.make_async_remote_copy(
            source,
            target,
            sems.at[(0,) + at],
            sems.at[(1,) + at],
            device_id=partner,
            device_id_type=MESH,
        )

    other = {SECTION: 1 - section}

    def line(which, way, hop):
        step = 1 if way == 0 else -1
        target = place(which, section, head - step * hop, wide)
        source = owns[which] if hop == 0 else target
        return remote(source, target, line_sem, (which, way, hop), {HEAD: head + step})

    def across(which, axis, number, origin):
        target = place(which, section, origin, wide)
        source = owns[which] if number == 0 and which < 2 else target
        return remote(source, target, wide_sem, (which, axis, number), {WIDE: here[axis]})

    def across_in(which, axis, number, origin):
        target = place(which, section, origin, here[axis])
        return remote(target, target, wide_sem, (which, axis, number), {WIDE: here[axis]})

    def diagonal(which, axis, number, origin):
        target = place(which, section, origin, here[1 - axis], (1 - axis) * half, half)
        return remote(target, target, half_sem, (which, axis, number), {WIDE: here[axis]})

    def diagonal_in(which, axis, number, origin):
        target = place(which, section, origin, here[2], (1 - axis) * half, half)
        return remote(target, target, half_sem, (which, axis, number), {WIDE: here[axis]})

    def pair(which, kind, number, origin, layer):
        if kind == 0:
            target = place(which, layer, origin, wide)
        elif kind in (1, 2):
            target = place(which, layer, origin, here[kind - 1])
        else:
            target = place(which, layer, origin, here[2], (4 - kind) * half, half)
        return remote(target, target, pair_sem, (which, kind, number), other)

    def pair_own(which):
        target = place(which, section, head, wide)
        return remote(owns[which], target, pair_sem, (which, 0, 0), other)

    def swap(target):
        return remote(parts.at[1 - section], target, swap_sem, (), other)

    def shift(layer, source, distance):
        target_head = lax.rem(head + distance, heads)
        target = place(2, 0, head, wide) if layer == 0 else second_parts.at[head]
        return remote(
            source.at[target_head], target, shift_sem, (layer, distance), {HEAD: target_head}
        )

    def shift_in(layer, distance):
        origin = lax.rem(head + heads - distance, heads)
        target = place(2, 0, origin, wide) if layer == 0 else second_parts.at[origin]
        return remote(target, target, shift_sem, (layer, distance), {HEAD: head})

    def shift_all(layer, source):
        for here_at in range(heads):

            @pl.when(head == here_at)
            def _(here_at=here_at):
                others = [at for at in range(heads) if at != here_at]
                for at in sorted(others, key=lambda at: abs(at - here_at)):
                    shift(layer, source, (at - here_at) % heads).start()

        target = place(2, 0, head, wide) if layer == 0 else second_parts.at[head]
        pltpu.make_async_copy(source.at[head], target, local_sem.at[2 + layer]).start()

    def shift_own(layer):
        target = place(2, 0, head, wide) if layer == 0 else second_parts.at[head]
        return pltpu.make_async_copy(target, target, local_sem.at[2 + layer])

    shares = (tokens_in, grad_in)
    share_rows = sides.shape[2]
    tokens = grad_in.shape[0]

    def share(which, wide_at):
        return shares[which].at[pl.ds(pl.multiple_of(wide_at * share_rows, 16), share_rows)]

    def token(which, axis):
        source = sides.at[which, here[axis]]
        return remote(source, share(which, wide), token_sem, (which, axis), {WIDE: here[axis]})

    def token_in(which, axis):
        target = share(which, here[axis])
        return remote(target, target, token_sem, (which, axis), {WIDE: here[axis]})

    def token_own(which):
        return pltpu.make_async_copy(
            sides.at[which, wide], share(which, wide), local_sem.at[4 + which]
        )

    def swaps():
        yield block_swap(grad_in, grad_near, near_sem.at[0], head, 1)
        yield block_swap(grad_in, grad_far, near_sem.at[1], head, 3)

    greet_all(heads)
    first = section == 0
    second = section == 1

    for which in (0, 1):
        for way, go in ((0, head < heads - 1), (1, head > 0)):

            @pl.when(go)
            def _(which=which, way=way):
                line(which, way, 0).start()

    for which in (0, 1):
        for axis in (0, 1, 2):
            token(which, axis).start()
        token_own(which).start()

    small_all[section] = small_own[...]
    small_give = remote(small_own, small_all.at[section], small_sem, (), other)
    small_give.start()

    @pl.when(first)
    def _():
        swap(given_first).start()

    @pl.when(second)
    def _():
        swap(given_second).start()

    locals_ = [
        pltpu.make_async_copy(owns[which], place(which, section, head, wide), local_sem.at[which])
        for which in (0, 1)
    ]
    for which in (0, 1):
        locals_[which].start()
        for axis in (0, 1):
            across(which, axis, 0, head).start()
        pair_own(which).start()

    def each(hop):
        yield 2 * hop - 1, 0, head - hop, head >= hop, head < heads - 1
        yield 2 * hop, 1, head + hop, head + hop < heads, head > 0

    def forward_halves(number, origin):
        for which in (0, 1):
            for axis in (0, 1):
                across_in(which, axis, number, origin).wait_recv()
                diagonal(which, 1 - axis, number, origin).start()
                pair(which, 1 + axis, number, origin, section).start()

    def finish_halves(number, origin):
        for which in (0, 1):
            for axis in (0, 1):
                diagonal_in(which, axis, number, origin).wait_recv()
                pair(which, 3 + axis, number, origin, section).start()

    for hop in range(1, heads):
        for number, way, origin, comes, goes in each(hop):

            @pl.when(comes)
            def _(number=number, way=way, origin=origin, goes=goes, hop=hop):
                for which in (0, 1):
                    arrived = place(which, section, origin, wide)
                    remote(
                        arrived, arrived, line_sem, (which, way, hop - 1), {HEAD: head}
                    ).wait_recv()

                    @pl.when(goes)
                    def _(which=which):
                        line(which, way, hop).start()

                    for axis in (0, 1):
                        across(which, axis, number, origin).start()
                    pair(which, 0, number, origin, section).start()

        if hop == 1:
            forward_halves(0, head)
        else:
            for number, way, origin, comes, goes in each(hop - 1):

                @pl.when(comes)
                def _(number=number, origin=origin):
                    forward_halves(number, origin)

    @pl.when(first)
    def _():
        swap(given_second).wait_recv()
        shift_all(0, parts.at[0])

    @pl.when(second)
    def _():
        swap(given_first).wait_recv()
        shift_all(0, given_first)

    for number, way, origin, comes, goes in each(heads - 1):

        @pl.when(comes)
        def _(number=number, origin=origin):
            forward_halves(number, origin)

    def spread(number):
        for axis in (0, 1):
            across(2, axis, number, lax.rem(head + heads - number, heads)).start()

    shift_own(0).wait()
    spread(0)
    finish_halves(0, head)
    for hop in range(1, heads):
        for number, way, origin, comes, goes in each(hop):

            @pl.when(comes)
            def _(number=number, origin=origin):
                finish_halves(number, origin)

    for distance in range(1, heads):
        shift_in(0, distance).wait_recv()
        spread(distance)

    for which in (0, 1):
        token_own(which).wait()
        for axis in (0, 1, 2):
            token_in(which, axis).wait_recv()
            token(which, axis).wait_send()

    def forward_part(number):
        origin = lax.rem(head + heads - number, heads)
        for axis in (0, 1):
            across_in(2, axis, number, origin).wait_recv()
            diagonal(2, 1 - axis, number, origin).start()

    def received(number, origin):
        for which in (0, 1):
            for kind in range(5):
                pair(which, kind, number, origin, 1 - section).wait_recv()

    def all_received():
        received(0, head)
        for hop in range(1, heads):
            for number, way, origin, comes, goes in each(hop):

                @pl.when(comes)
                def _(number=number, origin=origin):
                    received(number, origin)

    pl.when(second)(all_received)
    for which in (0, 1):
        locals_[which].wait()
    loads = [
        pltpu.make_async_copy(qkv_all.at[0], scratch[0], local_sem.at[7]),
        pltpu.make_async_copy(out_all.at[0], scratch[1], local_sem.at[8]),
    ]
    fetch = pltpu.make_async_copy(tokens_in, block, local_sem.at[9])
    for load in loads:
        load.start()
    fetch.start()
    fetch.wait()
    layer_in[...] = block[...].astype(jnp.float32)
    small_give.wait_send()
    small_theirs = small_all.at[1 - section]
    remote(small_theirs, small_theirs, small_sem, (), other).wait_recv()
    operands = (layer_in, small_all, cosine, sine, own_pos, key_pos)

    def met():
        @pl.when(first)
        def _():
            shift_all(1, given_second)

        @pl.when(second)
        def _():
            shift_all(1, parts.at[1])

        for swap_block in swaps():
            swap_block.start()
        forward_part(1)

    attention_body(
        0, operands, results, scratch, loads, lambda: None, lambda: forward_part(0), met
    )
    for number in range(2, heads):
        forward_part(number)

    for number in range(heads):
        origin = lax.rem(head + heads - number, heads)
        for axis in (0, 1):
            diagonal_in(2, axis, number, origin).wait_recv()
            diagonal(2, axis, number, origin).wait_send()
            across(2, axis, number, origin).wait_send()

    def settle(number, origin):
        for which in (0, 1):
            for axis in (0, 1):
                across(which, axis, number, origin).wait_send()
                diagonal(which, axis, number, origin).wait_send()
            for kind in range(5):
                if kind == 0 and number == 0:
                    pair_own(which).wait_send()
                else:
                    pair(which, kind, number, origin, section).wait_send()

    for which in (0, 1):
        for way, go in ((0, head < heads - 1), (1, head > 0)):

            @pl.when(go)
            def _(which=which, way=way):
                line(which, way, 0).wait_send()

    for swap_block in swaps():
        swap_block.wait()
    settle(0, head)
    for hop in range(1, heads):
        for number, way, origin, comes, goes in each(hop):

            @pl.when(comes)
            def _(number=number, way=way, origin=origin, goes=goes, hop=hop):
                settle(number, origin)

                @pl.when(goes)
                def _():
                    for which in (0, 1):
                        line(which, way, hop).wait_send()

    pl.when(first)(all_received)
    swap(given_first).wait_send()
    shift_own(1).wait()
    for distance in range(1, heads):
        for layer in (0, 1):
            shift(layer, given_first, distance).wait_send()
        shift_in(1, distance).wait_recv()


def start_weights(number, qkv_own, out_own, parts, sides, small_own, *tables):
    heads, wides = lax.axis_size(HEAD), lax.axis_size(WIDE)
    rows, qkv_cols = qkv_own.shape
    out_cols = out_own.shape[1]
    numbers = 2 * heads - 1
    tokens = sides.shape[1] * sides.shape[2]
    whole = heads * wides * rows
    dtype = parts.dtype
    dma = pltpu.SemaphoreType.DMA
    anywhere = pl.BlockSpec(memory_space=pl.ANY)
    vmem = pl.BlockSpec(memory_space=pltpu.VMEM)
    return pl.pallas_call(
        start_kernel,
        out_shape=(
            jax.ShapeDtypeStruct((2, whole, qkv_cols), dtype),
            jax.ShapeDtypeStruct((2, whole, out_cols), dtype),
            jax.ShapeDtypeStruct((whole, parts.shape[3]), dtype),
            jax.ShapeDtypeStruct(parts.shape[1:], dtype),
            jax.ShapeDtypeStruct((tokens, out_cols), dtype),
            jax.ShapeDtypeStruct((tokens, out_cols), dtype),
            jax.ShapeDtypeStruct((tokens, out_cols), dtype),
            jax.ShapeDtypeStruct((tokens, out_cols), dtype),
            jax.ShapeDtypeStruct((2,) + small_own.shape, jnp.float32),
        )
        + attention_shapes(tokens, out_cols, qkv_cols - out_cols, heads, dtype),
        in_specs=[anywhere] * 4 + [vmem] * 5,
        out_specs=(anywhere,) * 8 + (vmem,) * 10,
        scratch_shapes=attention_scratch(tokens, out_cols, qkv_cols, heads, dtype)
        + [
            pltpu.VMEM((tokens, out_cols), dtype),
            pltpu.VMEM((tokens, out_cols), jnp.float32),
            pltpu.VMEM(parts.shape[1:], dtype),
            pltpu.VMEM(parts.shape[1:], dtype),
            dma((2,)),
            dma((10,)),
            dma((2,)),
            dma((2, 2, heads)),
            dma((2, 2, 2, heads)),
            dma((2, 3, 2, numbers)),
            dma((2, 3, 2, numbers)),
            dma((2, 2, 5, numbers)),
            dma((2, 2, 3)),
            dma((2, 2)),
        ],
        compiler_params=pltpu.CompilerParams(
            collective_id=number, has_side_effects=True, vmem_limit_bytes=60 * 2**20
        ),
    )(qkv_own, out_own, parts, sides, small_own, *tables)


def finish_kernel(
    first_terms,
    second_terms,
    small,
    first_parts,
    second_parts,
    tokens_in,
    totals,
    small_total,
    low_parts,
    high_parts,
    tokens_out,
    near_buf,
    middle,
    far_buf,
    sums,
    line_buf,
    small_sum,
    small_buf,
    shifted,
    give,
    local_sem,
    shift_sem,
    swap_sem,
    near_sem,
    far_sem,
    line_sem,
    small_sem,
    give_sem,
    token_sem,
):
    section, head, wide = (lax.axis_index(axis) for axis in (SECTION, HEAD, WIDE))
    heads, wides = lax.axis_size(HEAD), lax.axis_size(WIDE)
    here = [beside(wide, 0), beside(wide, 1), beside(wide, 2)]
    rows, columns = first_terms.shape[1:]
    lots = heads * CUTS
    terms = (first_terms, second_terms)
    other = {SECTION: 1 - section}
    first, second = section == 0, section == 1
    sender_rows = tokens_in.shape[2]

    def remote(source, target, sems, at, partner):
        return pltpu.make_async_remote_copy(
            source,
            target,
            sems.at[(0,) + at],
            sems.at[(1,) + at],
            device_id=partner,
            device_id_type=MESH,
        )

    def shift(distance, target):
        target_head = lax.rem(head + distance, heads)
        return remote(
            first_parts.at[target_head],
            target.at[head],
            shift_sem,
            (distance,),
            {HEAD: target_head},
        )

    def shift_in(distance, target):
        arrived = target.at[lax.rem(head + heads - distance, heads)]
        return remote(arrived, arrived, shift_sem, (distance,), {HEAD: head})

    def near(side, turn, target):
        wide_at = here[side] if turn == 0 else here[2]
        return remote(
            terms[side].at[wide_at * lots + target],
            near_buf.at[side, turn, target],
            near_sem,
            (side, turn, target),
            {WIDE: here[side]},
        )

    def far(side, target):
        return remote(
            middle.at[side, target],
            far_buf.at[side, target],
            far_sem,
            (side, target),
            {WIDE: here[1 - side]},
        )

    def line(way, target, side):
        step = 1 if way == 0 else -1
        return remote(
            sums.at[target, side],
            line_buf.at[way, target, side],
            line_sem,
            (way, target, side),
            {HEAD: head + step},
        )

    def token_target(layer, which, sender_wide, sender_section):
        first_row = pl.multiple_of(sender_section * sender_rows, 16)
        return tokens_out.at[which, sender_wide, pl.ds(first_row, sender_rows)]

    def token(layer, which, turn):
        wide_at = wide if turn == 3 else here[turn]
        sems = (token_sem.at[0, layer, which, turn], token_sem.at[1, section, which, turn])
        return pltpu.make_async_remote_copy(
            tokens_in.at[which * 2 + layer, wide_at],
            token_target(layer, which, wide, section),
            *sems,
            device_id={SECTION: layer, WIDE: wide_at},
            device_id_type=MESH,
        )

    def token_in(from_section, which, turn):
        wide_at = wide if turn == 3 else here[turn]
        target = token_target(section, which, wide_at, from_section)
        sems = (token_sem.at[0, section, which, turn], token_sem.at[1, from_section, which, turn])
        return pltpu.make_async_remote_copy(
            target, target, *sems, device_id={HEAD: head}, device_id_type=MESH
        )

    barrier = pltpu.get_barrier_semaphore()
    partners = [other] + [{WIDE: wide_at} for wide_at in here]
    partners += [{SECTION: 1 - section, WIDE: wide_at} for wide_at in here]
    partners += [{HEAD: lax.rem(head + distance, heads)} for distance in range(1, heads)]
    for partner in partners:
        pl.semaphore_signal(barrier, 1, device_id=partner, device_id_type=MESH)
    pl.semaphore_wait(barrier, len(partners))

    order = []
    for at in range(heads // 2):
        for chip in (heads - 1 - at, at):
            order += [chip * CUTS + cut for cut in range(CUTS)]

    def start_near(turn, target):
        for side in (0, 1):
            near(side, turn, target).start()

    start_near(1, order[0])
    start_near(0, order[0])

    @pl.when(first)
    def _():
        for distance in range(1, heads):
            shift(distance, low_parts).start()
        remote(second_parts, low_parts, swap_sem, (0,), other).start()
        pltpu.make_async_copy(first_parts.at[head], low_parts.at[head], local_sem.at[0]).start()

    @pl.when(second)
    def _():
        for distance in range(1, heads):
            shift(distance, shifted).start()
        pltpu.make_async_copy(second_parts, high_parts, local_sem.at[1]).start()
        remote(
            first_parts.at[head], high_parts.at[head], swap_sem, (1,), other
        ).start()

    steps = [other, {WIDE: here[0]}, {WIDE: here[1]}]
    steps += [{HEAD: lax.rem(head + distance, heads)} for distance in range(1, heads)]

    def small_copy(at):
        source = small.at[1 - section] if at == 0 else small_sum.at[min(at, 3)]
        return remote(source, small_buf.at[at], small_sem, (at,), steps[at])

    for at in range(3):
        small_copy(at).start()
        small_copy(at).wait()
        small_sum[at + 1] = (small[section] if at == 0 else small_sum[at]) + small_buf[at]
    for at in range(3, len(steps)):
        small_copy(at).start()

    def across(number):
        target = order[number]
        for side in (0, 1):
            near(side, 1, target).wait_recv()
            middle[side, target] = (
                terms[side][here[1 - side] * lots + target].astype(jnp.float32)
                + near_buf[side, 1, target].astype(jnp.float32)
            ).astype(middle.dtype)
            far(side, target).start()
        if number + 1 < lots:
            start_near(1, order[number + 1])
        for side in (0, 1):
            near(side, 0, target).wait_recv()
        if number + 1 < lots:
            start_near(0, order[number + 1])

    def collect(target, last):
        for side in (0, 1):
            far(side, target).wait_recv()
            sums[target, side] = (
                terms[side][wide * lots + target].astype(jnp.float32)
                + near_buf[side, 0, target].astype(jnp.float32)
                + far_buf[side, target].astype(jnp.float32)
            ).astype(sums.dtype)
            if target >= CUTS:

                @pl.when(head == 0)
                def _(side=side):
                    line(0, target, side).start()

            if target < lots - CUTS:

                @pl.when(head == heads - 1)
                def _(side=side):
                    line(1, target, side).start()

    def pass_on(at_head, way, target):
        @pl.when(head == at_head)
        def _():
            for side in (0, 1):
                line(way, target, side).wait_recv()
                sums[target, side] = (
                    sums[target, side].astype(jnp.float32)
                    + line_buf[way, target, side].astype(jnp.float32)
                ).astype(sums.dtype)
                line(way, target, side).start()

    def send_tokens():
        for which in (0, 1):
            for turn in range(4):
                for layer in (0, 1):

                    @pl.when((turn < 3) | (section != layer))
                    def _(layer=layer, which=which, turn=turn):
                        token(layer, which, turn).start()

            pltpu.make_async_copy(
                tokens_in.at[which * 2 + section, wide],
                token_target(section, which, wide, section),
                local_sem.at[2 + which],
            ).start()

    passes = {
        1: [(1, 0, 3)],
        2: [(2, 0, 3), (2, 1, 0)],
        3: [(1, 1, 0), (1, 0, 2), (2, 1, 1)],
    }
    for number, target in enumerate(order):
        across(number)
        if number == lots - 1:
            send_tokens()
        collect(target, number == lots - 1)
        for at_head, way, chip in passes.get(number // CUTS, ()):
            pass_on(at_head, way, chip * CUTS + number % CUTS)

    @pl.when(second)
    def _():
        for distance in range(1, heads):
            shift_in(distance, shifted).wait_recv()
            origin = lax.rem(head + heads - distance, heads)
            remote(
                shifted.at[origin], high_parts.at[origin], swap_sem, (1 + distance,), other
            ).start()

    whole = small_sum[3]
    for at in range(3, len(steps)):
        small_copy(at).wait()
        whole = whole + small_buf[at]
    small_total[...] = whole

    for target in range(lots):
        chip = target // CUTS

        @pl.when(head == chip)
        def _(target=target, chip=chip):
            for side in (0, 1):
                value = sums[target, side].astype(jnp.float32)
                for way, comes in ((0, chip > 0), (1, chip < heads - 1)):
                    if comes:
                        line(way, target, side).wait_recv()
                        value = value + line_buf[way, target, side].astype(jnp.float32)
                give[side, pl.ds(target % CUTS * rows, rows)] = value

        for side in (0, 1):
            for turn in (0, 1):
                near(side, turn, target).wait_send()
            far(side, target).wait_send()

            @pl.when(head < chip)
            def _(target=target, side=side):
                line(0, target, side).wait_send()

            @pl.when(head > chip)
            def _(target=target, side=side):
                line(1, target, side).wait_send()

    handed = remote(give.at[1 - section], totals.at[section], give_sem, (), other)
    handed.start()
    totals[section] = give[section]

    for which in (0, 1):
        pltpu.make_async_copy(
            tokens_in.at[which * 2 + section, wide],
            token_target(section, which, wide, section),
            local_sem.at[2 + which],
        ).wait()
        for turn in range(4):
            for layer in (0, 1):

                @pl.when((turn < 3) | (section != layer))
                def _(layer=layer, which=which, turn=turn):
                    token(layer, which, turn).wait_send()
                    token_in(layer, which, turn).wait_recv()

    @pl.when(first)
    def _():
        for distance in range(1, heads):
            shift(distance, low_parts).wait_send()
            shift_in(distance, low_parts).wait_recv()
        remote(second_parts, low_parts, swap_sem, (0,), other).wait_send()
        pltpu.make_async_copy(first_parts.at[head], low_parts.at[head], local_sem.at[0]).wait()
        for distance in range(heads):
            arrived = high_parts.at[lax.rem(head + heads - distance, heads)]
            remote(arrived, arrived, swap_sem, (1 + distance,), other).wait_recv()

    @pl.when(second)
    def _():
        for distance in range(1, heads):
            shift(distance, shifted).wait_send()
        pltpu.make_async_copy(second_parts, high_parts, local_sem.at[1]).wait()
        for distance in range(heads):
            sent = high_parts.at[lax.rem(head + heads - distance, heads)]
            remote(sent, sent, swap_sem, (1 + distance,), other).wait_send()
        remote(second_parts, low_parts, swap_sem, (0,), other).wait_recv()

    handed.wait_send()
    remote(totals.at[1 - section], totals.at[1 - section], give_sem, (), other).wait_recv()


def finish_weights(
    first_terms, second_terms, small, first_parts, second_parts, tokens_in, number
):
    heads = lax.axis_size(HEAD)
    first_terms, second_terms = [
        terms.reshape(terms.shape[0] * CUTS, -1, terms.shape[2])
        for terms in (first_terms, second_terms)
    ]
    blocks, rows, columns = first_terms.shape
    lots = heads * CUTS
    dtype = first_terms.dtype
    dma = pltpu.SemaphoreType.DMA
    vmem = pl.BlockSpec(memory_space=pltpu.VMEM)
    anywhere = pl.BlockSpec(memory_space=pl.ANY)
    smalls = 2 + heads
    layers, wides, sender_rows, width = tokens_in.shape
    return pl.pallas_call(
        finish_kernel,
        out_shape=(
            jax.ShapeDtypeStruct((2, rows * CUTS, columns), jnp.float32),
            jax.ShapeDtypeStruct(small.shape[1:], jnp.float32),
            jax.ShapeDtypeStruct(first_parts.shape, dtype),
            jax.ShapeDtypeStruct(first_parts.shape, dtype),
            jax.ShapeDtypeStruct((2, wides, 2 * sender_rows, width), dtype),
        ),
        in_specs=[vmem, vmem, vmem, anywhere, anywhere, anywhere],
        out_specs=(vmem, vmem, anywhere, anywhere, anywhere),
        scratch_shapes=[
            pltpu.VMEM((2, 2, lots, rows, columns), dtype),
            pltpu.VMEM((2, lots, rows, columns), dtype),
            pltpu.VMEM((2, lots, rows, columns), dtype),
            pltpu.VMEM((lots, 2, rows, columns), dtype),
            pltpu.VMEM((2, lots, 2, rows, columns), dtype),
            pltpu.VMEM((4,) + small.shape[1:], jnp.float32),
            pltpu.VMEM((smalls,) + small.shape[1:], jnp.float32),
            pltpu.VMEM(first_parts.shape, dtype),
            pltpu.VMEM((2, rows * CUTS, columns), jnp.float32),
            dma((4,)),
            dma((2, heads)),
            dma((2, 1 + heads)),
            dma((2, 2, 2, lots)),
            dma((2, 2, lots)),
            dma((2, 2, lots, 2)),
            dma((2, smalls)),
            dma((2,)),
            dma((2, 2, 2, 4)),
        ],
        compiler_params=pltpu.CompilerParams(
            collective_id=number, has_side_effects=True, vmem_limit_bytes=60 * 2**20
        ),
    )(first_terms, second_terms, small, first_parts, second_parts, tokens_in)


def cut_kernel(
    gate, up, down, out, sides, gains, bias, parts, out_inner, sides_inner, small
):
    count, part = parts.shape[0], parts.shape[2] // 3
    heads, wides = lax.axis_size(HEAD), lax.axis_size(WIDE)
    size = out.shape[1] // (heads * wides)
    places = [(head * wides + wide) * size for wide in range(wides) for head in range(heads)]

    def inner(whole):
        return jnp.concatenate([whole[:, start : start + size] for start in places], 1)

    out_inner[...] = inner(out[...])

    @pl.when(pl.program_id(0) == 0)
    def _():
        sides_inner[...] = inner(sides[...])
        scales = inner(gains[...])
        width = gains.shape[1]
        for at in (0, 1):
            small[:, pl.ds(at * width, width)] = scales[at : at + 1]
        small[:, pl.ds(2 * width, bias.shape[1])] = bias[...]

    for at in range(count):
        size = min(part, gate.shape[1] - at * part)
        for which, weight in enumerate((gate, up, down)):
            start = which * part
            parts[at, :, pl.ds(start, size)] = weight[:, pl.ds(at * part, size)]
            if size < part:
                rest = part - size
                parts[at, :, pl.ds(start + size, rest)] = jnp.zeros(
                    (parts.shape[1], rest), parts.dtype
                )


def cut_parts(gate, up, down, out, sides, gains, bias, count, part):
    rows, columns = gate.shape
    step = 16
    weight = pl.BlockSpec((step, columns), lambda at: (at, 0))
    square = pl.BlockSpec((step, out.shape[1]), lambda at: (at, 0))
    wholes = [
        pl.BlockSpec(shape, lambda at: (0, 0))
        for shape in (sides.shape, gains.shape, bias.shape, (1, gains.size + bias.size))
    ]
    return pl.pallas_call(
        cut_kernel,
        grid=(rows // step,),
        out_shape=(
            jax.ShapeDtypeStruct((count, rows, 3 * part), gate.dtype),
            jax.ShapeDtypeStruct(out.shape, out.dtype),
            jax.ShapeDtypeStruct(sides.shape, sides.dtype),
            jax.ShapeDtypeStruct((1, gains.size + bias.size), jnp.float32),
        ),
        in_specs=[weight] * 3 + [square] + wholes[:3],
        out_specs=(
            pl.BlockSpec((count, step, 3 * part), lambda at: (0, at, 0)),
            square,
            wholes[0],
            wholes[3],
        ),
        compiler_params=pltpu.CompilerParams(vmem_limit_bytes=24 * 2**20),
    )(gate, up, down, out, sides, gains, bias)


def join_kernel(low, high, totals, small, gate, up, down, qkv, out, gains, bias):
    count, part = low.shape[0], low.shape[2] // 3
    for at in range(2 * count):
        size = min(part, gate.shape[2] - at * part)
        source = low if at < count else high
        for which, grad in enumerate((gate, up, down)):
            grad[0, :, pl.ds(at * part, size)] = source[
                at % count, :, pl.ds(which * part, size)
            ].astype(grad.dtype)
    cut, width = qkv.shape[2] // 2, out.shape[2]
    for at in (0, 1):
        qkv[0, :, pl.ds(at * cut, cut)] = totals[at, :, pl.ds(0, cut)]
    whole = jnp.concatenate([totals[at, :, pl.ds(cut, width // 2)] for at in (0, 1)], 1)
    heads, wides = lax.axis_size(HEAD), lax.axis_size(WIDE)
    size = width // (heads * wides)
    places = [(wide * heads + head) * size for head in range(heads) for wide in range(wides)]

    def outer(array):
        return jnp.concatenate([array[:, start : start + size] for start in places], 1)

    out[0] = outer(whole)

    @pl.when(pl.program_id(0) == 0)
    def _():
        for at in (0, 1):
            gains[0, at : at + 1] = outer(small[:, at * width : (at + 1) * width])
        bias[...] = small[:, pl.ds(2 * width, bias.shape[1])]


def join_parts(low, high, totals, small, columns, qkv_cols):
    count, rows, width = low.shape
    out_cols = 2 * totals.shape[2] - qkv_cols
    step = 16
    part = pl.BlockSpec((count, step, width), lambda at: (0, at, 0))
    total = pl.BlockSpec((2, step, totals.shape[2]), lambda at: (0, at, 0))
    sizes = (columns, columns, columns, qkv_cols, out_cols)
    return pl.pallas_call(
        join_kernel,
        grid=(rows // step,),
        out_shape=tuple(jax.ShapeDtypeStruct((1, rows, size), jnp.float32) for size in sizes)
        + (
            jax.ShapeDtypeStruct((1, 2, out_cols), jnp.float32),
            jax.ShapeDtypeStruct((1, qkv_cols), jnp.float32),
        ),
        in_specs=[part, part, total, pl.BlockSpec(small.shape, lambda at: (0, 0))],
        out_specs=tuple(pl.BlockSpec((1, step, size), lambda at: (0, at, 0)) for size in sizes)
        + (
            pl.BlockSpec((1, 2, out_cols), lambda at: (0, 0, 0)),
            pl.BlockSpec((1, qkv_cols), lambda at: (0, 0)),
        ),
        compiler_params=pltpu.CompilerParams(vmem_limit_bytes=24 * 2**20),
    )(low, high, totals, small)


def partner_of(head, turn):
    if turn == 1:
        return head + 1 - 2 * lax.rem(head, 2)
    return lax.rem(head + 2, 4) if turn == 2 else 3 - head


def block_swap(source, target, sems, head, turn):
    return pltpu.make_async_remote_copy(
        source,
        target,
        sems.at[0],
        sems.at[1],
        device_id={HEAD: partner_of(head, turn)},
        device_id_type=MESH,
    )


def visit(head, step, heads):
    inner_chip = jnp.minimum(jnp.minimum(head, heads - 1 - head), 1)
    at = step + inner_chip * (1 - lax.div(step, 2)) * (1 - 2 * step)
    return at + lax.div(2 * head, heads) * (heads - 1 - 2 * at)


def group_pipeline(block, everyone, outs, scratch, prepare, compute, settle, extras=()):
    (partial, pair_buf, sums, line_buf, own_sem, pair_sem, line_sem, swap_sem, chain_sem) = scratch
    section, head = lax.axis_index(SECTION), lax.axis_index(HEAD)
    heads = lax.axis_size(HEAD)
    tokens = block.shape[0]
    other = {SECTION: 1 - section}

    def place(section_at, origin, piece=None):
        size = tokens if piece is None else tokens // GATHER_PIECES
        start = (origin * 2 + section_at) * tokens + (piece or 0) * size
        return everyone.at[pl.ds(pl.multiple_of(start, size), size)]

    def remote(source, target, send, receive, partner):
        return pltpu.make_async_remote_copy(
            source, target, send, receive, device_id=partner, device_id_type=MESH
        )

    def pair(origin, source):
        target = place(section, origin)
        return remote(source, target, pair_sem.at[0, origin], pair_sem.at[1, origin], other)

    def pair_in(origin):
        target = place(1 - section, origin)
        return remote(target, target, pair_sem.at[0, origin], pair_sem.at[1, origin], other)

    def line(way, hop, piece):
        step = 1 - 2 * way
        size = tokens // GATHER_PIECES
        target = place(section, head - step * hop, piece)
        own = type(hop) is int and hop == 0
        source = block.at[pl.ds(piece * size, size)] if own else target
        sems = (line_sem.at[0, way, hop, piece], line_sem.at[1, way, hop, piece])
        return remote(source, target, *sems, {HEAD: head + step})

    def inside(place_at):
        return (place_at >= 0) & (place_at < heads)

    def accept(way, hop):
        step = 1 - 2 * way
        for piece in range(GATHER_PIECES):
            here = place(section, head - step * hop, piece)
            sems = (line_sem.at[0, way, hop - 1, piece], line_sem.at[1, way, hop - 1, piece])
            remote(here, here, *sems, {HEAD: head}).wait_recv()

            @pl.when(inside(head + step))
            def _(piece=piece):
                line(way, hop, piece).start()

        pair(head - step * hop, place(section, head - step * hop)).start()

    def swap(origin):
        return remote(
            partial.at[origin, 1 - section],
            pair_buf.at[origin],
            swap_sem.at[0, origin],
            swap_sem.at[1, origin],
            other,
        )

    def lot(piece):
        size = tokens // CHAIN_PIECES
        return pl.ds(piece * size, size)

    def chain(way, target, piece):
        return remote(
            sums.at[target, lot(piece)],
            line_buf.at[way, target, lot(piece)],
            chain_sem.at[0, way, target, piece],
            chain_sem.at[1, way, target, piece],
            {HEAD: head + 1 - 2 * way},
        )

    def send_pieces(way, target, last):
        for piece in range(CHAIN_PIECES):
            chain(way, target, piece).start()
            if last and piece < CHAIN_PIECES - 1:
                chain(way, target, piece).wait_send()

    def deliver(origin, last=False):
        swap(origin).wait_recv()
        sums[origin] = (
            partial[origin, section].astype(jnp.float32) + pair_buf[origin].astype(jnp.float32)
        ).astype(sums.dtype)

        @pl.when((head == 0) & (origin > 0))
        def _():
            send_pieces(0, origin, last)

        @pl.when((head == heads - 1) & (origin < heads - 1))
        def _():
            send_pieces(1, origin, last)

    def pass_on(way, target, piece):
        chain(way, target, piece).wait_recv()
        here = lot(piece)
        sums[target, here] = (
            sums[target, here].astype(jnp.float32) + line_buf[way, target, here].astype(jnp.float32)
        ).astype(sums.dtype)
        chain(way, target, piece).start()

    barrier = pltpu.get_barrier_semaphore()
    partners = [other] + [{HEAD: lax.rem(head + shift, heads)} for shift in range(1, heads)]
    for partner in partners:
        pl.semaphore_signal(barrier, 1, device_id=partner, device_id_type=MESH)
    pl.semaphore_wait(barrier, len(partners))

    for way in (0, 1):

        @pl.when(inside(head + 1 - 2 * way))
        def _(way=way):
            for piece in range(GATHER_PIECES):
                line(way, 0, piece).start()

    pair(head, block).start()
    own = pltpu.make_async_copy(block, place(section, head), own_sem)
    own.start()
    prepare()
    own.wait()

    def one(step, carry):
        origin = visit(head, step, heads)

        @pl.when(step >= 1)
        def _():
            deliver(visit(head, step - 1, heads))

        @pl.when(step == 1)
        def _():
            for way in (0, 1):

                @pl.when(inside(head - (1 - 2 * way)))
                def _(way=way):
                    accept(way, 1)

        hop = jnp.maximum(origin - head, head - origin)

        @pl.when((step >= 2) & (hop >= 2))
        def _():
            accept(lax.div(jnp.maximum(origin - head, 0) + heads - 2, heads), hop)

        pair_in(origin).wait_recv()
        compute(origin)
        swap(origin).start()
        return carry

    lax.fori_loop(0, heads, one, 0)
    deliver(visit(head, heads - 1, heads), True)

    between = (head > 0) & (head < heads - 1)
    side = lax.div(2 * head, heads)
    ends = ((1 - side) * (heads - 1), side * (heads - 1))
    extras = list(extras)

    def work(count):
        for _ in range(min(count, len(extras))):
            extras.pop(0)()

    work(2)

    @pl.when(between)
    def _():
        for piece in range(CHAIN_PIECES):
            pass_on(side, heads - 1 - head, piece)

    for piece in range(CHAIN_PIECES):

        @pl.when(between)
        def _(piece=piece):
            pass_on(side, ends[0], piece)
            pass_on(1 - side, ends[1], piece)

        work(1)

    work(len(extras))
    settle()
    spans = [pl.ds(at * block.shape[1], block.shape[1]) for at in range(len(outs))]
    for out, span in zip(outs, spans):
        out[...] = sums[head, :, span].astype(jnp.float32)
    for way, comes in ((0, head > 0), (1, head < heads - 1)):

        @pl.when(comes)
        def _(way=way):
            for piece in range(CHAIN_PIECES):
                chain(way, head, piece).wait_recv()
            for out, span in zip(outs, spans):
                out[...] += line_buf[way, head, :, span].astype(jnp.float32)

    for piece in range(CHAIN_PIECES):
        for target in range(1, heads):

            if target < heads - 1 or piece == CHAIN_PIECES - 1:

                @pl.when(head == 0)
                def _(piece=piece, target=target):
                    chain(0, target, piece).wait_send()

                @pl.when(head == heads - 1)
                def _(piece=piece, target=target):
                    chain(1, heads - 1 - target, piece).wait_send()

        @pl.when(between)
        def _(piece=piece):
            chain(side, heads - 1 - head, piece).wait_send()
            chain(side, ends[0], piece).wait_send()
            chain(1 - side, ends[1], piece).wait_send()

    for origin in range(heads):
        here = place(section, origin)
        pair(origin, here).wait_send()
        swap(origin).wait_send()

    for way in (0, 1):
        for hop in range(heads):
            step = 1 - 2 * way

            @pl.when(inside(head + step) & inside(head - step * hop))
            def _(way=way, hop=hop):
                for piece in range(GATHER_PIECES):
                    line(way, hop, piece).wait_send()


def pipeline_scratch(heads, tokens, columns, dtype):
    dma = pltpu.SemaphoreType.DMA
    return [
        pltpu.VMEM((heads, 2, tokens, columns), dtype),
        pltpu.VMEM((heads, tokens, columns), dtype),
        pltpu.VMEM((heads, tokens, columns), dtype),
        pltpu.VMEM((2, heads, tokens, columns), dtype),
        dma,
        dma((2, heads)),
        dma((2, 2, heads, GATHER_PIECES)),
        dma((2, heads)),
        dma((2, 2, heads, CHAIN_PIECES)),
    ]


PIPELINE_SCRATCH = 9
CHAIN_PIECES = 4
GATHER_PIECES = 2
TERM_ROWS = 512
TERM_SLOTS = 3
STEP_COLUMNS = 512
STEP_WIDTH = 512


def chunks(total, size):
    return [(at, min(size, total - at)) for at in range(0, total, size)]


def write_partial(partial, origin, left, weights, columns, offset=0):
    tokens = partial.shape[2]
    for start, count in chunks(weights.shape[0], STEP_WIDTH):
        piece = contract_last(left, weights[pl.ds(start, count), pl.ds(*columns)])
        piece = piece.astype(partial.dtype)
        partial[origin, 0, :, pl.ds(offset + start, count)] = piece[:tokens]
        partial[origin, 1, :, pl.ds(offset + start, count)] = piece[tokens:]


def forward_kernel(block, weights_hbm, out, everyone, gate_up_hbm, hidden_hbm, *scratch):
    shared, rest = scratch[:PIPELINE_SCRATCH], scratch[PIPELINE_SCRATCH:]
    weights, gate_up, hidden, load_sem, store_sem = rest
    partial = shared[0]
    heads = lax.axis_size(HEAD)
    rows = 2 * block.shape[0]
    part = hidden.shape[1]
    load = pltpu.make_async_copy(weights_hbm, weights, load_sem)

    def stores(origin):
        span = pl.ds(pl.multiple_of(origin * rows, rows), rows)
        return [
            pltpu.make_async_copy(gate_up.at[span], gate_up_hbm.at[span], store_sem.at[0, origin]),
            pltpu.make_async_copy(hidden.at[span], hidden_hbm.at[span], store_sem.at[1, origin]),
        ]

    def prepare():
        load.start()
        load.wait()

    def compute(origin):
        span = pl.ds(pl.multiple_of(origin * rows, rows), rows)
        left = everyone[span, :]
        for start, count in chunks(part, STEP_COLUMNS):
            gate = jnp.dot(
                left, weights[:, pl.ds(start, count)], preferred_element_type=jnp.float32
            )
            up = jnp.dot(
                left, weights[:, pl.ds(part + start, count)], preferred_element_type=jnp.float32
            )
            gate_up[span, pl.ds(start, count)] = gate.astype(gate_up.dtype)
            gate_up[span, pl.ds(part + start, count)] = up.astype(gate_up.dtype)
            hidden[span, pl.ds(start, count)] = (gate / (1.0 + jnp.exp(-gate)) * up).astype(
                hidden.dtype
            )
        write_partial(partial, origin, hidden[span, :], weights, (2 * part, part))
        for store in stores(origin):
            store.start()

    def settle():
        for origin in range(heads):
            for store in stores(origin):
                store.wait()

    group_pipeline(block, everyone, (out,), shared, prepare, compute, settle)


def term_tiles(operands, part, terms, terms_hbm, term_sem, loads=()):
    lefts, rights = operands
    width = terms_hbm.shape[0]
    tiles = [(which, start) for which in range(3) for start, _ in chunks(width, TERM_ROWS)]

    def store(number):
        which, start = tiles[number]
        slot = number % TERM_SLOTS
        target = terms_hbm.at[pl.ds(start, TERM_ROWS), pl.ds(which * part, part)]
        return pltpu.make_async_copy(terms.at[slot], target, term_sem.at[slot])

    def tile(number):
        which, start = tiles[number]
        if number == 0:
            for load in loads:
                load.wait()
        if number >= TERM_SLOTS:
            store(number - TERM_SLOTS).wait()
        left = lefts[which][:, pl.ds(start, TERM_ROWS)]
        right = rights[which][:, pl.ds(which % 2 * part if which < 2 else 0, part)]
        terms[number % TERM_SLOTS] = contract_first(left, right).astype(terms.dtype)
        store(number).start()

    def settle():
        for number in range(len(tiles) - TERM_SLOTS, len(tiles)):
            store(number).wait()

    return [functools.partial(tile, number) for number in range(len(tiles))], settle


def backward_kernel(
    block, weights_hbm, gate_up_hbm, normed_hbm, hidden_hbm, out, terms_hbm, *scratch
):
    shared, rest = scratch[:PIPELINE_SCRATCH], scratch[PIPELINE_SCRATCH:]
    everyone, weights, gate_up, normed, hidden, d_gate_up, terms, load_sem, term_sem = rest
    partial = shared[0]
    rows = 2 * block.shape[0]
    part = hidden.shape[1]
    sources = ((weights_hbm, weights), (gate_up_hbm, gate_up))
    sources += ((normed_hbm, normed), (hidden_hbm, hidden))
    loads = [
        pltpu.make_async_copy(source, target, load_sem.at[at])
        for at, (source, target) in enumerate(sources)
    ]

    def prepare():
        for load in loads:
            load.start()
        for load in loads[:2]:
            load.wait()

    def compute(origin):
        span = pl.ds(pl.multiple_of(origin * rows, rows), rows)
        left = everyone[span, :]
        for start, count in chunks(part, STEP_COLUMNS):
            d_hidden = jnp.dot(
                left, weights[:, pl.ds(2 * part + start, count)], preferred_element_type=jnp.float32
            )
            gate = gate_up[span, pl.ds(start, count)].astype(jnp.float32)
            up = gate_up[span, pl.ds(part + start, count)].astype(jnp.float32)
            sigmoid = 1.0 / (1.0 + jnp.exp(-gate))
            d_gate = d_hidden * up * sigmoid * (1.0 + gate * (1.0 - sigmoid))
            d_gate_up[span, pl.ds(start, count)] = d_gate.astype(d_gate_up.dtype)
            d_up = d_hidden * gate * sigmoid
            d_gate_up[span, pl.ds(part + start, count)] = d_up.astype(d_gate_up.dtype)
        write_partial(partial, origin, d_gate_up[span, :], weights, (0, 2 * part))

    operands = (normed, normed, everyone), (d_gate_up, d_gate_up, hidden)
    extras, settle = term_tiles(operands, part, terms, terms_hbm, term_sem, loads[2:])
    group_pipeline(block, everyone, (out,), shared, prepare, compute, settle, extras)


def turning_kernel(block, weights_hbm, *refs):
    blocks, (out, d_out, terms_hbm), scratch = refs[:4], refs[4:7], refs[7:]
    shared, rest = scratch[:PIPELINE_SCRATCH], scratch[PIPELINE_SCRATCH:]
    everyone, weights, grads, hidden, d_gate_up, terms, load_sem, give_sem, term_sem = rest
    partial = shared[0]
    rows, width = 2 * block.shape[0], block.shape[1]
    part = hidden.shape[1]
    section, head = lax.axis_index(SECTION), lax.axis_index(HEAD)
    tokens = block.shape[0]
    load = pltpu.make_async_copy(weights_hbm, weights, load_sem.at[4])

    def place(section_at, turn):
        origin = head if turn == 0 else partner_of(head, turn)
        first_row = pl.multiple_of((origin * 2 + section_at) * tokens, tokens)
        return grads.at[pl.ds(first_row, tokens)]

    def own(turn):
        return pltpu.make_async_copy(blocks[turn], place(section, turn), load_sem.at[turn])

    def give(turn, section_at):
        return pltpu.make_async_remote_copy(
            blocks[turn],
            place(section_at, turn),
            give_sem.at[0, turn],
            give_sem.at[1, turn],
            device_id={SECTION: 1 - section},
            device_id_type=MESH,
        )

    def prepare():
        load.start()
        for turn in range(4):
            own(turn).start()
            give(turn, section).start()
        for turn in range(4):
            own(turn).wait()
            give(turn, section).wait_send()
            give(turn, 1 - section).wait_recv()
        load.wait()

    def compute(origin):
        span = pl.ds(pl.multiple_of(origin * rows, rows), rows)
        left, grad = everyone[span, :], grads[span, :]
        for start, count in chunks(part, STEP_COLUMNS):
            gate, up, d_hidden = [
                jnp.dot(
                    source,
                    weights[:, pl.ds(which * part + start, count)],
                    preferred_element_type=jnp.float32,
                )
                for which, source in enumerate((left, left, grad))
            ]
            sigmoid = 1.0 / (1.0 + jnp.exp(-gate))
            hidden[span, pl.ds(start, count)] = (gate * sigmoid * up).astype(hidden.dtype)
            d_gate = d_hidden * up * sigmoid * (1.0 + gate * (1.0 - sigmoid))
            d_gate_up[span, pl.ds(start, count)] = d_gate.astype(d_gate_up.dtype)
            d_up = d_hidden * gate * sigmoid
            d_gate_up[span, pl.ds(part + start, count)] = d_up.astype(d_gate_up.dtype)
        write_partial(partial, origin, hidden[span, :], weights, (2 * part, part))
        write_partial(partial, origin, d_gate_up[span, :], weights, (0, 2 * part), width)

    operands = (everyone, everyone, grads), (d_gate_up, d_gate_up, hidden)
    extras, settle = term_tiles(operands, part, terms, terms_hbm, term_sem)
    group_pipeline(block, everyone, (out, d_out), shared, prepare, compute, settle, extras)


def turning_point(block, weights, grads, number):
    heads = lax.axis_size(HEAD)
    tokens, width = block.shape
    part = weights.shape[1] // 3
    count = 2 * heads * tokens
    dtype = block.dtype
    vmem = pl.BlockSpec(memory_space=pltpu.VMEM)
    anywhere = pl.BlockSpec(memory_space=pl.ANY)
    return pl.pallas_call(
        turning_kernel,
        out_shape=(
            jax.ShapeDtypeStruct((tokens, width), jnp.float32),
            jax.ShapeDtypeStruct((tokens, width), jnp.float32),
            jax.ShapeDtypeStruct(weights.shape, dtype),
        ),
        in_specs=[vmem] + [anywhere] * 5,
        out_specs=(vmem, vmem, anywhere),
        scratch_shapes=pipeline_scratch(heads, tokens, 2 * width, dtype)
        + [
            pltpu.VMEM((count, width), dtype),
            pltpu.VMEM(weights.shape, dtype),
            pltpu.VMEM((count, width), dtype),
            pltpu.VMEM((count, part), dtype),
            pltpu.VMEM((count, 2 * part), dtype),
            pltpu.VMEM((TERM_SLOTS, TERM_ROWS, part), dtype),
            pltpu.SemaphoreType.DMA((5,)),
            pltpu.SemaphoreType.DMA((2, 4)),
            pltpu.SemaphoreType.DMA((TERM_SLOTS,)),
        ],
        compiler_params=pltpu.CompilerParams(
            collective_id=number, has_side_effects=True, vmem_limit_bytes=60 * 2**20
        ),
        cost_estimate=pl.CostEstimate(
            flops=18 * count * width * part, bytes_accessed=4 * weights.size, transcendentals=0
        ),
    )(block, weights, *grads)


def feed_forward(block, weights, number):
    heads = lax.axis_size(HEAD)
    tokens, width = block.shape
    part = weights.shape[1] // 3
    count = 2 * heads * tokens
    dtype = block.dtype
    vmem = pl.BlockSpec(memory_space=pltpu.VMEM)
    anywhere = pl.BlockSpec(memory_space=pl.ANY)
    return pl.pallas_call(
        forward_kernel,
        out_shape=(
            jax.ShapeDtypeStruct((tokens, width), jnp.float32),
            jax.ShapeDtypeStruct((count, width), dtype),
            jax.ShapeDtypeStruct((count, 2 * part), dtype),
            jax.ShapeDtypeStruct((count, part), dtype),
        ),
        in_specs=[vmem, anywhere],
        out_specs=(vmem, vmem, anywhere, anywhere),
        scratch_shapes=pipeline_scratch(heads, tokens, width, dtype)
        + [
            pltpu.VMEM(weights.shape, dtype),
            pltpu.VMEM((count, 2 * part), dtype),
            pltpu.VMEM((count, part), dtype),
            pltpu.SemaphoreType.DMA,
            pltpu.SemaphoreType.DMA((2, heads)),
        ],
        compiler_params=pltpu.CompilerParams(
            collective_id=number, has_side_effects=True, vmem_limit_bytes=60 * 2**20
        ),
        cost_estimate=pl.CostEstimate(
            flops=6 * count * width * part, bytes_accessed=2 * weights.size, transcendentals=0
        ),
    )(block, weights)


def feed_backward(block, weights, gate_up, normed, hidden, number):
    heads = lax.axis_size(HEAD)
    tokens, width = block.shape
    part = hidden.shape[1]
    count = 2 * heads * tokens
    dtype = block.dtype
    vmem = pl.BlockSpec(memory_space=pltpu.VMEM)
    anywhere = pl.BlockSpec(memory_space=pl.ANY)
    return pl.pallas_call(
        backward_kernel,
        out_shape=(
            jax.ShapeDtypeStruct((tokens, width), jnp.float32),
            jax.ShapeDtypeStruct(weights.shape, dtype),
        ),
        in_specs=[vmem] + [anywhere] * 4,
        out_specs=(vmem, anywhere),
        scratch_shapes=pipeline_scratch(heads, tokens, width, dtype)
        + [
            pltpu.VMEM((count, width), dtype),
            pltpu.VMEM(weights.shape, dtype),
            pltpu.VMEM(gate_up.shape, dtype),
            pltpu.VMEM((count, width), dtype),
            pltpu.VMEM((count, part), dtype),
            pltpu.VMEM((count, 2 * part), dtype),
            pltpu.VMEM((TERM_SLOTS, TERM_ROWS, part), dtype),
            pltpu.SemaphoreType.DMA((4,)),
            pltpu.SemaphoreType.DMA((TERM_SLOTS,)),
        ],
        compiler_params=pltpu.CompilerParams(
            collective_id=number, has_side_effects=True, vmem_limit_bytes=58 * 2**20
        ),
        cost_estimate=pl.CostEstimate(
            flops=12 * count * width * part, bytes_accessed=4 * weights.size, transcendentals=0
        ),
    )(block, weights, gate_up, normed, hidden)


GROUP = 3


def turn(tensor, cosine, sine):
    return tensor * cosine + pltpu.roll(tensor, tensor.shape[1] // 2, 1) * sine


def attention_grad_kernel(
    layer,
    moves,
    d_normed2,
    midway,
    scale2,
    out_grad,
    small_rows,
    queries,
    keyval,
    log_total,
    attended,
    normed,
    layer_in,
    scale1,
    cosine,
    sine,
    own_pos,
    key_pos,
    w_out_hbm,
    w_qkv_hbm,
    parts_in,
    d_in,
    small,
    terms_hbm,
    parts_out,
    w_out,
    w_qkv,
    d_midway,
    g_attn,
    d_attended,
    d_qkv,
    d_normed,
    d_keyval,
    terms,
    their_normed,
    their_attended,
    their_g,
    their_d,
    sums,
    pair_buf,
    line_buf,
    load_sem,
    give_sem,
    pair_sem,
    line_sem,
    shift_sem,
):
    section, head = lax.axis_index(SECTION), lax.axis_index(HEAD)
    heads, wides = lax.axis_size(HEAD), lax.axis_size(WIDE)
    tokens, width = normed.shape
    qkv_cols = d_qkv.shape[1]
    kv_width = KV * HDIM
    rows = width // (heads * wides)
    scaling = HDIM**-0.5
    other = {SECTION: 1 - section}

    def remote(source, target, sems, at, partner):
        return pltpu.make_async_remote_copy(
            source,
            target,
            sems.at[(0,) + at],
            sems.at[(1,) + at],
            device_id=partner,
            device_id_type=MESH,
        )

    def half(array, at):
        count = array.shape[1] // 2
        return array.at[:, pl.ds(pl.multiple_of(at * count, 128), count)]

    gives = [
        remote(normed, their_normed, give_sem, (0,), other),
        remote(attended, their_attended, give_sem, (1,), other),
        remote(half(g_attn, 1 - section), their_g, give_sem, (2,), other),
        remote(half(d_qkv, 1 - section), their_d, give_sem, (3,), other),
    ]
    loads = [
        pltpu.make_async_copy(w_out_hbm.at[layer], w_out, load_sem.at[0]),
        pltpu.make_async_copy(w_qkv_hbm.at[layer], w_qkv, load_sem.at[1]),
    ]
    for load in loads:
        load.start()

    def shift(distance):
        target = lax.rem(head + distance, heads)
        return remote(
            parts_in.at[target], parts_out.at[head], shift_sem, (distance,), {HEAD: target}
        )

    def shift_in(distance):
        arrived = parts_out.at[lax.rem(head + heads - distance, heads)]
        return remote(arrived, arrived, shift_sem, (distance,), {HEAD: head})

    def shift_own():
        return pltpu.make_async_copy(parts_in.at[head], parts_out.at[head], load_sem.at[4])

    barrier = pltpu.get_barrier_semaphore()
    partners = [other] + [{HEAD: lax.rem(head + distance, heads)} for distance in range(1, heads)]
    for partner in partners:
        pl.semaphore_signal(barrier, 1, device_id=partner, device_id_type=MESH)
    pl.semaphore_wait(barrier, len(partners))
    for give in gives[:2]:
        give.start()
    if moves:
        shift_own().start()
        for distance in range(1, heads):
            shift(distance).start()

    grad = out_grad[...].astype(jnp.float32)
    unit = midway[...] * scale2[...]
    gain2_grad = jnp.sum(d_normed2[...] * unit, 0, keepdims=True)
    scaled = d_normed2[...] * small_rows[layer, :, pl.ds(width, width)]
    d_midway[...] = (
        scale2[...] * (scaled - unit * jnp.mean(scaled * unit, -1, keepdims=True)) + grad
    )
    g_attn[...] = d_midway[...].astype(g_attn.dtype)
    gives[2].start()
    small[:, pl.ds(width, width)] = gain2_grad
    loads[0].wait()
    for start, count in chunks(width, STEP_WIDTH):
        d_attended[:, pl.ds(start, count)] = contract_last(
            g_attn[...], w_out[pl.ds(start, count), :]
        ).astype(d_attended.dtype)

    allowed = own_pos[...] >= key_pos[...]
    allowed = jnp.concatenate([allowed.astype(jnp.int32)] * GROUP, 0) > 0
    groups = HEADS // GROUP
    for group in range(groups):
        kv = group * KV // groups
        spans = [pl.ds((group * GROUP + at) * HDIM, HDIM) for at in range(GROUP)]
        query = jnp.concatenate([queries[group * GROUP + at] for at in range(GROUP)], 0)
        total = jnp.concatenate([log_total[group * GROUP + at] for at in range(GROUP)], 0)
        key = keyval[:, pl.ds(kv * HDIM, HDIM)]
        value = keyval[:, pl.ds(kv_width + kv * HDIM, HDIM)]
        d_out = jnp.concatenate([d_attended[:, span] for span in spans], 0)
        scores = jnp.where(allowed, contract_last(query, key) * scaling, -1e30)
        probs = jnp.exp(scores - total)
        d_probs = contract_last(d_out, value)
        row_dot = jnp.sum(probs * d_probs, -1, keepdims=True)
        d_scores = (probs * (d_probs - row_dot)).astype(jnp.bfloat16)
        d_query = jnp.dot(d_scores, key, preferred_element_type=jnp.float32) * scaling
        d_query = d_query.astype(jnp.bfloat16).astype(jnp.float32)
        for at, span in enumerate(spans):
            d_qkv[:, span] = turn(
                d_query[at * tokens : (at + 1) * tokens], cosine[...], sine[...]
            ).astype(d_qkv.dtype)
        d_key = contract_first(d_scores, query) * scaling
        d_value = contract_first(probs.astype(jnp.bfloat16), d_out)
        first = group % (groups // KV) == 0
        for column, part in ((kv * HDIM, d_key), (kv_width + kv * HDIM, d_value)):
            part = part if first else part + d_keyval[:, pl.ds(column, HDIM)]
            d_keyval[:, pl.ds(column, HDIM)] = part

    def place(section_at, head_at):
        return pl.ds(pl.multiple_of((section_at * heads + head_at) * tokens, tokens), tokens)

    sent = terms.at[pl.ds(0, 2 * heads * tokens), pl.ds(0, d_keyval.shape[1])]
    sent[...] = d_keyval[...].astype(sent.dtype)

    def pair(target):
        source = sent.at[place(1 - section, target)]
        return remote(source, pair_buf.at[target], pair_sem, (target,), other)

    def line(way, target):
        partner = {HEAD: head + 1 - 2 * way}
        return remote(sums.at[target], line_buf.at[way, target], line_sem, (way, target), partner)

    order = []
    for at in range(heads // 2):
        order += [heads - 1 - at, at]
    for target in order:
        pair(target).start()
    for target in order:
        pair(target).wait_recv()
        sums[target] = (
            sent[place(section, target), :].astype(jnp.float32)
            + pair_buf[target].astype(jnp.float32)
        ).astype(sums.dtype)
        if target > 0:

            @pl.when(head == 0)
            def _(target=target):
                line(0, target).start()

        if target < heads - 1:

            @pl.when(head == heads - 1)
            def _(target=target):
                line(1, target).start()

    for target in order:
        pair(target).wait_send()

    def pass_on(way, target):
        line(way, target).wait_recv()
        sums[target] = (
            sums[target].astype(jnp.float32) + line_buf[way, target].astype(jnp.float32)
        ).astype(sums.dtype)
        line(way, target).start()

    loads[1].wait()
    for start, count in chunks(width, STEP_WIDTH):
        d_normed[:, pl.ds(start, count)] = contract_last(
            d_qkv[:, pl.ds(0, width)], w_qkv[pl.ds(start, count), pl.ds(0, width)]
        )
    gives[1].wait_recv()
    gives[2].wait_recv()
    pair_g = jnp.concatenate([half(g_attn, section)[...], their_g[...]], 0)

    def out_terms(head_at):
        span = pl.ds(head_at * wides * rows, wides * rows)
        left = jnp.concatenate([attended[:, span], their_attended[:, span]], 0)
        piece = contract_first(left, pair_g).astype(terms.dtype)
        for wide_at in range(wides):
            target = pl.ds((wide_at * heads + head_at) * rows, rows)
            terms[target, pl.ds(qkv_cols // 2, width // 2)] = piece[
                wide_at * rows : (wide_at + 1) * rows
            ]

    for at in range(heads - 1):
        right, left = heads - 1 - at, at

        @pl.when((head > 0) & (head < right))
        def _(right=right):
            pass_on(0, right)

        @pl.when((head < heads - 1) & (head > left))
        def _(left=left):
            pass_on(1, left)

        out_terms(at)

    out_terms(heads - 1)

    def store(at):
        start, count = ((0, qkv_cols // 2), (qkv_cols // 2, width // 2))[at]
        span = pl.ds(start, count)
        return pltpu.make_async_copy(terms.at[:, span], terms_hbm.at[:, span], load_sem.at[2 + at])

    store(1).start()
    d_keyval[pl.ds(0, tokens), :] = sums[head].astype(jnp.float32)
    for way, comes in ((0, head > 0), (1, head < heads - 1)):

        @pl.when(comes)
        def _(way=way):
            line(way, head).wait_recv()
            d_keyval[pl.ds(0, tokens), :] += line_buf[way, head].astype(jnp.float32)

    for kv in range(KV):
        span = pl.ds(kv * HDIM, HDIM)
        d_qkv[:, pl.ds(width + kv * HDIM, HDIM)] = turn(
            d_keyval[pl.ds(0, tokens), span], cosine[...], sine[...]
        ).astype(d_qkv.dtype)
    d_qkv[:, pl.ds(width + kv_width, kv_width)] = d_keyval[
        pl.ds(0, tokens), pl.ds(kv_width, kv_width)
    ].astype(d_qkv.dtype)
    gives[3].start()
    small[:, pl.ds(2 * width, qkv_cols)] = jnp.sum(
        d_qkv[...].astype(jnp.float32), 0, keepdims=True
    )
    rest = pl.ds(width, qkv_cols - width)
    for start, count in chunks(width, STEP_WIDTH):
        d_normed[:, pl.ds(start, count)] += contract_last(
            d_qkv[:, rest], w_qkv[pl.ds(start, count), rest]
        )

    unit = layer_in[...] * scale1[...]
    small[:, pl.ds(0, width)] = jnp.sum(d_normed[...] * unit, 0, keepdims=True)
    scaled = d_normed[...] * small_rows[layer, :, pl.ds(0, width)]
    d_in[...] = (
        scale1[...] * (scaled - unit * jnp.mean(scaled * unit, -1, keepdims=True)) + d_midway[...]
    ).astype(d_in.dtype)

    gives[0].wait_recv()
    gives[3].wait_recv()
    pair_d = jnp.concatenate([half(d_qkv, section)[...], their_d[...]], 0)
    for start, count in chunks(width, STEP_WIDTH):
        span = pl.ds(start, count)
        left = jnp.concatenate([normed[:, span], their_normed[:, span]], 0)
        terms[span, pl.ds(0, qkv_cols // 2)] = contract_first(left, pair_d).astype(terms.dtype)
    store(0).start()
    for give in gives:
        give.wait_send()
    for target in range(heads):

        @pl.when(head < target)
        def _(target=target):
            line(0, target).wait_send()

        @pl.when(head > target)
        def _(target=target):
            line(1, target).wait_send()

    for at in (0, 1):
        store(at).wait()
    if moves:
        shift_own().wait()
        for distance in range(1, heads):
            shift(distance).wait_send()
            shift_in(distance).wait_recv()


def attention_grad(layer, number, w_out, w_qkv, parts_in, *operands):
    heads = lax.axis_size(HEAD)
    normed = operands[9]
    tokens, width = normed.shape
    qkv_cols = w_qkv.shape[2]
    kv_cols = qkv_cols - width
    dtype = normed.dtype
    float32 = jnp.float32
    dma = pltpu.SemaphoreType.DMA
    vmem = pl.BlockSpec(memory_space=pltpu.VMEM)
    anywhere = pl.BlockSpec(memory_space=pl.ANY)
    columns = qkv_cols // 2 + width // 2
    moves = parts_in is not None
    parts_in = parts_in if moves else jnp.zeros((heads, 16, 128), dtype)
    return pl.pallas_call(
        functools.partial(attention_grad_kernel, layer, moves),
        out_shape=(
            jax.ShapeDtypeStruct((tokens, width), dtype),
            jax.ShapeDtypeStruct((1, 2 * width + qkv_cols), float32),
            jax.ShapeDtypeStruct((width, columns), dtype),
            jax.ShapeDtypeStruct(parts_in.shape, dtype),
        ),
        in_specs=[vmem] * len(operands) + [anywhere] * 3,
        out_specs=(vmem, vmem, anywhere, anywhere),
        scratch_shapes=[
            pltpu.VMEM(w_out.shape[1:], dtype),
            pltpu.VMEM(w_qkv.shape[1:], dtype),
            pltpu.VMEM((tokens, width), float32),
            pltpu.VMEM((tokens, width), dtype),
            pltpu.VMEM((tokens, width), dtype),
            pltpu.VMEM((tokens, qkv_cols), dtype),
            pltpu.VMEM((tokens, width), float32),
            pltpu.VMEM((2 * heads * tokens, kv_cols), float32),
            pltpu.VMEM((width, columns), dtype),
            pltpu.VMEM((tokens, width), dtype),
            pltpu.VMEM((tokens, width), dtype),
            pltpu.VMEM((tokens, width // 2), dtype),
            pltpu.VMEM((tokens, qkv_cols // 2), dtype),
            pltpu.VMEM((heads, tokens, kv_cols), dtype),
            pltpu.VMEM((heads, tokens, kv_cols), dtype),
            pltpu.VMEM((2, heads, tokens, kv_cols), dtype),
            dma((5,)),
            dma((2, 4)),
            dma((2, heads)),
            dma((2, 2, heads)),
            dma((2, heads)),
        ],
        compiler_params=pltpu.CompilerParams(
            collective_id=number, has_side_effects=True, vmem_limit_bytes=60 * 2**20
        ),
        cost_estimate=pl.CostEstimate(
            flops=40 * tokens * width * qkv_cols,
            bytes_accessed=2 * w_out.size + 2 * w_qkv.size,
            transcendentals=0,
        ),
    )(*operands, w_out, w_qkv, parts_in)


def attention_body(
    layer, operands, results, scratch, loads, ready, breath=lambda: None, met=lambda: None
):
    layer_in, small, cosine, sine, own_pos, key_pos = operands
    normed, queries, keyval, log_total, attended, midway, normed2, scale1, scale2 = results
    w_qkv, w_out, mine, own_sem, pair_sem, line_sem = scratch
    section, head = lax.axis_index(SECTION), lax.axis_index(HEAD)
    heads = lax.axis_size(HEAD)
    tokens, width = normed.shape
    kv_width = KV * HDIM
    other = {SECTION: 1 - section}

    def gain(at):
        return small[layer, :, pl.ds(at * width, width)]

    def remote(source, target, sems, at, partner):
        return pltpu.make_async_remote_copy(
            source,
            target,
            sems.at[(0,) + at],
            sems.at[(1,) + at],
            device_id=partner,
            device_id_type=MESH,
        )

    def place(section_at, head_at):
        start = (section_at * heads + head_at) * tokens
        return keyval.at[pl.ds(pl.multiple_of(start, tokens), tokens)]

    def pair(number, head_at, source):
        return remote(source, place(section, head_at), pair_sem, (number,), other)

    def pair_in(number, head_at):
        target = place(1 - section, head_at)
        return remote(target, target, pair_sem, (number,), other)

    def line(way, hop, source):
        step = 1 - 2 * way
        target = place(section, head - step * hop)
        return remote(source, target, line_sem, (way, hop), {HEAD: head + step})

    scale = lax.rsqrt(
        jnp.mean(layer_in[...] * layer_in[...], -1, keepdims=True) + EPSILON
    )
    scale1[...] = scale
    normed[...] = (layer_in[...] * scale * gain(0)).astype(normed.dtype)
    ready()

    def project(start, count):
        span = pl.ds(start, count)
        return (
            jnp.dot(normed[...], w_qkv[:, span], preferred_element_type=jnp.float32)
            + small[layer, :, pl.ds(2 * width + start, count)]
        )

    loads[0].wait()
    for kv in range(KV):
        key = project(width + kv * HDIM, HDIM)
        mine[:, pl.ds(kv * HDIM, HDIM)] = turn(key, cosine[...], sine[...]).astype(mine.dtype)
    mine[:, pl.ds(kv_width, kv_width)] = project(width + kv_width, kv_width).astype(mine.dtype)
    ways = ((0, head < heads - 1), (1, head > 0))
    for way, go in ways:

        @pl.when(go)
        def _(way=way):
            line(way, 0, mine).start()

    pair(0, head, mine).start()
    own = pltpu.make_async_copy(mine, place(section, head), own_sem)
    own.start()
    breath()

    def arrivals(hop):
        yield 0, head - hop, head >= hop, head < heads - 1
        yield 1, head + hop, head + hop < heads, head > 0

    per_hop = HEADS // (heads - 1)
    for hop in range(1, heads):
        start = (hop - 1) * per_hop * HDIM
        block = project(start, per_hop * HDIM)
        for at in range(per_hop):
            query = block[:, at * HDIM : (at + 1) * HDIM]
            queries[(hop - 1) * per_hop + at] = turn(query, cosine[...], sine[...]).astype(
                queries.dtype
            )
        for way, origin, comes, goes in arrivals(hop):

            @pl.when(comes)
            def _(way=way, origin=origin, goes=goes, hop=hop):
                here = place(section, origin)
                line(way, hop - 1, here).wait_recv()

                @pl.when(goes)
                def _():
                    line(way, hop, here).start()

                pair(2 * hop - 1 + way, origin, here).start()

    own.wait()
    pair_in(0, head).wait_recv()
    for hop in range(1, heads):
        for way, origin, comes, goes in arrivals(hop):

            @pl.when(comes)
            def _(way=way, origin=origin, hop=hop):
                pair_in(2 * hop - 1 + way, origin).wait_recv()

    met()
    allowed = own_pos[...] >= key_pos[...]
    allowed = jnp.concatenate([allowed.astype(jnp.int32)] * GROUP, 0) > 0
    groups = HEADS // GROUP
    for group in range(groups):
        kv = group * KV // groups
        query = jnp.concatenate([queries[group * GROUP + at] for at in range(GROUP)], 0)
        key = keyval[:, pl.ds(kv * HDIM, HDIM)]
        value = keyval[:, pl.ds(kv_width + kv * HDIM, HDIM)]
        scores = jnp.where(allowed, contract_last(query, key) * HDIM**-0.5, -1e30)
        highest = jnp.max(scores, -1, keepdims=True)
        weights_exp = jnp.exp(scores - highest)
        partition = jnp.sum(weights_exp, -1, keepdims=True)
        probs = (weights_exp / partition).astype(jnp.bfloat16)
        result = jnp.dot(probs, value, preferred_element_type=jnp.float32)
        total = highest + jnp.log(partition)
        for at in range(GROUP):
            span = slice(at * tokens, (at + 1) * tokens)
            attended[:, pl.ds((group * GROUP + at) * HDIM, HDIM)] = result[span].astype(
                attended.dtype
            )
            log_total[group * GROUP + at] = total[span]

    loads[1].wait()
    for start, count in chunks(width, STEP_WIDTH):
        span = pl.ds(start, count)
        midway[:, span] = layer_in[:, span] + jnp.dot(
            attended[...], w_out[:, span], preferred_element_type=jnp.float32
        )
    scale = lax.rsqrt(jnp.mean(midway[...] * midway[...], -1, keepdims=True) + EPSILON)
    scale2[...] = scale
    normed2[...] = (midway[...] * scale * gain(1)).astype(normed2.dtype)

    pair(0, head, mine).wait_send()
    for way, go in ways:

        @pl.when(go)
        def _(way=way):
            line(way, 0, mine).wait_send()

    for hop in range(1, heads):
        for way, origin, comes, goes in arrivals(hop):

            @pl.when(comes)
            def _(way=way, origin=origin, goes=goes, hop=hop):
                here = place(section, origin)

                @pl.when(goes)
                def _():
                    line(way, hop, here).wait_send()

                pair(2 * hop - 1 + way, origin, here).wait_send()


def attention_kernel(layer, *refs):
    operands, (w_qkv_hbm, w_out_hbm, swap_in), refs = refs[:6], refs[6:9], refs[9:]
    results, swap_out, scratch, (load_sem, swap_sem) = refs[:9], refs[9], refs[10:16], refs[16:]
    section, head = lax.axis_index(SECTION), lax.axis_index(HEAD)
    heads = lax.axis_size(HEAD)
    loads = [
        pltpu.make_async_copy(w_qkv_hbm.at[layer], scratch[0], load_sem.at[0]),
        pltpu.make_async_copy(w_out_hbm.at[layer], scratch[1], load_sem.at[1]),
    ]
    for load in loads:
        load.start()

    def ready():
        barrier = pltpu.get_barrier_semaphore()
        partners = [{SECTION: 1 - section}]
        partners += [{HEAD: lax.rem(head + distance, heads)} for distance in range(1, heads)]
        for partner in partners:
            pl.semaphore_signal(barrier, 1, device_id=partner, device_id_type=MESH)
        pl.semaphore_wait(barrier, len(partners))

    swap = block_swap(swap_in, swap_out, swap_sem, head, 2)
    attention_body(layer, operands, results, scratch, loads, ready, met=swap.start)
    swap.wait()


def attention_shapes(tokens, width, kv_cols, heads, dtype):
    float32 = jnp.float32
    return (
        jax.ShapeDtypeStruct((tokens, width), dtype),
        jax.ShapeDtypeStruct((HEADS, tokens, HDIM), dtype),
        jax.ShapeDtypeStruct((2 * heads * tokens, kv_cols), dtype),
        jax.ShapeDtypeStruct((HEADS, tokens, 1), float32),
        jax.ShapeDtypeStruct((tokens, width), dtype),
        jax.ShapeDtypeStruct((tokens, width), float32),
        jax.ShapeDtypeStruct((tokens, width), dtype),
        jax.ShapeDtypeStruct((tokens, 1), float32),
        jax.ShapeDtypeStruct((tokens, 1), float32),
    )


def attention_scratch(tokens, width, qkv_cols, heads, dtype):
    dma = pltpu.SemaphoreType.DMA
    return [
        pltpu.VMEM((width, qkv_cols), dtype),
        pltpu.VMEM((width, width), dtype),
        pltpu.VMEM((tokens, qkv_cols - width), dtype),
        dma,
        dma((2, 2 * heads - 1)),
        dma((2, 2, heads)),
    ]


def attention_forward(layer, number, w_qkv, w_out, swap_in, *operands):
    heads = lax.axis_size(HEAD)
    tokens, width = operands[0].shape
    qkv_cols = w_qkv.shape[2]
    dtype = w_qkv.dtype
    vmem = pl.BlockSpec(memory_space=pltpu.VMEM)
    anywhere = pl.BlockSpec(memory_space=pl.ANY)
    return pl.pallas_call(
        functools.partial(attention_kernel, layer),
        out_shape=attention_shapes(tokens, width, qkv_cols - width, heads, dtype)
        + (jax.ShapeDtypeStruct(swap_in.shape, dtype),),
        in_specs=[vmem] * len(operands) + [anywhere] * 3,
        out_specs=(vmem,) * 9 + (anywhere,),
        scratch_shapes=attention_scratch(tokens, width, qkv_cols, heads, dtype)
        + [pltpu.SemaphoreType.DMA((2,)), pltpu.SemaphoreType.DMA((2,))],
        compiler_params=pltpu.CompilerParams(
            collective_id=number, has_side_effects=True, vmem_limit_bytes=60 * 2**20
        ),
        cost_estimate=pl.CostEstimate(
            flops=20 * tokens * width * qkv_cols,
            bytes_accessed=2 * w_out.size + 2 * w_qkv.size,
            transcendentals=0,
        ),
    )(*operands, w_qkv, w_out, swap_in)


def local_grouped(
    inputs,
    cotangent,
    norm_gains,
    qkv_weight,
    qkv_bias,
    out_weight,
    gate_weight,
    up_weight,
    down_weight,
):
    head_count = lax.axis_size(HEAD)
    wide_count = lax.axis_size(WIDE)
    section_count = lax.axis_size(SECTION)
    section = lax.axis_index(SECTION)
    head = lax.axis_index(HEAD)
    micro_count, short_len, width = inputs.shape
    half_len = short_len // section_count
    tokens = wide_count * half_len
    rows = qkv_weight.shape[1]
    query_width = HEADS * HDIM
    kv_width = KV * HDIM
    qkv_cols = qkv_weight.shape[2]
    ff_cols = gate_weight.shape[2]
    parts = section_count * head_count
    part_cols = -(-ff_cols // (parts * 128)) * 128

    def inner(array):
        split = array.shape[:-1] + (head_count, wide_count, rows)
        return jnp.swapaxes(array.reshape(split), -3, -2).reshape(array.shape)

    def outer(array):
        split = array.shape[:-1] + (wide_count, head_count, rows)
        return jnp.swapaxes(array.reshape(split), -3, -2).reshape(array.shape)

    sides = jnp.stack(
        [
            lax.dynamic_slice_in_dim(each, section * half_len, half_len, 1)
            for each in (inputs, cotangent)
        ]
    )
    mlp_parts, out_own, sides, small_own = cut_parts(
        gate_weight[0],
        up_weight[0],
        down_weight[0],
        out_weight[0],
        sides.reshape(-1, width),
        norm_gains[0],
        qkv_bias,
        parts,
        part_cols,
    )
    order = np.indices((section_count, head_count, wide_count, half_len)).reshape(4, -1)
    key_pos = (order[1] * wide_count + order[2]) * short_len + order[0] * half_len + order[3]
    half_dim = HDIM // 2
    angles = key_pos[:, None] * ROPE_BASE ** (-np.arange(half_dim) / half_dim)
    tables = np.concatenate([np.cos(angles)] * 2 + [np.sin(angles), -np.sin(angles)], 1)
    first_row = (section * head_count + head) * tokens
    own_table = lax.dynamic_slice_in_dim(jnp.asarray(tables, jnp.float32), first_row, tokens, 0)
    head_cosine, head_sine = own_table[:, :HDIM], own_table[:, HDIM:]
    key_pos = jnp.asarray(key_pos, jnp.int32)
    own_pos = lax.dynamic_slice_in_dim(key_pos, first_row, tokens, 0)
    tables = (head_cosine, -head_sine, own_pos[:, None], key_pos[None, :])

    (
        qkv_weights,
        out_weights,
        first_mlp,
        second_parts,
        tokens_in,
        last_grad,
        grad_near,
        grad_far,
        small,
        *first_attention,
    ) = start_weights(
        5,
        qkv_weight[0],
        out_own,
        mlp_parts.reshape(section_count, head_count, rows, 3 * part_cols),
        sides.reshape(2, micro_count, half_len, width),
        small_own,
        *tables,
    )
    second_mlp = lax.all_gather(second_parts, WIDE, axis=0).reshape(width, 3 * part_cols)
    mlp_weights = [first_mlp, second_mlp]

    layer_in = tokens_in.astype(jnp.float32)

    records = []
    outputs_list = []
    for layer in range(section_count):
        attention = first_attention
        if layer > 0:
            *attention, grad_mid = attention_forward(
                layer, 8, qkv_weights, out_weights, last_grad, layer_in, small, *tables
            )
        (
            normed,
            queries,
            keyval,
            log_total,
            attended,
            midway,
            normed2,
            scale_first,
            scale_second,
        ) = attention
        w_mlp = mlp_weights[layer]
        if layer == section_count - 1:
            grads = (last_grad, grad_near, grad_mid, grad_far)
            mlp_out, d_normed2, mlp_term = turning_point(normed2, w_mlp, grads, 1)
            gate_up = hidden = None
        else:
            mlp_out, normed2, gate_up, hidden = feed_forward(normed2, w_mlp, 9)
        result = midway + mlp_out
        records.append(
            (
                layer_in,
                scale_first,
                normed,
                queries,
                keyval,
                log_total,
                attended,
                midway,
                scale_second,
                normed2,
                gate_up,
                hidden,
            )
        )
        carried = result.astype(jnp.bfloat16)
        outputs_list.append(carried)
        layer_in = carried.astype(jnp.float32)

    out_grad = last_grad
    grads_list = [None] * section_count
    attention_terms = [None] * section_count
    small_terms = [None] * section_count
    for layer in reversed(range(section_count)):
        w_mlp = mlp_weights[layer]
        (
            layer_in,
            scale_first,
            normed,
            queries,
            keyval,
            log_total,
            attended,
            midway,
            scale_second,
            normed2,
            gate_up,
            hidden,
        ) = records[layer]
        if layer < section_count - 1:
            d_normed2, mlp_term = feed_backward(out_grad, w_mlp, gate_up, normed2, hidden, 3)
        mlp_term = mlp_term.reshape(wide_count, head_count, rows, -1)
        mlp_sum = lax.psum_scatter(mlp_term, WIDE, scatter_dimension=0)
        if layer == 1:
            second_sum = lax.optimization_barrier(mlp_sum)
        out_grad, small_terms[layer], attention_terms[layer], second_parts = attention_grad(
            layer,
            (4, 7)[layer],
            out_weights,
            qkv_weights,
            second_sum if layer == 0 else None,
            d_normed2,
            midway,
            scale_second,
            out_grad,
            small,
            queries,
            keyval,
            log_total,
            attended,
            normed,
            layer_in,
            scale_first,
            head_cosine,
            head_sine,
            *tables[2:],
        )
        grads_list[layer] = out_grad

    sides = jnp.stack([outer(each) for each in outputs_list + grads_list])
    totals, small_total, low_parts, high_parts, owned = finish_weights(
        *[term.reshape(wide_count * head_count, rows, -1) for term in attention_terms],
        jnp.stack(small_terms),
        mlp_sum,
        second_parts,
        sides.reshape(2 * section_count, wide_count, half_len, width),
        6,
    )
    gate_grad, up_grad, down_grad, qkv_grad, out_weight_grad, gains_grad, bias_grad = join_parts(
        low_parts, high_parts, totals, small_total, ff_cols, qkv_cols
    )
    return (
        owned[:1],
        owned[1:],
        gains_grad,
        qkv_grad,
        bias_grad,
        out_weight_grad,
        gate_grad,
        up_grad,
        down_grad,
    )


def local(inputs, *rest):
    sizes = [lax.axis_size(axis) for axis in (SECTION, HEAD, WIDE)]
    if sizes == [2, 4, 4] and inputs.shape[0] == 4:
        return local_grouped(inputs, *rest)
    return local_streamed(inputs, *rest)


def solution(mesh):
    return jax.shard_map(
        local,
        mesh=mesh,
        in_specs=(
            P(None, (HEAD, WIDE), None),
            P(None, (HEAD, WIDE), None),
            P(SECTION, None, None),
            P(SECTION, (HEAD, WIDE), None),
            P(SECTION, None),
            P(SECTION, (HEAD, WIDE), None),
            P(SECTION, (HEAD, WIDE), None),
            P(SECTION, (HEAD, WIDE), None),
            P(SECTION, (HEAD, WIDE), None),
        ),
        out_specs=(
            P(SECTION, None, (HEAD, WIDE), None),
            P(SECTION, None, (HEAD, WIDE), None),
            P(SECTION, None, None),
            P(SECTION, (HEAD, WIDE), None),
            P(SECTION, None),
            P(SECTION, (HEAD, WIDE), None),
            P(SECTION, (HEAD, WIDE), None),
            P(SECTION, (HEAD, WIDE), None),
            P(SECTION, (HEAD, WIDE), None),
        ),
        check_vma=False,
    )
```
